32 devices in a mesh: grp: 4 (over y, x), sub: 8 (over z, core).
Axes of the slice: x: 2, y: 2, z: 4, core: 2. Of those that a mesh axis runs over, the one named last changes fastest.
Arguments:
- populations: float32 [19, 16, 32, 384], P(None, 'sub', 'grp')
- heat_pops: float32 [7, 16, 32, 384], P(None, 'sub', 'grp')
- solid_frac: float32 [16, 32, 384], P('sub', 'grp'), may hold values from 0 to 0.5
- coupled_grid_point: int32 [4, 4096], P('grp', 'sub'), may hold values from 0 to 6143
- dest_index: int32 [4, 4096, 1], P('grp', 'sub'), may hold values from 0 to 7; in each aligned block of 512 rows (0 to 511, 512 to 1023, ..., all dimensions but the last counted through in order) at most 128 rows name the same one
- heat_coeff: float32 [4, 4096], P('grp', 'sub'), may hold values from 0.5 to 2
- slot_node: int32 [4, 8192], P('grp', 'sub'), may hold values from 0 to 1023
- node_diag: float32 [4, 64, 128], P('grp', 'sub'), may hold values from 2.5 to 5
- coupling: float32 [4, 64, 128, 128], P('grp', 'sub'), may hold values from 0 to 0.0078125
- block_pattern: int32 [4, 64], P('grp', 'sub'), may hold values from 0 to 7, as said below
- heat_source: float32 [4, 64, 128], P('grp', 'sub')
- solid_start: float32 [4, 64, 128], P('grp', 'sub'), may hold values from -6 to 6
Outputs:
- gas_hotness_after: float32 [16, 32, 384], P('sub', 'grp')
- gas_motion_amount: float32 [3, 16, 32, 384], P(None, 'sub', 'grp')
- solid_temp: float32 [4, 64, 128], P('grp', 'sub')
- fibre_surface_hotness: float32 [4, 4096], P('grp', 'sub')
The draws below stay inside these ranges and needn't reach their ends.
Inputs may be any that keep to these rules, and one draw needn't show every extreme that they name: `dest_index`: among one device's rows, no owner is named by more than 128 rows, a bound that some block reaches. `block_pattern`: on each device, block b's partner is (b + t) mod 8 for one shift t of 0 to 7 of that device, so every block is the partner of exactly one block.
All inputs are finite; a program needn't handle non-finite values.
Results may differ from the reference program's by a relative error of at most 0.0003.
Values sent between devices are 32-bit elements; how exact they have to be, the bound alone decides.
No kernel may reach another device: no remote copies, remote signals or barrier semaphores. Data moves between devices by JAX's collectives and lax.ppermute only.
A program may use at most 64 MiB of HBM per device.

```python
import math
import jax
import jax.numpy as jnp
import numpy as np
from jax import lax

CX = 8
CY = 384
CZ = 2
NB = 8
CORE_MESH_PIECE = 128
ROWS_DEV = 512
STEPS = 2
ITERS = 2
LATERAL_BANDS = 4
SLABS = 8
NZ = 16
NX = 32
CAP = 128
COUPLED_ENTRIES = 4096
PIECES_PER_BAND = 64


flow_lift = np.array([0, 0, 0, 0, 0, 1, -1, 0, 0, 0, 0, 1, -1, -1, 1, 1, -1, -1, 1], dtype=np.float32)


lattice_share = np.array([1.0 / 3.0] + [1.0 / 18.0] * 6 + [1.0 / 36.0] * 12, dtype=np.float32)


thermal_share = np.array([0.25] + [0.125] * 6, dtype=np.float32)


def draw_populations(key, part):
    shape = (19, NZ, NX, CY)
    base = jax.random.uniform(key, shape, jnp.float32, 0.85, 1.15)
    lift = 0.15
    tilt = lift * jnp.asarray(flow_lift)[:, None, None, None]
    weights = jnp.asarray(lattice_share)[:, None, None, None]
    return (weights * (base + tilt)).astype(jnp.float32)


def draw_heat_pops(key, part):
    first = jax.random.fold_in(key, 11)
    second = jax.random.fold_in(key, 12)
    level = jax.random.uniform(first, (1, NZ, NX, CY), jnp.float32, 0.5, 1.5)
    rough = jax.random.uniform(second, (7, NZ, NX, CY), jnp.float32, 0.9, 1.1)
    return (jnp.asarray(thermal_share)[:, None, None, None] * level * rough).astype(jnp.float32)


def draw_heat_source(key, part):
    noise = jax.random.normal(key, (LATERAL_BANDS, PIECES_PER_BAND, CORE_MESH_PIECE), jnp.float32)
    device = jnp.arange(LATERAL_BANDS)[:, None] * SLABS + jnp.arange(PIECES_PER_BAND)[None, :] // NB
    frac = device.astype(jnp.float32) / (LATERAL_BANDS * SLABS - 1)
    scale = 3.0 ** frac
    return (scale[:, :, None] * noise).astype(jnp.float32)


def draw_block_pattern(key, part):
    shift = jax.random.randint(jax.random.fold_in(key, 21), (LATERAL_BANDS, SLABS, 1), 0, NB)
    blocks = jnp.arange(NB, dtype=jnp.int32)[None, None, :]
    return ((blocks + shift) % NB).reshape(LATERAL_BANDS, PIECES_PER_BAND).astype(jnp.int32)


def set_ends(values, own_key, smallest, largest):
    longest = values.shape.index(max(values.shape))
    spots = []
    for shift in (0, 1):
        where = [jax.random.randint(jax.random.fold_in(own_key, axis), (), 0, length) for axis, length in enumerate(values.shape)]
        where[longest] = (where[longest] + shift) % values.shape[longest]
        spots.append(tuple(where))
    return values.at[spots[0]].set(smallest).at[spots[1]].set(largest)


def shard_levels(rng, shape, shards, smallest, largest):
    loudness = 1.0
    for axis_at, shards_of in shards:
        draws = jax.random.uniform(jax.random.fold_in(jax.random.fold_in(rng, 6), axis_at), (shards_of,), jnp.float32, smallest / len(shards), largest / len(shards))
        loudness = loudness * jnp.repeat(jnp.exp(draws), shape[axis_at] // shards_of).reshape((-1,) + (1,) * (len(shape) - 1 - axis_at))
    return loudness


def routed_block(own_key, own, number, rows, count, top, bound, slope):
    sequence = jax.random.permutation(own_key, count)
    heavy_load, ordinary = shares(count, rows * top, bound, slope, True), shares(count, rows * top, bound, slope, False)
    places = jnp.arange(count)

    def named(lengths, offset_by):
        used = int((lengths > 0).sum())
        fixed = max(1, used // 4)
        shifted = fixed + (places - fixed + offset_by * (used - fixed)) % max(1, count - fixed)
        return jnp.zeros((count,), jnp.int32).at[sequence[jnp.where(places < fixed, places, shifted)]].set(jnp.asarray(lengths, jnp.int32))

    lengths = jnp.where(number % 4 == 0, named(heavy_load, number // 4), named(ordinary, number - number // 4 - 1))
    mixed = jax.random.permutation(jax.random.fold_in(own, 3), count)
    source_of, sink = mixed[0:count // 2 * 2:2], mixed[1:count // 2 * 2:2]
    slack = jnp.minimum(lengths[source_of] - 1, bound - lengths[sink]) // 2
    slack = jnp.where((source_of == sequence[0]) | (sink == sequence[0]) | (lengths[sink] == 0), 0, jnp.maximum(slack, 0))
    shifted = jax.random.randint(jax.random.fold_in(own, 4), (count // 2,), 0, 1 << 20) % (slack + 1)
    lengths = lengths.at[source_of].add(-shifted).at[sink].add(shifted)
    members = jnp.searchsorted(jnp.cumsum(lengths), jnp.arange(rows * top), side="right").astype(jnp.int32)
    listing = members.reshape(top, rows).T
    listing = listing[jax.random.permutation(jax.random.fold_in(own, 1), rows)]
    offset_by = jax.random.randint(jax.random.fold_in(own, 2), (rows, 1), 0, top)
    return jnp.take_along_axis(listing, (jnp.arange(top)[None, :] + offset_by) % top, axis=1)


def shares(amount, total, reach, slope, full):
    portions = [(1 << 20) // math.isqrt(standing ** slope) + 1 for standing in range(1, amount + 1)]
    largest = reach if full else min(reach, max(-(-total // amount), total * portions[0] // sum(portions)))
    least = 1 if total - largest >= amount - 1 else 0
    given, spare = [largest] + [least] * (amount - 1), total - largest - least * (amount - 1)
    while spare > 0:
        candidates = [i for i in range(1, amount) if given[i] < largest] or [i for i in range(1, amount) if given[i] < reach]
        whole, remaining = sum([portions[i] for i in candidates]), spare
        for i in candidates:
            extra = min(reach - given[i], max(1, remaining * portions[i] // whole), spare)
            given[i] = given[i] + extra
            spare = spare - extra
    return np.array(given)


def gaussian(rng, dims, width, most, pieces=(), kind=jnp.bfloat16):
    gain = shard_levels(rng, dims, pieces, -0.22, 0.18) if pieces else 1.0
    entries = jax.random.normal(rng, dims, jnp.float32) * width * gain
    return jnp.minimum(jnp.maximum(entries, -most), most).astype(kind)


def setup_inputs(seed: int = 0) -> dict:
    splits = jax.random.split(jax.random.key(seed), 13)
    populations = draw_populations(jax.random.fold_in(splits[12], 71), 0)
    heat_pops = draw_heat_pops(jax.random.fold_in(splits[12], 71), 0)
    solid_frac = jnp.clip(0.5 * jax.random.uniform(splits[2], (NZ, NX, CY), jnp.float32) ** shard_levels(splits[2], (NZ, NX, CY), ((0, 8), (1, 4)), -0.2, 0.2), 0.0, 0.5)
    coupled_grid_point = set_ends(jax.random.randint(splits[3], (LATERAL_BANDS, COUPLED_ENTRIES), 0, CZ * CX * CY), jax.random.fold_in(splits[3], 1), 0, (CZ * CX * CY) - 1).astype(jnp.int32)
    dest_index_keys = jax.random.split(jax.random.fold_in(splits[4], 1), LATERAL_BANDS * COUPLED_ENTRIES // ROWS_DEV)
    dest_index_turns = jax.random.permutation(jax.random.fold_in(splits[4], 3), LATERAL_BANDS * COUPLED_ENTRIES // ROWS_DEV)
    dest_index = jax.vmap(lambda own, number: routed_block(jax.random.fold_in(splits[4], 2), own, number, ROWS_DEV, SLABS, 1, CAP, 2))(dest_index_keys, dest_index_turns).reshape((LATERAL_BANDS, COUPLED_ENTRIES, 1))
    heat_coeff = jnp.clip(jnp.exp(math.log(2.0) - 1.3862944 * jax.random.uniform(splits[5], (LATERAL_BANDS, COUPLED_ENTRIES), jnp.float32) ** shard_levels(splits[5], (LATERAL_BANDS, COUPLED_ENTRIES), ((0, 4), (1, 8)), -0.2, 0.2)), 0.5, 2.0)
    slot_node = set_ends(jax.random.randint(splits[6], (LATERAL_BANDS, SLABS * SLABS * CAP), 0, NB * CORE_MESH_PIECE), jax.random.fold_in(splits[6], 1), 0, (NB * CORE_MESH_PIECE) - 1).astype(jnp.int32)
    node_diag = jnp.clip(2.5 + 2.5 * jax.random.uniform(splits[7], (LATERAL_BANDS, PIECES_PER_BAND, CORE_MESH_PIECE), jnp.float32) ** shard_levels(splits[7], (LATERAL_BANDS, PIECES_PER_BAND, CORE_MESH_PIECE), ((0, 4), (1, 8)), -0.2, 0.2), 2.5, 5.0)
    coupling = jnp.clip(0.0078125 * jax.random.uniform(splits[8], (LATERAL_BANDS, PIECES_PER_BAND, CORE_MESH_PIECE, CORE_MESH_PIECE), jnp.float32) ** shard_levels(splits[8], (LATERAL_BANDS, PIECES_PER_BAND, CORE_MESH_PIECE, CORE_MESH_PIECE), ((0, 4), (1, 8)), -0.2, 0.2), 0.0, 0.0078125)
    block_pattern = draw_block_pattern(jax.random.fold_in(splits[12], 71), 0)
    heat_source = draw_heat_source(jax.random.fold_in(splits[12], 71), 0)
    solid_start = gaussian(splits[11], (LATERAL_BANDS, PIECES_PER_BAND, CORE_MESH_PIECE), 1.0, 6.0, ((0, 4), (1, 8)), jnp.float32)
    return {"populations": populations, "heat_pops": heat_pops, "solid_frac": solid_frac, "coupled_grid_point": coupled_grid_point, "dest_index": dest_index, "heat_coeff": heat_coeff, "slot_node": slot_node, "node_diag": node_diag, "coupling": coupling, "block_pattern": block_pattern, "heat_source": heat_source, "solid_start": solid_start}


flow_velocity = np.array([[0, 0, 0], [1, 0, 0], [-1, 0, 0], [0, 1, 0], [0, -1, 0], [0, 0, 1], [0, 0, -1], [1, 1, 0], [-1, -1, 0], [1, -1, 0], [-1, 1, 0], [1, 0, 1], [-1, 0, -1], [1, 0, -1], [-1, 0, 1], [0, 1, 1], [0, -1, -1], [0, 1, -1], [0, -1, 1]], dtype=np.int32)
flow_weight = np.array([1.0 / 3.0] + [1.0 / 18.0] * 6 + [1.0 / 36.0] * 12)
flow_opposite = np.array([0, 2, 1, 4, 3, 6, 5, 8, 7, 10, 9, 12, 11, 14, 13, 16, 15, 18, 17], dtype=np.int32)
heat_velocity = flow_velocity[:7]
heat_weight = np.array([0.25] + [0.125] * 6)
tau_flow = 0.8
tau_heat = 0.7
highest = lax.Precision.HIGHEST


def flow_moments(flow):
    lattice = jnp.asarray(flow_velocity, flow.dtype)
    return jnp.tensordot(lattice, flow, axes=(0, 0), precision=highest)


def collide(flow, caloric_population, solidity):
    lattice = jnp.asarray(flow_velocity, flow.dtype)
    density = jnp.sum(flow, axis=0)
    velocity_field = flow_moments(flow) / density
    speed_square = jnp.sum(velocity_field * velocity_field, axis=0)
    projected = jnp.tensordot(lattice, velocity_field, axes=(1, 0), precision=highest)
    weights = jnp.asarray(flow_weight, flow.dtype)[:, None, None, None]
    balance = weights * density * (1.0 + 3.0 * projected + 4.5 * projected * projected - 1.5 * speed_square)
    flow_post = (1.0 - solidity) * (flow - (flow - balance) / tau_flow) + solidity * flow[flow_opposite]
    stream_hotness = jnp.sum(caloric_population, axis=0)
    heat_lattice = jnp.asarray(heat_velocity, flow.dtype)
    caloric_moment_reduce = jnp.tensordot(heat_lattice, velocity_field, axes=(1, 0), precision=highest)
    caloric_stencil_shares = jnp.asarray(heat_weight, flow.dtype)[:, None, None, None]
    conserved_power_ledger = caloric_stencil_shares * stream_hotness * (1.0 + 4.0 * caloric_moment_reduce)
    heat_post = caloric_population - (caloric_population - conserved_power_ledger) / tau_heat
    return flow_post, heat_post


def collide_all(flow, caloric_population, solidity):
    def layer_block(slab, carry):
        flow_out, heat_out = carry
        start = (slab * CZ).astype(jnp.int32)
        flow_part = lax.dynamic_slice_in_dim(flow, start, CZ, 1)
        heat_part = lax.dynamic_slice_in_dim(caloric_population, start, CZ, 1)
        solid_part = lax.dynamic_slice_in_dim(solidity, start, CZ, 0)
        flow_post, heat_post = collide(flow_part, heat_part, solid_part)
        flow_out = lax.dynamic_update_slice_in_dim(flow_out, flow_post, start, 1)
        heat_out = lax.dynamic_update_slice_in_dim(heat_out, heat_post, start, 1)
        return flow_out, heat_out

    return lax.fori_loop(0, SLABS, layer_block, (jnp.zeros_like(flow), jnp.zeros_like(caloric_population)))


def stream_all(post, velocity):
    lanes = []
    for lane in range(post.shape[0]):
        step_x, step_y, step_z = velocity[lane]
        lanes.append(jnp.roll(post[lane], (int(step_z), int(step_x), int(step_y)), axis=(0, 1, 2)))
    return jnp.stack(lanes)


def apply_solid(vector, diagonal, coupling, picker):
    partner = jnp.einsum('csbd,csdk->csbk', picker, vector, precision=highest)
    forward = jnp.einsum('csbij,csbj->csbi', coupling, partner, precision=highest)
    backward_terms = jnp.einsum('csbji,csbj->csbi', coupling, vector, precision=highest)
    backward = jnp.einsum('csbd,csbk->csdk', picker, backward_terms, precision=highest)
    return diagonal * vector - forward - backward


def reference(populations, heat_pops, solid_frac, coupled_grid_point, dest_index, heat_coeff, slot_node, node_diag, coupling, block_pattern, heat_source, solid_start):
    flow = populations
    caloric_population = heat_pops
    for step in range(STEPS):
        flow_post, heat_post = collide_all(flow, caloric_population, solid_frac)
        flow = stream_all(flow_post, flow_velocity)
        caloric_population = stream_all(heat_post, heat_velocity)
    gas_hotness_after = jnp.sum(caloric_population, axis=0)
    gas_motion_amount = flow_moments(flow)
    band_identifiers = jnp.arange(LATERAL_BANDS, dtype=jnp.int32)[:, None, None]
    plate_identifiers = jnp.arange(SLABS, dtype=jnp.int32)[None, :, None]
    temp_rows = gas_hotness_after.reshape(SLABS, CZ, LATERAL_BANDS, CX, CY).transpose(2, 0, 1, 3, 4).reshape(LATERAL_BANDS, SLABS, CZ * CX * CY)
    voxels = coupled_grid_point.reshape(LATERAL_BANDS, SLABS, ROWS_DEV).astype(jnp.int32)
    coupling_conductivities = heat_coeff.reshape(LATERAL_BANDS, SLABS, ROWS_DEV)
    interface_flux_rows = coupling_conductivities * jnp.take_along_axis(temp_rows, voxels, axis=2)
    aimed_entry = dest_index.reshape(LATERAL_BANDS, SLABS, ROWS_DEV).astype(jnp.int32)
    member = (aimed_entry[..., None] == jnp.arange(SLABS, dtype=jnp.int32)).astype(jnp.int32)
    current_place = jnp.sum((jnp.cumsum(member, axis=2) - member) * member, axis=3).astype(jnp.int32)
    opening_ordinal = aimed_entry * CAP + current_place
    send_flux = jnp.zeros((LATERAL_BANDS, SLABS, SLABS * CAP), interface_flux_rows.dtype).at[band_identifiers, plate_identifiers, opening_ordinal].set(interface_flux_rows)
    send_coeff = jnp.zeros((LATERAL_BANDS, SLABS, SLABS * CAP), coupling_conductivities.dtype).at[band_identifiers, plate_identifiers, opening_ordinal].set(coupling_conductivities)
    recv_flux = send_flux.reshape(LATERAL_BANDS, SLABS, SLABS, CAP).transpose(0, 2, 1, 3).reshape(LATERAL_BANDS, SLABS, SLABS * CAP)
    recv_coeff = send_coeff.reshape(LATERAL_BANDS, SLABS, SLABS, CAP).transpose(0, 2, 1, 3).reshape(LATERAL_BANDS, SLABS, SLABS * CAP)
    node_index = slot_node.reshape(LATERAL_BANDS, SLABS, SLABS * CAP).astype(jnp.int32)
    added_source = jnp.zeros((LATERAL_BANDS, SLABS, NB * CORE_MESH_PIECE), recv_flux.dtype).at[band_identifiers, plate_identifiers, node_index].add(recv_flux)
    added_diag = jnp.zeros((LATERAL_BANDS, SLABS, NB * CORE_MESH_PIECE), recv_coeff.dtype).at[band_identifiers, plate_identifiers, node_index].add(recv_coeff)
    shape4 = (LATERAL_BANDS, SLABS, NB, CORE_MESH_PIECE)
    diagonal = node_diag.reshape(shape4) + added_diag.reshape(shape4)
    right_side = heat_source.reshape(shape4) + added_source.reshape(shape4)
    blocks = coupling.reshape(LATERAL_BANDS, SLABS, NB, CORE_MESH_PIECE, CORE_MESH_PIECE)
    pattern = block_pattern.reshape(LATERAL_BANDS, SLABS, NB).astype(jnp.int32)
    picker = (pattern[..., None] == jnp.arange(NB, dtype=jnp.int32)).astype(node_diag.dtype)
    conduction_approximant = solid_start.reshape(shape4)
    residual = right_side - apply_solid(conduction_approximant, diagonal, blocks, picker)
    direction = residual
    norm_now = jnp.sum(residual * residual)
    for step in range(ITERS):
        image = apply_solid(direction, diagonal, blocks, picker)
        step_size = norm_now / jnp.sum(direction * image)
        conduction_approximant = conduction_approximant + step_size * direction
        residual = residual - step_size * image
        norm_next = jnp.sum(residual * residual)
        direction = residual + (norm_next / norm_now) * direction
        norm_now = norm_next
    opening_hotness = jnp.take_along_axis(conduction_approximant.reshape(LATERAL_BANDS, SLABS, NB * CORE_MESH_PIECE), node_index, axis=2).reshape(LATERAL_BANDS, SLABS, SLABS, CAP)
    fibre_surface_hotness = opening_hotness[band_identifiers, aimed_entry, plate_identifiers, current_place]
    return gas_hotness_after, gas_motion_amount, conduction_approximant.reshape(LATERAL_BANDS, PIECES_PER_BAND, CORE_MESH_PIECE), fibre_surface_hotness.reshape(LATERAL_BANDS, COUPLED_ENTRIES)
```

```python
import functools
import jax
import jax.numpy as jnp
import numpy as np
from jax import lax
from jax.experimental import pallas as pl
from jax.experimental.pallas import tpu as pltpu
from jax.sharding import PartitionSpec as P

FLOW_VELOCITY = [
    (0, 0, 0),
    (1, 0, 0),
    (-1, 0, 0),
    (0, 1, 0),
    (0, -1, 0),
    (0, 0, 1),
    (0, 0, -1),
    (1, 1, 0),
    (-1, -1, 0),
    (1, -1, 0),
    (-1, 1, 0),
    (1, 0, 1),
    (-1, 0, -1),
    (1, 0, -1),
    (-1, 0, 1),
    (0, 1, 1),
    (0, -1, -1),
    (0, 1, -1),
    (0, -1, 1),
]
VELOCITY = FLOW_VELOCITY + FLOW_VELOCITY[:7]
FLOWS, HEATS = 19, 7
LANES_ALL = range(FLOWS + HEATS)
UP = [i for i in LANES_ALL if VELOCITY[i][2] == 1]
DOWN = [i for i in LANES_ALL if VELOCITY[i][2] == -1]
RIGHT = [i for i in LANES_ALL if VELOCITY[i][0] == 1]
LEFT = [i for i in LANES_ALL if VELOCITY[i][0] == -1]
STILL = [i for i in LANES_ALL if VELOCITY[i][0] == 0]
FACE_RIGHT = STILL + RIGHT
FACE_LEFT = STILL + LEFT
FACE = len(FACE_RIGHT) + len(RIGHT) + 1
WIDTH = 128
f32 = jnp.float32
bf16 = jnp.bfloat16


def signed_sum(terms):
    total = None
    for sign, term in terms:
        if sign == 0:
            continue
        if total is None:
            total = term if sign > 0 else -term
        else:
            total = total + term if sign > 0 else total - term
    return total


def collide(flow, heat, solid):
    pairs = range(1, FLOWS, 2)
    density = flow[0]
    for i in pairs:
        density = density + (flow[i] + flow[i + 1])
    gaps = {i: flow[i] - flow[i + 1] for i in pairs}
    scale = 1.0 / density
    speed = [
        signed_sum([(FLOW_VELOCITY[i][axis], gaps[i]) for i in pairs]) * scale for axis in range(3)
    ]
    square = speed[0] * speed[0] + speed[1] * speed[1] + speed[2] * speed[2]
    base = 1.0 - 1.5 * square
    gas = 1.0 - solid
    keep = gas * (1.0 - 1.0 / 0.8)
    pull = gas * (density * (1.0 / 0.8))
    flow_post = [None] * FLOWS
    flow_post[0] = (keep + solid) * flow[0] + (pull * (1.0 / 3.0)) * base
    shares = {1: pull * (1.0 / 18.0), 2: pull * (1.0 / 36.0)}
    for i in pairs:
        share = shares[sum(abs(c) for c in FLOW_VELOCITY[i])]
        along = signed_sum([(FLOW_VELOCITY[i][axis], speed[axis]) for axis in range(3)])
        even = base + 4.5 * along * along
        odd = 3.0 * along
        flow_post[i] = keep * flow[i] + share * (even + odd) + solid * flow[i + 1]
        flow_post[i + 1] = keep * flow[i + 1] + share * (even - odd) + solid * flow[i]
    hotness = heat[0]
    for j in range(1, HEATS):
        hotness = hotness + heat[j]
    stay = 1.0 - 1.0 / 0.7
    heat_post = [stay * heat[0] + (0.25 / 0.7) * hotness]
    level = (0.125 / 0.7) * hotness
    for j in range(1, HEATS, 2):
        axis = (j - 1) // 2
        drift = 4.0 * speed[axis]
        heat_post.append(stay * heat[j] + level * (1.0 + drift))
        heat_post.append(stay * heat[j + 1] + level * (1.0 - drift))
    return flow_post + heat_post


def three_parts(value):
    high = value.astype(bf16).astype(f32)
    rest = value - high
    middle = rest.astype(bf16).astype(f32)
    return [high, middle, rest - middle]


def times_transposed(left, right):
    return lax.dot_general(
        left.astype(bf16), right.astype(bf16), (((1,), (1,)), ((), ())), preferred_element_type=f32
    )


def spread(row):
    return jnp.broadcast_to(row, (8, row.shape[-1]))


def lane_gather(row, lane):
    return jnp.take_along_axis(spread(row), lane, axis=1, mode="promise_in_bounds")


def table_gather(table, index):
    place, lane = index >> 7, index & 127
    out = jnp.zeros(index.shape, f32)
    for row in range(table.shape[0]):
        out = jnp.where(place == row, lane_gather(table[row : row + 1], lane), out)
    return out


def stacked(row):
    return jnp.concatenate(
        [row[:, k * WIDTH : (k + 1) * WIDTH] for k in range(row.shape[1] // WIDTH)], axis=0
    )


def first_kernel(
    cap, pops, heat, solid, voxel, dest, coeff, post, up, down, face_r, face_l, ordinal
):
    layers, across, along = solid.shape
    for z in range(layers):
        for start in range(0, along, WIDTH):
            lanes = slice(start, start + WIDTH)
            out = collide(
                [pops[i, z, :, lanes] for i in range(FLOWS)],
                [heat[j, z, :, lanes] for j in range(HEATS)],
                solid[z, :, lanes],
            )
            for i in LANES_ALL:
                post[i, z, :, lanes] = out[i]
            if z == layers - 1:
                for n, i in enumerate(UP):
                    up[n, :, lanes] = out[i]
            if z == 0:
                for n, i in enumerate(DOWN):
                    down[n, :, lanes] = out[i]
            for face, lists, near, far in (
                (face_r, (STILL, RIGHT), across - 1, across - 2),
                (face_l, (STILL, LEFT), 0, 1),
            ):
                rows = [(i, near) for i in lists[0]] + [(i, far) for i in lists[1]]
                rows = rows + [(i, near) for i in lists[1]]
                for n, (i, column) in enumerate(rows):
                    at = n * layers + z
                    face[at : at + 1, lanes] = out[i][column : column + 1]
                at = len(rows) * layers + z
                face[at : at + 1, lanes] = solid[z, near : near + 1, lanes]
    rows_here = dest.shape[1]
    owner = dest[...].astype(f32)
    chunks = rows_here // WIDTH
    tall = stacked(owner)
    tall = jnp.concatenate([tall] + [jnp.zeros((8 - chunks, WIDTH), f32)] * (chunks < 8), axis=0)
    upright = tall.T
    first = lax.broadcasted_iota(jnp.int32, (WIDTH, WIDTH), 0)
    second = lax.broadcasted_iota(jnp.int32, (WIDTH, WIDTH), 1)
    slot_row = lax.broadcasted_iota(jnp.int32, (8, WIDTH), 0)
    table = jnp.zeros((40, WIDTH), f32)
    for c in range(chunks):
        lanes = slice(c * WIDTH, (c + 1) * WIDTH)
        here = owner[:, lanes]
        count = jnp.zeros((WIDTH, WIDTH), f32)
        for other in range(c + 1):
            same = upright[:, other : other + 1] == here
            if other == c:
                same = same & (first < second)
            count = count + jnp.where(same, 1.0, 0.0)
        rank = jnp.sum(count, axis=0, keepdims=True)
        place = (here * float(cap) + rank).astype(jnp.int32)
        ordinal[:, lanes] = place
        mine = slot_row == (place >> 7)
        spot = voxel[:, lanes]
        parts = [(spot >> 7).astype(f32), (spot & 127).astype(f32)] + three_parts(coeff[:, lanes])
        values = jnp.concatenate([jnp.where(mine, part, 0.0) for part in parts], axis=0)
        table = table + times_transposed(values, jnp.where(first == (place & 127), 1.0, 0.0))
    spots = table[0:8] * float(WIDTH) + table[8:16]
    coeffs = (table[16:24] + table[24:32]) + table[32:40]
    extra = len(UP)
    for plane in (up, down):
        plane[extra] = jnp.zeros(plane.shape[1:], f32)
        plane[extra, :, 0:WIDTH] = spots
        plane[extra, :, WIDTH : 2 * WIDTH] = coeffs


def edge_kernel(layers, face_r, face_l, below, above, out_r, out_l):
    out_r[...] = face_r[...]
    out_l[...] = face_l[...]
    across = below.shape[1]
    for out, lists, near, far in (
        (out_r, (STILL, RIGHT), across - 1, across - 2),
        (out_l, (STILL, LEFT), 0, 1),
    ):
        rows = [(i, near) for i in lists[0]] + [(i, far) for i in lists[1]]
        rows = rows + [(i, near) for i in lists[1]]
        for n, (i, column) in enumerate(rows):
            rise = VELOCITY[i][2]
            if rise == 0:
                continue
            moved = range(layers - 1, 0, -1) if rise == 1 else range(layers - 1)
            for z in moved:
                at, source = n * layers + z, n * layers + z - rise
                out[at : at + 1, :] = out[source : source + 1, :]
            z = 0 if rise == 1 else layers - 1
            at = n * layers + z
            if rise == 1:
                out[at : at + 1, :] = below[UP.index(i), column : column + 1, :]
            else:
                out[at : at + 1, :] = above[DOWN.index(i), column : column + 1, :]


def turned(tile, step):
    return tile if step == 0 else pltpu.roll(tile, step % tile.shape[1], 1)


def second_kernel(
    post,
    below,
    above,
    own_r,
    own_l,
    from_l,
    from_r,
    solid,
    own_table,
    hot,
    motion,
    send_up,
    send_down,
    fluxes,
    moved,
    halo,
):
    layers, across, along = solid.shape
    slot = lax.broadcasted_iota(jnp.int32, (across, along), 0)
    inner = len(FACE_RIGHT)
    for i in LANES_ALL:
        ex, ey, ez = VELOCITY[i]
        for z in range(layers):
            if z - ez < 0:
                tile = below[UP.index(i)]
            elif z - ez >= layers:
                tile = above[DOWN.index(i)]
            else:
                tile = post[i, z - ez]
            if ex == 1:
                at = (inner + RIGHT.index(i)) * layers + z
                tile = jnp.where(slot == 0, from_l[at : at + 1, :], pltpu.roll(tile, 1, 0))
            elif ex == -1:
                at = (inner + LEFT.index(i)) * layers + z
                tile = jnp.where(
                    slot == across - 1, from_r[at : at + 1, :], pltpu.roll(tile, across - 1, 0)
                )
            moved[i, z] = turned(tile, ey)
        if ex == -1:
            at = (inner + LEFT.index(i)) * layers
            low = own_l[at : at + layers, :]
        else:
            at = FACE_RIGHT.index(i) * layers
            low = from_l[at : at + layers, :]
        if ex == 1:
            at = (inner + RIGHT.index(i)) * layers
            high = own_r[at : at + layers, :]
        else:
            at = FACE_LEFT.index(i) * layers
            high = from_r[at : at + layers, :]
        sides = [low, high]
        if 2 * layers < 8:
            sides.append(jnp.ones((8 - 2 * layers, along), f32))
        halo[i] = turned(jnp.concatenate(sides, axis=0), ey)
    at = (FACE - 1) * layers
    edge_solid = [from_l[at : at + layers, :], from_r[at : at + layers, :]]
    if 2 * layers < 8:
        edge_solid.append(jnp.zeros((8 - 2 * layers, along), f32))
    edge_solid = jnp.concatenate(edge_solid, axis=0)
    for start in range(0, along, WIDTH):
        lanes = slice(start, start + WIDTH)
        for z in range(layers):
            out = collide(
                [moved[i, z, :, lanes] for i in range(FLOWS)],
                [moved[FLOWS + j, z, :, lanes] for j in range(HEATS)],
                solid[z, :, lanes],
            )
            for i in LANES_ALL:
                moved[i, z, :, lanes] = out[i]
        out = collide(
            [halo[i, :, lanes] for i in range(FLOWS)],
            [halo[FLOWS + j, :, lanes] for j in range(HEATS)],
            edge_solid[:, lanes],
        )
        for i in RIGHT + LEFT:
            halo[i, :, lanes] = out[i]
    sums = {}

    def add(key, sign, tile):
        if sign == 0:
            return
        if key in sums:
            sums[key] = sums[key] + tile if sign > 0 else sums[key] - tile
        else:
            sums[key] = tile if sign > 0 else -tile

    for z in range(layers):
        for i in LANES_ALL:
            ex, ey, ez = VELOCITY[i]
            if i == 0:
                continue
            tile = moved[i, z]
            if ex == 1:
                tile = jnp.where(slot == 0, halo[i, z : z + 1, :], pltpu.roll(tile, 1, 0))
            elif ex == -1:
                at = layers + z
                tile = jnp.where(
                    slot == across - 1, halo[i, at : at + 1, :], pltpu.roll(tile, across - 1, 0)
                )
            tile = turned(tile, ey)
            target = z + ez
            if i >= FLOWS:
                add((3, target), 1, tile)
            else:
                add((0, target), ex, tile)
                add((1, target), ey, tile)
                add((2, target), ez, tile)
    for z in range(layers):
        hot[z] = sums[3, z]
        for axis in range(3):
            motion[axis, z] = sums[axis, z]
    for part in range(4):
        send_up[part] = sums[part, layers]
        send_down[part] = sums[part, -1]
    extra = len(UP)
    per_line = along // WIDTH
    per_layer = across * per_line

    def flux(table, planes):
        index = table[:, 0:WIDTH].astype(jnp.int32)
        place, lane = index >> 7, index & 127
        out = jnp.zeros(lane.shape, f32)
        for z, plane in planes:
            for x in range(across):
                for c in range(per_line):
                    row = plane[x : x + 1, c * WIDTH : (c + 1) * WIDTH]
                    out = jnp.where(
                        place == z * per_layer + x * per_line + c, lane_gather(row, lane), out
                    )
        return out * table[:, WIDTH : 2 * WIDTH]

    mine = own_table[extra]
    fluxes[:, 0, :] = flux(mine, [(z, sums[3, z]) for z in range(layers)])
    fluxes[:, 1, :] = flux(above[extra], [(0, sums[3, layers])])
    fluxes[:, 2, :] = flux(below[extra], [(layers - 1, sums[3, -1])])
    fluxes[:, 3, :] = mine[:, WIDTH : 2 * WIDTH]


def coupled(vector, blocks, flipped, shift):
    count = vector.shape[0]
    upright = vector.T
    ahead, back = [], []
    for b in range(count):
        column = upright[:, b : b + 1]
        back.append(jnp.sum(blocks[b] * column, axis=0, keepdims=True))
        ahead.append(jnp.sum(flipped[b] * column, axis=0, keepdims=True))
    ahead = jnp.concatenate(ahead, axis=0)
    back = jnp.concatenate(back, axis=0)
    return pltpu.roll(ahead, lax.rem(count - shift, count), 0) + pltpu.roll(back, shift, 0)


def ready_kernel(pattern, nodes, diagonal, source, start, coupling, hits, flipped, rest, slots):
    shift = pattern[0, 0]
    count = start.shape[1]
    for b in range(count):
        flipped[lax.rem(b + shift, count)] = coupling[0, b].T
    vector = start[0]
    rest[...] = (
        source[0] - diagonal[0] * vector + coupled(vector, coupling.at[0], flipped, shift)
    )
    index = nodes[...]
    depth = lax.broadcasted_iota(jnp.int32, (WIDTH, index.shape[1]), 0)
    hits[...] = jnp.where(depth == (index & 127), 1.0, 0.0).astype(bf16)
    slots[...] = table_gather(vector, stacked(index))


def solve_kernel(
    cap, pattern, nodes, diagonal, start, coupling, hits, flipped, rest, slots, come, res, img, go
):
    shift = pattern[0, 0]
    count = start.shape[1]
    index = stacked(nodes[...])
    place = index >> 7
    own, low, high, coeff = come[:, 0, :], come[:, 1, :], come[:, 2, :], come[:, 3, :]
    if cap == WIDTH:
        low = pltpu.roll(low, 1, 0)
        high = pltpu.roll(high, low.shape[0] - 1, 0)
    parts = three_parts(own + low + high) + three_parts(coeff)
    block = lax.broadcasted_iota(jnp.int32, (count, WIDTH), 0)
    landed = jnp.zeros((len(parts) * count, WIDTH), f32)
    for s in range(index.shape[0]):
        mine = block == place[s : s + 1]
        values = jnp.concatenate([jnp.where(mine, part[s : s + 1], 0.0) for part in parts], axis=0)
        landed = landed + times_transposed(values, hits[:, s * WIDTH : (s + 1) * WIDTH])
    landed = [landed[k * count : (k + 1) * count] for k in range(len(parts))]
    added = (landed[0] + landed[1]) + landed[2]
    extra = (landed[3] + landed[4]) + landed[5]
    whole = diagonal[0] + extra
    residual = rest[...] + added - extra * start[0]
    blocks = coupling.at[0]
    image = whole * residual - coupled(residual, blocks, flipped, shift)

    def total(value):
        return jnp.sum(jnp.sum(value, axis=0, keepdims=True), axis=1, keepdims=True)

    norm = total(residual * residual)
    product = total(residual * image)
    ratio = jnp.where(norm > 0.0, product / norm, 0.0)
    offset = image - ratio * residual
    bend = whole * offset - coupled(offset, blocks, flipped, shift)
    spread_square = total(offset * offset)
    spread_energy = total(offset * bend)
    res[...] = residual
    img[...] = image
    lane = lax.broadcasted_iota(jnp.int32, (8, WIDTH), 1) % cap
    facts = jnp.where(lane == 0, norm, 0.0)
    facts = jnp.where(lane == 1, ratio, facts)
    facts = jnp.where(lane == 2, spread_square, facts)
    facts = jnp.where(lane == 3, spread_energy, facts)
    residual_slots = table_gather(residual, index)
    image_slots = table_gather(image, index)
    start_slots = slots[...]
    for band in range(go.shape[0]):
        go[band, :, 0, :] = start_slots
        go[band, :, 1, :] = residual_slots
        go[band, :, 2, :] = image_slots
        go[band, :, 3, :] = facts


def last_kernel(direct, here, come, own, start, res, img, ordinal, temp, seen):
    facts = come[:, 3, :]
    norm, ratio = facts[:, 0:1], facts[:, 1:2]
    square, energy = facts[:, 2:3], facts[:, 3:4]

    def total(value):
        return jnp.sum(value, axis=0, keepdims=True)

    all_norm = total(norm)
    mean = total(ratio * norm) / all_norm
    off = ratio - mean
    next_norm = total(square + off * off * norm) / (mean * mean)
    energy = total(energy + 2.0 * off * square + off * off * ratio * norm) / (mean * mean)
    growth = next_norm / all_norm
    step = next_norm / (energy - mean * growth * next_norm)
    of_residual = 1.0 / mean + step * (1.0 + growth)
    of_image = -step / mean
    temp[0] = start[0] + of_residual * res[...] + of_image * img[...]
    if direct:
        table = come[pl.ds(here[0] * start.shape[1], 8)]
    else:
        table = own[...]
    table = table[:, 0, :] + of_residual * table[:, 1, :] + of_image * table[:, 2, :]
    places = stacked(ordinal[...])
    chunks = places.shape[0]
    if chunks < 8:
        places = jnp.concatenate([places, jnp.zeros((8 - chunks, WIDTH), jnp.int32)], axis=0)
    found = table_gather(table, places)
    for c in range(chunks):
        seen[:, c * WIDTH : (c + 1) * WIDTH] = found[c : c + 1]


def join_kernel(hot, motion, below, above, hot_out, motion_out):
    layers = hot.shape[0]
    for z in range(layers):
        for part in range(4):
            tile = hot[z] if part == 3 else motion[part, z]
            if z == 0:
                tile = tile + below[part]
            if z == layers - 1:
                tile = tile + above[part]
            if part == 3:
                hot_out[z] = tile
            else:
                motion_out[part, z] = tile


VMEM = pl.BlockSpec(memory_space=pltpu.VMEM)
SMEM = pl.BlockSpec(memory_space=pltpu.SMEM)


def call(kernel, out, args, name, scalars=(), scratch=(), flops=1 << 20):
    total = sum(int(np.prod(a.shape)) * a.dtype.itemsize for a in list(args) + list(out))
    return pl.pallas_call(
        kernel,
        out_shape=out,
        in_specs=[SMEM if n in scalars else VMEM for n in range(len(args))],
        out_specs=[VMEM] * len(out),
        scratch_shapes=scratch,
        compiler_params=pltpu.CompilerParams(vmem_limit_bytes=24 << 20),
        cost_estimate=pl.CostEstimate(flops=flops, bytes_accessed=total, transcendentals=0),
        name=name,
    )(*args)


def shape(*dims, dtype=f32):
    return jax.ShapeDtypeStruct(dims, dtype)


def ring(axis):
    count = lax.axis_size(axis)
    onward = [(k, (k + 1) % count) for k in range(count)]
    return onward, [(b, a) for a, b in onward]


def body(
    populations,
    heat_pops,
    solid_frac,
    coupled_grid_point,
    dest_index,
    heat_coeff,
    slot_node,
    node_diag,
    coupling,
    block_pattern,
    heat_source,
    solid_start,
):
    layers, across, along = solid_frac.shape
    slabs, bands = lax.axis_size("sub"), lax.axis_size("grp")
    slots = slot_node.shape[1]
    cap = slots // slabs
    rows = coupled_grid_point.shape[1]
    blocks, piece = node_diag.shape[1:]
    lines = slots // WIDTH
    assert lines == 8 and across == 8 and along >= 2 * WIDTH and along % WIDTH == 0
    assert piece == WIDTH and blocks == 8 and WIDTH % cap == 0 and cap >= 4
    assert rows % WIDTH == 0 and rows <= 8 * WIDTH and layers <= 4
    face_rows = -(-FACE * layers // 8) * 8
    planes = len(UP) + 1
    post, up, down, face_r, face_l, ordinal = call(
        functools.partial(first_kernel, cap),
        [
            shape(FLOWS + HEATS, layers, across, along),
            shape(planes, across, along),
            shape(planes, across, along),
            shape(face_rows, along),
            shape(face_rows, along),
            shape(1, rows, dtype=jnp.int32),
        ],
        [
            populations,
            heat_pops,
            solid_frac,
            coupled_grid_point,
            dest_index.reshape(1, rows),
            heat_coeff,
        ],
        "collide_first",
    )
    onward, backward = ring("sub")
    below = lax.ppermute(up, "sub", onward)
    above = lax.ppermute(down, "sub", backward)
    hits, flipped, rest, start_slots = call(
        ready_kernel,
        [
            shape(WIDTH, slots, dtype=bf16),
            shape(blocks, piece, piece),
            shape(blocks, piece),
            shape(lines, WIDTH),
        ],
        [block_pattern, slot_node, node_diag, heat_source, solid_start, coupling],
        "solid_ready",
        scalars=(0,),
    )
    own_r, own_l = call(
        functools.partial(edge_kernel, layers),
        [shape(face_rows, along)] * 2,
        [face_r, face_l, below, above],
        "x_faces",
    )
    forth, back = ring("grp")
    from_l = lax.ppermute(own_r, "grp", forth)
    from_r = lax.ppermute(own_l, "grp", back)
    hot, motion, send_up, send_down, fluxes = call(
        second_kernel,
        [
            shape(layers, across, along),
            shape(3, layers, across, along),
            shape(4, across, along),
            shape(4, across, along),
            shape(lines, 4, WIDTH),
        ],
        [post, below, above, own_r, own_l, from_l, from_r, solid_frac, up],
        "collide_second",
        scratch=[
            pltpu.VMEM((FLOWS + HEATS, layers, across, along), f32),
            pltpu.VMEM((FLOWS + HEATS, 8, along), f32),
        ],
    )
    settled = cap != WIDTH
    if settled:
        fluxes = fluxes.reshape(lines, 4, WIDTH // cap, cap).transpose(0, 2, 1, 3)
        fluxes = fluxes.reshape(slabs, 4, cap)
    landed = lax.all_to_all(fluxes, "sub", split_axis=0, concat_axis=0, tiled=True)
    if settled:
        landed = jnp.stack(
            [
                landed[:, 0],
                jnp.roll(landed[:, 1], 1, axis=0),
                jnp.roll(landed[:, 2], -1, axis=0),
                landed[:, 3],
            ]
        )
        landed = landed.reshape(4, lines, WIDTH).transpose(1, 0, 2)
    from_below = lax.ppermute(send_up, "sub", onward)
    from_above = lax.ppermute(send_down, "sub", backward)
    residual, image, go = call(
        functools.partial(solve_kernel, cap),
        [shape(blocks, piece), shape(blocks, piece), shape(bands, lines, 4, WIDTH)],
        [
            block_pattern,
            slot_node,
            node_diag,
            solid_start,
            coupling,
            hits,
            flipped,
            rest,
            start_slots,
            landed,
        ],
        "solve",
        scalars=(0,),
    )
    if settled:
        go = go.reshape(bands, lines, 4, WIDTH // cap, cap).transpose(0, 1, 3, 2, 4)
    go = go.reshape(bands * slabs, 4, cap)
    come = lax.all_to_all(go, ("grp", "sub"), split_axis=0, concat_axis=0, tiled=True)
    hot_out, motion_out = call(
        join_kernel,
        [shape(*hot.shape), shape(*motion.shape)],
        [hot, motion, from_below, from_above],
        "join",
    )
    band = lax.axis_index("grp")
    if settled:
        own = lax.dynamic_slice_in_dim(come, band * slabs, slabs, 0)
        own = own.transpose(1, 0, 2).reshape(4, lines, WIDTH).transpose(1, 0, 2)
        come = jnp.pad(come, ((0, 0), (0, 0), (0, WIDTH - cap)))
    else:
        own = rest
    temp, seen = call(
        functools.partial(last_kernel, not settled),
        [shape(1, blocks, piece), shape(1, rows)],
        [
            band.astype(jnp.int32).reshape(1),
            come,
            own,
            solid_start,
            residual,
            image,
            ordinal,
        ],
        "finish",
        scalars=(0,),
    )
    return hot_out, motion_out, temp, seen


def solution(mesh):
    placed = (
        P(None, "sub", "grp", None),
        P(None, "sub", "grp", None),
        P("sub", "grp", None),
        P("grp", "sub"),
        P("grp", "sub", None),
        P("grp", "sub"),
        P("grp", "sub"),
        P("grp", "sub", None),
        P("grp", "sub", None, None),
        P("grp", "sub"),
        P("grp", "sub", None),
        P("grp", "sub", None),
    )
    return jax.shard_map(
        body,
        mesh=mesh,
        in_specs=placed,
        out_specs=(
            P("sub", "grp", None),
            P(None, "sub", "grp", None),
            P("grp", "sub", None),
            P("grp", "sub"),
        ),
        check_vma=False,
    )
```

```python
import functools
import jax
import jax.numpy as jnp
import numpy as np
from jax import lax
from jax.experimental import pallas as pl
from jax.experimental.pallas import tpu as pltpu
from jax.sharding import PartitionSpec as P

FLOW_VELOCITY = [
    (0, 0, 0),
    (1, 0, 0),
    (-1, 0, 0),
    (0, 1, 0),
    (0, -1, 0),
    (0, 0, 1),
    (0, 0, -1),
    (1, 1, 0),
    (-1, -1, 0),
    (1, -1, 0),
    (-1, 1, 0),
    (1, 0, 1),
    (-1, 0, -1),
    (1, 0, -1),
    (-1, 0, 1),
    (0, 1, 1),
    (0, -1, -1),
    (0, 1, -1),
    (0, -1, 1),
]
VELOCITY = FLOW_VELOCITY + FLOW_VELOCITY[:7]
FLOWS, HEATS = 19, 7
LANES_ALL = range(FLOWS + HEATS)
UP = [i for i in LANES_ALL if VELOCITY[i][2] == 1]
DOWN = [i for i in LANES_ALL if VELOCITY[i][2] == -1]
RIGHT = [i for i in LANES_ALL if VELOCITY[i][0] == 1]
LEFT = [i for i in LANES_ALL if VELOCITY[i][0] == -1]
STILL = [i for i in LANES_ALL if VELOCITY[i][0] == 0]
FACE_RIGHT = STILL + RIGHT
FACE_LEFT = STILL + LEFT
FACE = len(FACE_RIGHT) + len(RIGHT) + 1
WIDTH = 128
f32 = jnp.float32
bf16 = jnp.bfloat16


def signed_sum(terms):
    total = None
    for sign, term in terms:
        if sign == 0:
            continue
        if total is None:
            total = term if sign > 0 else -term
        else:
            total = total + term if sign > 0 else total - term
    return total


def collide(flow, heat, solid):
    pairs = range(1, FLOWS, 2)
    density = flow[0]
    for i in pairs:
        density = density + (flow[i] + flow[i + 1])
    gaps = {i: flow[i] - flow[i + 1] for i in pairs}
    scale = 1.0 / density
    speed = [
        signed_sum([(FLOW_VELOCITY[i][axis], gaps[i]) for i in pairs]) * scale for axis in range(3)
    ]
    square = speed[0] * speed[0] + speed[1] * speed[1] + speed[2] * speed[2]
    base = 1.0 - 1.5 * square
    gas = 1.0 - solid
    keep = gas * (1.0 - 1.0 / 0.8)
    pull = gas * (density * (1.0 / 0.8))
    flow_post = [None] * FLOWS
    flow_post[0] = (keep + solid) * flow[0] + (pull * (1.0 / 3.0)) * base
    shares = {1: pull * (1.0 / 18.0), 2: pull * (1.0 / 36.0)}
    for i in pairs:
        share = shares[sum(abs(c) for c in FLOW_VELOCITY[i])]
        along = signed_sum([(FLOW_VELOCITY[i][axis], speed[axis]) for axis in range(3)])
        even = base + 4.5 * along * along
        odd = 3.0 * along
        flow_post[i] = keep * flow[i] + share * (even + odd) + solid * flow[i + 1]
        flow_post[i + 1] = keep * flow[i + 1] + share * (even - odd) + solid * flow[i]
    hotness = heat[0]
    for j in range(1, HEATS):
        hotness = hotness + heat[j]
    stay = 1.0 - 1.0 / 0.7
    heat_post = [stay * heat[0] + (0.25 / 0.7) * hotness]
    level = (0.125 / 0.7) * hotness
    for j in range(1, HEATS, 2):
        axis = (j - 1) // 2
        drift = 4.0 * speed[axis]
        heat_post.append(stay * heat[j] + level * (1.0 + drift))
        heat_post.append(stay * heat[j + 1] + level * (1.0 - drift))
    return flow_post + heat_post


def three_parts(value):
    high = value.astype(bf16).astype(f32)
    rest = value - high
    middle = rest.astype(bf16).astype(f32)
    return [high, middle, rest - middle]


def times_transposed(left, right):
    return lax.dot_general(
        left.astype(bf16), right.astype(bf16), (((1,), (1,)), ((), ())), preferred_element_type=f32
    )


def spread(row):
    return jnp.broadcast_to(row, (8, row.shape[-1]))


def lane_gather(row, lane):
    return jnp.take_along_axis(spread(row), lane, axis=1, mode="promise_in_bounds")


def table_gather(table, index):
    place, lane = index >> 7, index & 127
    out = jnp.zeros(index.shape, f32)
    for row in range(table.shape[0]):
        out = jnp.where(place == row, lane_gather(table[row : row + 1], lane), out)
    return out


def stacked(row):
    return jnp.concatenate(
        [row[:, k * WIDTH : (k + 1) * WIDTH] for k in range(row.shape[1] // WIDTH)], axis=0
    )


def slot_tables(cap, voxel, dest, coeff, ordinal):
    rows_here = dest.shape[1]
    owner = dest[...].astype(f32)
    chunks = rows_here // WIDTH
    tall = stacked(owner)
    tall = jnp.concatenate([tall] + [jnp.zeros((8 - chunks, WIDTH), f32)] * (chunks < 8), axis=0)
    upright = tall.T
    first = lax.broadcasted_iota(jnp.int32, (WIDTH, WIDTH), 0)
    second = lax.broadcasted_iota(jnp.int32, (WIDTH, WIDTH), 1)
    slot_row = lax.broadcasted_iota(jnp.int32, (8, WIDTH), 0)
    table = jnp.zeros((40, WIDTH), f32)
    for c in range(chunks):
        lanes = slice(c * WIDTH, (c + 1) * WIDTH)
        here = owner[:, lanes]
        count = jnp.zeros((WIDTH, WIDTH), f32)
        for other in range(c + 1):
            same = upright[:, other : other + 1] == here
            if other == c:
                same = same & (first < second)
            count = count + jnp.where(same, 1.0, 0.0)
        rank = jnp.sum(count, axis=0, keepdims=True)
        place = (here * float(cap) + rank).astype(jnp.int32)
        ordinal[:, lanes] = place
        mine = slot_row == (place >> 7)
        spot = voxel[:, lanes]
        parts = [(spot >> 7).astype(f32), (spot & 127).astype(f32)] + three_parts(coeff[:, lanes])
        values = jnp.concatenate([jnp.where(mine, part, 0.0) for part in parts], axis=0)
        table = table + times_transposed(values, jnp.where(first == (place & 127), 1.0, 0.0))
    spots = table[0:8] * float(WIDTH) + table[8:16]
    coeffs = (table[16:24] + table[24:32]) + table[32:40]
    return spots, coeffs


def on_even(axis="sub"):
    return lax.rem(lax.axis_index(axis), 2) == 0


def first_kernel(cap, *refs):
    given, (post, to_near, to_next, face_r, face_l, ordinal) = refs[:6], refs[6:12]
    held, arrived = refs[12:18], refs[18]
    copies = [
        pltpu.make_async_copy(source, target, arrived.at[n])
        for n, (source, target) in enumerate(zip(given, held))
    ]
    for n in (0, 1, 4, 3, 5, 2):
        copies[n].start()
    pops, heat, solid, voxel, dest, coeff = held
    layers, across, along = solid.shape
    even = on_even()
    for n in (4, 3, 5):
        copies[n].wait()
    spots, coeffs = slot_tables(cap, voxel, dest, coeff, ordinal)
    extra = len(UP)
    for plane in (to_near, to_next):
        plane[extra] = jnp.zeros(plane.shape[1:], f32)
        plane[extra, :, 0:WIDTH] = spots
        plane[extra, :, WIDTH : 2 * WIDTH] = coeffs
    for n in (0, 1, 2):
        copies[n].wait()
    for z in range(layers):
        for start in range(0, along, WIDTH):
            lanes = slice(start, start + WIDTH)
            out = collide(
                [pops[i, z, :, lanes] for i in range(FLOWS)],
                [heat[j, z, :, lanes] for j in range(HEATS)],
                solid[z, :, lanes],
            )
            for i in LANES_ALL:
                post[i, z, :, lanes] = out[i]
            for face, lists, near, far in (
                (face_r, (STILL, RIGHT), across - 1, across - 2),
                (face_l, (STILL, LEFT), 0, 1),
            ):
                rows = [(i, near) for i in lists[0]] + [(i, far) for i in lists[1]]
                rows = rows + [(i, near) for i in lists[1]]
                for n, (i, column) in enumerate(rows):
                    at = n * layers + z
                    face[at : at + 1, lanes] = out[i][column : column + 1]
                at = len(rows) * layers + z
                face[at : at + 1, lanes] = solid[z, near : near + 1, lanes]
    for n, (above, below) in enumerate(zip(UP, DOWN)):
        above, below = post[above, layers - 1], post[below, 0]
        to_near[n] = jnp.where(even, above, below)
        to_next[n] = jnp.where(even, below, above)


def edge_kernel(layers, face_r, face_l, near, next_, to_a, to_b, out_r, out_l):
    out_r[...] = face_r[...]
    out_l[...] = face_l[...]
    across = near.shape[1]
    even = on_even()
    for out, lists, edge, inside in (
        (out_r, (STILL, RIGHT), across - 1, across - 2),
        (out_l, (STILL, LEFT), 0, 1),
    ):
        rows = [(i, edge) for i in lists[0]] + [(i, inside) for i in lists[1]]
        rows = rows + [(i, edge) for i in lists[1]]
        for n, (i, column) in enumerate(rows):
            rise = VELOCITY[i][2]
            if rise == 0:
                continue
            moved = range(layers - 1, 0, -1) if rise == 1 else range(layers - 1)
            for z in moved:
                at, source = n * layers + z, n * layers + z - rise
                out[at : at + 1, :] = out[source : source + 1, :]
            z = 0 if rise == 1 else layers - 1
            at = n * layers + z
            k = (UP if rise == 1 else DOWN).index(i)
            one, two = near[k, column : column + 1, :], next_[k, column : column + 1, :]
            out[at : at + 1, :] = jnp.where(even == (rise == 1), two, one)
    right, left, band_even = out_r[...], out_l[...], on_even("grp")
    to_a[...] = jnp.where(band_even, right, left)
    to_b[...] = jnp.where(band_even, left, right)


def turned(tile, step):
    return tile if step == 0 else pltpu.roll(tile, step % tile.shape[1], 1)


def second_kernel(
    post,
    near,
    next_,
    to_a,
    to_b,
    faces_a,
    faces_b,
    solid,
    own_table,
    tie,
    hot,
    motion,
    send_near,
    send_next,
    fluxes,
    moved,
    halo,
):
    layers, across, along = solid.shape
    even = on_even()
    band_even = on_even("grp")
    own_r = jnp.where(band_even, to_a[...], to_b[...])
    own_l = jnp.where(band_even, to_b[...], to_a[...])
    below = [jnp.where(even, next_[n], near[n]) for n in range(len(UP) + 1)]
    above = [jnp.where(even, near[n], next_[n]) for n in range(len(UP) + 1)]
    from_l = jnp.where(band_even, faces_b[...], faces_a[...])
    from_r = jnp.where(band_even, faces_a[...], faces_b[...])
    slot = lax.broadcasted_iota(jnp.int32, (across, along), 0)
    inner = len(FACE_RIGHT)
    for i in LANES_ALL:
        ex, ey, ez = VELOCITY[i]
        for z in range(layers):
            if z - ez < 0:
                tile = below[UP.index(i)]
            elif z - ez >= layers:
                tile = above[DOWN.index(i)]
            else:
                tile = post[i, z - ez]
            if ex == 1:
                at = (inner + RIGHT.index(i)) * layers + z
                tile = jnp.where(slot == 0, from_l[at : at + 1, :], pltpu.roll(tile, 1, 0))
            elif ex == -1:
                at = (inner + LEFT.index(i)) * layers + z
                tile = jnp.where(
                    slot == across - 1, from_r[at : at + 1, :], pltpu.roll(tile, across - 1, 0)
                )
            moved[i, z] = turned(tile, ey)
        if ex == -1:
            at = (inner + LEFT.index(i)) * layers
            low = own_l[at : at + layers, :]
        else:
            at = FACE_RIGHT.index(i) * layers
            low = from_l[at : at + layers, :]
        if ex == 1:
            at = (inner + RIGHT.index(i)) * layers
            high = own_r[at : at + layers, :]
        else:
            at = FACE_LEFT.index(i) * layers
            high = from_r[at : at + layers, :]
        sides = [low, high]
        if 2 * layers < 8:
            sides.append(jnp.ones((8 - 2 * layers, along), f32))
        halo[i] = turned(jnp.concatenate(sides, axis=0), ey)
    at = (FACE - 1) * layers
    edge_solid = [from_l[at : at + layers, :], from_r[at : at + layers, :]]
    if 2 * layers < 8:
        edge_solid.append(jnp.zeros((8 - 2 * layers, along), f32))
    edge_solid = jnp.concatenate(edge_solid, axis=0)
    for start in range(0, along, WIDTH):
        lanes = slice(start, start + WIDTH)
        for z in range(layers):
            out = collide(
                [moved[i, z, :, lanes] for i in range(FLOWS)],
                [moved[FLOWS + j, z, :, lanes] for j in range(HEATS)],
                solid[z, :, lanes],
            )
            for i in LANES_ALL:
                moved[i, z, :, lanes] = out[i]
        out = collide(
            [halo[i, :, lanes] for i in range(FLOWS)],
            [halo[FLOWS + j, :, lanes] for j in range(HEATS)],
            edge_solid[:, lanes],
        )
        for i in RIGHT + LEFT:
            halo[i, :, lanes] = out[i]
    sums = {}

    def add(key, sign, tile):
        if sign == 0:
            return
        if key in sums:
            sums[key] = sums[key] + tile if sign > 0 else sums[key] - tile
        else:
            sums[key] = tile if sign > 0 else -tile

    for z in range(layers):
        for i in LANES_ALL:
            ex, ey, ez = VELOCITY[i]
            if i == 0:
                continue
            tile = moved[i, z]
            if ex == 1:
                tile = jnp.where(slot == 0, halo[i, z : z + 1, :], pltpu.roll(tile, 1, 0))
            elif ex == -1:
                at = layers + z
                tile = jnp.where(
                    slot == across - 1, halo[i, at : at + 1, :], pltpu.roll(tile, across - 1, 0)
                )
            tile = turned(tile, ey)
            target = z + ez
            if i >= FLOWS:
                add((3, target), 1, tile)
            else:
                add((0, target), ex, tile)
                add((1, target), ey, tile)
                add((2, target), ez, tile)
    for z in range(layers):
        hot[z] = sums[3, z]
        for axis in range(3):
            motion[axis, z] = sums[axis, z]
    for part in range(4):
        send_near[part] = jnp.where(even, sums[part, layers], sums[part, -1])
        send_next[part] = jnp.where(even, sums[part, -1], sums[part, layers])
    extra = len(UP)
    per_line = along // WIDTH
    per_layer = across * per_line

    def flux(table, planes):
        index = table[:, 0:WIDTH].astype(jnp.int32)
        place, lane = index >> 7, index & 127
        out = jnp.zeros(lane.shape, f32)
        for z, plane in planes:
            for x in range(across):
                for c in range(per_line):
                    row = plane[x : x + 1, c * WIDTH : (c + 1) * WIDTH]
                    out = jnp.where(
                        place == z * per_layer + x * per_line + c, lane_gather(row, lane), out
                    )
        return out * table[:, WIDTH : 2 * WIDTH]

    mine = own_table[extra]
    fluxes[:, 0, :] = flux(mine, [(z, sums[3, z]) for z in range(layers)])
    fluxes[:, 1, :] = flux(above[extra], [(0, sums[3, layers])])
    fluxes[:, 2, :] = flux(below[extra], [(layers - 1, sums[3, -1])])
    fluxes[:, 3, :] = mine[:, WIDTH : 2 * WIDTH]


def coupled(vector, blocks, flipped, shift):
    count = vector.shape[0]
    upright = vector.T
    ahead, back = [], []
    for b in range(count):
        column = upright[:, b : b + 1]
        back.append(jnp.sum(blocks[b] * column, axis=0, keepdims=True))
        ahead.append(jnp.sum(flipped[b] * column, axis=0, keepdims=True))
    ahead = jnp.concatenate(ahead, axis=0)
    back = jnp.concatenate(back, axis=0)
    return pltpu.roll(ahead, lax.rem(count - shift, count), 0) + pltpu.roll(back, shift, 0)


def ready_kernel(
    pattern, nodes, diagonal, source, start, coupling, tie, hits, flipped, rest, slots, level
):
    shift = pattern[0, 0]
    count = start.shape[1]
    for b in range(count):
        flipped[lax.rem(b + shift, count)] = coupling[0, b].T
    vector = start[0]
    rest[...] = (
        source[0] - diagonal[0] * vector + coupled(vector, coupling.at[0], flipped, shift)
    )
    index = nodes[...]
    depth = lax.broadcasted_iota(jnp.int32, (WIDTH, index.shape[1]), 0)
    hits[...] = jnp.where(depth == (index & 127), 1.0, 0.0).astype(bf16)
    slots[...] = table_gather(vector, stacked(index))
    mean = jnp.sum(jnp.sum(diagonal[0], axis=0, keepdims=True), axis=1, keepdims=True)
    level[...] = jnp.broadcast_to(mean * (1.0 / (count * WIDTH)), level.shape)


def solve_kernel(
    cap,
    pattern,
    nodes,
    diagonal,
    start,
    coupling,
    hits,
    flipped,
    rest,
    slots,
    level,
    come,
    res,
    img,
    go,
):
    shift = pattern[0, 0]
    count = start.shape[1]
    index = stacked(nodes[...])
    place = index >> 7
    own, low, high, coeff = come[:, 0, :], come[:, 1, :], come[:, 2, :], come[:, 3, :]
    if cap == WIDTH:
        low = pltpu.roll(low, 1, 0)
        high = pltpu.roll(high, low.shape[0] - 1, 0)
    parts = three_parts(own + low + high) + three_parts(coeff)
    block = lax.broadcasted_iota(jnp.int32, (count, WIDTH), 0)
    landed = jnp.zeros((len(parts) * count, WIDTH), f32)
    for s in range(index.shape[0]):
        mine = block == place[s : s + 1]
        values = jnp.concatenate([jnp.where(mine, part[s : s + 1], 0.0) for part in parts], axis=0)
        landed = landed + times_transposed(values, hits[:, s * WIDTH : (s + 1) * WIDTH])
    landed = [landed[k * count : (k + 1) * count] for k in range(len(parts))]
    added = (landed[0] + landed[1]) + landed[2]
    extra = (landed[3] + landed[4]) + landed[5]
    whole = diagonal[0] + extra
    residual = rest[...] + added - extra * start[0]
    blocks = coupling.at[0]
    image = whole * residual - coupled(residual, blocks, flipped, shift)

    def total(value):
        return jnp.sum(jnp.sum(value, axis=0, keepdims=True), axis=1, keepdims=True)

    ratio = level[0:1, :]
    offset = image - ratio * residual
    bend = whole * offset - coupled(offset, blocks, flipped, shift)
    totals = [
        total(residual * residual),
        total(residual * offset),
        total(offset * offset),
        total(offset * bend),
        ratio,
    ]
    res[...] = residual
    img[...] = image
    lane = lax.broadcasted_iota(jnp.int32, (8, WIDTH), 1) % cap
    facts = jnp.zeros((8, WIDTH), f32)
    for n, fact in enumerate(totals):
        facts = jnp.where(lane == n, fact, facts)
    residual_slots = table_gather(residual, index)
    image_slots = table_gather(image, index)
    start_slots = slots[...]
    for band in range(go.shape[0]):
        go[band, :, 0, :] = start_slots
        go[band, :, 1, :] = residual_slots
        go[band, :, 2, :] = image_slots
        go[band, :, 3, :] = facts


def last_kernel(direct, come, own, start, res, img, ordinal, temp, seen):
    facts = come[:, 3, :]
    norm, cross, square, energy, ratio = (facts[:, n : n + 1] for n in range(5))

    def total(value):
        return jnp.sum(value, axis=0, keepdims=True)

    product = ratio * norm + cross
    all_norm = total(norm)
    mean = total(product) / all_norm
    off = ratio - mean
    next_norm = total(square + off * (2.0 * cross + off * norm)) / (mean * mean)
    energy = energy + off * (2.0 * (square + ratio * cross) + off * product)
    energy = total(energy) / (mean * mean)
    growth = next_norm / all_norm
    step = next_norm / (energy - mean * growth * next_norm)
    of_residual = 1.0 / mean + step * (1.0 + growth)
    of_image = -step / mean
    temp[0] = start[0] + of_residual * res[...] + of_image * img[...]
    if direct:
        table = come[pl.ds(lax.axis_index("grp") * 8, 8)]
    else:
        table = own[...]
    table = table[:, 0, :] + of_residual * table[:, 1, :] + of_image * table[:, 2, :]
    places = stacked(ordinal[...])
    chunks = places.shape[0]
    if chunks < 8:
        places = jnp.concatenate([places, jnp.zeros((8 - chunks, WIDTH), jnp.int32)], axis=0)
    found = table_gather(table, places)
    for c in range(chunks):
        seen[:, c * WIDTH : (c + 1) * WIDTH] = found[c : c + 1]


def join_kernel(hot, motion, near, next_, hot_out, motion_out):
    layers = hot.shape[0]
    even = on_even()
    below = [jnp.where(even, next_[n], near[n]) for n in range(4)]
    above = [jnp.where(even, near[n], next_[n]) for n in range(4)]
    for z in range(layers):
        for part in range(4):
            tile = hot[z] if part == 3 else motion[part, z]
            if z == 0:
                tile = tile + below[part]
            if z == layers - 1:
                tile = tile + above[part]
            if part == 3:
                hot_out[z] = tile
            else:
                motion_out[part, z] = tile


VMEM = pl.BlockSpec(memory_space=pltpu.VMEM)
ANYWHERE = pl.BlockSpec(memory_space=pl.ANY)
SMEM = pl.BlockSpec(memory_space=pltpu.SMEM)


def call(kernel, out, args, name, scalars=(), scratch=(), far=False):
    total = sum(int(np.prod(a.shape)) * a.dtype.itemsize for a in list(args) + list(out))
    if far:
        args = [pltpu.with_memory_space_constraint(a, pltpu.HBM) for a in args]
    return pl.pallas_call(
        kernel,
        out_shape=out,
        in_specs=[
            ANYWHERE if far else SMEM if n in scalars else VMEM for n in range(len(args))
        ],
        out_specs=[VMEM] * len(out),
        scratch_shapes=scratch,
        compiler_params=pltpu.CompilerParams(vmem_limit_bytes=24 << 20),
        cost_estimate=pl.CostEstimate(flops=1 << 20, bytes_accessed=total, transcendentals=0),
        name=name,
    )(*args)


def shape(*dims, dtype=f32):
    return jax.ShapeDtypeStruct(dims, dtype)


def swaps(axis):
    count = lax.axis_size(axis)
    assert count % 2 == 0
    near = [(k, k + 1 - 2 * (k % 2)) for k in range(count)]
    return near, [(k, (k - 1 + 2 * (k % 2)) % count) for k in range(count)]


def body(
    populations,
    heat_pops,
    solid_frac,
    coupled_grid_point,
    dest_index,
    heat_coeff,
    slot_node,
    node_diag,
    coupling,
    block_pattern,
    heat_source,
    solid_start,
):
    layers, across, along = solid_frac.shape
    slabs, bands = lax.axis_size("sub"), lax.axis_size("grp")
    slots = slot_node.shape[1]
    cap = slots // slabs
    rows = coupled_grid_point.shape[1]
    blocks, piece = node_diag.shape[1:]
    lines = slots // WIDTH
    assert lines == 8 and across == 8 and along >= 2 * WIDTH and along % WIDTH == 0
    assert piece == WIDTH and blocks == 8 and WIDTH % cap == 0 and cap >= 8
    assert rows % WIDTH == 0 and rows <= 8 * WIDTH and layers <= 4
    face_rows = -(-FACE * layers // 8) * 8
    planes = len(UP) + 1
    post, to_near, to_next, face_r, face_l, ordinal = call(
        functools.partial(first_kernel, cap),
        [
            shape(FLOWS + HEATS, layers, across, along),
            shape(planes, across, along),
            shape(planes, across, along),
            shape(face_rows, along),
            shape(face_rows, along),
            shape(1, rows, dtype=jnp.int32),
        ],
        [
            populations,
            heat_pops,
            solid_frac,
            coupled_grid_point,
            dest_index.reshape(1, rows),
            heat_coeff,
        ],
        "collide_first",
        scratch=[
            pltpu.VMEM(solid_like, kind)
            for solid_like, kind in (
                (populations.shape, f32),
                (heat_pops.shape, f32),
                (solid_frac.shape, f32),
                ((1, rows), jnp.int32),
                ((1, rows), jnp.int32),
                ((1, rows), f32),
            )
        ]
        + [pltpu.SemaphoreType.DMA((6,))],
        far=True,
    )
    near_pairs, next_pairs = swaps("sub")
    near = lax.ppermute(to_near, "sub", near_pairs)
    next_ = lax.ppermute(to_next, "sub", next_pairs)
    to_a, to_b = call(
        functools.partial(edge_kernel, layers),
        [shape(face_rows, along)] * 2,
        [face_r, face_l, near, next_],
        "x_faces",
        scratch=[pltpu.VMEM((face_rows, along), f32)] * 2,
    )
    hits, flipped, rest, start_slots, level = call(
        ready_kernel,
        [
            shape(WIDTH, slots, dtype=bf16),
            shape(blocks, piece, piece),
            shape(blocks, piece),
            shape(lines, WIDTH),
            shape(8, WIDTH),
        ],
        [block_pattern, slot_node, node_diag, heat_source, solid_start, coupling, to_a],
        "solid_ready",
        scalars=(0,),
    )
    side_a, side_b = swaps("grp")
    faces_a = lax.ppermute(to_a, "grp", side_a)
    faces_b = lax.ppermute(to_b, "grp", side_b)
    hot, motion, send_near, send_next, fluxes = call(
        second_kernel,
        [
            shape(layers, across, along),
            shape(3, layers, across, along),
            shape(4, across, along),
            shape(4, across, along),
            shape(lines, 4, WIDTH),
        ],
        [post, near, next_, to_a, to_b, faces_a, faces_b, solid_frac, to_near, rest],
        "collide_second",
        scratch=[
            pltpu.VMEM((FLOWS + HEATS, layers, across, along), f32),
            pltpu.VMEM((FLOWS + HEATS, 8, along), f32),
        ],
    )
    settled = cap != WIDTH
    if settled:
        fluxes = fluxes.reshape(lines, 4, WIDTH // cap, cap).transpose(0, 2, 1, 3)
        fluxes = fluxes.reshape(slabs, 4, cap)
    landed = lax.all_to_all(fluxes, "sub", split_axis=0, concat_axis=0, tiled=True)
    if settled:
        landed = jnp.stack(
            [
                landed[:, 0],
                jnp.roll(landed[:, 1], 1, axis=0),
                jnp.roll(landed[:, 2], -1, axis=0),
                landed[:, 3],
            ]
        )
        landed = landed.reshape(4, lines, WIDTH).transpose(1, 0, 2)
    from_near = lax.ppermute(send_near, "sub", near_pairs)
    from_next = lax.ppermute(send_next, "sub", next_pairs)
    residual, image, go = call(
        functools.partial(solve_kernel, cap),
        [shape(blocks, piece), shape(blocks, piece), shape(bands, lines, 4, WIDTH)],
        [
            block_pattern,
            slot_node,
            node_diag,
            solid_start,
            coupling,
            hits,
            flipped,
            rest,
            start_slots,
            level,
            landed,
        ],
        "solve",
        scalars=(0,),
    )
    if settled:
        go = go.reshape(bands, lines, 4, WIDTH // cap, cap).transpose(0, 1, 3, 2, 4)
    go = go.reshape(bands * slabs, 4, cap)
    come = lax.all_to_all(go, ("grp", "sub"), split_axis=0, concat_axis=0, tiled=True)
    hot_out, motion_out = call(
        join_kernel,
        [shape(*hot.shape), shape(*motion.shape)],
        [hot, motion, from_near, from_next],
        "join",
    )
    if settled:
        own = lax.dynamic_slice_in_dim(come, lax.axis_index("grp") * slabs, slabs, 0)
        own = own.transpose(1, 0, 2).reshape(4, lines, WIDTH).transpose(1, 0, 2)
        come = jnp.pad(come, ((0, 0), (0, 0), (0, WIDTH - cap)))
    else:
        own = rest
    temp, seen = call(
        functools.partial(last_kernel, not settled),
        [shape(1, blocks, piece), shape(1, rows)],
        [
            come,
            own,
            solid_start,
            residual,
            image,
            ordinal,
        ],
        "finish",
    )
    return hot_out, motion_out, temp, seen


def solution(mesh):
    placed = (
        P(None, "sub", "grp", None),
        P(None, "sub", "grp", None),
        P("sub", "grp", None),
        P("grp", "sub"),
        P("grp", "sub", None),
        P("grp", "sub"),
        P("grp", "sub"),
        P("grp", "sub", None),
        P("grp", "sub", None, None),
        P("grp", "sub"),
        P("grp", "sub", None),
        P("grp", "sub", None),
    )
    return jax.shard_map(
        body,
        mesh=mesh,
        in_specs=placed,
        out_specs=(
            P("sub", "grp", None),
            P(None, "sub", "grp", None),
            P("grp", "sub", None),
            P("grp", "sub"),
        ),
        check_vma=False,
    )
```

```python
import functools
import jax
import jax.numpy as jnp
import numpy as np
from jax import lax
from jax.experimental import pallas as pl
from jax.experimental.pallas import tpu as pltpu
from jax.sharding import PartitionSpec as P

FLOW_VELOCITY = [
    (0, 0, 0),
    (1, 0, 0),
    (-1, 0, 0),
    (0, 1, 0),
    (0, -1, 0),
    (0, 0, 1),
    (0, 0, -1),
    (1, 1, 0),
    (-1, -1, 0),
    (1, -1, 0),
    (-1, 1, 0),
    (1, 0, 1),
    (-1, 0, -1),
    (1, 0, -1),
    (-1, 0, 1),
    (0, 1, 1),
    (0, -1, -1),
    (0, 1, -1),
    (0, -1, 1),
]
VELOCITY = FLOW_VELOCITY + FLOW_VELOCITY[:7]
FLOWS, HEATS = 19, 7
LANES_ALL = range(FLOWS + HEATS)
UP = [i for i in LANES_ALL if VELOCITY[i][2] == 1]
DOWN = [i for i in LANES_ALL if VELOCITY[i][2] == -1]
RIGHT = [i for i in LANES_ALL if VELOCITY[i][0] == 1]
LEFT = [i for i in LANES_ALL if VELOCITY[i][0] == -1]
STILL = [i for i in LANES_ALL if VELOCITY[i][0] == 0]
FACE_RIGHT = STILL + RIGHT
FACE_LEFT = STILL + LEFT
FACE = len(FACE_RIGHT) + len(RIGHT) + 1
WIDTH = 128
f32 = jnp.float32
bf16 = jnp.bfloat16


def signed_sum(terms):
    total = None
    for sign, term in terms:
        if sign == 0:
            continue
        if total is None:
            total = term if sign > 0 else -term
        else:
            total = total + term if sign > 0 else total - term
    return total


def collide(flow, heat, solid):
    pairs = range(1, FLOWS, 2)
    density = flow[0]
    for i in pairs:
        density = density + (flow[i] + flow[i + 1])
    gaps = {i: flow[i] - flow[i + 1] for i in pairs}
    scale = 1.0 / density
    speed = [
        signed_sum([(FLOW_VELOCITY[i][axis], gaps[i]) for i in pairs]) * scale for axis in range(3)
    ]
    square = speed[0] * speed[0] + speed[1] * speed[1] + speed[2] * speed[2]
    base = 1.0 - 1.5 * square
    gas = 1.0 - solid
    keep = gas * (1.0 - 1.0 / 0.8)
    pull = gas * (density * (1.0 / 0.8))
    flow_post = [None] * FLOWS
    flow_post[0] = (keep + solid) * flow[0] + (pull * (1.0 / 3.0)) * base
    shares = {1: pull * (1.0 / 18.0), 2: pull * (1.0 / 36.0)}
    for i in pairs:
        share = shares[sum(abs(c) for c in FLOW_VELOCITY[i])]
        along = signed_sum([(FLOW_VELOCITY[i][axis], speed[axis]) for axis in range(3)])
        even = base + 4.5 * along * along
        odd = 3.0 * along
        flow_post[i] = keep * flow[i] + share * (even + odd) + solid * flow[i + 1]
        flow_post[i + 1] = keep * flow[i + 1] + share * (even - odd) + solid * flow[i]
    hotness = heat[0]
    for j in range(1, HEATS):
        hotness = hotness + heat[j]
    stay = 1.0 - 1.0 / 0.7
    heat_post = [stay * heat[0] + (0.25 / 0.7) * hotness]
    level = (0.125 / 0.7) * hotness
    for j in range(1, HEATS, 2):
        axis = (j - 1) // 2
        drift = 4.0 * speed[axis]
        heat_post.append(stay * heat[j] + level * (1.0 + drift))
        heat_post.append(stay * heat[j + 1] + level * (1.0 - drift))
    return flow_post + heat_post


def three_parts(value):
    high = value.astype(bf16).astype(f32)
    rest = value - high
    middle = rest.astype(bf16).astype(f32)
    return [high, middle, rest - middle]


def times_transposed(left, right):
    return lax.dot_general(
        left.astype(bf16), right.astype(bf16), (((1,), (1,)), ((), ())), preferred_element_type=f32
    )


def spread(row):
    return jnp.broadcast_to(row, (8, row.shape[-1]))


def lane_gather(row, lane):
    return jnp.take_along_axis(spread(row), lane, axis=1, mode="promise_in_bounds")


def table_gather(table, index):
    place, lane = index >> 7, index & 127
    out = jnp.zeros(index.shape, f32)
    for row in range(table.shape[0]):
        out = jnp.where(place == row, lane_gather(table[row : row + 1], lane), out)
    return out


def stacked(row):
    return jnp.concatenate(
        [row[:, k * WIDTH : (k + 1) * WIDTH] for k in range(row.shape[1] // WIDTH)], axis=0
    )


def slot_tables(cap, voxel, dest, coeff, ordinal):
    rows_here = dest.shape[1]
    owner = dest[...].astype(f32)
    chunks = rows_here // WIDTH
    tall = stacked(owner)
    tall = jnp.concatenate([tall] + [jnp.zeros((8 - chunks, WIDTH), f32)] * (chunks < 8), axis=0)
    upright = tall.T
    first = lax.broadcasted_iota(jnp.int32, (WIDTH, WIDTH), 0)
    second = lax.broadcasted_iota(jnp.int32, (WIDTH, WIDTH), 1)
    slot_row = lax.broadcasted_iota(jnp.int32, (8, WIDTH), 0)
    table = jnp.zeros((40, WIDTH), f32)
    for c in range(chunks):
        lanes = slice(c * WIDTH, (c + 1) * WIDTH)
        here = owner[:, lanes]
        count = jnp.zeros((WIDTH, WIDTH), f32)
        for other in range(c + 1):
            same = upright[:, other : other + 1] == here
            if other == c:
                same = same & (first < second)
            count = count + jnp.where(same, 1.0, 0.0)
        rank = jnp.sum(count, axis=0, keepdims=True)
        place = (here * float(cap) + rank).astype(jnp.int32)
        ordinal[:, lanes] = place
        mine = slot_row == (place >> 7)
        spot = voxel[:, lanes]
        parts = [(spot >> 7).astype(f32), (spot & 127).astype(f32)] + three_parts(coeff[:, lanes])
        values = jnp.concatenate([jnp.where(mine, part, 0.0) for part in parts], axis=0)
        table = table + times_transposed(values, jnp.where(first == (place & 127), 1.0, 0.0))
    spots = table[0:8] * float(WIDTH) + table[8:16]
    coeffs = (table[16:24] + table[24:32]) + table[32:40]
    return spots, coeffs


def on_even(axis="sub"):
    return lax.rem(lax.axis_index(axis), 2) == 0


def first_kernel(cap, *refs):
    given, (post, to_near, to_next, face_r, face_l, ordinal) = refs[:6], refs[6:12]
    held, arrived = refs[12:18], refs[18]
    copies = [
        pltpu.make_async_copy(source, target, arrived.at[n])
        for n, (source, target) in enumerate(zip(given, held))
    ]
    for n in (4, 3, 5, 0, 1, 2):
        copies[n].start()
    pops, heat, solid, voxel, dest, coeff = held
    layers, across, along = solid.shape
    even = on_even()
    for n in (4, 3, 5):
        copies[n].wait()
    spots, coeffs = slot_tables(cap, voxel, dest, coeff, ordinal)
    extra = len(UP)
    for plane in (to_near, to_next):
        plane[extra] = jnp.zeros(plane.shape[1:], f32)
        plane[extra, :, 0:WIDTH] = spots
        plane[extra, :, WIDTH : 2 * WIDTH] = coeffs
    for n in (0, 1, 2):
        copies[n].wait()
    for z in range(layers):
        for start in range(0, along, WIDTH):
            lanes = slice(start, start + WIDTH)
            out = collide(
                [pops[i, z, :, lanes] for i in range(FLOWS)],
                [heat[j, z, :, lanes] for j in range(HEATS)],
                solid[z, :, lanes],
            )
            for i in LANES_ALL:
                post[i, z, :, lanes] = out[i]
            for face, lists, near, far in (
                (face_r, (STILL, RIGHT), across - 1, across - 2),
                (face_l, (STILL, LEFT), 0, 1),
            ):
                rows = [(i, near) for i in lists[0]] + [(i, far) for i in lists[1]]
                rows = rows + [(i, near) for i in lists[1]]
                for n, (i, column) in enumerate(rows):
                    at = n * layers + z
                    face[at : at + 1, lanes] = out[i][column : column + 1]
                at = len(rows) * layers + z
                face[at : at + 1, lanes] = solid[z, near : near + 1, lanes]
    for n, (above, below) in enumerate(zip(UP, DOWN)):
        above, below = post[above, layers - 1], post[below, 0]
        to_near[n] = jnp.where(even, above, below)
        to_next[n] = jnp.where(even, below, above)


def edge_kernel(layers, face_r, face_l, near, next_, to_a, to_b, out_r, out_l):
    out_r[...] = face_r[...]
    out_l[...] = face_l[...]
    across = near.shape[1]
    even = on_even()
    for out, lists, edge, inside in (
        (out_r, (STILL, RIGHT), across - 1, across - 2),
        (out_l, (STILL, LEFT), 0, 1),
    ):
        rows = [(i, edge) for i in lists[0]] + [(i, inside) for i in lists[1]]
        rows = rows + [(i, edge) for i in lists[1]]
        for n, (i, column) in enumerate(rows):
            rise = VELOCITY[i][2]
            if rise == 0:
                continue
            moved = range(layers - 1, 0, -1) if rise == 1 else range(layers - 1)
            for z in moved:
                at, source = n * layers + z, n * layers + z - rise
                out[at : at + 1, :] = out[source : source + 1, :]
            z = 0 if rise == 1 else layers - 1
            at = n * layers + z
            k = (UP if rise == 1 else DOWN).index(i)
            one, two = near[k, column : column + 1, :], next_[k, column : column + 1, :]
            out[at : at + 1, :] = jnp.where(even == (rise == 1), two, one)
    right, left, band_even = out_r[...], out_l[...], on_even("grp")
    to_a[...] = jnp.where(band_even, right, left)
    to_b[...] = jnp.where(band_even, left, right)


def turned(tile, step):
    return tile if step == 0 else pltpu.roll(tile, step % tile.shape[1], 1)


def second_kernel(
    post,
    near,
    next_,
    to_a,
    to_b,
    faces_a,
    faces_b,
    solid,
    own_table,
    tie,
    hot,
    motion,
    send_near,
    send_next,
    fluxes,
    moved,
    halo,
):
    layers, across, along = solid.shape
    even = on_even()
    band_even = on_even("grp")
    own_r = jnp.where(band_even, to_a[...], to_b[...])
    own_l = jnp.where(band_even, to_b[...], to_a[...])
    below = [jnp.where(even, next_[n], near[n]) for n in range(len(UP) + 1)]
    above = [jnp.where(even, near[n], next_[n]) for n in range(len(UP) + 1)]
    from_l = jnp.where(band_even, faces_b[...], faces_a[...])
    from_r = jnp.where(band_even, faces_a[...], faces_b[...])
    slot = lax.broadcasted_iota(jnp.int32, (across, along), 0)
    inner = len(FACE_RIGHT)
    for i in LANES_ALL:
        ex, ey, ez = VELOCITY[i]
        for z in range(layers):
            if z - ez < 0:
                tile = below[UP.index(i)]
            elif z - ez >= layers:
                tile = above[DOWN.index(i)]
            else:
                tile = post[i, z - ez]
            if ex == 1:
                at = (inner + RIGHT.index(i)) * layers + z
                tile = jnp.where(slot == 0, from_l[at : at + 1, :], pltpu.roll(tile, 1, 0))
            elif ex == -1:
                at = (inner + LEFT.index(i)) * layers + z
                tile = jnp.where(
                    slot == across - 1, from_r[at : at + 1, :], pltpu.roll(tile, across - 1, 0)
                )
            moved[i, z] = turned(tile, ey)
        if ex == -1:
            at = (inner + LEFT.index(i)) * layers
            low = own_l[at : at + layers, :]
        else:
            at = FACE_RIGHT.index(i) * layers
            low = from_l[at : at + layers, :]
        if ex == 1:
            at = (inner + RIGHT.index(i)) * layers
            high = own_r[at : at + layers, :]
        else:
            at = FACE_LEFT.index(i) * layers
            high = from_r[at : at + layers, :]
        sides = [low, high]
        if 2 * layers < 8:
            sides.append(jnp.ones((8 - 2 * layers, along), f32))
        halo[i] = turned(jnp.concatenate(sides, axis=0), ey)
    at = (FACE - 1) * layers
    edge_solid = [from_l[at : at + layers, :], from_r[at : at + layers, :]]
    if 2 * layers < 8:
        edge_solid.append(jnp.zeros((8 - 2 * layers, along), f32))
    edge_solid = jnp.concatenate(edge_solid, axis=0)
    for start in range(0, along, WIDTH):
        lanes = slice(start, start + WIDTH)
        for z in range(layers):
            out = collide(
                [moved[i, z, :, lanes] for i in range(FLOWS)],
                [moved[FLOWS + j, z, :, lanes] for j in range(HEATS)],
                solid[z, :, lanes],
            )
            for i in LANES_ALL:
                moved[i, z, :, lanes] = out[i]
        out = collide(
            [halo[i, :, lanes] for i in range(FLOWS)],
            [halo[FLOWS + j, :, lanes] for j in range(HEATS)],
            edge_solid[:, lanes],
        )
        for i in RIGHT + LEFT:
            halo[i, :, lanes] = out[i]
    sums = {}

    def add(key, sign, tile):
        if sign == 0:
            return
        if key in sums:
            sums[key] = sums[key] + tile if sign > 0 else sums[key] - tile
        else:
            sums[key] = tile if sign > 0 else -tile

    for z in range(layers):
        for i in LANES_ALL:
            ex, ey, ez = VELOCITY[i]
            if i == 0:
                continue
            tile = moved[i, z]
            if ex == 1:
                tile = jnp.where(slot == 0, halo[i, z : z + 1, :], pltpu.roll(tile, 1, 0))
            elif ex == -1:
                at = layers + z
                tile = jnp.where(
                    slot == across - 1, halo[i, at : at + 1, :], pltpu.roll(tile, across - 1, 0)
                )
            tile = turned(tile, ey)
            target = z + ez
            if i >= FLOWS:
                add((3, target), 1, tile)
            else:
                add((0, target), ex, tile)
                add((1, target), ey, tile)
                add((2, target), ez, tile)
    for z in range(layers):
        hot[z] = sums[3, z]
        for axis in range(3):
            motion[axis, z] = sums[axis, z]
    for part in range(4):
        send_near[part] = jnp.where(even, sums[part, layers], sums[part, -1])
        send_next[part] = jnp.where(even, sums[part, -1], sums[part, layers])
    extra = len(UP)
    per_line = along // WIDTH
    per_layer = across * per_line

    def flux(table, planes):
        index = table[:, 0:WIDTH].astype(jnp.int32)
        place, lane = index >> 7, index & 127
        out = jnp.zeros(lane.shape, f32)
        for z, plane in planes:
            for x in range(across):
                for c in range(per_line):
                    row = plane[x : x + 1, c * WIDTH : (c + 1) * WIDTH]
                    out = jnp.where(
                        place == z * per_layer + x * per_line + c, lane_gather(row, lane), out
                    )
        return out * table[:, WIDTH : 2 * WIDTH]

    mine = own_table[extra]
    fluxes[:, 0, :] = flux(mine, [(z, sums[3, z]) for z in range(layers)])
    fluxes[:, 1, :] = flux(above[extra], [(0, sums[3, layers])])
    fluxes[:, 2, :] = flux(below[extra], [(layers - 1, sums[3, -1])])
    fluxes[:, 3, :] = mine[:, WIDTH : 2 * WIDTH]


def coupled(vector, blocks, flipped, shift):
    count = vector.shape[0]
    upright = vector.T
    ahead, back = [], []
    for b in range(count):
        column = upright[:, b : b + 1]
        back.append(jnp.sum(blocks[b] * column, axis=0, keepdims=True))
        ahead.append(jnp.sum(flipped[b] * column, axis=0, keepdims=True))
    ahead = jnp.concatenate(ahead, axis=0)
    back = jnp.concatenate(back, axis=0)
    return pltpu.roll(ahead, lax.rem(count - shift, count), 0) + pltpu.roll(back, shift, 0)


def ready_kernel(
    pattern, nodes, diagonal, source, start, coupling, tie, hits, flipped, rest, slots, level
):
    shift = pattern[0, 0]
    count = start.shape[1]
    for b in range(count):
        flipped[lax.rem(b + shift, count)] = coupling[0, b].T
    vector = start[0]
    rest[...] = (
        source[0] - diagonal[0] * vector + coupled(vector, coupling.at[0], flipped, shift)
    )
    index = nodes[...]
    index = stacked(index)
    slots[...] = table_gather(vector, index)
    upright = (index & 127).astype(f32).T.astype(jnp.int32)
    lane = lax.broadcasted_iota(jnp.int32, (WIDTH, WIDTH), 1)
    for s in range(index.shape[0]):
        hit = jnp.where(upright[:, s : s + 1] == lane, 1.0, 0.0)
        hits[s * WIDTH : (s + 1) * WIDTH] = hit.astype(bf16)
    mean = jnp.sum(jnp.sum(diagonal[0], axis=0, keepdims=True), axis=1, keepdims=True)
    level[...] = jnp.broadcast_to(mean * (1.0 / (count * WIDTH)), level.shape)


def solve_kernel(
    cap,
    pattern,
    nodes,
    diagonal,
    start,
    coupling,
    hits,
    flipped,
    rest,
    slots,
    level,
    come,
    res,
    img,
    go,
):
    shift = pattern[0, 0]
    count = start.shape[1]
    index = stacked(nodes[...])
    place = index >> 7
    own, low, high, coeff = come[:, 0, :], come[:, 1, :], come[:, 2, :], come[:, 3, :]
    if cap == WIDTH:
        low = pltpu.roll(low, 1, 0)
        high = pltpu.roll(high, low.shape[0] - 1, 0)
    parts = three_parts(own + low + high) + three_parts(coeff)
    block = lax.broadcasted_iota(jnp.int32, (count, WIDTH), 0)
    values = []
    for s in range(index.shape[0]):
        mine = block == place[s : s + 1]
        values.append(
            jnp.concatenate([jnp.where(mine, part[s : s + 1], 0.0) for part in parts], axis=0)
        )
    values = jnp.concatenate(values, axis=1).astype(bf16)
    landed = jnp.dot(values, hits[...], preferred_element_type=f32)
    landed = [landed[k * count : (k + 1) * count] for k in range(len(parts))]
    added = (landed[0] + landed[1]) + landed[2]
    extra = (landed[3] + landed[4]) + landed[5]
    whole = diagonal[0] + extra
    residual = rest[...] + added - extra * start[0]
    blocks = coupling.at[0]
    image = whole * residual - coupled(residual, blocks, flipped, shift)

    def total(value):
        return jnp.sum(jnp.sum(value, axis=0, keepdims=True), axis=1, keepdims=True)

    ratio = level[0:1, :]
    offset = image - ratio * residual
    bend = whole * offset - coupled(offset, blocks, flipped, shift)
    totals = [
        total(residual * residual),
        total(residual * offset),
        total(offset * offset),
        total(offset * bend),
        ratio,
    ]
    res[...] = residual
    img[...] = image
    lane = lax.broadcasted_iota(jnp.int32, (8, WIDTH), 1) % cap
    facts = jnp.zeros((8, WIDTH), f32)
    for n, fact in enumerate(totals):
        facts = jnp.where(lane == n, fact, facts)
    residual_slots = table_gather(residual, index)
    image_slots = table_gather(image, index)
    start_slots = slots[...]
    for band in range(go.shape[0]):
        go[band, :, 0, :] = start_slots
        go[band, :, 1, :] = residual_slots
        go[band, :, 2, :] = image_slots
        go[band, :, 3, :] = facts


def last_kernel(direct, come, own, start, res, img, ordinal, temp, seen):
    facts = come[:, 3, :]
    norm, cross, square, energy, ratio = (facts[:, n : n + 1] for n in range(5))

    def total(value):
        return jnp.sum(value, axis=0, keepdims=True)

    product = ratio * norm + cross
    all_norm = total(norm)
    mean = total(product) / all_norm
    off = ratio - mean
    next_norm = total(square + off * (2.0 * cross + off * norm)) / (mean * mean)
    energy = energy + off * (2.0 * (square + ratio * cross) + off * product)
    energy = total(energy) / (mean * mean)
    growth = next_norm / all_norm
    step = next_norm / (energy - mean * growth * next_norm)
    of_residual = 1.0 / mean + step * (1.0 + growth)
    of_image = -step / mean
    temp[0] = start[0] + of_residual * res[...] + of_image * img[...]
    if direct:
        table = come[pl.ds(lax.axis_index("grp") * 8, 8)]
    else:
        table = own[...]
    table = table[:, 0, :] + of_residual * table[:, 1, :] + of_image * table[:, 2, :]
    places = stacked(ordinal[...])
    chunks = places.shape[0]
    if chunks < 8:
        places = jnp.concatenate([places, jnp.zeros((8 - chunks, WIDTH), jnp.int32)], axis=0)
    found = table_gather(table, places)
    for c in range(chunks):
        seen[:, c * WIDTH : (c + 1) * WIDTH] = found[c : c + 1]


def join_kernel(hot, motion, near, next_, hot_out, motion_out):
    layers = hot.shape[0]
    even = on_even()
    below = [jnp.where(even, next_[n], near[n]) for n in range(4)]
    above = [jnp.where(even, near[n], next_[n]) for n in range(4)]
    for z in range(layers):
        for part in range(4):
            tile = hot[z] if part == 3 else motion[part, z]
            if z == 0:
                tile = tile + below[part]
            if z == layers - 1:
                tile = tile + above[part]
            if part == 3:
                hot_out[z] = tile
            else:
                motion_out[part, z] = tile


VMEM = pl.BlockSpec(memory_space=pltpu.VMEM)
ANYWHERE = pl.BlockSpec(memory_space=pl.ANY)
SMEM = pl.BlockSpec(memory_space=pltpu.SMEM)


def call(kernel, out, args, name, scalars=(), scratch=(), far=False):
    total = sum(int(np.prod(a.shape)) * a.dtype.itemsize for a in list(args) + list(out))
    if far:
        args = [pltpu.with_memory_space_constraint(a, pltpu.HBM) for a in args]
    return pl.pallas_call(
        kernel,
        out_shape=out,
        in_specs=[
            ANYWHERE if far else SMEM if n in scalars else VMEM for n in range(len(args))
        ],
        out_specs=[VMEM] * len(out),
        scratch_shapes=scratch,
        compiler_params=pltpu.CompilerParams(vmem_limit_bytes=24 << 20),
        cost_estimate=pl.CostEstimate(flops=1 << 20, bytes_accessed=total, transcendentals=0),
        name=name,
    )(*args)


def shape(*dims, dtype=f32):
    return jax.ShapeDtypeStruct(dims, dtype)


def swaps(axis):
    count = lax.axis_size(axis)
    assert count % 2 == 0
    near = [(k, k + 1 - 2 * (k % 2)) for k in range(count)]
    return near, [(k, (k - 1 + 2 * (k % 2)) % count) for k in range(count)]


def body(
    populations,
    heat_pops,
    solid_frac,
    coupled_grid_point,
    dest_index,
    heat_coeff,
    slot_node,
    node_diag,
    coupling,
    block_pattern,
    heat_source,
    solid_start,
):
    layers, across, along = solid_frac.shape
    slabs, bands = lax.axis_size("sub"), lax.axis_size("grp")
    slots = slot_node.shape[1]
    cap = slots // slabs
    rows = coupled_grid_point.shape[1]
    blocks, piece = node_diag.shape[1:]
    lines = slots // WIDTH
    assert lines == 8 and across == 8 and along >= 2 * WIDTH and along % WIDTH == 0
    assert piece == WIDTH and blocks == 8 and WIDTH % cap == 0 and cap >= 8
    assert rows % WIDTH == 0 and rows <= 8 * WIDTH and layers <= 4
    face_rows = -(-FACE * layers // 8) * 8
    planes = len(UP) + 1
    post, to_near, to_next, face_r, face_l, ordinal = call(
        functools.partial(first_kernel, cap),
        [
            shape(FLOWS + HEATS, layers, across, along),
            shape(planes, across, along),
            shape(planes, across, along),
            shape(face_rows, along),
            shape(face_rows, along),
            shape(1, rows, dtype=jnp.int32),
        ],
        [
            populations,
            heat_pops,
            solid_frac,
            coupled_grid_point,
            dest_index.reshape(1, rows),
            heat_coeff,
        ],
        "collide_first",
        scratch=[
            pltpu.VMEM(solid_like, kind)
            for solid_like, kind in (
                (populations.shape, f32),
                (heat_pops.shape, f32),
                (solid_frac.shape, f32),
                ((1, rows), jnp.int32),
                ((1, rows), jnp.int32),
                ((1, rows), f32),
            )
        ]
        + [pltpu.SemaphoreType.DMA((6,))],
        far=True,
    )
    near_pairs, next_pairs = swaps("sub")
    near = lax.ppermute(to_near, "sub", near_pairs)
    next_ = lax.ppermute(to_next, "sub", next_pairs)
    to_a, to_b = call(
        functools.partial(edge_kernel, layers),
        [shape(face_rows, along)] * 2,
        [face_r, face_l, near, next_],
        "x_faces",
        scratch=[pltpu.VMEM((face_rows, along), f32)] * 2,
    )
    hits, flipped, rest, start_slots, level = call(
        ready_kernel,
        [
            shape(slots, WIDTH, dtype=bf16),
            shape(blocks, piece, piece),
            shape(blocks, piece),
            shape(lines, WIDTH),
            shape(8, WIDTH),
        ],
        [block_pattern, slot_node, node_diag, heat_source, solid_start, coupling, to_a],
        "solid_ready",
        scalars=(0,),
    )
    side_a, side_b = swaps("grp")
    faces_a = lax.ppermute(to_a, "grp", side_a)
    faces_b = lax.ppermute(to_b, "grp", side_b)
    hot, motion, send_near, send_next, fluxes = call(
        second_kernel,
        [
            shape(layers, across, along),
            shape(3, layers, across, along),
            shape(4, across, along),
            shape(4, across, along),
            shape(lines, 4, WIDTH),
        ],
        [post, near, next_, to_a, to_b, faces_a, faces_b, solid_frac, to_near, rest],
        "collide_second",
        scratch=[
            pltpu.VMEM((FLOWS + HEATS, layers, across, along), f32),
            pltpu.VMEM((FLOWS + HEATS, 8, along), f32),
        ],
    )
    settled = cap != WIDTH
    if settled:
        fluxes = fluxes.reshape(lines, 4, WIDTH // cap, cap).transpose(0, 2, 1, 3)
        fluxes = fluxes.reshape(slabs, 4, cap)
    landed = lax.all_to_all(fluxes, "sub", split_axis=0, concat_axis=0, tiled=True)
    if settled:
        landed = jnp.stack(
            [
                landed[:, 0],
                jnp.roll(landed[:, 1], 1, axis=0),
                jnp.roll(landed[:, 2], -1, axis=0),
                landed[:, 3],
            ]
        )
        landed = landed.reshape(4, lines, WIDTH).transpose(1, 0, 2)
    from_near = lax.ppermute(send_near, "sub", near_pairs)
    from_next = lax.ppermute(send_next, "sub", next_pairs)
    residual, image, go = call(
        functools.partial(solve_kernel, cap),
        [shape(blocks, piece), shape(blocks, piece), shape(bands, lines, 4, WIDTH)],
        [
            block_pattern,
            slot_node,
            node_diag,
            solid_start,
            coupling,
            hits,
            flipped,
            rest,
            start_slots,
            level,
            landed,
        ],
        "solve",
        scalars=(0,),
    )
    if settled:
        go = go.reshape(bands, lines, 4, WIDTH // cap, cap).transpose(0, 1, 3, 2, 4)
    go = go.reshape(bands * slabs, 4, cap)
    come = lax.all_to_all(go, ("grp", "sub"), split_axis=0, concat_axis=0, tiled=True)
    hot_out, motion_out = call(
        join_kernel,
        [shape(*hot.shape), shape(*motion.shape)],
        [hot, motion, from_near, from_next],
        "join",
    )
    if settled:
        own = lax.dynamic_slice_in_dim(come, lax.axis_index("grp") * slabs, slabs, 0)
        own = own.transpose(1, 0, 2).reshape(4, lines, WIDTH).transpose(1, 0, 2)
        come = jnp.pad(come, ((0, 0), (0, 0), (0, WIDTH - cap)))
    else:
        own = rest
    temp, seen = call(
        functools.partial(last_kernel, not settled),
        [shape(1, blocks, piece), shape(1, rows)],
        [
            come,
            own,
            solid_start,
            residual,
            image,
            ordinal,
        ],
        "finish",
    )
    return hot_out, motion_out, temp, seen


def solution(mesh):
    placed = (
        P(None, "sub", "grp", None),
        P(None, "sub", "grp", None),
        P("sub", "grp", None),
        P("grp", "sub"),
        P("grp", "sub", None),
        P("grp", "sub"),
        P("grp", "sub"),
        P("grp", "sub", None),
        P("grp", "sub", None, None),
        P("grp", "sub"),
        P("grp", "sub", None),
        P("grp", "sub", None),
    )
    return jax.shard_map(
        body,
        mesh=mesh,
        in_specs=placed,
        out_specs=(
            P("sub", "grp", None),
            P(None, "sub", "grp", None),
            P("grp", "sub", None),
            P("grp", "sub"),
        ),
        check_vma=False,
    )
```

```python
import functools
import jax
import jax.numpy as jnp
import numpy as np
from jax import lax
from jax.experimental import pallas as pl
from jax.experimental.pallas import tpu as pltpu
from jax.sharding import PartitionSpec as P

FLOW_VELOCITY = [
    (0, 0, 0),
    (1, 0, 0),
    (-1, 0, 0),
    (0, 1, 0),
    (0, -1, 0),
    (0, 0, 1),
    (0, 0, -1),
    (1, 1, 0),
    (-1, -1, 0),
    (1, -1, 0),
    (-1, 1, 0),
    (1, 0, 1),
    (-1, 0, -1),
    (1, 0, -1),
    (-1, 0, 1),
    (0, 1, 1),
    (0, -1, -1),
    (0, 1, -1),
    (0, -1, 1),
]
VELOCITY = FLOW_VELOCITY + FLOW_VELOCITY[:7]
FLOWS, HEATS = 19, 7
LANES_ALL = range(FLOWS + HEATS)
UP = [i for i in LANES_ALL if VELOCITY[i][2] == 1]
DOWN = [i for i in LANES_ALL if VELOCITY[i][2] == -1]
RIGHT = [i for i in LANES_ALL if VELOCITY[i][0] == 1]
LEFT = [
    next(j for j in LANES_ALL if VELOCITY[j] == (-1,) + VELOCITY[i][1:] and (j < 19) == (i < 19))
    for i in RIGHT
]
TURNED = [
    next(n for n, j in enumerate(RIGHT[:-1]) if VELOCITY[j][1:] == (-VELOCITY[i][1], -VELOCITY[i][2]))
    for i in RIGHT[:-1]
]
STILL = [i for i in LANES_ALL if VELOCITY[i][0] == 0]
GATHERED = len(STILL) + 2 * len(RIGHT) + 1
SUMS = 4
FACE = SUMS + 2 * len(RIGHT) + 1
WIDTH = 128
f32 = jnp.float32
bf16 = jnp.bfloat16


def signed_sum(terms):
    total = None
    for sign, term in terms:
        if sign == 0:
            continue
        if total is None:
            total = term if sign > 0 else -term
        else:
            total = total + term if sign > 0 else total - term
    return total


def collide(flow, heat, solid):
    pairs = range(1, FLOWS, 2)
    density = flow[0]
    for i in pairs:
        density = density + (flow[i] + flow[i + 1])
    gaps = {i: flow[i] - flow[i + 1] for i in pairs}
    scale = 1.0 / density
    speed = [
        signed_sum([(FLOW_VELOCITY[i][axis], gaps[i]) for i in pairs]) * scale for axis in range(3)
    ]
    square = speed[0] * speed[0] + speed[1] * speed[1] + speed[2] * speed[2]
    base = 1.0 - 1.5 * square
    gas = 1.0 - solid
    keep = gas * (1.0 - 1.0 / 0.8)
    pull = gas * (density * (1.0 / 0.8))
    flow_post = [None] * FLOWS
    flow_post[0] = (keep + solid) * flow[0] + (pull * (1.0 / 3.0)) * base
    shares = {1: pull * (1.0 / 18.0), 2: pull * (1.0 / 36.0)}
    for i in pairs:
        share = shares[sum(abs(c) for c in FLOW_VELOCITY[i])]
        along = signed_sum([(FLOW_VELOCITY[i][axis], speed[axis]) for axis in range(3)])
        even = base + 4.5 * along * along
        odd = 3.0 * along
        flow_post[i] = keep * flow[i] + share * (even + odd) + solid * flow[i + 1]
        flow_post[i + 1] = keep * flow[i + 1] + share * (even - odd) + solid * flow[i]
    hotness = heat[0]
    for j in range(1, HEATS):
        hotness = hotness + heat[j]
    stay = 1.0 - 1.0 / 0.7
    heat_post = [stay * heat[0] + (0.25 / 0.7) * hotness]
    level = (0.125 / 0.7) * hotness
    for j in range(1, HEATS, 2):
        axis = (j - 1) // 2
        drift = 4.0 * speed[axis]
        heat_post.append(stay * heat[j] + level * (1.0 + drift))
        heat_post.append(stay * heat[j + 1] + level * (1.0 - drift))
    return flow_post + heat_post


def collide_halo(still, inward, outward, solid):
    flows = RIGHT[:-1]
    density, along_y, along_z, hotness = still
    pairs = [(a + b, a - b) for a, b in zip(inward, outward)]
    across = None
    for n, i in enumerate(flows):
        _, ey, ez = VELOCITY[i]
        whole, gap = pairs[n]
        density = density + whole
        across = gap if across is None else across + gap
        along_y = signed_sum([(1, along_y), (ey, whole)])
        along_z = signed_sum([(1, along_z), (ez, whole)])
    hotness = hotness + pairs[-1][0]
    scale = 1.0 / density
    speed = [across * scale, along_y * scale, along_z * scale]
    square = speed[0] * speed[0] + speed[1] * speed[1] + speed[2] * speed[2]
    base = 1.0 - 1.5 * square
    gas = 1.0 - solid
    keep = gas * (1.0 - 1.0 / 0.8)
    pull = gas * (density * (1.0 / 0.8))
    shares = {1: pull * (1.0 / 18.0), 2: pull * (1.0 / 36.0)}
    out = []
    for n, i in enumerate(flows):
        share = shares[sum(abs(c) for c in VELOCITY[i])]
        along = signed_sum([(VELOCITY[i][axis], speed[axis]) for axis in range(3)])
        feq = share * (base + 4.5 * along * along + 3.0 * along)
        out.append(keep * inward[n] + feq + solid * outward[TURNED[n]])
    level = (0.125 / 0.7) * hotness
    out.append((1.0 - 1.0 / 0.7) * inward[-1] + level * (1.0 + 4.0 * speed[0]))
    return out


def three_parts(value):
    high = value.astype(bf16).astype(f32)
    rest = value - high
    middle = rest.astype(bf16).astype(f32)
    return [high, middle, rest - middle]


def times_transposed(left, right):
    return lax.dot_general(
        left.astype(bf16), right.astype(bf16), (((1,), (1,)), ((), ())), preferred_element_type=f32
    )


def spread(row):
    return jnp.broadcast_to(row, (8, row.shape[-1]))


def lane_gather(row, lane):
    return jnp.take_along_axis(spread(row), lane, axis=1, mode="promise_in_bounds")


def table_gather(table, index):
    place, lane = index >> 7, index & 127
    out = jnp.zeros(index.shape, f32)
    for row in range(table.shape[0]):
        out = jnp.where(place == row, lane_gather(table[row : row + 1], lane), out)
    return out


def stacked(row):
    return jnp.concatenate(
        [row[:, k * WIDTH : (k + 1) * WIDTH] for k in range(row.shape[1] // WIDTH)], axis=0
    )


def slot_tables(cap, voxel, dest, coeff, ordinal):
    rows_here = dest.shape[1]
    owner = dest[...].astype(f32)
    chunks = rows_here // WIDTH
    tall = stacked(owner)
    tall = jnp.concatenate([tall] + [jnp.zeros((8 - chunks, WIDTH), f32)] * (chunks < 8), axis=0)
    upright = tall.T
    first = lax.broadcasted_iota(jnp.int32, (WIDTH, WIDTH), 0)
    second = lax.broadcasted_iota(jnp.int32, (WIDTH, WIDTH), 1)
    slot_row = lax.broadcasted_iota(jnp.int32, (8, WIDTH), 0)
    table = jnp.zeros((40, WIDTH), f32)
    for c in range(chunks):
        lanes = slice(c * WIDTH, (c + 1) * WIDTH)
        here = owner[:, lanes]
        count = jnp.zeros((WIDTH, WIDTH), f32)
        for other in range(c + 1):
            same = upright[:, other : other + 1] == here
            if other == c:
                same = same & (first < second)
            count = count + jnp.where(same, 1.0, 0.0)
        rank = jnp.sum(count, axis=0, keepdims=True)
        place = (here * float(cap) + rank).astype(jnp.int32)
        ordinal[:, lanes] = place
        mine = slot_row == (place >> 7)
        spot = voxel[:, lanes]
        parts = [(spot >> 7).astype(f32), (spot & 127).astype(f32)] + three_parts(coeff[:, lanes])
        values = jnp.concatenate([jnp.where(mine, part, 0.0) for part in parts], axis=0)
        table = table + times_transposed(values, jnp.where(first == (place & 127), 1.0, 0.0))
    spots = table[0:8] * float(WIDTH) + table[8:16]
    coeffs = (table[16:24] + table[24:32]) + table[32:40]
    return spots, coeffs


def on_even(axis="sub"):
    return lax.rem(lax.axis_index(axis), 2) == 0


def first_kernel(cap, *refs):
    given, (post, to_near, to_next, face_r, face_l, ordinal) = refs[:6], refs[6:12]
    held, arrived = refs[12:18], refs[18]
    copies = [
        pltpu.make_async_copy(source, target, arrived.at[n])
        for n, (source, target) in enumerate(zip(given, held))
    ]
    for n in (4, 3, 5, 0, 1, 2):
        copies[n].start()
    pops, heat, solid, voxel, dest, coeff = held
    layers, across, along = solid.shape
    even = on_even()
    for n in (4, 3, 5):
        copies[n].wait()
    spots, coeffs = slot_tables(cap, voxel, dest, coeff, ordinal)
    extra = len(UP)
    for plane in (to_near, to_next):
        plane[extra] = jnp.zeros(plane.shape[1:], f32)
        plane[extra, :, 0:WIDTH] = spots
        plane[extra, :, WIDTH : 2 * WIDTH] = coeffs
    for n in (0, 1, 2):
        copies[n].wait()
    for z in range(layers):
        for start in range(0, along, WIDTH):
            lanes = slice(start, start + WIDTH)
            out = collide(
                [pops[i, z, :, lanes] for i in range(FLOWS)],
                [heat[j, z, :, lanes] for j in range(HEATS)],
                solid[z, :, lanes],
            )
            for i in LANES_ALL:
                post[i, z, :, lanes] = out[i]
            for face, lists, near, far in (
                (face_r, (STILL, RIGHT), across - 1, across - 2),
                (face_l, (STILL, LEFT), 0, 1),
            ):
                rows = [(i, near) for i in lists[0]] + [(i, far) for i in lists[1]]
                rows = rows + [(i, near) for i in lists[1]]
                for n, (i, column) in enumerate(rows):
                    at = n * layers + z
                    face[at : at + 1, lanes] = out[i][column : column + 1]
                at = len(rows) * layers + z
                face[at : at + 1, lanes] = solid[z, near : near + 1, lanes]
    for n, (above, below) in enumerate(zip(UP, DOWN)):
        above, below = post[above, layers - 1], post[below, 0]
        to_near[n] = jnp.where(even, above, below)
        to_next[n] = jnp.where(even, below, above)


def turned(tile, step):
    return tile if step == 0 else pltpu.roll(tile, step % tile.shape[1], 1)


def edge_kernel(layers, face_r, face_l, near, next_, to_a, to_b, out_r, out_l):
    out_r[...] = face_r[...]
    out_l[...] = face_l[...]
    across = near.shape[1]
    even = on_even()
    for out, lists, edge, inside in (
        (out_r, (STILL, RIGHT), across - 1, across - 2),
        (out_l, (STILL, LEFT), 0, 1),
    ):
        rows = [(i, edge) for i in lists[0]] + [(i, inside) for i in lists[1]]
        rows = rows + [(i, edge) for i in lists[1]]
        for n, (i, column) in enumerate(rows):
            rise = VELOCITY[i][2]
            if rise == 0:
                continue
            moved = range(layers - 1, 0, -1) if rise == 1 else range(layers - 1)
            for z in moved:
                at, source = n * layers + z, n * layers + z - rise
                out[at : at + 1, :] = out[source : source + 1, :]
            z = 0 if rise == 1 else layers - 1
            at = n * layers + z
            k = (UP if rise == 1 else DOWN).index(i)
            one, two = near[k, column : column + 1, :], next_[k, column : column + 1, :]
            out[at : at + 1, :] = jnp.where(even == (rise == 1), two, one)
    band_even = on_even("grp")

    def both(n):
        at = slice(n * layers, (n + 1) * layers)
        return jnp.concatenate([out_r[at, :], out_l[at, :]], axis=0)

    def send(n, tile):
        at = slice(n * layers, (n + 1) * layers)
        right, left = tile[0:layers], tile[layers : 2 * layers]
        to_a[at, :] = jnp.where(band_even, right, left)
        to_b[at, :] = jnp.where(band_even, left, right)

    sums = [[] for _ in range(SUMS)]
    for n, i in enumerate(STILL):
        _, ey, ez = VELOCITY[i]
        tile = turned(both(n), ey)
        if i >= FLOWS:
            sums[3].append((1, tile))
        else:
            sums[0].append((1, tile))
            sums[1].append((ey, tile))
            sums[2].append((ez, tile))
    for n in range(SUMS):
        send(n, signed_sum(sums[n]))
    for n, i in enumerate(RIGHT):
        send(SUMS + n, turned(both(len(STILL) + n), VELOCITY[i][1]))
    for n in range(len(STILL) + len(RIGHT), GATHERED):
        send(n - len(STILL) + SUMS, both(n))


def second_kernel(
    post,
    near,
    next_,
    to_a,
    to_b,
    faces_a,
    faces_b,
    solid,
    own_table,
    tie,
    hot,
    motion,
    send_near,
    send_next,
    fluxes,
    moved,
    halo,
):
    layers, across, along = solid.shape
    even = on_even()
    band_even = on_even("grp")
    own_r = jnp.where(band_even, to_a[...], to_b[...])
    own_l = jnp.where(band_even, to_b[...], to_a[...])
    below = [jnp.where(even, next_[n], near[n]) for n in range(len(UP) + 1)]
    above = [jnp.where(even, near[n], next_[n]) for n in range(len(UP) + 1)]
    from_l = jnp.where(band_even, faces_b[...], faces_a[...])
    from_r = jnp.where(band_even, faces_a[...], faces_b[...])
    slot = lax.broadcasted_iota(jnp.int32, (across, along), 0)
    edge = SUMS + len(RIGHT)
    for i in LANES_ALL:
        ex, ey, ez = VELOCITY[i]
        for z in range(layers):
            if z - ez < 0:
                tile = below[UP.index(i)]
            elif z - ez >= layers:
                tile = above[DOWN.index(i)]
            else:
                tile = post[i, z - ez]
            if ex == 1:
                at = (edge + RIGHT.index(i)) * layers + z
                tile = jnp.where(slot == 0, from_l[at : at + 1, :], pltpu.roll(tile, 1, 0))
            elif ex == -1:
                at = (edge + LEFT.index(i)) * layers + z
                tile = jnp.where(
                    slot == across - 1, from_r[at : at + 1, :], pltpu.roll(tile, across - 1, 0)
                )
            moved[i, z] = turned(tile, ey)

    def halves(low, high, n):
        at = slice(n * layers, (n + 1) * layers)
        parts = [low[at], high[at]]
        if 2 * layers < 8:
            parts.append(jnp.ones((8 - 2 * layers, along), f32))
        return jnp.concatenate(parts, axis=0)

    for n in range(edge):
        halo[n] = halves(from_l, from_r, n)
    for n, i in enumerate(RIGHT):
        halo[edge + n] = turned(halves(own_l, own_r, edge + n), VELOCITY[i][1])
    edge_solid = halves(from_l, from_r, FACE - 1)
    for start in range(0, along, WIDTH):
        lanes = slice(start, start + WIDTH)
        for z in range(layers):
            out = collide(
                [moved[i, z, :, lanes] for i in range(FLOWS)],
                [moved[FLOWS + j, z, :, lanes] for j in range(HEATS)],
                solid[z, :, lanes],
            )
            for i in LANES_ALL:
                moved[i, z, :, lanes] = out[i]
        out = collide_halo(
            [halo[n, :, lanes] for n in range(SUMS)],
            [halo[SUMS + n, :, lanes] for n in range(len(RIGHT))],
            [halo[edge + n, :, lanes] for n in range(len(RIGHT))],
            edge_solid[:, lanes],
        )
        for n in range(len(RIGHT)):
            halo[SUMS + n, :, lanes] = out[n]
    sums = {}

    def add(key, sign, tile):
        if sign == 0:
            return
        if key in sums:
            sums[key] = sums[key] + tile if sign > 0 else sums[key] - tile
        else:
            sums[key] = tile if sign > 0 else -tile

    for z in range(layers):
        for i in LANES_ALL:
            ex, ey, ez = VELOCITY[i]
            if i == 0:
                continue
            tile = moved[i, z]
            if ex == 1:
                side = halo[SUMS + RIGHT.index(i), z : z + 1, :]
                tile = jnp.where(slot == 0, side, pltpu.roll(tile, 1, 0))
            elif ex == -1:
                at = layers + z
                side = halo[SUMS + LEFT.index(i), at : at + 1, :]
                tile = jnp.where(slot == across - 1, side, pltpu.roll(tile, across - 1, 0))
            tile = turned(tile, ey)
            target = z + ez
            if i >= FLOWS:
                add((3, target), 1, tile)
            else:
                add((0, target), ex, tile)
                add((1, target), ey, tile)
                add((2, target), ez, tile)
    for z in range(layers):
        hot[z] = sums[3, z]
        for axis in range(3):
            motion[axis, z] = sums[axis, z]
    for part in range(4):
        send_near[part] = jnp.where(even, sums[part, layers], sums[part, -1])
        send_next[part] = jnp.where(even, sums[part, -1], sums[part, layers])
    extra = len(UP)
    per_line = along // WIDTH
    per_layer = across * per_line

    def flux(table, planes):
        index = table[:, 0:WIDTH].astype(jnp.int32)
        place, lane = index >> 7, index & 127
        out = jnp.zeros(lane.shape, f32)
        for z, plane in planes:
            for x in range(across):
                for c in range(per_line):
                    row = plane[x : x + 1, c * WIDTH : (c + 1) * WIDTH]
                    out = jnp.where(
                        place == z * per_layer + x * per_line + c, lane_gather(row, lane), out
                    )
        return out * table[:, WIDTH : 2 * WIDTH]

    mine = own_table[extra]
    fluxes[:, 0, :] = flux(mine, [(z, sums[3, z]) for z in range(layers)])
    fluxes[:, 1, :] = flux(above[extra], [(0, sums[3, layers])])
    fluxes[:, 2, :] = flux(below[extra], [(layers - 1, sums[3, -1])])
    fluxes[:, 3, :] = mine[:, WIDTH : 2 * WIDTH]


def coupled(vector, blocks, flipped, shift):
    count = vector.shape[0]
    upright = vector.T
    ahead, back = [], []
    for b in range(count):
        column = upright[:, b : b + 1]
        back.append(jnp.sum(blocks[b] * column, axis=0, keepdims=True))
        ahead.append(jnp.sum(flipped[b] * column, axis=0, keepdims=True))
    ahead = jnp.concatenate(ahead, axis=0)
    back = jnp.concatenate(back, axis=0)
    return pltpu.roll(ahead, lax.rem(count - shift, count), 0) + pltpu.roll(back, shift, 0)


def ready_kernel(
    pattern, nodes, diagonal, source, start, coupling, tie, hits, flipped, rest, slots, level
):
    shift = pattern[0, 0]
    count = start.shape[1]
    for b in range(count):
        flipped[lax.rem(b + shift, count)] = coupling[0, b].T
    vector = start[0]
    rest[...] = (
        source[0] - diagonal[0] * vector + coupled(vector, coupling.at[0], flipped, shift)
    )
    index = nodes[...]
    index = stacked(index)
    slots[...] = table_gather(vector, index)
    upright = (index & 127).astype(f32).T.astype(jnp.int32)
    lane = lax.broadcasted_iota(jnp.int32, (WIDTH, WIDTH), 1)
    for s in range(index.shape[0]):
        hit = jnp.where(upright[:, s : s + 1] == lane, 1.0, 0.0)
        hits[s * WIDTH : (s + 1) * WIDTH] = hit.astype(bf16)
    mean = jnp.sum(jnp.sum(diagonal[0], axis=0, keepdims=True), axis=1, keepdims=True)
    level[...] = jnp.broadcast_to(mean * (1.0 / (count * WIDTH)), level.shape)


def solve_kernel(
    cap,
    pattern,
    nodes,
    diagonal,
    start,
    coupling,
    hits,
    flipped,
    rest,
    slots,
    level,
    come,
    res,
    img,
    go,
):
    shift = pattern[0, 0]
    count = start.shape[1]
    index = stacked(nodes[...])
    place = index >> 7
    own, low, high, coeff = come[:, 0, :], come[:, 1, :], come[:, 2, :], come[:, 3, :]
    if cap == WIDTH:
        low = pltpu.roll(low, 1, 0)
        high = pltpu.roll(high, low.shape[0] - 1, 0)
    parts = three_parts(own + low + high) + three_parts(coeff)
    block = lax.broadcasted_iota(jnp.int32, (count, WIDTH), 0)
    values = []
    for s in range(index.shape[0]):
        mine = block == place[s : s + 1]
        values.append(
            jnp.concatenate([jnp.where(mine, part[s : s + 1], 0.0) for part in parts], axis=0)
        )
    values = jnp.concatenate(values, axis=1).astype(bf16)
    landed = jnp.dot(values, hits[...], preferred_element_type=f32)
    landed = [landed[k * count : (k + 1) * count] for k in range(len(parts))]
    added = (landed[0] + landed[1]) + landed[2]
    extra = (landed[3] + landed[4]) + landed[5]
    whole = diagonal[0] + extra
    residual = rest[...] + added - extra * start[0]
    blocks = coupling.at[0]
    image = whole * residual - coupled(residual, blocks, flipped, shift)

    def total(value):
        return jnp.sum(jnp.sum(value, axis=0, keepdims=True), axis=1, keepdims=True)

    ratio = level[0:1, :]
    offset = image - ratio * residual
    bend = whole * offset - coupled(offset, blocks, flipped, shift)
    totals = [
        total(residual * residual),
        total(residual * offset),
        total(offset * offset),
        total(offset * bend),
        ratio,
    ]
    res[...] = residual
    img[...] = image
    lane = lax.broadcasted_iota(jnp.int32, (8, WIDTH), 1) % cap
    facts = jnp.zeros((8, WIDTH), f32)
    for n, fact in enumerate(totals):
        facts = jnp.where(lane == n, fact, facts)
    residual_slots = table_gather(residual, index)
    image_slots = table_gather(image, index)
    start_slots = slots[...]
    for band in range(go.shape[0]):
        go[band, :, 0, :] = start_slots
        go[band, :, 1, :] = residual_slots
        go[band, :, 2, :] = image_slots
        go[band, :, 3, :] = facts


def last_kernel(direct, come, own, start, res, img, ordinal, temp, seen):
    facts = come[:, 3, :]
    norm, cross, square, energy, ratio = (facts[:, n : n + 1] for n in range(5))

    def total(value):
        return jnp.sum(value, axis=0, keepdims=True)

    product = ratio * norm + cross
    all_norm = total(norm)
    mean = total(product) / all_norm
    off = ratio - mean
    next_norm = total(square + off * (2.0 * cross + off * norm)) / (mean * mean)
    energy = energy + off * (2.0 * (square + ratio * cross) + off * product)
    energy = total(energy) / (mean * mean)
    growth = next_norm / all_norm
    step = next_norm / (energy - mean * growth * next_norm)
    of_residual = 1.0 / mean + step * (1.0 + growth)
    of_image = -step / mean
    temp[0] = start[0] + of_residual * res[...] + of_image * img[...]
    if direct:
        table = come[pl.ds(lax.axis_index("grp") * 8, 8)]
    else:
        table = own[...]
    table = table[:, 0, :] + of_residual * table[:, 1, :] + of_image * table[:, 2, :]
    places = stacked(ordinal[...])
    chunks = places.shape[0]
    if chunks < 8:
        places = jnp.concatenate([places, jnp.zeros((8 - chunks, WIDTH), jnp.int32)], axis=0)
    found = table_gather(table, places)
    for c in range(chunks):
        seen[:, c * WIDTH : (c + 1) * WIDTH] = found[c : c + 1]


def join_kernel(hot, motion, near, next_, hot_out, motion_out):
    layers = hot.shape[0]
    even = on_even()
    below = [jnp.where(even, next_[n], near[n]) for n in range(4)]
    above = [jnp.where(even, near[n], next_[n]) for n in range(4)]
    for z in range(layers):
        for part in range(4):
            tile = hot[z] if part == 3 else motion[part, z]
            if z == 0:
                tile = tile + below[part]
            if z == layers - 1:
                tile = tile + above[part]
            if part == 3:
                hot_out[z] = tile
            else:
                motion_out[part, z] = tile


VMEM = pl.BlockSpec(memory_space=pltpu.VMEM)
ANYWHERE = pl.BlockSpec(memory_space=pl.ANY)
SMEM = pl.BlockSpec(memory_space=pltpu.SMEM)


def call(kernel, out, args, name, scalars=(), scratch=(), far=False):
    total = sum(int(np.prod(a.shape)) * a.dtype.itemsize for a in list(args) + list(out))
    if far:
        args = [pltpu.with_memory_space_constraint(a, pltpu.HBM) for a in args]
    return pl.pallas_call(
        kernel,
        out_shape=out,
        in_specs=[
            ANYWHERE if far else SMEM if n in scalars else VMEM for n in range(len(args))
        ],
        out_specs=[VMEM] * len(out),
        scratch_shapes=scratch,
        compiler_params=pltpu.CompilerParams(vmem_limit_bytes=24 << 20),
        cost_estimate=pl.CostEstimate(flops=1 << 20, bytes_accessed=total, transcendentals=0),
        name=name,
    )(*args)


def shape(*dims, dtype=f32):
    return jax.ShapeDtypeStruct(dims, dtype)


def swaps(axis):
    count = lax.axis_size(axis)
    assert count % 2 == 0
    near = [(k, k + 1 - 2 * (k % 2)) for k in range(count)]
    return near, [(k, (k - 1 + 2 * (k % 2)) % count) for k in range(count)]


def body(
    populations,
    heat_pops,
    solid_frac,
    coupled_grid_point,
    dest_index,
    heat_coeff,
    slot_node,
    node_diag,
    coupling,
    block_pattern,
    heat_source,
    solid_start,
):
    layers, across, along = solid_frac.shape
    slabs, bands = lax.axis_size("sub"), lax.axis_size("grp")
    slots = slot_node.shape[1]
    cap = slots // slabs
    rows = coupled_grid_point.shape[1]
    blocks, piece = node_diag.shape[1:]
    lines = slots // WIDTH
    assert lines == 8 and across == 8 and along >= 2 * WIDTH and along % WIDTH == 0
    assert piece == WIDTH and blocks == 8 and WIDTH % cap == 0 and cap >= 8
    assert rows % WIDTH == 0 and rows <= 8 * WIDTH and layers <= 4
    gathered_rows = -(-GATHERED * layers // 8) * 8
    face_rows = -(-FACE * layers // 8) * 8
    planes = len(UP) + 1
    post, to_near, to_next, face_r, face_l, ordinal = call(
        functools.partial(first_kernel, cap),
        [
            shape(FLOWS + HEATS, layers, across, along),
            shape(planes, across, along),
            shape(planes, across, along),
            shape(gathered_rows, along),
            shape(gathered_rows, along),
            shape(1, rows, dtype=jnp.int32),
        ],
        [
            populations,
            heat_pops,
            solid_frac,
            coupled_grid_point,
            dest_index.reshape(1, rows),
            heat_coeff,
        ],
        "collide_first",
        scratch=[
            pltpu.VMEM(solid_like, kind)
            for solid_like, kind in (
                (populations.shape, f32),
                (heat_pops.shape, f32),
                (solid_frac.shape, f32),
                ((1, rows), jnp.int32),
                ((1, rows), jnp.int32),
                ((1, rows), f32),
            )
        ]
        + [pltpu.SemaphoreType.DMA((6,))],
        far=True,
    )
    near_pairs, next_pairs = swaps("sub")
    near = lax.ppermute(to_near, "sub", near_pairs)
    next_ = lax.ppermute(to_next, "sub", next_pairs)
    to_a, to_b = call(
        functools.partial(edge_kernel, layers),
        [shape(face_rows, along)] * 2,
        [face_r, face_l, near, next_],
        "x_faces",
        scratch=[pltpu.VMEM((gathered_rows, along), f32)] * 2,
    )
    hits, flipped, rest, start_slots, level = call(
        ready_kernel,
        [
            shape(slots, WIDTH, dtype=bf16),
            shape(blocks, piece, piece),
            shape(blocks, piece),
            shape(lines, WIDTH),
            shape(8, WIDTH),
        ],
        [block_pattern, slot_node, node_diag, heat_source, solid_start, coupling, to_a],
        "solid_ready",
        scalars=(0,),
    )
    side_a, side_b = swaps("grp")
    faces_a = lax.ppermute(to_a, "grp", side_a)
    faces_b = lax.ppermute(to_b, "grp", side_b)
    hot, motion, send_near, send_next, fluxes = call(
        second_kernel,
        [
            shape(layers, across, along),
            shape(3, layers, across, along),
            shape(4, across, along),
            shape(4, across, along),
            shape(lines, 4, WIDTH),
        ],
        [post, near, next_, to_a, to_b, faces_a, faces_b, solid_frac, to_near, rest],
        "collide_second",
        scratch=[
            pltpu.VMEM((FLOWS + HEATS, layers, across, along), f32),
            pltpu.VMEM((FACE - 1, 8, along), f32),
        ],
    )
    settled = cap != WIDTH
    if settled:
        fluxes = fluxes.reshape(lines, 4, WIDTH // cap, cap).transpose(0, 2, 1, 3)
        fluxes = fluxes.reshape(slabs, 4, cap)
    landed = lax.all_to_all(fluxes, "sub", split_axis=0, concat_axis=0, tiled=True)
    if settled:
        landed = jnp.stack(
            [
                landed[:, 0],
                jnp.roll(landed[:, 1], 1, axis=0),
                jnp.roll(landed[:, 2], -1, axis=0),
                landed[:, 3],
            ]
        )
        landed = landed.reshape(4, lines, WIDTH).transpose(1, 0, 2)
    from_near = lax.ppermute(send_near, "sub", near_pairs)
    from_next = lax.ppermute(send_next, "sub", next_pairs)
    residual, image, go = call(
        functools.partial(solve_kernel, cap),
        [shape(blocks, piece), shape(blocks, piece), shape(bands, lines, 4, WIDTH)],
        [
            block_pattern,
            slot_node,
            node_diag,
            solid_start,
            coupling,
            hits,
            flipped,
            rest,
            start_slots,
            level,
            landed,
        ],
        "solve",
        scalars=(0,),
    )
    if settled:
        go = go.reshape(bands, lines, 4, WIDTH // cap, cap).transpose(0, 1, 3, 2, 4)
    go = go.reshape(bands * slabs, 4, cap)
    come = lax.all_to_all(go, ("grp", "sub"), split_axis=0, concat_axis=0, tiled=True)
    hot_out, motion_out = call(
        join_kernel,
        [shape(*hot.shape), shape(*motion.shape)],
        [hot, motion, from_near, from_next],
        "join",
    )
    if settled:
        own = lax.dynamic_slice_in_dim(come, lax.axis_index("grp") * slabs, slabs, 0)
        own = own.transpose(1, 0, 2).reshape(4, lines, WIDTH).transpose(1, 0, 2)
        come = jnp.pad(come, ((0, 0), (0, 0), (0, WIDTH - cap)))
    else:
        own = rest
    temp, seen = call(
        functools.partial(last_kernel, not settled),
        [shape(1, blocks, piece), shape(1, rows)],
        [
            come,
            own,
            solid_start,
            residual,
            image,
            ordinal,
        ],
        "finish",
    )
    return hot_out, motion_out, temp, seen


def solution(mesh):
    placed = (
        P(None, "sub", "grp", None),
        P(None, "sub", "grp", None),
        P("sub", "grp", None),
        P("grp", "sub"),
        P("grp", "sub", None),
        P("grp", "sub"),
        P("grp", "sub"),
        P("grp", "sub", None),
        P("grp", "sub", None, None),
        P("grp", "sub"),
        P("grp", "sub", None),
        P("grp", "sub", None),
    )
    return jax.shard_map(
        body,
        mesh=mesh,
        in_specs=placed,
        out_specs=(
            P("sub", "grp", None),
            P(None, "sub", "grp", None),
            P("grp", "sub", None),
            P("grp", "sub"),
        ),
        check_vma=False,
    )
```

```python
import functools
import jax
import jax.numpy as jnp
import numpy as np
from jax import lax
from jax.experimental import pallas as pl
from jax.experimental.pallas import tpu as pltpu
from jax.sharding import PartitionSpec as P

FLOW_VELOCITY = [
    (0, 0, 0),
    (1, 0, 0),
    (-1, 0, 0),
    (0, 1, 0),
    (0, -1, 0),
    (0, 0, 1),
    (0, 0, -1),
    (1, 1, 0),
    (-1, -1, 0),
    (1, -1, 0),
    (-1, 1, 0),
    (1, 0, 1),
    (-1, 0, -1),
    (1, 0, -1),
    (-1, 0, 1),
    (0, 1, 1),
    (0, -1, -1),
    (0, 1, -1),
    (0, -1, 1),
]
VELOCITY = FLOW_VELOCITY + FLOW_VELOCITY[:7]
FLOWS, HEATS = 19, 7
LANES_ALL = range(FLOWS + HEATS)
UP = [i for i in LANES_ALL if VELOCITY[i][2] == 1]
DOWN = [i for i in LANES_ALL if VELOCITY[i][2] == -1]
RIGHT = [i for i in LANES_ALL if VELOCITY[i][0] == 1]
LEFT = [
    next(j for j in LANES_ALL if VELOCITY[j] == (-1,) + VELOCITY[i][1:] and (j < 19) == (i < 19))
    for i in RIGHT
]
TURNED = [
    next(n for n, j in enumerate(RIGHT[:-1]) if VELOCITY[j][1:] == (-VELOCITY[i][1], -VELOCITY[i][2]))
    for i in RIGHT[:-1]
]
STILL = [i for i in LANES_ALL if VELOCITY[i][0] == 0]
GATHERED = len(STILL) + 2 * len(RIGHT) + 1
SUMS = 4
FACE = SUMS + 2 * len(RIGHT) + 1
WIDTH = 128
SHIFT = 4.0
f32 = jnp.float32
bf16 = jnp.bfloat16


def signed_sum(terms):
    total = None
    for sign, term in terms:
        if sign == 0:
            continue
        if total is None:
            total = term if sign > 0 else -term
        else:
            total = total + term if sign > 0 else total - term
    return total


def collide(flow, heat, solid):
    pairs = range(1, FLOWS, 2)
    density = flow[0]
    for i in pairs:
        density = density + (flow[i] + flow[i + 1])
    gaps = {i: flow[i] - flow[i + 1] for i in pairs}
    scale = 1.0 / density
    speed = [
        signed_sum([(FLOW_VELOCITY[i][axis], gaps[i]) for i in pairs]) * scale for axis in range(3)
    ]
    square = speed[0] * speed[0] + speed[1] * speed[1] + speed[2] * speed[2]
    base = 1.0 - 1.5 * square
    gas = 1.0 - solid
    keep = gas * (1.0 - 1.0 / 0.8)
    pull = gas * (density * (1.0 / 0.8))
    flow_post = [None] * FLOWS
    flow_post[0] = (keep + solid) * flow[0] + (pull * (1.0 / 3.0)) * base
    shares = {1: pull * (1.0 / 18.0), 2: pull * (1.0 / 36.0)}
    for i in pairs:
        share = shares[sum(abs(c) for c in FLOW_VELOCITY[i])]
        along = signed_sum([(FLOW_VELOCITY[i][axis], speed[axis]) for axis in range(3)])
        even = base + 4.5 * along * along
        odd = 3.0 * along
        flow_post[i] = keep * flow[i] + share * (even + odd) + solid * flow[i + 1]
        flow_post[i + 1] = keep * flow[i + 1] + share * (even - odd) + solid * flow[i]
    hotness = heat[0]
    for j in range(1, HEATS):
        hotness = hotness + heat[j]
    stay = 1.0 - 1.0 / 0.7
    heat_post = [stay * heat[0] + (0.25 / 0.7) * hotness]
    level = (0.125 / 0.7) * hotness
    for j in range(1, HEATS, 2):
        axis = (j - 1) // 2
        drift = 4.0 * speed[axis]
        heat_post.append(stay * heat[j] + level * (1.0 + drift))
        heat_post.append(stay * heat[j + 1] + level * (1.0 - drift))
    return flow_post + heat_post


def collide_halo(still, inward, outward, solid):
    flows = RIGHT[:-1]
    density, along_y, along_z, hotness = still
    pairs = [(a + b, a - b) for a, b in zip(inward, outward)]
    across = None
    for n, i in enumerate(flows):
        _, ey, ez = VELOCITY[i]
        whole, gap = pairs[n]
        density = density + whole
        across = gap if across is None else across + gap
        along_y = signed_sum([(1, along_y), (ey, whole)])
        along_z = signed_sum([(1, along_z), (ez, whole)])
    hotness = hotness + pairs[-1][0]
    scale = 1.0 / density
    speed = [across * scale, along_y * scale, along_z * scale]
    square = speed[0] * speed[0] + speed[1] * speed[1] + speed[2] * speed[2]
    base = 1.0 - 1.5 * square
    gas = 1.0 - solid
    keep = gas * (1.0 - 1.0 / 0.8)
    pull = gas * (density * (1.0 / 0.8))
    shares = {1: pull * (1.0 / 18.0), 2: pull * (1.0 / 36.0)}
    out = []
    for n, i in enumerate(flows):
        share = shares[sum(abs(c) for c in VELOCITY[i])]
        along = signed_sum([(VELOCITY[i][axis], speed[axis]) for axis in range(3)])
        feq = share * (base + 4.5 * along * along + 3.0 * along)
        out.append(keep * inward[n] + feq + solid * outward[TURNED[n]])
    level = (0.125 / 0.7) * hotness
    out.append((1.0 - 1.0 / 0.7) * inward[-1] + level * (1.0 + 4.0 * speed[0]))
    return out


def three_parts(value):
    high = value.astype(bf16).astype(f32)
    rest = value - high
    middle = rest.astype(bf16).astype(f32)
    return [high, middle, rest - middle]


def times_transposed(left, right):
    return lax.dot_general(
        left.astype(bf16), right.astype(bf16), (((1,), (1,)), ((), ())), preferred_element_type=f32
    )


def spread(row):
    return jnp.broadcast_to(row, (8, row.shape[-1]))


def lane_gather(row, lane):
    return jnp.take_along_axis(spread(row), lane, axis=1, mode="promise_in_bounds")


def table_gather(table, index):
    place, lane = index >> 7, index & 127
    out = jnp.zeros(index.shape, f32)
    for row in range(table.shape[0]):
        out = jnp.where(place == row, lane_gather(table[row : row + 1], lane), out)
    return out


def stacked(row):
    return jnp.concatenate(
        [row[:, k * WIDTH : (k + 1) * WIDTH] for k in range(row.shape[1] // WIDTH)], axis=0
    )


def slot_tables(cap, voxel, dest, coeff, ordinal):
    rows_here = dest.shape[1]
    owner = dest[...].astype(f32)
    chunks = rows_here // WIDTH
    tall = stacked(owner)
    tall = jnp.concatenate([tall] + [jnp.zeros((8 - chunks, WIDTH), f32)] * (chunks < 8), axis=0)
    upright = tall.T
    first = lax.broadcasted_iota(jnp.int32, (WIDTH, WIDTH), 0)
    second = lax.broadcasted_iota(jnp.int32, (WIDTH, WIDTH), 1)
    slot_row = lax.broadcasted_iota(jnp.int32, (8, WIDTH), 0)
    table = jnp.zeros((40, WIDTH), f32)
    for c in range(chunks):
        lanes = slice(c * WIDTH, (c + 1) * WIDTH)
        here = owner[:, lanes]
        count = jnp.zeros((WIDTH, WIDTH), f32)
        for other in range(c + 1):
            same = upright[:, other : other + 1] == here
            if other == c:
                same = same & (first < second)
            count = count + jnp.where(same, 1.0, 0.0)
        rank = jnp.sum(count, axis=0, keepdims=True)
        place = (here * float(cap) + rank).astype(jnp.int32)
        ordinal[:, lanes] = place
        mine = slot_row == (place >> 7)
        spot = voxel[:, lanes]
        parts = [(spot >> 7).astype(f32), (spot & 127).astype(f32)] + three_parts(coeff[:, lanes])
        values = jnp.concatenate([jnp.where(mine, part, 0.0) for part in parts], axis=0)
        table = table + times_transposed(values, jnp.where(first == (place & 127), 1.0, 0.0))
    spots = table[0:8] * float(WIDTH) + table[8:16]
    coeffs = (table[16:24] + table[24:32]) + table[32:40]
    return spots, coeffs


def on_even(axis="sub"):
    return lax.rem(lax.axis_index(axis), 2) == 0


def first_kernel(cap, *refs):
    given, (post, to_near, to_next, face_r, face_l, ordinal) = refs[:6], refs[6:12]
    held, arrived = refs[12:18], refs[18]
    copies = [
        pltpu.make_async_copy(source, target, arrived.at[n])
        for n, (source, target) in enumerate(zip(given, held))
    ]
    for n in (4, 3, 5, 0, 1, 2):
        copies[n].start()
    pops, heat, solid, voxel, dest, coeff = held
    layers, across, along = solid.shape
    even = on_even()
    for n in (4, 3, 5):
        copies[n].wait()
    spots, coeffs = slot_tables(cap, voxel, dest, coeff, ordinal)
    extra = len(UP)
    for plane in (to_near, to_next):
        plane[extra] = jnp.zeros(plane.shape[1:], f32)
        plane[extra, :, 0:WIDTH] = spots
        plane[extra, :, WIDTH : 2 * WIDTH] = coeffs
    for n in (0, 1, 2):
        copies[n].wait()
    for z in range(layers):
        for start in range(0, along, WIDTH):
            lanes = slice(start, start + WIDTH)
            out = collide(
                [pops[i, z, :, lanes] for i in range(FLOWS)],
                [heat[j, z, :, lanes] for j in range(HEATS)],
                solid[z, :, lanes],
            )
            for i in LANES_ALL:
                post[i, z, :, lanes] = out[i]
            for face, lists, near, far in (
                (face_r, (STILL, RIGHT), across - 1, across - 2),
                (face_l, (STILL, LEFT), 0, 1),
            ):
                rows = [(i, near) for i in lists[0]] + [(i, far) for i in lists[1]]
                rows = rows + [(i, near) for i in lists[1]]
                for n, (i, column) in enumerate(rows):
                    at = n * layers + z
                    face[at : at + 1, lanes] = out[i][column : column + 1]
                at = len(rows) * layers + z
                face[at : at + 1, lanes] = solid[z, near : near + 1, lanes]
    for n, (above, below) in enumerate(zip(UP, DOWN)):
        above, below = post[above, layers - 1], post[below, 0]
        to_near[n] = jnp.where(even, above, below)
        to_next[n] = jnp.where(even, below, above)


def turned(tile, step):
    return tile if step == 0 else pltpu.roll(tile, step % tile.shape[1], 1)


def edge_kernel(layers, face_r, face_l, near, next_, to_a, to_b, out_r, out_l):
    out_r[...] = face_r[...]
    out_l[...] = face_l[...]
    across = near.shape[1]
    even = on_even()
    for out, lists, edge, inside in (
        (out_r, (STILL, RIGHT), across - 1, across - 2),
        (out_l, (STILL, LEFT), 0, 1),
    ):
        rows = [(i, edge) for i in lists[0]] + [(i, inside) for i in lists[1]]
        rows = rows + [(i, edge) for i in lists[1]]
        for n, (i, column) in enumerate(rows):
            rise = VELOCITY[i][2]
            if rise == 0:
                continue
            moved = range(layers - 1, 0, -1) if rise == 1 else range(layers - 1)
            for z in moved:
                at, source = n * layers + z, n * layers + z - rise
                out[at : at + 1, :] = out[source : source + 1, :]
            z = 0 if rise == 1 else layers - 1
            at = n * layers + z
            k = (UP if rise == 1 else DOWN).index(i)
            one, two = near[k, column : column + 1, :], next_[k, column : column + 1, :]
            out[at : at + 1, :] = jnp.where(even == (rise == 1), two, one)
    band_even = on_even("grp")

    def both(n):
        at = slice(n * layers, (n + 1) * layers)
        return jnp.concatenate([out_r[at, :], out_l[at, :]], axis=0)

    def send(n, tile):
        at = slice(n * layers, (n + 1) * layers)
        right, left = tile[0:layers], tile[layers : 2 * layers]
        to_a[at, :] = jnp.where(band_even, right, left)
        to_b[at, :] = jnp.where(band_even, left, right)

    sums = [[] for _ in range(SUMS)]
    for n, i in enumerate(STILL):
        _, ey, ez = VELOCITY[i]
        tile = turned(both(n), ey)
        if i >= FLOWS:
            sums[3].append((1, tile))
        else:
            sums[0].append((1, tile))
            sums[1].append((ey, tile))
            sums[2].append((ez, tile))
    for n in range(SUMS):
        send(n, signed_sum(sums[n]))
    for n, i in enumerate(RIGHT):
        send(SUMS + n, turned(both(len(STILL) + n), VELOCITY[i][1]))
    for n in range(len(STILL) + len(RIGHT), GATHERED):
        send(n - len(STILL) + SUMS, both(n))


def second_kernel(
    post,
    near,
    next_,
    to_a,
    to_b,
    faces_a,
    faces_b,
    solid,
    own_table,
    tie,
    hot,
    motion,
    send_near,
    send_next,
    fluxes,
    moved,
    halo,
):
    layers, across, along = solid.shape
    even = on_even()
    band_even = on_even("grp")
    own_r = jnp.where(band_even, to_a[...], to_b[...])
    own_l = jnp.where(band_even, to_b[...], to_a[...])
    below = [jnp.where(even, next_[n], near[n]) for n in range(len(UP) + 1)]
    above = [jnp.where(even, near[n], next_[n]) for n in range(len(UP) + 1)]
    from_l = jnp.where(band_even, faces_b[...], faces_a[...])
    from_r = jnp.where(band_even, faces_a[...], faces_b[...])
    slot = lax.broadcasted_iota(jnp.int32, (across, along), 0)
    edge = SUMS + len(RIGHT)
    for i in LANES_ALL:
        ex, ey, ez = VELOCITY[i]
        for z in range(layers):
            if z - ez < 0:
                tile = below[UP.index(i)]
            elif z - ez >= layers:
                tile = above[DOWN.index(i)]
            else:
                tile = post[i, z - ez]
            if ex == 1:
                at = (edge + RIGHT.index(i)) * layers + z
                tile = jnp.where(slot == 0, from_l[at : at + 1, :], pltpu.roll(tile, 1, 0))
            elif ex == -1:
                at = (edge + LEFT.index(i)) * layers + z
                tile = jnp.where(
                    slot == across - 1, from_r[at : at + 1, :], pltpu.roll(tile, across - 1, 0)
                )
            moved[i, z] = turned(tile, ey)

    def halves(low, high, n):
        at = slice(n * layers, (n + 1) * layers)
        parts = [low[at], high[at]]
        if 2 * layers < 8:
            parts.append(jnp.ones((8 - 2 * layers, along), f32))
        return jnp.concatenate(parts, axis=0)

    for n in range(edge):
        halo[n] = halves(from_l, from_r, n)
    for n, i in enumerate(RIGHT):
        halo[edge + n] = turned(halves(own_l, own_r, edge + n), VELOCITY[i][1])
    edge_solid = halves(from_l, from_r, FACE - 1)
    for start in range(0, along, WIDTH):
        lanes = slice(start, start + WIDTH)
        for z in range(layers):
            out = collide(
                [moved[i, z, :, lanes] for i in range(FLOWS)],
                [moved[FLOWS + j, z, :, lanes] for j in range(HEATS)],
                solid[z, :, lanes],
            )
            for i in LANES_ALL:
                moved[i, z, :, lanes] = out[i]
        out = collide_halo(
            [halo[n, :, lanes] for n in range(SUMS)],
            [halo[SUMS + n, :, lanes] for n in range(len(RIGHT))],
            [halo[edge + n, :, lanes] for n in range(len(RIGHT))],
            edge_solid[:, lanes],
        )
        for n in range(len(RIGHT)):
            halo[SUMS + n, :, lanes] = out[n]
    sums = {}

    def add(key, sign, tile):
        if sign == 0:
            return
        if key in sums:
            sums[key] = sums[key] + tile if sign > 0 else sums[key] - tile
        else:
            sums[key] = tile if sign > 0 else -tile

    for z in range(layers):
        for i in LANES_ALL:
            ex, ey, ez = VELOCITY[i]
            if i == 0:
                continue
            tile = moved[i, z]
            if ex == 1:
                side = halo[SUMS + RIGHT.index(i), z : z + 1, :]
                tile = jnp.where(slot == 0, side, pltpu.roll(tile, 1, 0))
            elif ex == -1:
                at = layers + z
                side = halo[SUMS + LEFT.index(i), at : at + 1, :]
                tile = jnp.where(slot == across - 1, side, pltpu.roll(tile, across - 1, 0))
            tile = turned(tile, ey)
            target = z + ez
            if i >= FLOWS:
                add((3, target), 1, tile)
            else:
                add((0, target), ex, tile)
                add((1, target), ey, tile)
                add((2, target), ez, tile)
    for z in range(layers):
        hot[z] = sums[3, z]
        for axis in range(3):
            motion[axis, z] = sums[axis, z]
    for part in range(4):
        send_near[part] = jnp.where(even, sums[part, layers], sums[part, -1])
        send_next[part] = jnp.where(even, sums[part, -1], sums[part, layers])
    extra = len(UP)
    per_line = along // WIDTH
    per_layer = across * per_line

    def flux(table, planes):
        index = table[:, 0:WIDTH].astype(jnp.int32)
        place, lane = index >> 7, index & 127
        out = jnp.zeros(lane.shape, f32)
        for z, plane in planes:
            for x in range(across):
                for c in range(per_line):
                    row = plane[x : x + 1, c * WIDTH : (c + 1) * WIDTH]
                    out = jnp.where(
                        place == z * per_layer + x * per_line + c, lane_gather(row, lane), out
                    )
        return out * table[:, WIDTH : 2 * WIDTH]

    mine = own_table[extra]
    fluxes[:, 0, :] = flux(mine, [(z, sums[3, z]) for z in range(layers)])
    fluxes[:, 1, :] = flux(above[extra], [(0, sums[3, layers])])
    fluxes[:, 2, :] = flux(below[extra], [(layers - 1, sums[3, -1])])
    fluxes[:, 3, :] = mine[:, WIDTH : 2 * WIDTH]


def two_parts(value):
    high = value.astype(bf16).astype(f32)
    return high, value - high


def coupled(vector, weights, shift):
    count = vector.shape[0]
    high, low = two_parts(vector)
    block = lax.broadcasted_iota(jnp.int32, vector.shape, 0)
    zero = jnp.zeros_like(vector)
    left = []
    for b in range(count):
        mine = block == b
        high_here, low_here = jnp.where(mine, high, zero), jnp.where(mine, low, zero)
        left.append(jnp.concatenate([high_here, low_here], axis=0))
        left.append(jnp.concatenate([high_here, zero], axis=0))
    left = jnp.concatenate(left, axis=1).astype(bf16)
    out = jnp.dot(left, weights[...], preferred_element_type=f32)
    out = out[0:count] + out[count:]
    back, ahead = out[:, 0:WIDTH], out[:, WIDTH:]
    return pltpu.roll(ahead, lax.rem(count - shift, count), 0) + pltpu.roll(back, shift, 0)


def ready_kernel(
    pattern, nodes, diagonal, source, start, coupling, tie, hits, weights, rest, slots
):
    shift = pattern[0, 0]
    count = start.shape[1]
    for b in range(count):
        block = coupling[0, b]
        other = lax.rem(b + shift, count)
        for part, (straight, flipped) in enumerate(zip(two_parts(block), two_parts(block.T))):
            at = (2 * b + part) * WIDTH
            weights[at : at + WIDTH, 0:WIDTH] = straight.astype(bf16)
            at = pl.multiple_of((2 * other + part) * WIDTH, WIDTH)
            weights[pl.ds(at, WIDTH), WIDTH : 2 * WIDTH] = flipped.astype(bf16)
    vector = start[0]
    rest[...] = source[0] - diagonal[0] * vector + coupled(vector, weights, shift)
    index = stacked(nodes[...])
    slots[...] = table_gather(vector, index)
    upright = (index & 127).astype(f32).T.astype(jnp.int32)
    lane = lax.broadcasted_iota(jnp.int32, (WIDTH, WIDTH), 1)
    for s in range(index.shape[0]):
        hit = jnp.where(upright[:, s : s + 1] == lane, 1.0, 0.0)
        hits[s * WIDTH : (s + 1) * WIDTH] = hit.astype(bf16)


def solve_kernel(
    cap,
    pattern,
    nodes,
    diagonal,
    start,
    hits,
    weights,
    rest,
    slots,
    come,
    res,
    img,
    go,
):
    shift = pattern[0, 0]
    count = start.shape[1]
    index = stacked(nodes[...])
    place = index >> 7
    own, low, high, coeff = come[:, 0, :], come[:, 1, :], come[:, 2, :], come[:, 3, :]
    if cap == WIDTH:
        low = pltpu.roll(low, 1, 0)
        high = pltpu.roll(high, low.shape[0] - 1, 0)
    parts = three_parts(own + low + high) + three_parts(coeff)
    block = lax.broadcasted_iota(jnp.int32, (count, WIDTH), 0)
    values = []
    for s in range(index.shape[0]):
        mine = block == place[s : s + 1]
        values.append(
            jnp.concatenate([jnp.where(mine, part[s : s + 1], 0.0) for part in parts], axis=0)
        )
    values = jnp.concatenate(values, axis=1).astype(bf16)
    landed = jnp.dot(values, hits[...], preferred_element_type=f32)
    landed = [landed[k * count : (k + 1) * count] for k in range(len(parts))]
    added = (landed[0] + landed[1]) + landed[2]
    extra = (landed[3] + landed[4]) + landed[5]
    whole = diagonal[0] + extra
    residual = rest[...] + added - extra * start[0]
    image = whole * residual - coupled(residual, weights, shift)

    def total(value):
        return jnp.sum(jnp.sum(value, axis=0, keepdims=True), axis=1, keepdims=True)

    offset = image - SHIFT * residual
    bend = whole * offset - coupled(offset, weights, shift)
    totals = [
        total(residual * residual),
        total(residual * offset),
        total(offset * offset),
        total(offset * bend),
    ]
    res[...] = residual
    img[...] = image
    lane = lax.broadcasted_iota(jnp.int32, (8, WIDTH), 1) % cap
    facts = jnp.zeros((8, WIDTH), f32)
    for n, fact in enumerate(totals):
        facts = jnp.where(lane == n, fact, facts)
    residual_slots = table_gather(residual, index)
    image_slots = table_gather(image, index)
    start_slots = slots[...]
    for band in range(go.shape[0]):
        go[band, :, 0, :] = start_slots
        go[band, :, 1, :] = residual_slots
        go[band, :, 2, :] = image_slots
        go[band, :, 3, :] = facts


def last_kernel(direct, come, own, start, res, img, ordinal, temp, seen):
    facts = jnp.sum(come[:, 3, :], axis=0, keepdims=True)
    all_norm, cross, square, energy = (facts[:, n : n + 1] for n in range(4))
    product = SHIFT * all_norm + cross
    mean = product / all_norm
    off = SHIFT - mean
    scale = 1.0 / (mean * mean)
    next_norm = (square + off * (2.0 * cross + off * all_norm)) * scale
    energy = (energy + off * (2.0 * (square + SHIFT * cross) + off * product)) * scale
    growth = next_norm / all_norm
    step = next_norm / (energy - mean * growth * next_norm)
    of_residual = 1.0 / mean + step * (1.0 + growth)
    of_image = -step / mean
    temp[0] = start[0] + of_residual * res[...] + of_image * img[...]
    if direct:
        table = come[pl.ds(lax.axis_index("grp") * 8, 8)]
    else:
        table = own[...]
    table = table[:, 0, :] + of_residual * table[:, 1, :] + of_image * table[:, 2, :]
    places = stacked(ordinal[...])
    chunks = places.shape[0]
    if chunks < 8:
        places = jnp.concatenate([places, jnp.zeros((8 - chunks, WIDTH), jnp.int32)], axis=0)
    found = table_gather(table, places)
    for c in range(chunks):
        seen[:, c * WIDTH : (c + 1) * WIDTH] = found[c : c + 1]


def join_kernel(hot, motion, near, next_, hot_out, motion_out):
    layers = hot.shape[0]
    even = on_even()
    below = [jnp.where(even, next_[n], near[n]) for n in range(4)]
    above = [jnp.where(even, near[n], next_[n]) for n in range(4)]
    for z in range(layers):
        for part in range(4):
            tile = hot[z] if part == 3 else motion[part, z]
            if z == 0:
                tile = tile + below[part]
            if z == layers - 1:
                tile = tile + above[part]
            if part == 3:
                hot_out[z] = tile
            else:
                motion_out[part, z] = tile


VMEM = pl.BlockSpec(memory_space=pltpu.VMEM)
ANYWHERE = pl.BlockSpec(memory_space=pl.ANY)
SMEM = pl.BlockSpec(memory_space=pltpu.SMEM)


def call(kernel, out, args, name, scalars=(), scratch=(), far=False):
    total = sum(int(np.prod(a.shape)) * a.dtype.itemsize for a in list(args) + list(out))
    if far:
        args = [pltpu.with_memory_space_constraint(a, pltpu.HBM) for a in args]
    return pl.pallas_call(
        kernel,
        out_shape=out,
        in_specs=[
            ANYWHERE if far else SMEM if n in scalars else VMEM for n in range(len(args))
        ],
        out_specs=[VMEM] * len(out),
        scratch_shapes=scratch,
        compiler_params=pltpu.CompilerParams(vmem_limit_bytes=24 << 20),
        cost_estimate=pl.CostEstimate(flops=1 << 20, bytes_accessed=total, transcendentals=0),
        name=name,
    )(*args)


def shape(*dims, dtype=f32):
    return jax.ShapeDtypeStruct(dims, dtype)


def swaps(axis):
    count = lax.axis_size(axis)
    assert count % 2 == 0
    near = [(k, k + 1 - 2 * (k % 2)) for k in range(count)]
    return near, [(k, (k - 1 + 2 * (k % 2)) % count) for k in range(count)]


def body(
    populations,
    heat_pops,
    solid_frac,
    coupled_grid_point,
    dest_index,
    heat_coeff,
    slot_node,
    node_diag,
    coupling,
    block_pattern,
    heat_source,
    solid_start,
):
    layers, across, along = solid_frac.shape
    slabs, bands = lax.axis_size("sub"), lax.axis_size("grp")
    slots = slot_node.shape[1]
    cap = slots // slabs
    rows = coupled_grid_point.shape[1]
    blocks, piece = node_diag.shape[1:]
    lines = slots // WIDTH
    assert lines == 8 and across == 8 and along >= 2 * WIDTH and along % WIDTH == 0
    assert piece == WIDTH and blocks == 8 and WIDTH % cap == 0 and cap >= 8
    assert rows % WIDTH == 0 and rows <= 8 * WIDTH and layers <= 4
    gathered_rows = -(-GATHERED * layers // 8) * 8
    face_rows = -(-FACE * layers // 8) * 8
    planes = len(UP) + 1
    post, to_near, to_next, face_r, face_l, ordinal = call(
        functools.partial(first_kernel, cap),
        [
            shape(FLOWS + HEATS, layers, across, along),
            shape(planes, across, along),
            shape(planes, across, along),
            shape(gathered_rows, along),
            shape(gathered_rows, along),
            shape(1, rows, dtype=jnp.int32),
        ],
        [
            populations,
            heat_pops,
            solid_frac,
            coupled_grid_point,
            dest_index.reshape(1, rows),
            heat_coeff,
        ],
        "collide_first",
        scratch=[
            pltpu.VMEM(solid_like, kind)
            for solid_like, kind in (
                (populations.shape, f32),
                (heat_pops.shape, f32),
                (solid_frac.shape, f32),
                ((1, rows), jnp.int32),
                ((1, rows), jnp.int32),
                ((1, rows), f32),
            )
        ]
        + [pltpu.SemaphoreType.DMA((6,))],
        far=True,
    )
    near_pairs, next_pairs = swaps("sub")
    near = lax.ppermute(to_near, "sub", near_pairs)
    next_ = lax.ppermute(to_next, "sub", next_pairs)
    to_a, to_b = call(
        functools.partial(edge_kernel, layers),
        [shape(face_rows, along)] * 2,
        [face_r, face_l, near, next_],
        "x_faces",
        scratch=[pltpu.VMEM((gathered_rows, along), f32)] * 2,
    )
    hits, weights, rest, start_slots = call(
        ready_kernel,
        [
            shape(slots, WIDTH, dtype=bf16),
            shape(2 * blocks * piece, 2 * piece, dtype=bf16),
            shape(blocks, piece),
            shape(lines, WIDTH),
        ],
        [block_pattern, slot_node, node_diag, heat_source, solid_start, coupling, to_a],
        "solid_ready",
        scalars=(0,),
    )
    side_a, side_b = swaps("grp")
    faces_a = lax.ppermute(to_a, "grp", side_a)
    faces_b = lax.ppermute(to_b, "grp", side_b)
    hot, motion, send_near, send_next, fluxes = call(
        second_kernel,
        [
            shape(layers, across, along),
            shape(3, layers, across, along),
            shape(4, across, along),
            shape(4, across, along),
            shape(lines, 4, WIDTH),
        ],
        [post, near, next_, to_a, to_b, faces_a, faces_b, solid_frac, to_near, rest],
        "collide_second",
        scratch=[
            pltpu.VMEM((FLOWS + HEATS, layers, across, along), f32),
            pltpu.VMEM((FACE - 1, 8, along), f32),
        ],
    )
    settled = cap != WIDTH
    if settled:
        fluxes = fluxes.reshape(lines, 4, WIDTH // cap, cap).transpose(0, 2, 1, 3)
        fluxes = fluxes.reshape(slabs, 4, cap)
    landed = lax.all_to_all(fluxes, "sub", split_axis=0, concat_axis=0, tiled=True)
    if settled:
        landed = jnp.stack(
            [
                landed[:, 0],
                jnp.roll(landed[:, 1], 1, axis=0),
                jnp.roll(landed[:, 2], -1, axis=0),
                landed[:, 3],
            ]
        )
        landed = landed.reshape(4, lines, WIDTH).transpose(1, 0, 2)
    from_near = lax.ppermute(send_near, "sub", near_pairs)
    from_next = lax.ppermute(send_next, "sub", next_pairs)
    residual, image, go = call(
        functools.partial(solve_kernel, cap),
        [shape(blocks, piece), shape(blocks, piece), shape(bands, lines, 4, WIDTH)],
        [
            block_pattern,
            slot_node,
            node_diag,
            solid_start,
            hits,
            weights,
            rest,
            start_slots,
            landed,
        ],
        "solve",
        scalars=(0,),
    )
    if settled:
        go = go.reshape(bands, lines, 4, WIDTH // cap, cap).transpose(0, 1, 3, 2, 4)
    go = go.reshape(bands * slabs, 4, cap)
    come = lax.all_to_all(go, ("grp", "sub"), split_axis=0, concat_axis=0, tiled=True)
    hot_out, motion_out = call(
        join_kernel,
        [shape(*hot.shape), shape(*motion.shape)],
        [hot, motion, from_near, from_next],
        "join",
    )
    if settled:
        own = lax.dynamic_slice_in_dim(come, lax.axis_index("grp") * slabs, slabs, 0)
        own = own.transpose(1, 0, 2).reshape(4, lines, WIDTH).transpose(1, 0, 2)
        come = jnp.pad(come, ((0, 0), (0, 0), (0, WIDTH - cap)))
    else:
        own = rest
    temp, seen = call(
        functools.partial(last_kernel, not settled),
        [shape(1, blocks, piece), shape(1, rows)],
        [
            come,
            own,
            solid_start,
            residual,
            image,
            ordinal,
        ],
        "finish",
    )
    return hot_out, motion_out, temp, seen


def solution(mesh):
    placed = (
        P(None, "sub", "grp", None),
        P(None, "sub", "grp", None),
        P("sub", "grp", None),
        P("grp", "sub"),
        P("grp", "sub", None),
        P("grp", "sub"),
        P("grp", "sub"),
        P("grp", "sub", None),
        P("grp", "sub", None, None),
        P("grp", "sub"),
        P("grp", "sub", None),
        P("grp", "sub", None),
    )
    return jax.shard_map(
        body,
        mesh=mesh,
        in_specs=placed,
        out_specs=(
            P("sub", "grp", None),
            P(None, "sub", "grp", None),
            P("grp", "sub", None),
            P("grp", "sub"),
        ),
        check_vma=False,
    )
```

```python
import functools
import jax
import jax.numpy as jnp
import numpy as np
from jax import lax
from jax.experimental import pallas as pl
from jax.experimental.pallas import tpu as pltpu
from jax.sharding import PartitionSpec as P

FLOW_VELOCITY = [
    (0, 0, 0),
    (1, 0, 0),
    (-1, 0, 0),
    (0, 1, 0),
    (0, -1, 0),
    (0, 0, 1),
    (0, 0, -1),
    (1, 1, 0),
    (-1, -1, 0),
    (1, -1, 0),
    (-1, 1, 0),
    (1, 0, 1),
    (-1, 0, -1),
    (1, 0, -1),
    (-1, 0, 1),
    (0, 1, 1),
    (0, -1, -1),
    (0, 1, -1),
    (0, -1, 1),
]
VELOCITY = FLOW_VELOCITY + FLOW_VELOCITY[:7]
FLOWS, HEATS = 19, 7
LANES_ALL = range(FLOWS + HEATS)
UP = [i for i in LANES_ALL if VELOCITY[i][2] == 1]
DOWN = [i for i in LANES_ALL if VELOCITY[i][2] == -1]
RIGHT = [i for i in LANES_ALL if VELOCITY[i][0] == 1]
LEFT = [
    next(j for j in LANES_ALL if VELOCITY[j] == (-1,) + VELOCITY[i][1:] and (j < 19) == (i < 19))
    for i in RIGHT
]
TURNED = [
    next(n for n, j in enumerate(RIGHT[:-1]) if VELOCITY[j][1:] == (-VELOCITY[i][1], -VELOCITY[i][2]))
    for i in RIGHT[:-1]
]
STILL = [i for i in LANES_ALL if VELOCITY[i][0] == 0]
GATHERED = len(STILL) + 2 * len(RIGHT) + 1
SUMS = 4
FACE = SUMS + 2 * len(RIGHT) + 1
WIDTH = 128
SHIFT = 4.0
f32 = jnp.float32
bf16 = jnp.bfloat16


def signed_sum(terms):
    total = None
    for sign, term in terms:
        if sign == 0:
            continue
        if total is None:
            total = term if sign > 0 else -term
        else:
            total = total + term if sign > 0 else total - term
    return total


def collide(flow, heat, solid):
    pairs = range(1, FLOWS, 2)
    density = flow[0]
    for i in pairs:
        density = density + (flow[i] + flow[i + 1])
    gaps = {i: flow[i] - flow[i + 1] for i in pairs}
    scale = 1.0 / density
    speed = [
        signed_sum([(FLOW_VELOCITY[i][axis], gaps[i]) for i in pairs]) * scale for axis in range(3)
    ]
    square = speed[0] * speed[0] + speed[1] * speed[1] + speed[2] * speed[2]
    base = 1.0 - 1.5 * square
    gas = 1.0 - solid
    keep = gas * (1.0 - 1.0 / 0.8)
    pull = gas * (density * (1.0 / 0.8))
    flow_post = [None] * FLOWS
    flow_post[0] = (keep + solid) * flow[0] + (pull * (1.0 / 3.0)) * base
    shares = {1: pull * (1.0 / 18.0), 2: pull * (1.0 / 36.0)}
    for i in pairs:
        share = shares[sum(abs(c) for c in FLOW_VELOCITY[i])]
        along = signed_sum([(FLOW_VELOCITY[i][axis], speed[axis]) for axis in range(3)])
        even = base + 4.5 * along * along
        odd = 3.0 * along
        flow_post[i] = keep * flow[i] + share * (even + odd) + solid * flow[i + 1]
        flow_post[i + 1] = keep * flow[i + 1] + share * (even - odd) + solid * flow[i]
    hotness = heat[0]
    for j in range(1, HEATS):
        hotness = hotness + heat[j]
    stay = 1.0 - 1.0 / 0.7
    heat_post = [stay * heat[0] + (0.25 / 0.7) * hotness]
    level = (0.125 / 0.7) * hotness
    for j in range(1, HEATS, 2):
        axis = (j - 1) // 2
        drift = 4.0 * speed[axis]
        heat_post.append(stay * heat[j] + level * (1.0 + drift))
        heat_post.append(stay * heat[j + 1] + level * (1.0 - drift))
    return flow_post + heat_post


def collide_halo(still, inward, outward, solid):
    flows = RIGHT[:-1]
    density, along_y, along_z, hotness = still
    pairs = [(a + b, a - b) for a, b in zip(inward, outward)]
    across = None
    for n, i in enumerate(flows):
        _, ey, ez = VELOCITY[i]
        whole, gap = pairs[n]
        density = density + whole
        across = gap if across is None else across + gap
        along_y = signed_sum([(1, along_y), (ey, whole)])
        along_z = signed_sum([(1, along_z), (ez, whole)])
    hotness = hotness + pairs[-1][0]
    scale = 1.0 / density
    speed = [across * scale, along_y * scale, along_z * scale]
    square = speed[0] * speed[0] + speed[1] * speed[1] + speed[2] * speed[2]
    base = 1.0 - 1.5 * square
    gas = 1.0 - solid
    keep = gas * (1.0 - 1.0 / 0.8)
    pull = gas * (density * (1.0 / 0.8))
    shares = {1: pull * (1.0 / 18.0), 2: pull * (1.0 / 36.0)}
    out = []
    for n, i in enumerate(flows):
        share = shares[sum(abs(c) for c in VELOCITY[i])]
        along = signed_sum([(VELOCITY[i][axis], speed[axis]) for axis in range(3)])
        feq = share * (base + 4.5 * along * along + 3.0 * along)
        out.append(keep * inward[n] + feq + solid * outward[TURNED[n]])
    level = (0.125 / 0.7) * hotness
    out.append((1.0 - 1.0 / 0.7) * inward[-1] + level * (1.0 + 4.0 * speed[0]))
    return out


def three_parts(value):
    high = value.astype(bf16).astype(f32)
    rest = value - high
    middle = rest.astype(bf16).astype(f32)
    return [high, middle, rest - middle]


def times_transposed(left, right):
    return lax.dot_general(
        left.astype(bf16), right.astype(bf16), (((1,), (1,)), ((), ())), preferred_element_type=f32
    )


def spread(row):
    return jnp.broadcast_to(row, (8, row.shape[-1]))


def lane_gather(row, lane):
    return jnp.take_along_axis(spread(row), lane, axis=1, mode="promise_in_bounds")


def table_gather(table, index):
    place, lane = index >> 7, index & 127
    out = jnp.zeros(index.shape, f32)
    for row in range(table.shape[0]):
        out = jnp.where(place == row, lane_gather(table[row : row + 1], lane), out)
    return out


def stacked(row):
    return jnp.concatenate(
        [row[:, k * WIDTH : (k + 1) * WIDTH] for k in range(row.shape[1] // WIDTH)], axis=0
    )


def slot_tables(cap, voxel, dest, coeff, ordinal):
    rows_here = dest.shape[1]
    owner = dest[...].astype(f32)
    chunks = rows_here // WIDTH
    tall = stacked(owner)
    tall = jnp.concatenate([tall] + [jnp.zeros((8 - chunks, WIDTH), f32)] * (chunks < 8), axis=0)
    upright = tall.T
    first = lax.broadcasted_iota(jnp.int32, (WIDTH, WIDTH), 0)
    second = lax.broadcasted_iota(jnp.int32, (WIDTH, WIDTH), 1)
    slot_row = lax.broadcasted_iota(jnp.int32, (8, WIDTH), 0)
    table = jnp.zeros((40, WIDTH), f32)
    for c in range(chunks):
        lanes = slice(c * WIDTH, (c + 1) * WIDTH)
        here = owner[:, lanes]
        count = jnp.zeros((WIDTH, WIDTH), f32)
        for other in range(c + 1):
            same = upright[:, other : other + 1] == here
            if other == c:
                same = same & (first < second)
            count = count + jnp.where(same, 1.0, 0.0)
        rank = jnp.sum(count, axis=0, keepdims=True)
        place = (here * float(cap) + rank).astype(jnp.int32)
        ordinal[:, lanes] = place
        mine = slot_row == (place >> 7)
        spot = voxel[:, lanes]
        parts = [(spot >> 7).astype(f32), (spot & 127).astype(f32)] + three_parts(coeff[:, lanes])
        values = jnp.concatenate([jnp.where(mine, part, 0.0) for part in parts], axis=0)
        table = table + times_transposed(values, jnp.where(first == (place & 127), 1.0, 0.0))
    spots = table[0:8] * float(WIDTH) + table[8:16]
    coeffs = (table[16:24] + table[24:32]) + table[32:40]
    return spots, coeffs


def on_even(axis="sub"):
    return lax.rem(lax.axis_index(axis), 2) == 0


def first_kernel(cap, *refs):
    given, (post, to_near, to_next, face_r, face_l, ordinal) = refs[:6], refs[6:12]
    held, arrived = refs[12:18], refs[18]
    copies = [
        pltpu.make_async_copy(source, target, arrived.at[n])
        for n, (source, target) in enumerate(zip(given, held))
    ]
    for n in (4, 3, 5, 0, 1, 2):
        copies[n].start()
    pops, heat, solid, voxel, dest, coeff = held
    layers, across, along = solid.shape
    even = on_even()
    for n in (4, 3, 5):
        copies[n].wait()
    spots, coeffs = slot_tables(cap, voxel, dest, coeff, ordinal)
    extra = len(UP)
    for plane in (to_near, to_next):
        plane[extra] = jnp.zeros(plane.shape[1:], f32)
        plane[extra, :, 0:WIDTH] = spots
        plane[extra, :, WIDTH : 2 * WIDTH] = coeffs
    for n in (0, 1, 2):
        copies[n].wait()
    for z in range(layers):
        for start in range(0, along, WIDTH):
            lanes = slice(start, start + WIDTH)
            out = collide(
                [pops[i, z, :, lanes] for i in range(FLOWS)],
                [heat[j, z, :, lanes] for j in range(HEATS)],
                solid[z, :, lanes],
            )
            for i in LANES_ALL:
                post[i, z, :, lanes] = out[i]
            for face, lists, near, far in (
                (face_r, (STILL, RIGHT), across - 1, across - 2),
                (face_l, (STILL, LEFT), 0, 1),
            ):
                rows = [(i, near) for i in lists[0]] + [(i, far) for i in lists[1]]
                rows = rows + [(i, near) for i in lists[1]]
                for n, (i, column) in enumerate(rows):
                    at = n * layers + z
                    face[at : at + 1, lanes] = out[i][column : column + 1]
                at = len(rows) * layers + z
                face[at : at + 1, lanes] = solid[z, near : near + 1, lanes]
    for n, (above, below) in enumerate(zip(UP, DOWN)):
        above, below = post[above, layers - 1], post[below, 0]
        to_near[n] = jnp.where(even, above, below)
        to_next[n] = jnp.where(even, below, above)


def turned(tile, step):
    return tile if step == 0 else pltpu.roll(tile, step % tile.shape[1], 1)


def edge_kernel(layers, face_r, face_l, near, next_, to_a, to_b, out_r, out_l):
    out_r[...] = face_r[...]
    out_l[...] = face_l[...]
    across = near.shape[1]
    even = on_even()
    for out, lists, edge, inside in (
        (out_r, (STILL, RIGHT), across - 1, across - 2),
        (out_l, (STILL, LEFT), 0, 1),
    ):
        rows = [(i, edge) for i in lists[0]] + [(i, inside) for i in lists[1]]
        rows = rows + [(i, edge) for i in lists[1]]
        for n, (i, column) in enumerate(rows):
            rise = VELOCITY[i][2]
            if rise == 0:
                continue
            moved = range(layers - 1, 0, -1) if rise == 1 else range(layers - 1)
            for z in moved:
                at, source = n * layers + z, n * layers + z - rise
                out[at : at + 1, :] = out[source : source + 1, :]
            z = 0 if rise == 1 else layers - 1
            at = n * layers + z
            k = (UP if rise == 1 else DOWN).index(i)
            one, two = near[k, column : column + 1, :], next_[k, column : column + 1, :]
            out[at : at + 1, :] = jnp.where(even == (rise == 1), two, one)
    band_even = on_even("grp")

    def both(n):
        at = slice(n * layers, (n + 1) * layers)
        return jnp.concatenate([out_r[at, :], out_l[at, :]], axis=0)

    def send(n, tile):
        at = slice(n * layers, (n + 1) * layers)
        right, left = tile[0:layers], tile[layers : 2 * layers]
        to_a[at, :] = jnp.where(band_even, right, left)
        to_b[at, :] = jnp.where(band_even, left, right)

    sums = [[] for _ in range(SUMS)]
    for n, i in enumerate(STILL):
        _, ey, ez = VELOCITY[i]
        tile = turned(both(n), ey)
        if i >= FLOWS:
            sums[3].append((1, tile))
        else:
            sums[0].append((1, tile))
            sums[1].append((ey, tile))
            sums[2].append((ez, tile))
    for n in range(SUMS):
        send(n, signed_sum(sums[n]))
    for n, i in enumerate(RIGHT):
        send(SUMS + n, turned(both(len(STILL) + n), VELOCITY[i][1]))
    for n in range(len(STILL) + len(RIGHT), GATHERED):
        send(n - len(STILL) + SUMS, both(n))


def second_kernel(
    post,
    near,
    next_,
    to_a,
    to_b,
    faces_a,
    faces_b,
    solid,
    own_table,
    tie,
    hot,
    motion,
    send_near,
    send_next,
    fluxes,
    moved,
    halo,
):
    layers, across, along = solid.shape
    even = on_even()
    band_even = on_even("grp")
    own_r = jnp.where(band_even, to_a[...], to_b[...])
    own_l = jnp.where(band_even, to_b[...], to_a[...])
    below = [jnp.where(even, next_[n], near[n]) for n in range(len(UP) + 1)]
    above = [jnp.where(even, near[n], next_[n]) for n in range(len(UP) + 1)]
    from_l = jnp.where(band_even, faces_b[...], faces_a[...])
    from_r = jnp.where(band_even, faces_a[...], faces_b[...])
    slot = lax.broadcasted_iota(jnp.int32, (across, along), 0)
    edge = SUMS + len(RIGHT)
    for i in LANES_ALL:
        ex, ey, ez = VELOCITY[i]
        for z in range(layers):
            if z - ez < 0:
                tile = below[UP.index(i)]
            elif z - ez >= layers:
                tile = above[DOWN.index(i)]
            else:
                tile = post[i, z - ez]
            if ex == 1:
                at = (edge + RIGHT.index(i)) * layers + z
                tile = jnp.where(slot == 0, from_l[at : at + 1, :], pltpu.roll(tile, 1, 0))
            elif ex == -1:
                at = (edge + LEFT.index(i)) * layers + z
                tile = jnp.where(
                    slot == across - 1, from_r[at : at + 1, :], pltpu.roll(tile, across - 1, 0)
                )
            moved[i, z] = turned(tile, ey)

    def halves(low, high, n):
        at = slice(n * layers, (n + 1) * layers)
        parts = [low[at], high[at]]
        if 2 * layers < 8:
            parts.append(jnp.ones((8 - 2 * layers, along), f32))
        return jnp.concatenate(parts, axis=0)

    for n in range(edge):
        halo[n] = halves(from_l, from_r, n)
    for n, i in enumerate(RIGHT):
        halo[edge + n] = turned(halves(own_l, own_r, edge + n), VELOCITY[i][1])
    edge_solid = halves(from_l, from_r, FACE - 1)
    for start in range(0, along, WIDTH):
        lanes = slice(start, start + WIDTH)
        for z in range(layers):
            out = collide(
                [moved[i, z, :, lanes] for i in range(FLOWS)],
                [moved[FLOWS + j, z, :, lanes] for j in range(HEATS)],
                solid[z, :, lanes],
            )
            for i in LANES_ALL:
                moved[i, z, :, lanes] = out[i]
        out = collide_halo(
            [halo[n, :, lanes] for n in range(SUMS)],
            [halo[SUMS + n, :, lanes] for n in range(len(RIGHT))],
            [halo[edge + n, :, lanes] for n in range(len(RIGHT))],
            edge_solid[:, lanes],
        )
        for n in range(len(RIGHT)):
            halo[SUMS + n, :, lanes] = out[n]
    sums = {}

    def add(key, sign, tile):
        if sign == 0:
            return
        if key in sums:
            sums[key] = sums[key] + tile if sign > 0 else sums[key] - tile
        else:
            sums[key] = tile if sign > 0 else -tile

    for z in range(layers):
        for i in LANES_ALL:
            ex, ey, ez = VELOCITY[i]
            if i == 0:
                continue
            tile = moved[i, z]
            if ex == 1:
                side = halo[SUMS + RIGHT.index(i), z : z + 1, :]
                tile = jnp.where(slot == 0, side, pltpu.roll(tile, 1, 0))
            elif ex == -1:
                at = layers + z
                side = halo[SUMS + LEFT.index(i), at : at + 1, :]
                tile = jnp.where(slot == across - 1, side, pltpu.roll(tile, across - 1, 0))
            tile = turned(tile, ey)
            target = z + ez
            if i >= FLOWS:
                add((3, target), 1, tile)
            else:
                add((0, target), ex, tile)
                add((1, target), ey, tile)
                add((2, target), ez, tile)
    for z in range(layers):
        hot[z] = sums[3, z]
        for axis in range(3):
            motion[axis, z] = sums[axis, z]
    for part in range(4):
        send_near[part] = jnp.where(even, sums[part, layers], sums[part, -1])
        send_next[part] = jnp.where(even, sums[part, -1], sums[part, layers])
    extra = len(UP)
    per_line = along // WIDTH
    per_layer = across * per_line

    def flux(table, planes):
        index = table[:, 0:WIDTH].astype(jnp.int32)
        place, lane = index >> 7, index & 127
        out = jnp.zeros(lane.shape, f32)
        for z, plane in planes:
            for x in range(across):
                for c in range(per_line):
                    row = plane[x : x + 1, c * WIDTH : (c + 1) * WIDTH]
                    out = jnp.where(
                        place == z * per_layer + x * per_line + c, lane_gather(row, lane), out
                    )
        return out * table[:, WIDTH : 2 * WIDTH]

    mine = own_table[extra]
    fluxes[:, 0, :] = flux(mine, [(z, sums[3, z]) for z in range(layers)])
    fluxes[:, 1, :] = flux(above[extra], [(0, sums[3, layers])])
    fluxes[:, 2, :] = flux(below[extra], [(layers - 1, sums[3, -1])])
    fluxes[:, 3, :] = mine[:, WIDTH : 2 * WIDTH]


def coupled(vector, blocks, flipped, shift):
    count = vector.shape[0]
    upright = vector.T
    ahead, back = [], []
    for b in range(count):
        column = jnp.broadcast_to(upright[:, b : b + 1], blocks.shape[1:])
        back.append(jnp.sum(blocks[b] * column, axis=0, keepdims=True))
        ahead.append(jnp.sum(flipped[b] * column, axis=0, keepdims=True))
    ahead = jnp.concatenate(ahead, axis=0)
    back = jnp.concatenate(back, axis=0)
    return pltpu.roll(ahead, lax.rem(count - shift, count), 0) + pltpu.roll(back, shift, 0)


def ready_kernel(
    pattern, nodes, diagonal, source, start, coupling, tie, hits, flipped, rest, slots
):
    shift = pattern[0, 0]
    count = start.shape[1]
    for b in range(count):
        flipped[lax.rem(b + shift, count)] = coupling[0, b].T
    vector = start[0]
    rest[...] = (
        source[0] - diagonal[0] * vector + coupled(vector, coupling.at[0], flipped, shift)
    )
    index = stacked(nodes[...])
    slots[...] = table_gather(vector, index)
    upright = (index & 127).astype(f32).T.astype(jnp.int32)
    lane = lax.broadcasted_iota(jnp.int32, (WIDTH, WIDTH), 1)
    for s in range(index.shape[0]):
        hit = jnp.where(upright[:, s : s + 1] == lane, 1.0, 0.0)
        hits[s * WIDTH : (s + 1) * WIDTH] = hit.astype(bf16)


def solve_kernel(
    cap,
    pattern,
    nodes,
    diagonal,
    start,
    coupling,
    hits,
    flipped,
    rest,
    slots,
    come,
    res,
    img,
    go,
):
    shift = pattern[0, 0]
    count = start.shape[1]
    index = stacked(nodes[...])
    place = index >> 7
    own, low, high, coeff = come[:, 0, :], come[:, 1, :], come[:, 2, :], come[:, 3, :]
    if cap == WIDTH:
        low = pltpu.roll(low, 1, 0)
        high = pltpu.roll(high, low.shape[0] - 1, 0)
    parts = three_parts(own + low + high) + three_parts(coeff)
    block = lax.broadcasted_iota(jnp.int32, (count, WIDTH), 0)
    values = []
    for s in range(index.shape[0]):
        mine = block == place[s : s + 1]
        values.append(
            jnp.concatenate([jnp.where(mine, part[s : s + 1], 0.0) for part in parts], axis=0)
        )
    values = jnp.concatenate(values, axis=1).astype(bf16)
    landed = jnp.dot(values, hits[...], preferred_element_type=f32)
    landed = [landed[k * count : (k + 1) * count] for k in range(len(parts))]
    added = (landed[0] + landed[1]) + landed[2]
    extra = (landed[3] + landed[4]) + landed[5]
    whole = diagonal[0] + extra
    blocks = coupling.at[0]
    residual = rest[...] + added - extra * start[0]
    image = whole * residual - coupled(residual, blocks, flipped, shift)

    def total(value):
        return jnp.sum(jnp.sum(value, axis=0, keepdims=True), axis=1, keepdims=True)

    offset = image - SHIFT * residual
    bend = whole * offset - coupled(offset, blocks, flipped, shift)
    totals = [
        total(residual * residual),
        total(residual * offset),
        total(offset * offset),
        total(offset * bend),
    ]
    res[...] = residual
    img[...] = image
    lane = lax.broadcasted_iota(jnp.int32, (8, WIDTH), 1) % cap
    facts = jnp.zeros((8, WIDTH), f32)
    for n, fact in enumerate(totals):
        facts = jnp.where(lane == n, fact, facts)
    residual_slots = table_gather(residual, index)
    image_slots = table_gather(image, index)
    start_slots = slots[...]
    for band in range(go.shape[0]):
        go[band, :, 0, :] = start_slots
        go[band, :, 1, :] = residual_slots
        go[band, :, 2, :] = image_slots
        go[band, :, 3, :] = facts


def last_kernel(direct, come, own, start, res, img, ordinal, temp, seen):
    facts = jnp.sum(come[:, 3, :], axis=0, keepdims=True)
    all_norm, cross, square, energy = (facts[:, n : n + 1] for n in range(4))
    product = SHIFT * all_norm + cross
    inverse = 1.0 / product
    ratio = cross / all_norm
    spread_square = square - cross * ratio
    energy = energy - ratio * (2.0 * (square + SHIFT * cross) - ratio * product)
    small = spread_square * inverse
    first = all_norm * inverse
    step = spread_square / (energy - spread_square * small)
    of_residual = first + step * (1.0 + small * first)
    of_image = -step * first
    temp[0] = start[0] + of_residual * res[...] + of_image * img[...]
    if direct:
        table = come[pl.ds(lax.axis_index("grp") * 8, 8)]
    else:
        table = own[...]
    table = table[:, 0, :] + of_residual * table[:, 1, :] + of_image * table[:, 2, :]
    places = stacked(ordinal[...])
    chunks = places.shape[0]
    if chunks < 8:
        places = jnp.concatenate([places, jnp.zeros((8 - chunks, WIDTH), jnp.int32)], axis=0)
    found = table_gather(table, places)
    for c in range(chunks):
        seen[:, c * WIDTH : (c + 1) * WIDTH] = found[c : c + 1]


def join_kernel(hot, motion, near, next_, hot_out, motion_out):
    layers = hot.shape[0]
    even = on_even()
    below = [jnp.where(even, next_[n], near[n]) for n in range(4)]
    above = [jnp.where(even, near[n], next_[n]) for n in range(4)]
    for z in range(layers):
        for part in range(4):
            tile = hot[z] if part == 3 else motion[part, z]
            if z == 0:
                tile = tile + below[part]
            if z == layers - 1:
                tile = tile + above[part]
            if part == 3:
                hot_out[z] = tile
            else:
                motion_out[part, z] = tile


VMEM = pl.BlockSpec(memory_space=pltpu.VMEM)
ANYWHERE = pl.BlockSpec(memory_space=pl.ANY)
SMEM = pl.BlockSpec(memory_space=pltpu.SMEM)


def call(kernel, out, args, name, scalars=(), scratch=(), far=False):
    total = sum(int(np.prod(a.shape)) * a.dtype.itemsize for a in list(args) + list(out))
    if far:
        args = [pltpu.with_memory_space_constraint(a, pltpu.HBM) for a in args]
    return pl.pallas_call(
        kernel,
        out_shape=out,
        in_specs=[
            ANYWHERE if far else SMEM if n in scalars else VMEM for n in range(len(args))
        ],
        out_specs=[VMEM] * len(out),
        scratch_shapes=scratch,
        compiler_params=pltpu.CompilerParams(vmem_limit_bytes=24 << 20),
        cost_estimate=pl.CostEstimate(flops=1 << 20, bytes_accessed=total, transcendentals=0),
        name=name,
    )(*args)


def shape(*dims, dtype=f32):
    return jax.ShapeDtypeStruct(dims, dtype)


def swaps(axis):
    count = lax.axis_size(axis)
    assert count % 2 == 0
    near = [(k, k + 1 - 2 * (k % 2)) for k in range(count)]
    return near, [(k, (k - 1 + 2 * (k % 2)) % count) for k in range(count)]


def body(
    populations,
    heat_pops,
    solid_frac,
    coupled_grid_point,
    dest_index,
    heat_coeff,
    slot_node,
    node_diag,
    coupling,
    block_pattern,
    heat_source,
    solid_start,
):
    layers, across, along = solid_frac.shape
    slabs, bands = lax.axis_size("sub"), lax.axis_size("grp")
    slots = slot_node.shape[1]
    cap = slots // slabs
    rows = coupled_grid_point.shape[1]
    blocks, piece = node_diag.shape[1:]
    lines = slots // WIDTH
    assert lines == 8 and across == 8 and along >= 2 * WIDTH and along % WIDTH == 0
    assert piece == WIDTH and blocks == 8 and WIDTH % cap == 0 and cap >= 8
    assert rows % WIDTH == 0 and rows <= 8 * WIDTH and layers <= 4
    gathered_rows = -(-GATHERED * layers // 8) * 8
    face_rows = -(-FACE * layers // 8) * 8
    planes = len(UP) + 1
    post, to_near, to_next, face_r, face_l, ordinal = call(
        functools.partial(first_kernel, cap),
        [
            shape(FLOWS + HEATS, layers, across, along),
            shape(planes, across, along),
            shape(planes, across, along),
            shape(gathered_rows, along),
            shape(gathered_rows, along),
            shape(1, rows, dtype=jnp.int32),
        ],
        [
            populations,
            heat_pops,
            solid_frac,
            coupled_grid_point,
            dest_index.reshape(1, rows),
            heat_coeff,
        ],
        "collide_first",
        scratch=[
            pltpu.VMEM(solid_like, kind)
            for solid_like, kind in (
                (populations.shape, f32),
                (heat_pops.shape, f32),
                (solid_frac.shape, f32),
                ((1, rows), jnp.int32),
                ((1, rows), jnp.int32),
                ((1, rows), f32),
            )
        ]
        + [pltpu.SemaphoreType.DMA((6,))],
        far=True,
    )
    near_pairs, next_pairs = swaps("sub")
    near = lax.ppermute(to_near, "sub", near_pairs)
    next_ = lax.ppermute(to_next, "sub", next_pairs)
    to_a, to_b = call(
        functools.partial(edge_kernel, layers),
        [shape(face_rows, along)] * 2,
        [face_r, face_l, near, next_],
        "x_faces",
        scratch=[pltpu.VMEM((gathered_rows, along), f32)] * 2,
    )
    hits, flipped, rest, start_slots = call(
        ready_kernel,
        [
            shape(slots, WIDTH, dtype=bf16),
            shape(blocks, piece, piece),
            shape(blocks, piece),
            shape(lines, WIDTH),
        ],
        [block_pattern, slot_node, node_diag, heat_source, solid_start, coupling, to_a],
        "solid_ready",
        scalars=(0,),
    )
    side_a, side_b = swaps("grp")
    faces_a = lax.ppermute(to_a, "grp", side_a)
    faces_b = lax.ppermute(to_b, "grp", side_b)
    hot, motion, send_near, send_next, fluxes = call(
        second_kernel,
        [
            shape(layers, across, along),
            shape(3, layers, across, along),
            shape(4, across, along),
            shape(4, across, along),
            shape(lines, 4, WIDTH),
        ],
        [post, near, next_, to_a, to_b, faces_a, faces_b, solid_frac, to_near, rest],
        "collide_second",
        scratch=[
            pltpu.VMEM((FLOWS + HEATS, layers, across, along), f32),
            pltpu.VMEM((FACE - 1, 8, along), f32),
        ],
    )
    settled = cap != WIDTH
    if settled:
        fluxes = fluxes.reshape(lines, 4, WIDTH // cap, cap).transpose(0, 2, 1, 3)
        fluxes = fluxes.reshape(slabs, 4, cap)
    landed = lax.all_to_all(fluxes, "sub", split_axis=0, concat_axis=0, tiled=True)
    if settled:
        landed = jnp.stack(
            [
                landed[:, 0],
                jnp.roll(landed[:, 1], 1, axis=0),
                jnp.roll(landed[:, 2], -1, axis=0),
                landed[:, 3],
            ]
        )
        landed = landed.reshape(4, lines, WIDTH).transpose(1, 0, 2)
    from_near = lax.ppermute(send_near, "sub", near_pairs)
    from_next = lax.ppermute(send_next, "sub", next_pairs)
    residual, image, go = call(
        functools.partial(solve_kernel, cap),
        [shape(blocks, piece), shape(blocks, piece), shape(bands, lines, 4, WIDTH)],
        [
            block_pattern,
            slot_node,
            node_diag,
            solid_start,
            coupling,
            hits,
            flipped,
            rest,
            start_slots,
            landed,
        ],
        "solve",
        scalars=(0,),
    )
    if settled:
        go = go.reshape(bands, lines, 4, WIDTH // cap, cap).transpose(0, 1, 3, 2, 4)
    go = go.reshape(bands * slabs, 4, cap)
    come = lax.all_to_all(go, ("grp", "sub"), split_axis=0, concat_axis=0, tiled=True)
    hot_out, motion_out = call(
        join_kernel,
        [shape(*hot.shape), shape(*motion.shape)],
        [hot, motion, from_near, from_next],
        "join",
    )
    if settled:
        own = lax.dynamic_slice_in_dim(come, lax.axis_index("grp") * slabs, slabs, 0)
        own = own.transpose(1, 0, 2).reshape(4, lines, WIDTH).transpose(1, 0, 2)
        come = jnp.pad(come, ((0, 0), (0, 0), (0, WIDTH - cap)))
    else:
        own = rest
    temp, seen = call(
        functools.partial(last_kernel, not settled),
        [shape(1, blocks, piece), shape(1, rows)],
        [
            come,
            own,
            solid_start,
            residual,
            image,
            ordinal,
        ],
        "finish",
    )
    return hot_out, motion_out, temp, seen


def solution(mesh):
    placed = (
        P(None, "sub", "grp", None),
        P(None, "sub", "grp", None),
        P("sub", "grp", None),
        P("grp", "sub"),
        P("grp", "sub", None),
        P("grp", "sub"),
        P("grp", "sub"),
        P("grp", "sub", None),
        P("grp", "sub", None, None),
        P("grp", "sub"),
        P("grp", "sub", None),
        P("grp", "sub", None),
    )
    return jax.shard_map(
        body,
        mesh=mesh,
        in_specs=placed,
        out_specs=(
            P("sub", "grp", None),
            P(None, "sub", "grp", None),
            P("grp", "sub", None),
            P("grp", "sub"),
        ),
        check_vma=False,
    )
```

```python
import functools
import jax
import jax.numpy as jnp
import numpy as np
from jax import lax
from jax.experimental import pallas as pl
from jax.experimental.pallas import tpu as pltpu
from jax.sharding import PartitionSpec as P

FLOW_VELOCITY = [
    (0, 0, 0),
    (1, 0, 0),
    (-1, 0, 0),
    (0, 1, 0),
    (0, -1, 0),
    (0, 0, 1),
    (0, 0, -1),
    (1, 1, 0),
    (-1, -1, 0),
    (1, -1, 0),
    (-1, 1, 0),
    (1, 0, 1),
    (-1, 0, -1),
    (1, 0, -1),
    (-1, 0, 1),
    (0, 1, 1),
    (0, -1, -1),
    (0, 1, -1),
    (0, -1, 1),
]
VELOCITY = FLOW_VELOCITY + FLOW_VELOCITY[:7]
FLOWS, HEATS = 19, 7
LANES_ALL = range(FLOWS + HEATS)
UP = [i for i in LANES_ALL if VELOCITY[i][2] == 1]
DOWN = [i for i in LANES_ALL if VELOCITY[i][2] == -1]
RIGHT = [i for i in LANES_ALL if VELOCITY[i][0] == 1]
LEFT = [
    next(j for j in LANES_ALL if VELOCITY[j] == (-1,) + VELOCITY[i][1:] and (j < 19) == (i < 19))
    for i in RIGHT
]
TURNED = [
    next(n for n, j in enumerate(RIGHT[:-1]) if VELOCITY[j][1:] == (-VELOCITY[i][1], -VELOCITY[i][2]))
    for i in RIGHT[:-1]
]
STILL = [i for i in LANES_ALL if VELOCITY[i][0] == 0]
GATHERED = len(STILL) + 2 * len(RIGHT) + 1
SUMS = 4
FACE = SUMS + 2 * len(RIGHT) + 1
WIDTH = 128
SHIFT = 4.0
f32 = jnp.float32
bf16 = jnp.bfloat16


def signed_sum(terms):
    total = None
    for sign, term in terms:
        if sign == 0:
            continue
        if total is None:
            total = term if sign > 0 else -term
        else:
            total = total + term if sign > 0 else total - term
    return total


def collide(flow, heat, solid):
    pairs = range(1, FLOWS, 2)
    density = flow[0]
    for i in pairs:
        density = density + (flow[i] + flow[i + 1])
    gaps = {i: flow[i] - flow[i + 1] for i in pairs}
    scale = 1.0 / density
    speed = [
        signed_sum([(FLOW_VELOCITY[i][axis], gaps[i]) for i in pairs]) * scale for axis in range(3)
    ]
    square = speed[0] * speed[0] + speed[1] * speed[1] + speed[2] * speed[2]
    base = 1.0 - 1.5 * square
    gas = 1.0 - solid
    keep = gas * (1.0 - 1.0 / 0.8)
    pull = gas * (density * (1.0 / 0.8))
    flow_post = [None] * FLOWS
    flow_post[0] = (keep + solid) * flow[0] + (pull * (1.0 / 3.0)) * base
    shares = {1: pull * (1.0 / 18.0), 2: pull * (1.0 / 36.0)}
    for i in pairs:
        share = shares[sum(abs(c) for c in FLOW_VELOCITY[i])]
        along = signed_sum([(FLOW_VELOCITY[i][axis], speed[axis]) for axis in range(3)])
        even = base + 4.5 * along * along
        odd = 3.0 * along
        flow_post[i] = keep * flow[i] + share * (even + odd) + solid * flow[i + 1]
        flow_post[i + 1] = keep * flow[i + 1] + share * (even - odd) + solid * flow[i]
    hotness = heat[0]
    for j in range(1, HEATS):
        hotness = hotness + heat[j]
    stay = 1.0 - 1.0 / 0.7
    heat_post = [stay * heat[0] + (0.25 / 0.7) * hotness]
    level = (0.125 / 0.7) * hotness
    for j in range(1, HEATS, 2):
        axis = (j - 1) // 2
        drift = 4.0 * speed[axis]
        heat_post.append(stay * heat[j] + level * (1.0 + drift))
        heat_post.append(stay * heat[j + 1] + level * (1.0 - drift))
    return flow_post + heat_post


def collide_halo(still, inward, outward, solid):
    flows = RIGHT[:-1]
    density, along_y, along_z, hotness = still
    pairs = [(a + b, a - b) for a, b in zip(inward, outward)]
    across = None
    for n, i in enumerate(flows):
        _, ey, ez = VELOCITY[i]
        whole, gap = pairs[n]
        density = density + whole
        across = gap if across is None else across + gap
        along_y = signed_sum([(1, along_y), (ey, whole)])
        along_z = signed_sum([(1, along_z), (ez, whole)])
    hotness = hotness + pairs[-1][0]
    scale = 1.0 / density
    speed = [across * scale, along_y * scale, along_z * scale]
    square = speed[0] * speed[0] + speed[1] * speed[1] + speed[2] * speed[2]
    base = 1.0 - 1.5 * square
    gas = 1.0 - solid
    keep = gas * (1.0 - 1.0 / 0.8)
    pull = gas * (density * (1.0 / 0.8))
    shares = {1: pull * (1.0 / 18.0), 2: pull * (1.0 / 36.0)}
    out = []
    for n, i in enumerate(flows):
        share = shares[sum(abs(c) for c in VELOCITY[i])]
        along = signed_sum([(VELOCITY[i][axis], speed[axis]) for axis in range(3)])
        feq = share * (base + 4.5 * along * along + 3.0 * along)
        out.append(keep * inward[n] + feq + solid * outward[TURNED[n]])
    level = (0.125 / 0.7) * hotness
    out.append((1.0 - 1.0 / 0.7) * inward[-1] + level * (1.0 + 4.0 * speed[0]))
    return out


def three_parts(value):
    high = value.astype(bf16).astype(f32)
    rest = value - high
    middle = rest.astype(bf16).astype(f32)
    return [high, middle, rest - middle]


def times_transposed(left, right):
    return lax.dot_general(
        left.astype(bf16), right.astype(bf16), (((1,), (1,)), ((), ())), preferred_element_type=f32
    )


def spread(row):
    return jnp.broadcast_to(row, (8, row.shape[-1]))


def lane_gather(row, lane):
    return jnp.take_along_axis(spread(row), lane, axis=1, mode="promise_in_bounds")


def table_gather(table, index):
    place, lane = index >> 7, index & 127
    out = jnp.zeros(index.shape, f32)
    for row in range(table.shape[0]):
        out = jnp.where(place == row, lane_gather(table[row : row + 1], lane), out)
    return out


def plane_rows(plane, first=0, count=8):
    return pl.ds(4 * first + plane, count, stride=4)


def stacked(row):
    return jnp.concatenate(
        [row[:, k * WIDTH : (k + 1) * WIDTH] for k in range(row.shape[1] // WIDTH)], axis=0
    )


def slot_tables(cap, voxel, dest, coeff, ordinal):
    rows_here = dest.shape[1]
    owner = dest[...].astype(f32)
    chunks = rows_here // WIDTH
    tall = stacked(owner)
    tall = jnp.concatenate([tall] + [jnp.zeros((8 - chunks, WIDTH), f32)] * (chunks < 8), axis=0)
    upright = tall.T
    first = lax.broadcasted_iota(jnp.int32, (WIDTH, WIDTH), 0)
    second = lax.broadcasted_iota(jnp.int32, (WIDTH, WIDTH), 1)
    slot_row = lax.broadcasted_iota(jnp.int32, (8, WIDTH), 0)
    table = jnp.zeros((40, WIDTH), f32)
    for c in range(chunks):
        lanes = slice(c * WIDTH, (c + 1) * WIDTH)
        here = owner[:, lanes]
        count = jnp.zeros((WIDTH, WIDTH), f32)
        for other in range(c + 1):
            same = upright[:, other : other + 1] == here
            if other == c:
                same = same & (first < second)
            count = count + jnp.where(same, 1.0, 0.0)
        rank = jnp.sum(count, axis=0, keepdims=True)
        place = (here * float(cap) + rank).astype(jnp.int32)
        ordinal[:, lanes] = place
        mine = slot_row == (place >> 7)
        spot = voxel[:, lanes]
        parts = [(spot >> 7).astype(f32), (spot & 127).astype(f32)] + three_parts(coeff[:, lanes])
        values = jnp.concatenate([jnp.where(mine, part, 0.0) for part in parts], axis=0)
        table = table + times_transposed(values, jnp.where(first == (place & 127), 1.0, 0.0))
    spots = table[0:8] * float(WIDTH) + table[8:16]
    coeffs = (table[16:24] + table[24:32]) + table[32:40]
    return spots, coeffs


def on_even(axis="sub"):
    return lax.rem(lax.axis_index(axis), 2) == 0


def first_kernel(cap, *refs):
    given, (post, to_near, to_next, face_r, face_l, ordinal) = refs[:6], refs[6:12]
    held, arrived = refs[12:18], refs[18]
    copies = [
        pltpu.make_async_copy(source, target, arrived.at[n])
        for n, (source, target) in enumerate(zip(given, held))
    ]
    for n in (4, 3, 5, 0, 1, 2):
        copies[n].start()
    pops, heat, solid, voxel, dest, coeff = held
    layers, across, along = solid.shape
    even = on_even()
    for n in (4, 3, 5):
        copies[n].wait()
    spots, coeffs = slot_tables(cap, voxel, dest, coeff, ordinal)
    extra = len(UP)
    for plane in (to_near, to_next):
        plane[extra] = jnp.zeros(plane.shape[1:], f32)
        plane[extra, :, 0:WIDTH] = spots
        plane[extra, :, WIDTH : 2 * WIDTH] = coeffs
    for n in (0, 1, 2):
        copies[n].wait()
    for z in range(layers):
        for start in range(0, along, WIDTH):
            lanes = slice(start, start + WIDTH)
            out = collide(
                [pops[i, z, :, lanes] for i in range(FLOWS)],
                [heat[j, z, :, lanes] for j in range(HEATS)],
                solid[z, :, lanes],
            )
            for i in LANES_ALL:
                post[i, z, :, lanes] = out[i]
            for face, lists, near, far in (
                (face_r, (STILL, RIGHT), across - 1, across - 2),
                (face_l, (STILL, LEFT), 0, 1),
            ):
                rows = [(i, near) for i in lists[0]] + [(i, far) for i in lists[1]]
                rows = rows + [(i, near) for i in lists[1]]
                for n, (i, column) in enumerate(rows):
                    at = n * layers + z
                    face[at : at + 1, lanes] = out[i][column : column + 1]
                at = len(rows) * layers + z
                face[at : at + 1, lanes] = solid[z, near : near + 1, lanes]
    for n, (above, below) in enumerate(zip(UP, DOWN)):
        above, below = post[above, layers - 1], post[below, 0]
        to_near[n] = jnp.where(even, above, below)
        to_next[n] = jnp.where(even, below, above)


def turned(tile, step):
    return tile if step == 0 else pltpu.roll(tile, step % tile.shape[1], 1)


def edge_kernel(layers, face_r, face_l, near, next_, to_a, to_b, out_r, out_l):
    out_r[...] = face_r[...]
    out_l[...] = face_l[...]
    across = near.shape[1]
    even = on_even()
    for out, lists, edge, inside in (
        (out_r, (STILL, RIGHT), across - 1, across - 2),
        (out_l, (STILL, LEFT), 0, 1),
    ):
        rows = [(i, edge) for i in lists[0]] + [(i, inside) for i in lists[1]]
        rows = rows + [(i, edge) for i in lists[1]]
        for n, (i, column) in enumerate(rows):
            rise = VELOCITY[i][2]
            if rise == 0:
                continue
            moved = range(layers - 1, 0, -1) if rise == 1 else range(layers - 1)
            for z in moved:
                at, source = n * layers + z, n * layers + z - rise
                out[at : at + 1, :] = out[source : source + 1, :]
            z = 0 if rise == 1 else layers - 1
            at = n * layers + z
            k = (UP if rise == 1 else DOWN).index(i)
            one, two = near[k, column : column + 1, :], next_[k, column : column + 1, :]
            out[at : at + 1, :] = jnp.where(even == (rise == 1), two, one)
    band_even = on_even("grp")

    def both(n):
        at = slice(n * layers, (n + 1) * layers)
        return jnp.concatenate([out_r[at, :], out_l[at, :]], axis=0)

    def send(n, tile):
        at = slice(n * layers, (n + 1) * layers)
        right, left = tile[0:layers], tile[layers : 2 * layers]
        to_a[at, :] = jnp.where(band_even, right, left)
        to_b[at, :] = jnp.where(band_even, left, right)

    sums = [[] for _ in range(SUMS)]
    for n, i in enumerate(STILL):
        _, ey, ez = VELOCITY[i]
        tile = turned(both(n), ey)
        if i >= FLOWS:
            sums[3].append((1, tile))
        else:
            sums[0].append((1, tile))
            sums[1].append((ey, tile))
            sums[2].append((ez, tile))
    for n in range(SUMS):
        send(n, signed_sum(sums[n]))
    for n, i in enumerate(RIGHT):
        send(SUMS + n, turned(both(len(STILL) + n), VELOCITY[i][1]))
    for n in range(len(STILL) + len(RIGHT), GATHERED):
        send(n - len(STILL) + SUMS, both(n))


def second_kernel(
    post,
    near,
    next_,
    to_a,
    to_b,
    faces_a,
    faces_b,
    solid,
    own_table,
    tie,
    hot,
    motion,
    send_near,
    send_next,
    fluxes,
    moved,
    halo,
):
    layers, across, along = solid.shape
    even = on_even()
    band_even = on_even("grp")
    own_r = jnp.where(band_even, to_a[...], to_b[...])
    own_l = jnp.where(band_even, to_b[...], to_a[...])
    below = [jnp.where(even, next_[n], near[n]) for n in range(len(UP) + 1)]
    above = [jnp.where(even, near[n], next_[n]) for n in range(len(UP) + 1)]
    from_l = jnp.where(band_even, faces_b[...], faces_a[...])
    from_r = jnp.where(band_even, faces_a[...], faces_b[...])
    slot = lax.broadcasted_iota(jnp.int32, (across, along), 0)
    edge = SUMS + len(RIGHT)
    for i in LANES_ALL:
        ex, ey, ez = VELOCITY[i]
        for z in range(layers):
            if z - ez < 0:
                tile = below[UP.index(i)]
            elif z - ez >= layers:
                tile = above[DOWN.index(i)]
            else:
                tile = post[i, z - ez]
            if ex == 1:
                at = (edge + RIGHT.index(i)) * layers + z
                tile = jnp.where(slot == 0, from_l[at : at + 1, :], pltpu.roll(tile, 1, 0))
            elif ex == -1:
                at = (edge + LEFT.index(i)) * layers + z
                tile = jnp.where(
                    slot == across - 1, from_r[at : at + 1, :], pltpu.roll(tile, across - 1, 0)
                )
            moved[i, z] = turned(tile, ey)

    def halves(low, high, n):
        at = slice(n * layers, (n + 1) * layers)
        parts = [low[at], high[at]]
        if 2 * layers < 8:
            parts.append(jnp.ones((8 - 2 * layers, along), f32))
        return jnp.concatenate(parts, axis=0)

    for n in range(edge):
        halo[n] = halves(from_l, from_r, n)
    for n, i in enumerate(RIGHT):
        halo[edge + n] = turned(halves(own_l, own_r, edge + n), VELOCITY[i][1])
    edge_solid = halves(from_l, from_r, FACE - 1)
    for start in range(0, along, WIDTH):
        lanes = slice(start, start + WIDTH)
        for z in range(layers):
            out = collide(
                [moved[i, z, :, lanes] for i in range(FLOWS)],
                [moved[FLOWS + j, z, :, lanes] for j in range(HEATS)],
                solid[z, :, lanes],
            )
            for i in LANES_ALL:
                moved[i, z, :, lanes] = out[i]
        out = collide_halo(
            [halo[n, :, lanes] for n in range(SUMS)],
            [halo[SUMS + n, :, lanes] for n in range(len(RIGHT))],
            [halo[edge + n, :, lanes] for n in range(len(RIGHT))],
            edge_solid[:, lanes],
        )
        for n in range(len(RIGHT)):
            halo[SUMS + n, :, lanes] = out[n]
    sums = {}

    def add(key, sign, tile):
        if sign == 0:
            return
        if key in sums:
            sums[key] = sums[key] + tile if sign > 0 else sums[key] - tile
        else:
            sums[key] = tile if sign > 0 else -tile

    for z in range(layers):
        for i in LANES_ALL:
            ex, ey, ez = VELOCITY[i]
            if i == 0:
                continue
            tile = moved[i, z]
            if ex == 1:
                side = halo[SUMS + RIGHT.index(i), z : z + 1, :]
                tile = jnp.where(slot == 0, side, pltpu.roll(tile, 1, 0))
            elif ex == -1:
                at = layers + z
                side = halo[SUMS + LEFT.index(i), at : at + 1, :]
                tile = jnp.where(slot == across - 1, side, pltpu.roll(tile, across - 1, 0))
            tile = turned(tile, ey)
            target = z + ez
            if i >= FLOWS:
                add((3, target), 1, tile)
            else:
                add((0, target), ex, tile)
                add((1, target), ey, tile)
                add((2, target), ez, tile)
    for z in range(layers):
        hot[z] = sums[3, z]
        for axis in range(3):
            motion[axis, z] = sums[axis, z]
    for part in range(4):
        send_near[part] = jnp.where(even, sums[part, layers], sums[part, -1])
        send_next[part] = jnp.where(even, sums[part, -1], sums[part, layers])
    extra = len(UP)
    per_line = along // WIDTH
    per_layer = across * per_line

    def flux(table, planes):
        index = table[:, 0:WIDTH].astype(jnp.int32)
        place, lane = index >> 7, index & 127
        out = jnp.zeros(lane.shape, f32)
        for z, plane in planes:
            for x in range(across):
                for c in range(per_line):
                    row = plane[x : x + 1, c * WIDTH : (c + 1) * WIDTH]
                    out = jnp.where(
                        place == z * per_layer + x * per_line + c, lane_gather(row, lane), out
                    )
        return out * table[:, WIDTH : 2 * WIDTH]

    mine = own_table[extra]
    fluxes[plane_rows(0), :] = flux(mine, [(z, sums[3, z]) for z in range(layers)])
    fluxes[plane_rows(1), :] = flux(above[extra], [(0, sums[3, layers])])
    fluxes[plane_rows(2), :] = flux(below[extra], [(layers - 1, sums[3, -1])])
    fluxes[plane_rows(3), :] = mine[:, WIDTH : 2 * WIDTH]


def coupled(vector, blocks, flipped, shift):
    count = vector.shape[0]
    upright = vector.T
    ahead, back = [], []
    for b in range(count):
        column = jnp.broadcast_to(upright[:, b : b + 1], blocks.shape[1:])
        back.append(jnp.sum(blocks[b] * column, axis=0, keepdims=True))
        ahead.append(jnp.sum(flipped[b] * column, axis=0, keepdims=True))
    ahead = jnp.concatenate(ahead, axis=0)
    back = jnp.concatenate(back, axis=0)
    return pltpu.roll(ahead, lax.rem(count - shift, count), 0) + pltpu.roll(back, shift, 0)


def ready_kernel(
    pattern, nodes, diagonal, source, start, coupling, tie, hits, flipped, rest, slots
):
    shift = pattern[0, 0]
    count = start.shape[1]
    for b in range(count):
        flipped[lax.rem(b + shift, count)] = coupling[0, b].T
    vector = start[0]
    rest[...] = (
        source[0] - diagonal[0] * vector + coupled(vector, coupling.at[0], flipped, shift)
    )
    index = stacked(nodes[...])
    slots[...] = table_gather(vector, index)
    upright = (index & 127).astype(f32).T.astype(jnp.int32)
    lane = lax.broadcasted_iota(jnp.int32, (WIDTH, WIDTH), 1)
    for s in range(index.shape[0]):
        hit = jnp.where(upright[:, s : s + 1] == lane, 1.0, 0.0)
        hits[s * WIDTH : (s + 1) * WIDTH] = hit.astype(bf16)


def solve_kernel(
    cap,
    pattern,
    nodes,
    diagonal,
    start,
    coupling,
    hits,
    flipped,
    rest,
    slots,
    come,
    res,
    img,
    go,
):
    shift = pattern[0, 0]
    count = start.shape[1]
    index = stacked(nodes[...])
    place = index >> 7
    own, low, high, coeff = (come[plane_rows(plane), :] for plane in range(4))
    if cap == WIDTH:
        low = pltpu.roll(low, 1, 0)
        high = pltpu.roll(high, low.shape[0] - 1, 0)
    parts = three_parts(own + low + high) + three_parts(coeff)
    block = lax.broadcasted_iota(jnp.int32, (count, WIDTH), 0)
    values = []
    for s in range(index.shape[0]):
        mine = block == place[s : s + 1]
        values.append(
            jnp.concatenate([jnp.where(mine, part[s : s + 1], 0.0) for part in parts], axis=0)
        )
    values = jnp.concatenate(values, axis=1).astype(bf16)
    landed = jnp.dot(values, hits[...], preferred_element_type=f32)
    landed = [landed[k * count : (k + 1) * count] for k in range(len(parts))]
    added = (landed[0] + landed[1]) + landed[2]
    extra = (landed[3] + landed[4]) + landed[5]
    whole = diagonal[0] + extra
    blocks = coupling.at[0]
    residual = rest[...] + added - extra * start[0]
    image = whole * residual - coupled(residual, blocks, flipped, shift)

    def total(value):
        return jnp.sum(jnp.sum(value, axis=0, keepdims=True), axis=1, keepdims=True)

    offset = image - SHIFT * residual
    bend = whole * offset - coupled(offset, blocks, flipped, shift)
    totals = [
        total(residual * residual),
        total(residual * offset),
        total(offset * offset),
        total(offset * bend),
    ]
    res[...] = residual
    img[...] = image
    lane = lax.broadcasted_iota(jnp.int32, (8, WIDTH), 1) & (cap - 1)
    facts = jnp.zeros((8, WIDTH), f32)
    for n, fact in enumerate(totals):
        facts = jnp.where(lane == n, fact, facts)
    residual_slots = table_gather(residual, index)
    image_slots = table_gather(image, index)
    start_slots = slots[...]
    for group in range(0, go.shape[0] // 4, 8):
        go[plane_rows(0, group), :] = start_slots
        go[plane_rows(1, group), :] = residual_slots
        go[plane_rows(2, group), :] = image_slots
        go[plane_rows(3, group), :] = facts


def last_kernel(direct, come, own, start, res, img, ordinal, temp, seen):
    places = stacked(ordinal[...])
    chunks = places.shape[0]
    if chunks < 8:
        places = jnp.concatenate([places, jnp.zeros((8 - chunks, WIDTH), jnp.int32)], axis=0)
    found = []
    for plane in range(3):
        if direct:
            table = come[plane_rows(plane, lax.axis_index("grp") * 8), :]
        else:
            table = own[plane_rows(plane), :]
        found.append(table_gather(table, places))
    facts = come[plane_rows(3, 0, come.shape[0] // 4), :]
    facts = jnp.sum(facts, axis=0, keepdims=True)
    all_norm, cross, square, energy = (
        lane_gather(facts, jnp.full((8, WIDTH), n, jnp.int32)) for n in range(4)
    )
    product = SHIFT * all_norm + cross
    inverse = 1.0 / product
    ratio = cross / all_norm
    spread_square = square - cross * ratio
    energy = energy - ratio * (2.0 * (square + SHIFT * cross) - ratio * product)
    small = spread_square * inverse
    first = all_norm * inverse
    step = spread_square / (energy - spread_square * small)
    of_residual = first + step * (1.0 + small * first)
    of_image = -step * first
    temp[0] = start[0] + of_residual * res[...] + of_image * img[...]
    found = found[0] + of_residual * found[1] + of_image * found[2]
    for c in range(chunks):
        seen[:, c * WIDTH : (c + 1) * WIDTH] = found[c : c + 1]


def join_kernel(hot, motion, near, next_, hot_out, motion_out):
    layers = hot.shape[0]
    even = on_even()
    below = [jnp.where(even, next_[n], near[n]) for n in range(4)]
    above = [jnp.where(even, near[n], next_[n]) for n in range(4)]
    for z in range(layers):
        for part in range(4):
            tile = hot[z] if part == 3 else motion[part, z]
            if z == 0:
                tile = tile + below[part]
            if z == layers - 1:
                tile = tile + above[part]
            if part == 3:
                hot_out[z] = tile
            else:
                motion_out[part, z] = tile


VMEM = pl.BlockSpec(memory_space=pltpu.VMEM)
ANYWHERE = pl.BlockSpec(memory_space=pl.ANY)
SMEM = pl.BlockSpec(memory_space=pltpu.SMEM)


def call(kernel, out, args, name, scalars=(), scratch=(), far=False):
    total = sum(int(np.prod(a.shape)) * a.dtype.itemsize for a in list(args) + list(out))
    if far:
        args = [pltpu.with_memory_space_constraint(a, pltpu.HBM) for a in args]
    return pl.pallas_call(
        kernel,
        out_shape=out,
        in_specs=[
            ANYWHERE if far else SMEM if n in scalars else VMEM for n in range(len(args))
        ],
        out_specs=[VMEM] * len(out),
        scratch_shapes=scratch,
        compiler_params=pltpu.CompilerParams(vmem_limit_bytes=24 << 20),
        cost_estimate=pl.CostEstimate(flops=1 << 20, bytes_accessed=total, transcendentals=0),
        name=name,
    )(*args)


def shape(*dims, dtype=f32):
    return jax.ShapeDtypeStruct(dims, dtype)


def swaps(axis):
    count = lax.axis_size(axis)
    assert count % 2 == 0
    near = [(k, k + 1 - 2 * (k % 2)) for k in range(count)]
    return near, [(k, (k - 1 + 2 * (k % 2)) % count) for k in range(count)]


def body(
    populations,
    heat_pops,
    solid_frac,
    coupled_grid_point,
    dest_index,
    heat_coeff,
    slot_node,
    node_diag,
    coupling,
    block_pattern,
    heat_source,
    solid_start,
):
    layers, across, along = solid_frac.shape
    slabs, bands = lax.axis_size("sub"), lax.axis_size("grp")
    slots = slot_node.shape[1]
    cap = slots // slabs
    rows = coupled_grid_point.shape[1]
    blocks, piece = node_diag.shape[1:]
    lines = slots // WIDTH
    assert lines == 8 and across == 8 and along >= 2 * WIDTH and along % WIDTH == 0
    assert piece == WIDTH and blocks == 8 and WIDTH % cap == 0 and cap >= 8
    assert rows % WIDTH == 0 and rows <= 8 * WIDTH and layers <= 4
    gathered_rows = -(-GATHERED * layers // 8) * 8
    face_rows = -(-FACE * layers // 8) * 8
    planes = len(UP) + 1
    post, to_near, to_next, face_r, face_l, ordinal = call(
        functools.partial(first_kernel, cap),
        [
            shape(FLOWS + HEATS, layers, across, along),
            shape(planes, across, along),
            shape(planes, across, along),
            shape(gathered_rows, along),
            shape(gathered_rows, along),
            shape(1, rows, dtype=jnp.int32),
        ],
        [
            populations,
            heat_pops,
            solid_frac,
            coupled_grid_point,
            dest_index.reshape(1, rows),
            heat_coeff,
        ],
        "collide_first",
        scratch=[
            pltpu.VMEM(solid_like, kind)
            for solid_like, kind in (
                (populations.shape, f32),
                (heat_pops.shape, f32),
                (solid_frac.shape, f32),
                ((1, rows), jnp.int32),
                ((1, rows), jnp.int32),
                ((1, rows), f32),
            )
        ]
        + [pltpu.SemaphoreType.DMA((6,))],
        far=True,
    )
    near_pairs, next_pairs = swaps("sub")
    near = lax.ppermute(to_near, "sub", near_pairs)
    next_ = lax.ppermute(to_next, "sub", next_pairs)
    to_a, to_b = call(
        functools.partial(edge_kernel, layers),
        [shape(face_rows, along)] * 2,
        [face_r, face_l, near, next_],
        "x_faces",
        scratch=[pltpu.VMEM((gathered_rows, along), f32)] * 2,
    )
    hits, flipped, rest, start_slots = call(
        ready_kernel,
        [
            shape(slots, WIDTH, dtype=bf16),
            shape(blocks, piece, piece),
            shape(blocks, piece),
            shape(lines, WIDTH),
        ],
        [block_pattern, slot_node, node_diag, heat_source, solid_start, coupling, to_a],
        "solid_ready",
        scalars=(0,),
    )
    side_a, side_b = swaps("grp")
    faces_a = lax.ppermute(to_a, "grp", side_a)
    faces_b = lax.ppermute(to_b, "grp", side_b)
    hot, motion, send_near, send_next, fluxes = call(
        second_kernel,
        [
            shape(layers, across, along),
            shape(3, layers, across, along),
            shape(4, across, along),
            shape(4, across, along),
            shape(4 * lines, WIDTH),
        ],
        [post, near, next_, to_a, to_b, faces_a, faces_b, solid_frac, to_near, rest],
        "collide_second",
        scratch=[
            pltpu.VMEM((FLOWS + HEATS, layers, across, along), f32),
            pltpu.VMEM((FACE - 1, 8, along), f32),
        ],
    )
    settled = cap != WIDTH
    if settled:
        fluxes = fluxes.reshape(lines, 4, WIDTH // cap, cap).transpose(0, 2, 1, 3)
    fluxes = fluxes.reshape(slabs, 4, cap)
    landed = lax.all_to_all(fluxes, "sub", split_axis=0, concat_axis=0, tiled=True)
    if settled:
        landed = jnp.stack(
            [
                landed[:, 0],
                jnp.roll(landed[:, 1], 1, axis=0),
                jnp.roll(landed[:, 2], -1, axis=0),
                landed[:, 3],
            ]
        )
        landed = landed.reshape(4, lines, WIDTH).transpose(1, 0, 2)
    landed = landed.reshape(4 * lines, WIDTH)
    from_near = lax.ppermute(send_near, "sub", near_pairs)
    from_next = lax.ppermute(send_next, "sub", next_pairs)
    residual, image, go = call(
        functools.partial(solve_kernel, cap),
        [shape(blocks, piece), shape(blocks, piece), shape(bands * lines * 4, WIDTH)],
        [
            block_pattern,
            slot_node,
            node_diag,
            solid_start,
            coupling,
            hits,
            flipped,
            rest,
            start_slots,
            landed,
        ],
        "solve",
        scalars=(0,),
    )
    if settled:
        go = go.reshape(bands, lines, 4, WIDTH // cap, cap).transpose(0, 1, 3, 2, 4)
    go = go.reshape(bands * slabs, 4, cap)
    come = lax.all_to_all(go, ("grp", "sub"), split_axis=0, concat_axis=0, tiled=True)
    hot_out, motion_out = call(
        join_kernel,
        [shape(*hot.shape), shape(*motion.shape)],
        [hot, motion, from_near, from_next],
        "join",
    )
    if settled:
        own = lax.dynamic_slice_in_dim(come, lax.axis_index("grp") * slabs, slabs, 0)
        own = own.transpose(1, 0, 2).reshape(4, lines, WIDTH).transpose(1, 0, 2)
        own = own.reshape(4 * lines, WIDTH)
        come = jnp.pad(come, ((0, 0), (0, 0), (0, WIDTH - cap)))
    else:
        own = rest
    come = come.reshape(4 * bands * slabs, WIDTH)
    temp, seen = call(
        functools.partial(last_kernel, not settled),
        [shape(1, blocks, piece), shape(1, rows)],
        [
            come,
            own,
            solid_start,
            residual,
            image,
            ordinal,
        ],
        "finish",
    )
    return hot_out, motion_out, temp, seen


def solution(mesh):
    placed = (
        P(None, "sub", "grp", None),
        P(None, "sub", "grp", None),
        P("sub", "grp", None),
        P("grp", "sub"),
        P("grp", "sub", None),
        P("grp", "sub"),
        P("grp", "sub"),
        P("grp", "sub", None),
        P("grp", "sub", None, None),
        P("grp", "sub"),
        P("grp", "sub", None),
        P("grp", "sub", None),
    )
    return jax.shard_map(
        body,
        mesh=mesh,
        in_specs=placed,
        out_specs=(
            P("sub", "grp", None),
            P(None, "sub", "grp", None),
            P("grp", "sub", None),
            P("grp", "sub"),
        ),
        check_vma=False,
    )
```

```python
import functools
import jax
import jax.numpy as jnp
import numpy as np
from jax import lax
from jax.experimental import pallas as pl
from jax.experimental.pallas import tpu as pltpu
from jax.sharding import PartitionSpec as P

FLOW_VELOCITY = [
    (0, 0, 0),
    (1, 0, 0),
    (-1, 0, 0),
    (0, 1, 0),
    (0, -1, 0),
    (0, 0, 1),
    (0, 0, -1),
    (1, 1, 0),
    (-1, -1, 0),
    (1, -1, 0),
    (-1, 1, 0),
    (1, 0, 1),
    (-1, 0, -1),
    (1, 0, -1),
    (-1, 0, 1),
    (0, 1, 1),
    (0, -1, -1),
    (0, 1, -1),
    (0, -1, 1),
]
VELOCITY = FLOW_VELOCITY + FLOW_VELOCITY[:7]
FLOWS, HEATS = 19, 7
LANES_ALL = range(FLOWS + HEATS)
UP = [i for i in LANES_ALL if VELOCITY[i][2] == 1]
DOWN = [i for i in LANES_ALL if VELOCITY[i][2] == -1]
RIGHT = [i for i in LANES_ALL if VELOCITY[i][0] == 1]
LEFT = [
    next(j for j in LANES_ALL if VELOCITY[j] == (-1,) + VELOCITY[i][1:] and (j < 19) == (i < 19))
    for i in RIGHT
]
TURNED = [
    next(n for n, j in enumerate(RIGHT[:-1]) if VELOCITY[j][1:] == (-VELOCITY[i][1], -VELOCITY[i][2]))
    for i in RIGHT[:-1]
]
STILL = [i for i in LANES_ALL if VELOCITY[i][0] == 0]
GATHERED = len(STILL) + 2 * len(RIGHT) + 1
SUMS = 4
FACE = SUMS + 2 * len(RIGHT) + 1
WIDTH = 128
SHIFT = 4.0
f32 = jnp.float32
bf16 = jnp.bfloat16


def signed_sum(terms):
    total = None
    for sign, term in terms:
        if sign == 0:
            continue
        if total is None:
            total = term if sign > 0 else -term
        else:
            total = total + term if sign > 0 else total - term
    return total


def collide(flow, heat, solid):
    pairs = range(1, FLOWS, 2)
    density = flow[0]
    for i in pairs:
        density = density + (flow[i] + flow[i + 1])
    gaps = {i: flow[i] - flow[i + 1] for i in pairs}
    scale = 1.0 / density
    speed = [
        signed_sum([(FLOW_VELOCITY[i][axis], gaps[i]) for i in pairs]) * scale for axis in range(3)
    ]
    square = speed[0] * speed[0] + speed[1] * speed[1] + speed[2] * speed[2]
    base = 1.0 - 1.5 * square
    gas = 1.0 - solid
    keep = gas * (1.0 - 1.0 / 0.8)
    pull = gas * (density * (1.0 / 0.8))
    flow_post = [None] * FLOWS
    flow_post[0] = (keep + solid) * flow[0] + (pull * (1.0 / 3.0)) * base
    shares = {1: pull * (1.0 / 18.0), 2: pull * (1.0 / 36.0)}
    for i in pairs:
        share = shares[sum(abs(c) for c in FLOW_VELOCITY[i])]
        along = signed_sum([(FLOW_VELOCITY[i][axis], speed[axis]) for axis in range(3)])
        even = base + 4.5 * along * along
        odd = 3.0 * along
        flow_post[i] = keep * flow[i] + share * (even + odd) + solid * flow[i + 1]
        flow_post[i + 1] = keep * flow[i + 1] + share * (even - odd) + solid * flow[i]
    hotness = heat[0]
    for j in range(1, HEATS):
        hotness = hotness + heat[j]
    stay = 1.0 - 1.0 / 0.7
    heat_post = [stay * heat[0] + (0.25 / 0.7) * hotness]
    level = (0.125 / 0.7) * hotness
    for j in range(1, HEATS, 2):
        axis = (j - 1) // 2
        drift = 4.0 * speed[axis]
        heat_post.append(stay * heat[j] + level * (1.0 + drift))
        heat_post.append(stay * heat[j + 1] + level * (1.0 - drift))
    return flow_post + heat_post


def collide_halo(still, inward, outward, solid):
    flows = RIGHT[:-1]
    density, along_y, along_z, hotness = still
    pairs = [(a + b, a - b) for a, b in zip(inward, outward)]
    across = None
    for n, i in enumerate(flows):
        _, ey, ez = VELOCITY[i]
        whole, gap = pairs[n]
        density = density + whole
        across = gap if across is None else across + gap
        along_y = signed_sum([(1, along_y), (ey, whole)])
        along_z = signed_sum([(1, along_z), (ez, whole)])
    hotness = hotness + pairs[-1][0]
    scale = 1.0 / density
    speed = [across * scale, along_y * scale, along_z * scale]
    square = speed[0] * speed[0] + speed[1] * speed[1] + speed[2] * speed[2]
    base = 1.0 - 1.5 * square
    gas = 1.0 - solid
    keep = gas * (1.0 - 1.0 / 0.8)
    pull = gas * (density * (1.0 / 0.8))
    shares = {1: pull * (1.0 / 18.0), 2: pull * (1.0 / 36.0)}
    out = []
    for n, i in enumerate(flows):
        share = shares[sum(abs(c) for c in VELOCITY[i])]
        along = signed_sum([(VELOCITY[i][axis], speed[axis]) for axis in range(3)])
        feq = share * (base + 4.5 * along * along + 3.0 * along)
        out.append(keep * inward[n] + feq + solid * outward[TURNED[n]])
    level = (0.125 / 0.7) * hotness
    out.append((1.0 - 1.0 / 0.7) * inward[-1] + level * (1.0 + 4.0 * speed[0]))
    return out


def three_parts(value):
    high = value.astype(bf16).astype(f32)
    rest = value - high
    middle = rest.astype(bf16).astype(f32)
    return [high, middle, rest - middle]


def times_transposed(left, right):
    return lax.dot_general(
        left.astype(bf16), right.astype(bf16), (((1,), (1,)), ((), ())), preferred_element_type=f32
    )


def spread(row):
    return jnp.broadcast_to(row, (8, row.shape[-1]))


def lane_gather(row, lane):
    return jnp.take_along_axis(spread(row), lane, axis=1, mode="promise_in_bounds")


def table_gather(table, index):
    place, lane = index >> 7, index & 127
    out = jnp.zeros(index.shape, f32)
    for row in range(table.shape[0]):
        out = jnp.where(place == row, lane_gather(table[row : row + 1], lane), out)
    return out


def plane_rows(plane, first=0, count=8):
    return pl.ds(4 * first + plane, count, stride=4)


def stacked(row):
    return jnp.concatenate(
        [row[:, k * WIDTH : (k + 1) * WIDTH] for k in range(row.shape[1] // WIDTH)], axis=0
    )


def slot_tables(cap, voxel, dest, coeff, ordinal):
    rows_here = dest.shape[1]
    owner = dest[...].astype(f32)
    chunks = rows_here // WIDTH
    tall = stacked(owner)
    tall = jnp.concatenate([tall] + [jnp.zeros((8 - chunks, WIDTH), f32)] * (chunks < 8), axis=0)
    upright = tall.T
    first = lax.broadcasted_iota(jnp.int32, (WIDTH, WIDTH), 0)
    second = lax.broadcasted_iota(jnp.int32, (WIDTH, WIDTH), 1)
    slot_row = lax.broadcasted_iota(jnp.int32, (8, WIDTH), 0)
    table = jnp.zeros((40, WIDTH), f32)
    for c in range(chunks):
        lanes = slice(c * WIDTH, (c + 1) * WIDTH)
        here = owner[:, lanes]
        count = jnp.zeros((WIDTH, WIDTH), f32)
        for other in range(c + 1):
            same = upright[:, other : other + 1] == here
            if other == c:
                same = same & (first < second)
            count = count + jnp.where(same, 1.0, 0.0)
        rank = jnp.sum(count, axis=0, keepdims=True)
        place = (here * float(cap) + rank).astype(jnp.int32)
        ordinal[:, lanes] = place
        mine = slot_row == (place >> 7)
        spot = voxel[:, lanes]
        parts = [(spot >> 7).astype(f32), (spot & 127).astype(f32)] + three_parts(coeff[:, lanes])
        values = jnp.concatenate([jnp.where(mine, part, 0.0) for part in parts], axis=0)
        table = table + times_transposed(values, jnp.where(first == (place & 127), 1.0, 0.0))
    spots = table[0:8] * float(WIDTH) + table[8:16]
    coeffs = (table[16:24] + table[24:32]) + table[32:40]
    return spots, coeffs


def on_even(axis="sub"):
    return lax.rem(lax.axis_index(axis), 2) == 0


def first_kernel(cap, *refs):
    given, (post, to_near, to_next, face_r, face_l, ordinal) = refs[:6], refs[6:12]
    held, arrived = refs[12:18], refs[18]
    pops, heat, solid, voxel, dest, coeff = held
    pieces = [(given[n], held[n]) for n in (4, 3, 5)]
    for z in range(solid.shape[0]):
        pieces += [(given[n].at[:, z], held[n].at[:, z]) for n in (0, 1)]
        pieces.append((given[2].at[z], held[2].at[z]))
    copies = [
        pltpu.make_async_copy(source, target, arrived.at[n])
        for n, (source, target) in enumerate(pieces)
    ]
    for copy in copies:
        copy.start()
    layers, across, along = solid.shape
    even = on_even()
    for copy in copies[:3]:
        copy.wait()
    spots, coeffs = slot_tables(cap, voxel, dest, coeff, ordinal)
    extra = len(UP)
    for plane in (to_near, to_next):
        plane[extra] = jnp.zeros(plane.shape[1:], f32)
        plane[extra, :, 0:WIDTH] = spots
        plane[extra, :, WIDTH : 2 * WIDTH] = coeffs
    for z in range(layers):
        for copy in copies[3 + 3 * z : 6 + 3 * z]:
            copy.wait()
        for start in range(0, along, WIDTH):
            lanes = slice(start, start + WIDTH)
            out = collide(
                [pops[i, z, :, lanes] for i in range(FLOWS)],
                [heat[j, z, :, lanes] for j in range(HEATS)],
                solid[z, :, lanes],
            )
            for i in LANES_ALL:
                post[i, z, :, lanes] = out[i]
            for face, lists, near, far in (
                (face_r, (STILL, RIGHT), across - 1, across - 2),
                (face_l, (STILL, LEFT), 0, 1),
            ):
                rows = [(i, near) for i in lists[0]] + [(i, far) for i in lists[1]]
                rows = rows + [(i, near) for i in lists[1]]
                for n, (i, column) in enumerate(rows):
                    at = n * layers + z
                    face[at : at + 1, lanes] = out[i][column : column + 1]
                at = len(rows) * layers + z
                face[at : at + 1, lanes] = solid[z, near : near + 1, lanes]
    for n, (above, below) in enumerate(zip(UP, DOWN)):
        above, below = post[above, layers - 1], post[below, 0]
        to_near[n] = jnp.where(even, above, below)
        to_next[n] = jnp.where(even, below, above)


def turned(tile, step):
    return tile if step == 0 else pltpu.roll(tile, step % tile.shape[1], 1)


def edge_kernel(layers, face_r, face_l, near, next_, to_a, to_b, out_r, out_l):
    out_r[...] = face_r[...]
    out_l[...] = face_l[...]
    across = near.shape[1]
    even = on_even()
    for out, lists, edge, inside in (
        (out_r, (STILL, RIGHT), across - 1, across - 2),
        (out_l, (STILL, LEFT), 0, 1),
    ):
        rows = [(i, edge) for i in lists[0]] + [(i, inside) for i in lists[1]]
        rows = rows + [(i, edge) for i in lists[1]]
        for n, (i, column) in enumerate(rows):
            rise = VELOCITY[i][2]
            if rise == 0:
                continue
            moved = range(layers - 1, 0, -1) if rise == 1 else range(layers - 1)
            for z in moved:
                at, source = n * layers + z, n * layers + z - rise
                out[at : at + 1, :] = out[source : source + 1, :]
            z = 0 if rise == 1 else layers - 1
            at = n * layers + z
            k = (UP if rise == 1 else DOWN).index(i)
            one, two = near[k, column : column + 1, :], next_[k, column : column + 1, :]
            out[at : at + 1, :] = jnp.where(even == (rise == 1), two, one)
    band_even = on_even("grp")

    def both(n):
        at = slice(n * layers, (n + 1) * layers)
        return jnp.concatenate([out_r[at, :], out_l[at, :]], axis=0)

    def send(n, tile):
        at = slice(n * layers, (n + 1) * layers)
        right, left = tile[0:layers], tile[layers : 2 * layers]
        to_a[at, :] = jnp.where(band_even, right, left)
        to_b[at, :] = jnp.where(band_even, left, right)

    sums = [[] for _ in range(SUMS)]
    for n, i in enumerate(STILL):
        _, ey, ez = VELOCITY[i]
        tile = turned(both(n), ey)
        if i >= FLOWS:
            sums[3].append((1, tile))
        else:
            sums[0].append((1, tile))
            sums[1].append((ey, tile))
            sums[2].append((ez, tile))
    for n in range(SUMS):
        send(n, signed_sum(sums[n]))
    for n, i in enumerate(RIGHT):
        send(SUMS + n, turned(both(len(STILL) + n), VELOCITY[i][1]))
    for n in range(len(STILL) + len(RIGHT), GATHERED):
        send(n - len(STILL) + SUMS, both(n))


def second_kernel(
    post,
    near,
    next_,
    to_a,
    to_b,
    faces_a,
    faces_b,
    solid,
    own_table,
    tie,
    hot,
    motion,
    send_near,
    send_next,
    fluxes,
    moved,
    halo,
):
    layers, across, along = solid.shape
    even = on_even()
    band_even = on_even("grp")
    own_r = jnp.where(band_even, to_a[...], to_b[...])
    own_l = jnp.where(band_even, to_b[...], to_a[...])
    below = [jnp.where(even, next_[n], near[n]) for n in range(len(UP) + 1)]
    above = [jnp.where(even, near[n], next_[n]) for n in range(len(UP) + 1)]
    from_l = jnp.where(band_even, faces_b[...], faces_a[...])
    from_r = jnp.where(band_even, faces_a[...], faces_b[...])
    slot = lax.broadcasted_iota(jnp.int32, (across, along), 0)
    edge = SUMS + len(RIGHT)
    for i in LANES_ALL:
        ex, ey, ez = VELOCITY[i]
        for z in range(layers):
            if z - ez < 0:
                tile = below[UP.index(i)]
            elif z - ez >= layers:
                tile = above[DOWN.index(i)]
            else:
                tile = post[i, z - ez]
            if ex == 1:
                at = (edge + RIGHT.index(i)) * layers + z
                tile = jnp.where(slot == 0, from_l[at : at + 1, :], pltpu.roll(tile, 1, 0))
            elif ex == -1:
                at = (edge + LEFT.index(i)) * layers + z
                tile = jnp.where(
                    slot == across - 1, from_r[at : at + 1, :], pltpu.roll(tile, across - 1, 0)
                )
            moved[i, z] = turned(tile, ey)

    def halves(low, high, n):
        at = slice(n * layers, (n + 1) * layers)
        parts = [low[at], high[at]]
        if 2 * layers < 8:
            parts.append(jnp.ones((8 - 2 * layers, along), f32))
        return jnp.concatenate(parts, axis=0)

    for n in range(edge):
        halo[n] = halves(from_l, from_r, n)
    for n, i in enumerate(RIGHT):
        halo[edge + n] = turned(halves(own_l, own_r, edge + n), VELOCITY[i][1])
    edge_solid = halves(from_l, from_r, FACE - 1)
    for start in range(0, along, WIDTH):
        lanes = slice(start, start + WIDTH)
        for z in range(layers):
            out = collide(
                [moved[i, z, :, lanes] for i in range(FLOWS)],
                [moved[FLOWS + j, z, :, lanes] for j in range(HEATS)],
                solid[z, :, lanes],
            )
            for i in LANES_ALL:
                moved[i, z, :, lanes] = out[i]
        out = collide_halo(
            [halo[n, :, lanes] for n in range(SUMS)],
            [halo[SUMS + n, :, lanes] for n in range(len(RIGHT))],
            [halo[edge + n, :, lanes] for n in range(len(RIGHT))],
            edge_solid[:, lanes],
        )
        for n in range(len(RIGHT)):
            halo[SUMS + n, :, lanes] = out[n]
    sums = {}

    def add(key, sign, tile):
        if sign == 0:
            return
        if key in sums:
            sums[key] = sums[key] + tile if sign > 0 else sums[key] - tile
        else:
            sums[key] = tile if sign > 0 else -tile

    for z in range(layers):
        for i in LANES_ALL:
            ex, ey, ez = VELOCITY[i]
            if i == 0:
                continue
            tile = moved[i, z]
            if ex == 1:
                side = halo[SUMS + RIGHT.index(i), z : z + 1, :]
                tile = jnp.where(slot == 0, side, pltpu.roll(tile, 1, 0))
            elif ex == -1:
                at = layers + z
                side = halo[SUMS + LEFT.index(i), at : at + 1, :]
                tile = jnp.where(slot == across - 1, side, pltpu.roll(tile, across - 1, 0))
            tile = turned(tile, ey)
            target = z + ez
            if i >= FLOWS:
                add((3, target), 1, tile)
            else:
                add((0, target), ex, tile)
                add((1, target), ey, tile)
                add((2, target), ez, tile)
    for z in range(layers):
        hot[z] = sums[3, z]
        for axis in range(3):
            motion[axis, z] = sums[axis, z]
    for part in range(4):
        send_near[part] = jnp.where(even, sums[part, layers], sums[part, -1])
        send_next[part] = jnp.where(even, sums[part, -1], sums[part, layers])
    extra = len(UP)
    per_line = along // WIDTH
    per_layer = across * per_line

    def flux(table, planes):
        index = table[:, 0:WIDTH].astype(jnp.int32)
        place, lane = index >> 7, index & 127
        out = jnp.zeros(lane.shape, f32)
        for z, plane in planes:
            for x in range(across):
                for c in range(per_line):
                    row = plane[x : x + 1, c * WIDTH : (c + 1) * WIDTH]
                    out = jnp.where(
                        place == z * per_layer + x * per_line + c, lane_gather(row, lane), out
                    )
        return out * table[:, WIDTH : 2 * WIDTH]

    mine = own_table[extra]
    fluxes[plane_rows(0), :] = flux(mine, [(z, sums[3, z]) for z in range(layers)])
    fluxes[plane_rows(1), :] = flux(above[extra], [(0, sums[3, layers])])
    fluxes[plane_rows(2), :] = flux(below[extra], [(layers - 1, sums[3, -1])])
    fluxes[plane_rows(3), :] = mine[:, WIDTH : 2 * WIDTH]


def sublane_gather(value, index):
    return jnp.take_along_axis(value, index, axis=0, mode="promise_in_bounds")


def coupled(vector, blocks, flipped, shift):
    count = vector.shape[0]
    upright = vector.T
    ahead, back = [], []
    for b in range(count):
        column = jnp.broadcast_to(upright[:, b : b + 1], blocks.shape[1:])
        back.append(jnp.sum(blocks[b] * column, axis=0, keepdims=True))
        ahead.append(jnp.sum(flipped[b] * column, axis=0, keepdims=True))
    ahead = jnp.concatenate(ahead, axis=0)
    back = jnp.concatenate(back, axis=0)
    block = lax.broadcasted_iota(jnp.int32, vector.shape, 0)
    ahead = sublane_gather(ahead, (block + shift) & (count - 1))
    return ahead + sublane_gather(back, (block - shift) & (count - 1))


def ready_kernel(
    pattern, nodes, diagonal, source, start, coupling, tie, hits, flipped, rest, slots, turn
):
    shift = pattern[0, 0]
    turn[...] = jnp.full(turn.shape, shift, jnp.int32)
    count = start.shape[1]
    for b in range(count):
        flipped[lax.rem(b + shift, count)] = coupling[0, b].T
    vector = start[0]
    rest[...] = (
        source[0] - diagonal[0] * vector + coupled(vector, coupling.at[0], flipped, turn[...])
    )
    index = stacked(nodes[...])
    slots[...] = table_gather(vector, index)
    upright = (index & 127).astype(f32).T.astype(jnp.int32)
    lane = lax.broadcasted_iota(jnp.int32, (WIDTH, WIDTH), 1)
    for s in range(index.shape[0]):
        hit = jnp.where(upright[:, s : s + 1] == lane, 1.0, 0.0)
        hits[s * WIDTH : (s + 1) * WIDTH] = hit.astype(bf16)


def solve_kernel(
    cap,
    turn,
    nodes,
    diagonal,
    start,
    coupling,
    hits,
    flipped,
    rest,
    slots,
    come,
    res,
    img,
    go,
):
    shift = turn[...]
    count = start.shape[1]
    index = stacked(nodes[...])
    place = index >> 7
    own, low, high, coeff = (come[plane_rows(plane), :] for plane in range(4))
    if cap == WIDTH:
        low = pltpu.roll(low, 1, 0)
        high = pltpu.roll(high, low.shape[0] - 1, 0)
    parts = three_parts(own + low + high) + three_parts(coeff)
    block = lax.broadcasted_iota(jnp.int32, (count, WIDTH), 0)
    values = []
    for s in range(index.shape[0]):
        mine = block == place[s : s + 1]
        values.append(
            jnp.concatenate([jnp.where(mine, part[s : s + 1], 0.0) for part in parts], axis=0)
        )
    values = jnp.concatenate(values, axis=1).astype(bf16)
    landed = jnp.dot(values, hits[...], preferred_element_type=f32)
    landed = [landed[k * count : (k + 1) * count] for k in range(len(parts))]
    added = (landed[0] + landed[1]) + landed[2]
    extra = (landed[3] + landed[4]) + landed[5]
    whole = diagonal[0] + extra
    blocks = coupling.at[0]
    residual = rest[...] + added - extra * start[0]
    image = whole * residual - coupled(residual, blocks, flipped, shift)

    def total(value):
        return jnp.sum(jnp.sum(value, axis=0, keepdims=True), axis=1, keepdims=True)

    offset = image - SHIFT * residual
    bend = whole * offset - coupled(offset, blocks, flipped, shift)
    totals = [
        total(residual * residual),
        total(residual * offset),
        total(offset * offset),
        total(offset * bend),
    ]
    res[...] = residual
    img[...] = image
    lane = lax.broadcasted_iota(jnp.int32, (8, WIDTH), 1) & (cap - 1)
    facts = jnp.zeros((8, WIDTH), f32)
    for n, fact in enumerate(totals):
        facts = jnp.where(lane == n, fact, facts)
    residual_slots = table_gather(residual, index)
    image_slots = table_gather(image, index)
    start_slots = slots[...]
    for group in range(0, go.shape[0] // 4, 8):
        go[plane_rows(0, group), :] = start_slots
        go[plane_rows(1, group), :] = residual_slots
        go[plane_rows(2, group), :] = image_slots
        go[plane_rows(3, group), :] = facts


def last_kernel(direct, come, own, start, res, img, ordinal, temp, seen):
    places = stacked(ordinal[...])
    chunks = places.shape[0]
    if chunks < 8:
        places = jnp.concatenate([places, jnp.zeros((8 - chunks, WIDTH), jnp.int32)], axis=0)
    found = []
    for plane in range(3):
        if direct:
            table = come[plane_rows(plane, lax.axis_index("grp") * 8), :]
        else:
            table = own[plane_rows(plane), :]
        found.append(table_gather(table, places))
    facts = come[plane_rows(3, 0, come.shape[0] // 4), :]
    facts = jnp.sum(facts, axis=0, keepdims=True)
    all_norm, cross, square, energy = (
        lane_gather(facts, jnp.full((8, WIDTH), n, jnp.int32)) for n in range(4)
    )
    product = SHIFT * all_norm + cross
    inverse = 1.0 / product
    ratio = cross / all_norm
    spread_square = square - cross * ratio
    energy = energy - ratio * (2.0 * (square + SHIFT * cross) - ratio * product)
    small = spread_square * inverse
    first = all_norm * inverse
    step = spread_square / (energy - spread_square * small)
    of_residual = first + step * (1.0 + small * first)
    of_image = -step * first
    temp[0] = start[0] + of_residual * res[...] + of_image * img[...]
    found = found[0] + of_residual * found[1] + of_image * found[2]
    for c in range(chunks):
        seen[:, c * WIDTH : (c + 1) * WIDTH] = found[c : c + 1]


def join_kernel(hot, motion, near, next_, hot_out, motion_out):
    layers = hot.shape[0]
    even = on_even()
    below = [jnp.where(even, next_[n], near[n]) for n in range(4)]
    above = [jnp.where(even, near[n], next_[n]) for n in range(4)]
    for z in range(layers):
        for part in range(4):
            tile = hot[z] if part == 3 else motion[part, z]
            if z == 0:
                tile = tile + below[part]
            if z == layers - 1:
                tile = tile + above[part]
            if part == 3:
                hot_out[z] = tile
            else:
                motion_out[part, z] = tile


VMEM = pl.BlockSpec(memory_space=pltpu.VMEM)
ANYWHERE = pl.BlockSpec(memory_space=pl.ANY)
SMEM = pl.BlockSpec(memory_space=pltpu.SMEM)


def call(kernel, out, args, name, scalars=(), scratch=(), far=False):
    total = sum(int(np.prod(a.shape)) * a.dtype.itemsize for a in list(args) + list(out))
    if far:
        args = [pltpu.with_memory_space_constraint(a, pltpu.HBM) for a in args]
    return pl.pallas_call(
        kernel,
        out_shape=out,
        in_specs=[
            ANYWHERE if far else SMEM if n in scalars else VMEM for n in range(len(args))
        ],
        out_specs=[VMEM] * len(out),
        scratch_shapes=scratch,
        compiler_params=pltpu.CompilerParams(vmem_limit_bytes=24 << 20),
        cost_estimate=pl.CostEstimate(flops=1 << 20, bytes_accessed=total, transcendentals=0),
        name=name,
    )(*args)


def shape(*dims, dtype=f32):
    return jax.ShapeDtypeStruct(dims, dtype)


def swaps(axis):
    count = lax.axis_size(axis)
    assert count % 2 == 0
    near = [(k, k + 1 - 2 * (k % 2)) for k in range(count)]
    return near, [(k, (k - 1 + 2 * (k % 2)) % count) for k in range(count)]


def body(
    populations,
    heat_pops,
    solid_frac,
    coupled_grid_point,
    dest_index,
    heat_coeff,
    slot_node,
    node_diag,
    coupling,
    block_pattern,
    heat_source,
    solid_start,
):
    layers, across, along = solid_frac.shape
    slabs, bands = lax.axis_size("sub"), lax.axis_size("grp")
    slots = slot_node.shape[1]
    cap = slots // slabs
    rows = coupled_grid_point.shape[1]
    blocks, piece = node_diag.shape[1:]
    lines = slots // WIDTH
    assert lines == 8 and across == 8 and along >= 2 * WIDTH and along % WIDTH == 0
    assert piece == WIDTH and blocks == 8 and WIDTH % cap == 0 and cap >= 8
    assert rows % WIDTH == 0 and rows <= 8 * WIDTH and layers <= 4
    gathered_rows = -(-GATHERED * layers // 8) * 8
    face_rows = -(-FACE * layers // 8) * 8
    planes = len(UP) + 1
    post, to_near, to_next, face_r, face_l, ordinal = call(
        functools.partial(first_kernel, cap),
        [
            shape(FLOWS + HEATS, layers, across, along),
            shape(planes, across, along),
            shape(planes, across, along),
            shape(gathered_rows, along),
            shape(gathered_rows, along),
            shape(1, rows, dtype=jnp.int32),
        ],
        [
            populations,
            heat_pops,
            solid_frac,
            coupled_grid_point,
            dest_index.reshape(1, rows),
            heat_coeff,
        ],
        "collide_first",
        scratch=[
            pltpu.VMEM(solid_like, kind)
            for solid_like, kind in (
                (populations.shape, f32),
                (heat_pops.shape, f32),
                (solid_frac.shape, f32),
                ((1, rows), jnp.int32),
                ((1, rows), jnp.int32),
                ((1, rows), f32),
            )
        ]
        + [pltpu.SemaphoreType.DMA((3 + 3 * layers,))],
        far=True,
    )
    near_pairs, next_pairs = swaps("sub")
    near = lax.ppermute(to_near, "sub", near_pairs)
    next_ = lax.ppermute(to_next, "sub", next_pairs)
    to_a, to_b = call(
        functools.partial(edge_kernel, layers),
        [shape(face_rows, along)] * 2,
        [face_r, face_l, near, next_],
        "x_faces",
        scratch=[pltpu.VMEM((gathered_rows, along), f32)] * 2,
    )
    hits, flipped, rest, start_slots, turn = call(
        ready_kernel,
        [
            shape(slots, WIDTH, dtype=bf16),
            shape(blocks, piece, piece),
            shape(blocks, piece),
            shape(lines, WIDTH),
            shape(blocks, WIDTH, dtype=jnp.int32),
        ],
        [block_pattern, slot_node, node_diag, heat_source, solid_start, coupling, to_a],
        "solid_ready",
        scalars=(0,),
    )
    side_a, side_b = swaps("grp")
    faces_a = lax.ppermute(to_a, "grp", side_a)
    faces_b = lax.ppermute(to_b, "grp", side_b)
    hot, motion, send_near, send_next, fluxes = call(
        second_kernel,
        [
            shape(layers, across, along),
            shape(3, layers, across, along),
            shape(4, across, along),
            shape(4, across, along),
            shape(4 * lines, WIDTH),
        ],
        [post, near, next_, to_a, to_b, faces_a, faces_b, solid_frac, to_near, rest],
        "collide_second",
        scratch=[
            pltpu.VMEM((FLOWS + HEATS, layers, across, along), f32),
            pltpu.VMEM((FACE - 1, 8, along), f32),
        ],
    )
    settled = cap != WIDTH
    if settled:
        fluxes = fluxes.reshape(lines, 4, WIDTH // cap, cap).transpose(0, 2, 1, 3)
    fluxes = fluxes.reshape(slabs, 4, cap)
    landed = lax.all_to_all(fluxes, "sub", split_axis=0, concat_axis=0, tiled=True)
    if settled:
        landed = jnp.stack(
            [
                landed[:, 0],
                jnp.roll(landed[:, 1], 1, axis=0),
                jnp.roll(landed[:, 2], -1, axis=0),
                landed[:, 3],
            ]
        )
        landed = landed.reshape(4, lines, WIDTH).transpose(1, 0, 2)
    landed = landed.reshape(4 * lines, WIDTH)
    from_near = lax.ppermute(send_near, "sub", near_pairs)
    from_next = lax.ppermute(send_next, "sub", next_pairs)
    residual, image, go = call(
        functools.partial(solve_kernel, cap),
        [shape(blocks, piece), shape(blocks, piece), shape(bands * lines * 4, WIDTH)],
        [
            turn,
            slot_node,
            node_diag,
            solid_start,
            coupling,
            hits,
            flipped,
            rest,
            start_slots,
            landed,
        ],
        "solve",
    )
    if settled:
        go = go.reshape(bands, lines, 4, WIDTH // cap, cap).transpose(0, 1, 3, 2, 4)
    go = go.reshape(bands * slabs, 4, cap)
    come = lax.all_to_all(go, ("grp", "sub"), split_axis=0, concat_axis=0, tiled=True)
    hot_out, motion_out = call(
        join_kernel,
        [shape(*hot.shape), shape(*motion.shape)],
        [hot, motion, from_near, from_next],
        "join",
    )
    if settled:
        own = lax.dynamic_slice_in_dim(come, lax.axis_index("grp") * slabs, slabs, 0)
        own = own.transpose(1, 0, 2).reshape(4, lines, WIDTH).transpose(1, 0, 2)
        own = own.reshape(4 * lines, WIDTH)
        come = jnp.pad(come, ((0, 0), (0, 0), (0, WIDTH - cap)))
    else:
        own = rest
    come = come.reshape(4 * bands * slabs, WIDTH)
    temp, seen = call(
        functools.partial(last_kernel, not settled),
        [shape(1, blocks, piece), shape(1, rows)],
        [
            come,
            own,
            solid_start,
            residual,
            image,
            ordinal,
        ],
        "finish",
    )
    return hot_out, motion_out, temp, seen


def solution(mesh):
    placed = (
        P(None, "sub", "grp", None),
        P(None, "sub", "grp", None),
        P("sub", "grp", None),
        P("grp", "sub"),
        P("grp", "sub", None),
        P("grp", "sub"),
        P("grp", "sub"),
        P("grp", "sub", None),
        P("grp", "sub", None, None),
        P("grp", "sub"),
        P("grp", "sub", None),
        P("grp", "sub", None),
    )
    return jax.shard_map(
        body,
        mesh=mesh,
        in_specs=placed,
        out_specs=(
            P("sub", "grp", None),
            P(None, "sub", "grp", None),
            P("grp", "sub", None),
            P("grp", "sub"),
        ),
        check_vma=False,
    )
```

```python
import functools
import jax
import jax.numpy as jnp
import numpy as np
from jax import lax
from jax.experimental import pallas as pl
from jax.experimental.pallas import tpu as pltpu
from jax.sharding import PartitionSpec as P

FLOW_VELOCITY = [
    (0, 0, 0),
    (1, 0, 0),
    (-1, 0, 0),
    (0, 1, 0),
    (0, -1, 0),
    (0, 0, 1),
    (0, 0, -1),
    (1, 1, 0),
    (-1, -1, 0),
    (1, -1, 0),
    (-1, 1, 0),
    (1, 0, 1),
    (-1, 0, -1),
    (1, 0, -1),
    (-1, 0, 1),
    (0, 1, 1),
    (0, -1, -1),
    (0, 1, -1),
    (0, -1, 1),
]
VELOCITY = FLOW_VELOCITY + FLOW_VELOCITY[:7]
FLOWS, HEATS = 19, 7
LANES_ALL = range(FLOWS + HEATS)
UP = [i for i in LANES_ALL if VELOCITY[i][2] == 1]
DOWN = [
    next(j for j in LANES_ALL if VELOCITY[j] == VELOCITY[i][:2] + (-1,) and (j < 19) == (i < 19))
    for i in UP
]
RIGHT = [i for i in LANES_ALL if VELOCITY[i][0] == 1]
LEFT = [
    next(j for j in LANES_ALL if VELOCITY[j] == (-1,) + VELOCITY[i][1:] and (j < 19) == (i < 19))
    for i in RIGHT
]
TURNED = [
    next(n for n, j in enumerate(RIGHT[:-1]) if VELOCITY[j][1:] == (-VELOCITY[i][1], -VELOCITY[i][2]))
    for i in RIGHT[:-1]
]
STILL = [i for i in LANES_ALL if VELOCITY[i][0] == 0]
GATHERED = len(STILL) + 2 * len(RIGHT) + 1
SUMS = 4
FACE = SUMS + 2 * len(RIGHT) + 1
CORNER_ROWS = 8


def place_of(lists, ex, ey, ez):
    return next(n for n, i in enumerate(lists) if VELOCITY[i] == (ex, ey, ez))


WIDTH = 128
SHIFT = 4.0
f32 = jnp.float32
bf16 = jnp.bfloat16


def signed_sum(terms):
    total = None
    for sign, term in terms:
        if sign == 0:
            continue
        if total is None:
            total = term if sign > 0 else -term
        else:
            total = total + term if sign > 0 else total - term
    return total


def collide(flow, heat, solid):
    pairs = range(1, FLOWS, 2)
    density = flow[0]
    for i in pairs:
        density = density + (flow[i] + flow[i + 1])
    gaps = {i: flow[i] - flow[i + 1] for i in pairs}
    scale = 1.0 / density
    speed = [
        signed_sum([(FLOW_VELOCITY[i][axis], gaps[i]) for i in pairs]) * scale for axis in range(3)
    ]
    square = speed[0] * speed[0] + speed[1] * speed[1] + speed[2] * speed[2]
    base = 1.0 - 1.5 * square
    gas = 1.0 - solid
    keep = gas * (1.0 - 1.0 / 0.8)
    pull = gas * (density * (1.0 / 0.8))
    flow_post = [None] * FLOWS
    flow_post[0] = (keep + solid) * flow[0] + (pull * (1.0 / 3.0)) * base
    shares = {1: pull * (1.0 / 18.0), 2: pull * (1.0 / 36.0)}
    for i in pairs:
        share = shares[sum(abs(c) for c in FLOW_VELOCITY[i])]
        along = signed_sum([(FLOW_VELOCITY[i][axis], speed[axis]) for axis in range(3)])
        even = base + 4.5 * along * along
        odd = 3.0 * along
        flow_post[i] = keep * flow[i] + share * (even + odd) + solid * flow[i + 1]
        flow_post[i + 1] = keep * flow[i + 1] + share * (even - odd) + solid * flow[i]
    hotness = heat[0]
    for j in range(1, HEATS):
        hotness = hotness + heat[j]
    stay = 1.0 - 1.0 / 0.7
    heat_post = [stay * heat[0] + (0.25 / 0.7) * hotness]
    level = (0.125 / 0.7) * hotness
    for j in range(1, HEATS, 2):
        axis = (j - 1) // 2
        drift = 4.0 * speed[axis]
        heat_post.append(stay * heat[j] + level * (1.0 + drift))
        heat_post.append(stay * heat[j + 1] + level * (1.0 - drift))
    return flow_post + heat_post


def collide_halo(still, inward, outward, solid):
    flows = RIGHT[:-1]
    density, along_y, along_z, hotness = still
    pairs = [(a + b, a - b) for a, b in zip(inward, outward)]
    across = None
    for n, i in enumerate(flows):
        _, ey, ez = VELOCITY[i]
        whole, gap = pairs[n]
        density = density + whole
        across = gap if across is None else across + gap
        along_y = signed_sum([(1, along_y), (ey, whole)])
        along_z = signed_sum([(1, along_z), (ez, whole)])
    hotness = hotness + pairs[-1][0]
    scale = 1.0 / density
    speed = [across * scale, along_y * scale, along_z * scale]
    square = speed[0] * speed[0] + speed[1] * speed[1] + speed[2] * speed[2]
    base = 1.0 - 1.5 * square
    gas = 1.0 - solid
    keep = gas * (1.0 - 1.0 / 0.8)
    pull = gas * (density * (1.0 / 0.8))
    shares = {1: pull * (1.0 / 18.0), 2: pull * (1.0 / 36.0)}
    out = []
    for n, i in enumerate(flows):
        share = shares[sum(abs(c) for c in VELOCITY[i])]
        along = signed_sum([(VELOCITY[i][axis], speed[axis]) for axis in range(3)])
        feq = share * (base + 4.5 * along * along + 3.0 * along)
        out.append(keep * inward[n] + feq + solid * outward[TURNED[n]])
    level = (0.125 / 0.7) * hotness
    out.append((1.0 - 1.0 / 0.7) * inward[-1] + level * (1.0 + 4.0 * speed[0]))
    return out


def three_parts(value):
    high = value.astype(bf16).astype(f32)
    rest = value - high
    middle = rest.astype(bf16).astype(f32)
    return [high, middle, rest - middle]


def times_transposed(left, right):
    return lax.dot_general(
        left.astype(bf16), right.astype(bf16), (((1,), (1,)), ((), ())), preferred_element_type=f32
    )


def spread(row):
    return jnp.broadcast_to(row, (8, row.shape[-1]))


def lane_gather(row, lane):
    return jnp.take_along_axis(spread(row), lane, axis=1, mode="promise_in_bounds")


def table_gather(table, index):
    place, lane = index >> 7, index & 127
    out = jnp.zeros(index.shape, f32)
    for row in range(table.shape[0]):
        out = jnp.where(place == row, lane_gather(table[row : row + 1], lane), out)
    return out


def plane_rows(plane, first=0, count=8):
    return pl.ds(4 * first + plane, count, stride=4)


def stacked(row):
    return jnp.concatenate(
        [row[:, k * WIDTH : (k + 1) * WIDTH] for k in range(row.shape[1] // WIDTH)], axis=0
    )


def slot_tables(cap, voxel, dest, coeff, ordinal):
    rows_here = dest.shape[1]
    owner = dest[...].astype(f32)
    chunks = rows_here // WIDTH
    tall = stacked(owner)
    tall = jnp.concatenate([tall] + [jnp.zeros((8 - chunks, WIDTH), f32)] * (chunks < 8), axis=0)
    upright = tall.T
    first = lax.broadcasted_iota(jnp.int32, (WIDTH, WIDTH), 0)
    second = lax.broadcasted_iota(jnp.int32, (WIDTH, WIDTH), 1)
    slot_row = lax.broadcasted_iota(jnp.int32, (8, WIDTH), 0)
    table = jnp.zeros((40, WIDTH), f32)
    for c in range(chunks):
        lanes = slice(c * WIDTH, (c + 1) * WIDTH)
        here = owner[:, lanes]
        count = jnp.zeros((WIDTH, WIDTH), f32)
        for other in range(c + 1):
            same = upright[:, other : other + 1] == here
            if other == c:
                same = same & (first < second)
            count = count + jnp.where(same, 1.0, 0.0)
        rank = jnp.sum(count, axis=0, keepdims=True)
        place = (here * float(cap) + rank).astype(jnp.int32)
        ordinal[:, lanes] = place
        mine = slot_row == (place >> 7)
        spot = voxel[:, lanes]
        parts = [(spot >> 7).astype(f32), (spot & 127).astype(f32)] + three_parts(coeff[:, lanes])
        values = jnp.concatenate([jnp.where(mine, part, 0.0) for part in parts], axis=0)
        table = table + times_transposed(values, jnp.where(first == (place & 127), 1.0, 0.0))
    spots = table[0:8] * float(WIDTH) + table[8:16]
    coeffs = (table[16:24] + table[24:32]) + table[32:40]
    return spots, coeffs


def on_even(axis="sub"):
    return lax.rem(lax.axis_index(axis), 2) == 0


def first_kernel(cap, *refs):
    given, (post, to_near, to_next, face_r, face_l, ordinal) = refs[:6], refs[6:12]
    held, arrived = refs[12:18], refs[18]
    pops, heat, solid, voxel, dest, coeff = held
    pieces = [(given[n], held[n]) for n in (4, 3, 5)]
    for z in range(solid.shape[0]):
        pieces += [(given[n].at[:, z], held[n].at[:, z]) for n in (0, 1)]
        pieces.append((given[2].at[z], held[2].at[z]))
    copies = [
        pltpu.make_async_copy(source, target, arrived.at[n])
        for n, (source, target) in enumerate(pieces)
    ]
    for copy in copies:
        copy.start()
    layers, across, along = solid.shape
    even = on_even()
    for copy in copies[:3]:
        copy.wait()
    spots, coeffs = slot_tables(cap, voxel, dest, coeff, ordinal)
    extra = len(UP)
    for plane in (to_near, to_next):
        plane[extra] = jnp.zeros(plane.shape[1:], f32)
        plane[extra, :, 0:WIDTH] = spots
        plane[extra, :, WIDTH : 2 * WIDTH] = coeffs
    for z in range(layers):
        for copy in copies[3 + 3 * z : 6 + 3 * z]:
            copy.wait()
        for start in range(0, along, WIDTH):
            lanes = slice(start, start + WIDTH)
            out = collide(
                [pops[i, z, :, lanes] for i in range(FLOWS)],
                [heat[j, z, :, lanes] for j in range(HEATS)],
                solid[z, :, lanes],
            )
            for i in LANES_ALL:
                post[i, z, :, lanes] = out[i]
            for face, lists, near, far in (
                (face_r, (STILL, RIGHT), across - 1, across - 2),
                (face_l, (STILL, LEFT), 0, 1),
            ):
                rows = [(i, near) for i in lists[0]] + [(i, far) for i in lists[1]]
                rows = rows + [(i, near) for i in lists[1]]
                for n, (i, column) in enumerate(rows):
                    at = n * layers + z
                    face[at : at + 1, lanes] = out[i][column : column + 1]
                at = len(rows) * layers + z
                face[at : at + 1, lanes] = solid[z, near : near + 1, lanes]
    for n, (above, below) in enumerate(zip(UP, DOWN)):
        above, below = post[above, layers - 1], post[below, 0]
        to_near[n] = jnp.where(even, above, below)
        to_next[n] = jnp.where(even, below, above)


def turned(tile, step):
    return tile if step == 0 else pltpu.roll(tile, step % tile.shape[1], 1)


def edge_kernel(layers, face_r, face_l, near, to_a, to_b, out_r, out_l):
    out_r[...] = face_r[...]
    out_l[...] = face_l[...]
    across = near.shape[1]
    even = on_even()
    for out, lists, edge, inside in (
        (out_r, (STILL, RIGHT), across - 1, across - 2),
        (out_l, (STILL, LEFT), 0, 1),
    ):
        rows = [(i, edge) for i in lists[0]] + [(i, inside) for i in lists[1]]
        rows = rows + [(i, edge) for i in lists[1]]
        for n, (i, column) in enumerate(rows):
            rise = VELOCITY[i][2]
            if rise == 0:
                continue
            moved = range(layers - 1, 0, -1) if rise == 1 else range(layers - 1)
            for z in moved:
                at, source = n * layers + z, n * layers + z - rise
                out[at : at + 1, :] = out[source : source + 1, :]
            z = 0 if rise == 1 else layers - 1
            at = n * layers + z
            k = (UP if rise == 1 else DOWN).index(i)
            share = near[k, column : column + 1, :]
            out[at : at + 1, :] = jnp.where(even == (rise == 1), 0.0, share)
    band_even = on_even("grp")

    def both(n):
        at = slice(n * layers, (n + 1) * layers)
        return jnp.concatenate([out_r[at, :], out_l[at, :]], axis=0)

    def send(n, tile):
        at = slice(n * layers, (n + 1) * layers)
        right, left = tile[0:layers], tile[layers : 2 * layers]
        to_a[at, :] = jnp.where(band_even, right, left)
        to_b[at, :] = jnp.where(band_even, left, right)

    sums = [[] for _ in range(SUMS)]
    for n, i in enumerate(STILL):
        _, ey, ez = VELOCITY[i]
        tile = turned(both(n), ey)
        if i >= FLOWS:
            sums[3].append((1, tile))
        else:
            sums[0].append((1, tile))
            sums[1].append((ey, tile))
            sums[2].append((ez, tile))
    for n in range(SUMS):
        send(n, signed_sum(sums[n]))
    for n, i in enumerate(RIGHT):
        send(SUMS + n, turned(both(len(STILL) + n), VELOCITY[i][1]))
    for n in range(len(STILL) + len(RIGHT), GATHERED):
        send(n - len(STILL) + SUMS, both(n))


def corner_kernel(next_, to_a, to_b):
    across = next_.shape[1]
    up, right, left, ahead, behind = (
        place_of(UP, ex, ey, 1) for ex, ey in ((0, 0), (1, 0), (-1, 0), (0, 1), (0, -1))
    )
    warm = len(UP) - 1
    sides = []
    for column, inside, outward in ((across - 1, across - 2, right), (0, 1, left)):

        def row(n, at):
            return next_[n, at : at + 1, :]

        one, two = turned(row(ahead, column), 1), turned(row(behind, column), -1)
        rows = [
            row(up, column) + (one + two),
            one - two,
            row(warm, column),
            row(outward, inside),
            row(outward, column),
        ]
        rows.append(jnp.zeros((CORNER_ROWS - len(rows), next_.shape[2]), f32))
        sides.append(jnp.concatenate(rows, axis=0))
    band_even = on_even("grp")
    to_a[...] = jnp.where(band_even, sides[0], sides[1])
    to_b[...] = jnp.where(band_even, sides[1], sides[0])


def add_corners(face, corner, layers, even, whole):
    edge = SUMS + len(RIGHT)
    for here, z, rise in ((even, 0, 1), (jnp.logical_not(even), layers - 1, -1)):
        k = place_of(RIGHT, 1, 0, rise)
        adds = [(edge + k, 1, 4)]
        if whole:
            adds += [(0, 1, 0), (1, 1, 1), (2, rise, 0), (3, 1, 2), (SUMS + k, 1, 3)]
        for n, sign, row in adds:
            at = n * layers + z
            share = jnp.where(here, corner[row : row + 1], 0.0)
            face[at : at + 1, :] = face[at : at + 1, :] + (share if sign > 0 else -share)


def second_kernel(
    post,
    near,
    next_,
    to_a,
    to_b,
    faces_a,
    faces_b,
    corner_a,
    corner_b,
    corners_a,
    corners_b,
    solid,
    own_table,
    tie,
    hot,
    motion,
    send_near,
    send_next,
    fluxes,
    moved,
    halo,
    own_r,
    own_l,
    from_l,
    from_r,
):
    layers, across, along = solid.shape
    even = on_even()
    band_even = on_even("grp")
    own_r[...] = jnp.where(band_even, to_a[...], to_b[...])
    own_l[...] = jnp.where(band_even, to_b[...], to_a[...])
    below = [jnp.where(even, next_[n], near[n]) for n in range(len(UP) + 1)]
    above = [jnp.where(even, near[n], next_[n]) for n in range(len(UP) + 1)]
    from_l[...] = jnp.where(band_even, faces_b[...], faces_a[...])
    from_r[...] = jnp.where(band_even, faces_a[...], faces_b[...])
    for face, one, two, whole in (
        (own_r, corner_a, corner_b, False),
        (own_l, corner_b, corner_a, False),
        (from_l, corners_b, corners_a, True),
        (from_r, corners_a, corners_b, True),
    ):
        corner = jnp.where(band_even, one[...], two[...])
        add_corners(face, corner, layers, even, whole)
    slot = lax.broadcasted_iota(jnp.int32, (across, along), 0)
    edge = SUMS + len(RIGHT)
    for i in LANES_ALL:
        ex, ey, ez = VELOCITY[i]
        for z in range(layers):
            if z - ez < 0:
                tile = below[UP.index(i)]
            elif z - ez >= layers:
                tile = above[DOWN.index(i)]
            else:
                tile = post[i, z - ez]
            if ex == 1:
                at = (edge + RIGHT.index(i)) * layers + z
                tile = jnp.where(slot == 0, from_l[at : at + 1, :], pltpu.roll(tile, 1, 0))
            elif ex == -1:
                at = (edge + LEFT.index(i)) * layers + z
                tile = jnp.where(
                    slot == across - 1, from_r[at : at + 1, :], pltpu.roll(tile, across - 1, 0)
                )
            moved[i, z] = turned(tile, ey)

    def halves(low, high, n):
        at = slice(n * layers, (n + 1) * layers)
        parts = [low[at, :], high[at, :]]
        if 2 * layers < 8:
            parts.append(jnp.ones((8 - 2 * layers, along), f32))
        return jnp.concatenate(parts, axis=0)

    for n in range(edge):
        halo[n] = halves(from_l, from_r, n)
    for n, i in enumerate(RIGHT):
        halo[edge + n] = turned(halves(own_l, own_r, edge + n), VELOCITY[i][1])
    edge_solid = halves(from_l, from_r, FACE - 1)
    for start in range(0, along, WIDTH):
        lanes = slice(start, start + WIDTH)
        for z in range(layers):
            out = collide(
                [moved[i, z, :, lanes] for i in range(FLOWS)],
                [moved[FLOWS + j, z, :, lanes] for j in range(HEATS)],
                solid[z, :, lanes],
            )
            for i in LANES_ALL:
                moved[i, z, :, lanes] = out[i]
        out = collide_halo(
            [halo[n, :, lanes] for n in range(SUMS)],
            [halo[SUMS + n, :, lanes] for n in range(len(RIGHT))],
            [halo[edge + n, :, lanes] for n in range(len(RIGHT))],
            edge_solid[:, lanes],
        )
        for n in range(len(RIGHT)):
            halo[SUMS + n, :, lanes] = out[n]
    sums = {}

    def add(key, sign, tile):
        if sign == 0:
            return
        if key in sums:
            sums[key] = sums[key] + tile if sign > 0 else sums[key] - tile
        else:
            sums[key] = tile if sign > 0 else -tile

    for z in range(layers):
        for i in LANES_ALL:
            ex, ey, ez = VELOCITY[i]
            if i == 0:
                continue
            tile = moved[i, z]
            if ex == 1:
                side = halo[SUMS + RIGHT.index(i), z : z + 1, :]
                tile = jnp.where(slot == 0, side, pltpu.roll(tile, 1, 0))
            elif ex == -1:
                at = layers + z
                side = halo[SUMS + LEFT.index(i), at : at + 1, :]
                tile = jnp.where(slot == across - 1, side, pltpu.roll(tile, across - 1, 0))
            tile = turned(tile, ey)
            target = z + ez
            if i >= FLOWS:
                add((3, target), 1, tile)
            else:
                add((0, target), ex, tile)
                add((1, target), ey, tile)
                add((2, target), ez, tile)
    for z in range(layers):
        hot[z] = sums[3, z]
        for axis in range(3):
            motion[axis, z] = sums[axis, z]
    for part in range(4):
        send_near[part] = jnp.where(even, sums[part, layers], sums[part, -1])
        send_next[part] = jnp.where(even, sums[part, -1], sums[part, layers])
    extra = len(UP)
    per_line = along // WIDTH
    per_layer = across * per_line

    def flux(table, planes):
        index = table[:, 0:WIDTH].astype(jnp.int32)
        place, lane = index >> 7, index & 127
        out = jnp.zeros(lane.shape, f32)
        for z, plane in planes:
            for x in range(across):
                for c in range(per_line):
                    row = plane[x : x + 1, c * WIDTH : (c + 1) * WIDTH]
                    out = jnp.where(
                        place == z * per_layer + x * per_line + c, lane_gather(row, lane), out
                    )
        return out * table[:, WIDTH : 2 * WIDTH]

    mine = own_table[extra]
    fluxes[plane_rows(0), :] = flux(mine, [(z, sums[3, z]) for z in range(layers)])
    fluxes[plane_rows(1), :] = flux(above[extra], [(0, sums[3, layers])])
    fluxes[plane_rows(2), :] = flux(below[extra], [(layers - 1, sums[3, -1])])
    fluxes[plane_rows(3), :] = mine[:, WIDTH : 2 * WIDTH]


def sublane_gather(value, index):
    return jnp.take_along_axis(value, index, axis=0, mode="promise_in_bounds")


def coupled(vector, blocks, flipped, shift):
    count = vector.shape[0]
    upright = vector.T
    ahead, back = [], []
    for b in range(count):
        column = jnp.broadcast_to(upright[:, b : b + 1], blocks.shape[1:])
        back.append(jnp.sum(blocks[b] * column, axis=0, keepdims=True))
        ahead.append(jnp.sum(flipped[b] * column, axis=0, keepdims=True))
    ahead = jnp.concatenate(ahead, axis=0)
    back = jnp.concatenate(back, axis=0)
    block = lax.broadcasted_iota(jnp.int32, vector.shape, 0)
    ahead = sublane_gather(ahead, (block + shift) & (count - 1))
    return ahead + sublane_gather(back, (block - shift) & (count - 1))


def ready_kernel(
    pattern, nodes, diagonal, source, start, coupling, tie, hits, flipped, rest, slots, turn
):
    shift = pattern[0, 0]
    turn[...] = jnp.full(turn.shape, shift, jnp.int32)
    count = start.shape[1]
    for b in range(count):
        flipped[lax.rem(b + shift, count)] = coupling[0, b].T
    vector = start[0]
    rest[...] = (
        source[0] - diagonal[0] * vector + coupled(vector, coupling.at[0], flipped, turn[...])
    )
    index = stacked(nodes[...])
    slots[...] = table_gather(vector, index)
    upright = (index & 127).astype(f32).T.astype(jnp.int32)
    lane = lax.broadcasted_iota(jnp.int32, (WIDTH, WIDTH), 1)
    for s in range(index.shape[0]):
        hit = jnp.where(upright[:, s : s + 1] == lane, 1.0, 0.0)
        hits[s * WIDTH : (s + 1) * WIDTH] = hit.astype(bf16)


def solve_kernel(
    cap,
    turn,
    nodes,
    diagonal,
    start,
    coupling,
    hits,
    flipped,
    rest,
    slots,
    come,
    res,
    img,
    go,
):
    shift = turn[...]
    count = start.shape[1]
    index = stacked(nodes[...])
    place = index >> 7
    own, low, high, coeff = (come[plane_rows(plane), :] for plane in range(4))
    if cap == WIDTH:
        low = pltpu.roll(low, 1, 0)
        high = pltpu.roll(high, low.shape[0] - 1, 0)
    parts = three_parts(own + low + high) + three_parts(coeff)
    block = lax.broadcasted_iota(jnp.int32, (count, WIDTH), 0)
    values = []
    for s in range(index.shape[0]):
        mine = block == place[s : s + 1]
        values.append(
            jnp.concatenate([jnp.where(mine, part[s : s + 1], 0.0) for part in parts], axis=0)
        )
    values = jnp.concatenate(values, axis=1).astype(bf16)
    landed = jnp.dot(values, hits[...], preferred_element_type=f32)
    landed = [landed[k * count : (k + 1) * count] for k in range(len(parts))]
    added = (landed[0] + landed[1]) + landed[2]
    extra = (landed[3] + landed[4]) + landed[5]
    whole = diagonal[0] + extra
    blocks = coupling.at[0]
    residual = rest[...] + added - extra * start[0]
    image = whole * residual - coupled(residual, blocks, flipped, shift)

    def total(value):
        return jnp.sum(jnp.sum(value, axis=0, keepdims=True), axis=1, keepdims=True)

    offset = image - SHIFT * residual
    bend = whole * offset - coupled(offset, blocks, flipped, shift)
    totals = [
        total(residual * residual),
        total(residual * offset),
        total(offset * offset),
        total(offset * bend),
    ]
    res[...] = residual
    img[...] = image
    lane = lax.broadcasted_iota(jnp.int32, (8, WIDTH), 1) & (cap - 1)
    facts = jnp.zeros((8, WIDTH), f32)
    for n, fact in enumerate(totals):
        facts = jnp.where(lane == n, fact, facts)
    residual_slots = table_gather(residual, index)
    image_slots = table_gather(image, index)
    start_slots = slots[...]
    for group in range(0, go.shape[0] // 4, 8):
        go[plane_rows(0, group), :] = start_slots
        go[plane_rows(1, group), :] = residual_slots
        go[plane_rows(2, group), :] = image_slots
        go[plane_rows(3, group), :] = facts


def last_kernel(direct, come, own, start, res, img, ordinal, temp, seen):
    places = stacked(ordinal[...])
    chunks = places.shape[0]
    if chunks < 8:
        places = jnp.concatenate([places, jnp.zeros((8 - chunks, WIDTH), jnp.int32)], axis=0)
    found = []
    for plane in range(3):
        if direct:
            table = come[plane_rows(plane, lax.axis_index("grp") * 8), :]
        else:
            table = own[plane_rows(plane), :]
        found.append(table_gather(table, places))
    facts = come[plane_rows(3, 0, come.shape[0] // 4), :]
    facts = jnp.sum(facts, axis=0, keepdims=True)
    all_norm, cross, square, energy = (
        lane_gather(facts, jnp.full((8, WIDTH), n, jnp.int32)) for n in range(4)
    )
    product = SHIFT * all_norm + cross
    inverse = 1.0 / product
    ratio = cross / all_norm
    spread_square = square - cross * ratio
    energy = energy - ratio * (2.0 * (square + SHIFT * cross) - ratio * product)
    small = spread_square * inverse
    first = all_norm * inverse
    step = spread_square / (energy - spread_square * small)
    of_residual = first + step * (1.0 + small * first)
    of_image = -step * first
    temp[0] = start[0] + of_residual * res[...] + of_image * img[...]
    found = found[0] + of_residual * found[1] + of_image * found[2]
    for c in range(chunks):
        seen[:, c * WIDTH : (c + 1) * WIDTH] = found[c : c + 1]


def join_kernel(hot, motion, near, next_, hot_out, motion_out):
    layers = hot.shape[0]
    even = on_even()
    below = [jnp.where(even, next_[n], near[n]) for n in range(4)]
    above = [jnp.where(even, near[n], next_[n]) for n in range(4)]
    for z in range(layers):
        for part in range(4):
            tile = hot[z] if part == 3 else motion[part, z]
            if z == 0:
                tile = tile + below[part]
            if z == layers - 1:
                tile = tile + above[part]
            if part == 3:
                hot_out[z] = tile
            else:
                motion_out[part, z] = tile


VMEM = pl.BlockSpec(memory_space=pltpu.VMEM)
ANYWHERE = pl.BlockSpec(memory_space=pl.ANY)
SMEM = pl.BlockSpec(memory_space=pltpu.SMEM)


def call(kernel, out, args, name, scalars=(), scratch=(), far=False):
    total = sum(int(np.prod(a.shape)) * a.dtype.itemsize for a in list(args) + list(out))
    if far:
        args = [pltpu.with_memory_space_constraint(a, pltpu.HBM) for a in args]
    return pl.pallas_call(
        kernel,
        out_shape=out,
        in_specs=[
            ANYWHERE if far else SMEM if n in scalars else VMEM for n in range(len(args))
        ],
        out_specs=[VMEM] * len(out),
        scratch_shapes=scratch,
        compiler_params=pltpu.CompilerParams(vmem_limit_bytes=24 << 20),
        cost_estimate=pl.CostEstimate(flops=1 << 20, bytes_accessed=total, transcendentals=0),
        name=name,
    )(*args)


def shape(*dims, dtype=f32):
    return jax.ShapeDtypeStruct(dims, dtype)


def swaps(axis):
    count = lax.axis_size(axis)
    assert count % 2 == 0
    near = [(k, k + 1 - 2 * (k % 2)) for k in range(count)]
    return near, [(k, (k - 1 + 2 * (k % 2)) % count) for k in range(count)]


def body(
    populations,
    heat_pops,
    solid_frac,
    coupled_grid_point,
    dest_index,
    heat_coeff,
    slot_node,
    node_diag,
    coupling,
    block_pattern,
    heat_source,
    solid_start,
):
    layers, across, along = solid_frac.shape
    slabs, bands = lax.axis_size("sub"), lax.axis_size("grp")
    slots = slot_node.shape[1]
    cap = slots // slabs
    rows = coupled_grid_point.shape[1]
    blocks, piece = node_diag.shape[1:]
    lines = slots // WIDTH
    assert lines == 8 and across == 8 and along >= 2 * WIDTH and along % WIDTH == 0
    assert piece == WIDTH and blocks == 8 and WIDTH % cap == 0 and cap >= 8
    assert rows % WIDTH == 0 and rows <= 8 * WIDTH and layers <= 4
    gathered_rows = -(-GATHERED * layers // 8) * 8
    face_rows = -(-FACE * layers // 8) * 8
    planes = len(UP) + 1
    post, to_near, to_next, face_r, face_l, ordinal = call(
        functools.partial(first_kernel, cap),
        [
            shape(FLOWS + HEATS, layers, across, along),
            shape(planes, across, along),
            shape(planes, across, along),
            shape(gathered_rows, along),
            shape(gathered_rows, along),
            shape(1, rows, dtype=jnp.int32),
        ],
        [
            populations,
            heat_pops,
            solid_frac,
            coupled_grid_point,
            dest_index.reshape(1, rows),
            heat_coeff,
        ],
        "collide_first",
        scratch=[
            pltpu.VMEM(solid_like, kind)
            for solid_like, kind in (
                (populations.shape, f32),
                (heat_pops.shape, f32),
                (solid_frac.shape, f32),
                ((1, rows), jnp.int32),
                ((1, rows), jnp.int32),
                ((1, rows), f32),
            )
        ]
        + [pltpu.SemaphoreType.DMA((3 + 3 * layers,))],
        far=True,
    )
    near_pairs, next_pairs = swaps("sub")
    near = lax.ppermute(to_near, "sub", near_pairs)
    next_ = lax.ppermute(to_next, "sub", next_pairs)
    to_a, to_b = call(
        functools.partial(edge_kernel, layers),
        [shape(face_rows, along)] * 2,
        [face_r, face_l, near],
        "x_faces",
        scratch=[pltpu.VMEM((gathered_rows, along), f32)] * 2,
    )
    side_a, side_b = swaps("grp")
    faces_a = lax.ppermute(to_a, "grp", side_a)
    faces_b = lax.ppermute(to_b, "grp", side_b)
    corner_a, corner_b = call(
        corner_kernel,
        [shape(CORNER_ROWS, along)] * 2,
        [next_],
        "x_corners",
    )
    corners_a = lax.ppermute(corner_a, "grp", side_a)
    corners_b = lax.ppermute(corner_b, "grp", side_b)
    hits, flipped, rest, start_slots, turn = call(
        ready_kernel,
        [
            shape(slots, WIDTH, dtype=bf16),
            shape(blocks, piece, piece),
            shape(blocks, piece),
            shape(lines, WIDTH),
            shape(blocks, WIDTH, dtype=jnp.int32),
        ],
        [block_pattern, slot_node, node_diag, heat_source, solid_start, coupling, corner_a],
        "solid_ready",
        scalars=(0,),
    )
    hot, motion, send_near, send_next, fluxes = call(
        second_kernel,
        [
            shape(layers, across, along),
            shape(3, layers, across, along),
            shape(4, across, along),
            shape(4, across, along),
            shape(4 * lines, WIDTH),
        ],
        [
            post,
            near,
            next_,
            to_a,
            to_b,
            faces_a,
            faces_b,
            corner_a,
            corner_b,
            corners_a,
            corners_b,
            solid_frac,
            to_near,
            rest,
        ],
        "collide_second",
        scratch=[
            pltpu.VMEM((FLOWS + HEATS, layers, across, along), f32),
            pltpu.VMEM((FACE - 1, 8, along), f32),
        ]
        + [pltpu.VMEM((face_rows, along), f32)] * 4,
    )
    settled = cap != WIDTH
    if settled:
        fluxes = fluxes.reshape(lines, 4, WIDTH // cap, cap).transpose(0, 2, 1, 3)
    fluxes = fluxes.reshape(slabs, 4, cap)
    landed = lax.all_to_all(fluxes, "sub", split_axis=0, concat_axis=0, tiled=True)
    if settled:
        landed = jnp.stack(
            [
                landed[:, 0],
                jnp.roll(landed[:, 1], 1, axis=0),
                jnp.roll(landed[:, 2], -1, axis=0),
                landed[:, 3],
            ]
        )
        landed = landed.reshape(4, lines, WIDTH).transpose(1, 0, 2)
    landed = landed.reshape(4 * lines, WIDTH)
    from_near = lax.ppermute(send_near, "sub", near_pairs)
    from_next = lax.ppermute(send_next, "sub", next_pairs)
    residual, image, go = call(
        functools.partial(solve_kernel, cap),
        [shape(blocks, piece), shape(blocks, piece), shape(bands * lines * 4, WIDTH)],
        [
            turn,
            slot_node,
            node_diag,
            solid_start,
            coupling,
            hits,
            flipped,
            rest,
            start_slots,
            landed,
        ],
        "solve",
    )
    if settled:
        go = go.reshape(bands, lines, 4, WIDTH // cap, cap).transpose(0, 1, 3, 2, 4)
    go = go.reshape(bands * slabs, 4, cap)
    come = lax.all_to_all(go, ("grp", "sub"), split_axis=0, concat_axis=0, tiled=True)
    hot_out, motion_out = call(
        join_kernel,
        [shape(*hot.shape), shape(*motion.shape)],
        [hot, motion, from_near, from_next],
        "join",
    )
    if settled:
        own = lax.dynamic_slice_in_dim(come, lax.axis_index("grp") * slabs, slabs, 0)
        own = own.transpose(1, 0, 2).reshape(4, lines, WIDTH).transpose(1, 0, 2)
        own = own.reshape(4 * lines, WIDTH)
        come = jnp.pad(come, ((0, 0), (0, 0), (0, WIDTH - cap)))
    else:
        own = rest
    come = come.reshape(4 * bands * slabs, WIDTH)
    temp, seen = call(
        functools.partial(last_kernel, not settled),
        [shape(1, blocks, piece), shape(1, rows)],
        [
            come,
            own,
            solid_start,
            residual,
            image,
            ordinal,
        ],
        "finish",
    )
    return hot_out, motion_out, temp, seen


def solution(mesh):
    placed = (
        P(None, "sub", "grp", None),
        P(None, "sub", "grp", None),
        P("sub", "grp", None),
        P("grp", "sub"),
        P("grp", "sub", None),
        P("grp", "sub"),
        P("grp", "sub"),
        P("grp", "sub", None),
        P("grp", "sub", None, None),
        P("grp", "sub"),
        P("grp", "sub", None),
        P("grp", "sub", None),
    )
    return jax.shard_map(
        body,
        mesh=mesh,
        in_specs=placed,
        out_specs=(
            P("sub", "grp", None),
            P(None, "sub", "grp", None),
            P("grp", "sub", None),
            P("grp", "sub"),
        ),
        check_vma=False,
    )
```

```python
import functools
import jax
import jax.numpy as jnp
import numpy as np
from jax import lax
from jax.experimental import pallas as pl
from jax.experimental.pallas import tpu as pltpu
from jax.sharding import PartitionSpec as P

FLOW_VELOCITY = [
    (0, 0, 0),
    (1, 0, 0),
    (-1, 0, 0),
    (0, 1, 0),
    (0, -1, 0),
    (0, 0, 1),
    (0, 0, -1),
    (1, 1, 0),
    (-1, -1, 0),
    (1, -1, 0),
    (-1, 1, 0),
    (1, 0, 1),
    (-1, 0, -1),
    (1, 0, -1),
    (-1, 0, 1),
    (0, 1, 1),
    (0, -1, -1),
    (0, 1, -1),
    (0, -1, 1),
]
VELOCITY = FLOW_VELOCITY + FLOW_VELOCITY[:7]
FLOWS, HEATS = 19, 7
LANES_ALL = range(FLOWS + HEATS)
UP = [i for i in LANES_ALL if VELOCITY[i][2] == 1]
DOWN = [
    next(j for j in LANES_ALL if VELOCITY[j] == VELOCITY[i][:2] + (-1,) and (j < 19) == (i < 19))
    for i in UP
]
RIGHT = [i for i in LANES_ALL if VELOCITY[i][0] == 1]
LEFT = [
    next(j for j in LANES_ALL if VELOCITY[j] == (-1,) + VELOCITY[i][1:] and (j < 19) == (i < 19))
    for i in RIGHT
]
TURNED = [
    next(n for n, j in enumerate(RIGHT[:-1]) if VELOCITY[j][1:] == (-VELOCITY[i][1], -VELOCITY[i][2]))
    for i in RIGHT[:-1]
]
STILL = [i for i in LANES_ALL if VELOCITY[i][0] == 0]
GATHERED = len(STILL) + 2 * len(RIGHT)
SUMS = 4
FACE = SUMS + 2 * len(RIGHT)
CORNER = 5


def place_of(lists, ex, ey, ez):
    return next(n for n, i in enumerate(lists) if VELOCITY[i] == (ex, ey, ez))


WIDTH = 128
SHIFT = 4.0
f32 = jnp.float32
bf16 = jnp.bfloat16


def signed_sum(terms):
    total = None
    for sign, term in terms:
        if sign == 0:
            continue
        if total is None:
            total = term if sign > 0 else -term
        else:
            total = total + term if sign > 0 else total - term
    return total


def collide(flow, heat, solid):
    pairs = range(1, FLOWS, 2)
    density = flow[0]
    for i in pairs:
        density = density + (flow[i] + flow[i + 1])
    gaps = {i: flow[i] - flow[i + 1] for i in pairs}
    scale = 1.0 / density
    speed = [
        signed_sum([(FLOW_VELOCITY[i][axis], gaps[i]) for i in pairs]) * scale for axis in range(3)
    ]
    square = speed[0] * speed[0] + speed[1] * speed[1] + speed[2] * speed[2]
    base = 1.0 - 1.5 * square
    gas = 1.0 - solid
    keep = gas * (1.0 - 1.0 / 0.8)
    pull = gas * (density * (1.0 / 0.8))
    flow_post = [None] * FLOWS
    flow_post[0] = (keep + solid) * flow[0] + (pull * (1.0 / 3.0)) * base
    shares = {1: pull * (1.0 / 18.0), 2: pull * (1.0 / 36.0)}
    for i in pairs:
        share = shares[sum(abs(c) for c in FLOW_VELOCITY[i])]
        along = signed_sum([(FLOW_VELOCITY[i][axis], speed[axis]) for axis in range(3)])
        even = base + 4.5 * along * along
        odd = 3.0 * along
        flow_post[i] = keep * flow[i] + share * (even + odd) + solid * flow[i + 1]
        flow_post[i + 1] = keep * flow[i + 1] + share * (even - odd) + solid * flow[i]
    hotness = heat[0]
    for j in range(1, HEATS):
        hotness = hotness + heat[j]
    stay = 1.0 - 1.0 / 0.7
    heat_post = [stay * heat[0] + (0.25 / 0.7) * hotness]
    level = (0.125 / 0.7) * hotness
    for j in range(1, HEATS, 2):
        axis = (j - 1) // 2
        drift = 4.0 * speed[axis]
        heat_post.append(stay * heat[j] + level * (1.0 + drift))
        heat_post.append(stay * heat[j + 1] + level * (1.0 - drift))
    return flow_post + heat_post


def collide_halo(still, inward, outward, solid):
    flows = RIGHT[:-1]
    density, along_y, along_z, hotness = still
    pairs = [(a + b, a - b) for a, b in zip(inward, outward)]
    across = None
    for n, i in enumerate(flows):
        _, ey, ez = VELOCITY[i]
        whole, gap = pairs[n]
        density = density + whole
        across = gap if across is None else across + gap
        along_y = signed_sum([(1, along_y), (ey, whole)])
        along_z = signed_sum([(1, along_z), (ez, whole)])
    hotness = hotness + pairs[-1][0]
    scale = 1.0 / density
    speed = [across * scale, along_y * scale, along_z * scale]
    square = speed[0] * speed[0] + speed[1] * speed[1] + speed[2] * speed[2]
    base = 1.0 - 1.5 * square
    gas = 1.0 - solid
    keep = gas * (1.0 - 1.0 / 0.8)
    pull = gas * (density * (1.0 / 0.8))
    shares = {1: pull * (1.0 / 18.0), 2: pull * (1.0 / 36.0)}
    out = []
    for n, i in enumerate(flows):
        share = shares[sum(abs(c) for c in VELOCITY[i])]
        along = signed_sum([(VELOCITY[i][axis], speed[axis]) for axis in range(3)])
        feq = share * (base + 4.5 * along * along + 3.0 * along)
        out.append(keep * inward[n] + feq + solid * outward[TURNED[n]])
    level = (0.125 / 0.7) * hotness
    out.append((1.0 - 1.0 / 0.7) * inward[-1] + level * (1.0 + 4.0 * speed[0]))
    return out


def three_parts(value):
    high = value.astype(bf16).astype(f32)
    rest = value - high
    middle = rest.astype(bf16).astype(f32)
    return [high, middle, rest - middle]


def times_transposed(left, right):
    return lax.dot_general(
        left.astype(bf16), right.astype(bf16), (((1,), (1,)), ((), ())), preferred_element_type=f32
    )


def spread(row):
    return jnp.broadcast_to(row, (8, row.shape[-1]))


def lane_gather(row, lane):
    return jnp.take_along_axis(spread(row), lane, axis=1, mode="promise_in_bounds")


def table_gather(table, index):
    place, lane = index >> 7, index & 127
    out = jnp.zeros(index.shape, f32)
    for row in range(table.shape[0]):
        out = jnp.where(place == row, lane_gather(table[row : row + 1], lane), out)
    return out


def plane_rows(plane, first=0, count=8):
    return pl.ds(4 * first + plane, count, stride=4)


def stacked(row):
    return jnp.concatenate(
        [row[:, k * WIDTH : (k + 1) * WIDTH] for k in range(row.shape[1] // WIDTH)], axis=0
    )


def slot_tables(cap, voxel, dest, coeff, ordinal):
    rows_here = dest.shape[1]
    owner = dest[...].astype(f32)
    chunks = rows_here // WIDTH
    tall = stacked(owner)
    tall = jnp.concatenate([tall] + [jnp.zeros((8 - chunks, WIDTH), f32)] * (chunks < 8), axis=0)
    upright = tall.T
    first = lax.broadcasted_iota(jnp.int32, (WIDTH, WIDTH), 0)
    second = lax.broadcasted_iota(jnp.int32, (WIDTH, WIDTH), 1)
    slot_row = lax.broadcasted_iota(jnp.int32, (8, WIDTH), 0)
    table = jnp.zeros((40, WIDTH), f32)
    for c in range(chunks):
        lanes = slice(c * WIDTH, (c + 1) * WIDTH)
        here = owner[:, lanes]
        count = jnp.zeros((WIDTH, WIDTH), f32)
        for other in range(c + 1):
            same = upright[:, other : other + 1] == here
            if other == c:
                same = same & (first < second)
            count = count + jnp.where(same, 1.0, 0.0)
        rank = jnp.sum(count, axis=0, keepdims=True)
        place = (here * float(cap) + rank).astype(jnp.int32)
        ordinal[:, lanes] = place
        mine = slot_row == (place >> 7)
        spot = voxel[:, lanes]
        parts = [(spot >> 7).astype(f32), (spot & 127).astype(f32)] + three_parts(coeff[:, lanes])
        values = jnp.concatenate([jnp.where(mine, part, 0.0) for part in parts], axis=0)
        table = table + times_transposed(values, jnp.where(first == (place & 127), 1.0, 0.0))
    spots = table[0:8] * float(WIDTH) + table[8:16]
    coeffs = (table[16:24] + table[24:32]) + table[32:40]
    return spots, coeffs


def on_even(axis="sub"):
    return lax.rem(lax.axis_index(axis), 2) == 0


def first_kernel(cap, *refs):
    given, (post, to_near, to_next, face_r, face_l, ordinal) = refs[:6], refs[6:12]
    held, arrived = refs[12:18], refs[18]
    pops, heat, solid, voxel, dest, coeff = held
    pieces = [(given[n], held[n]) for n in (4, 3, 5)]
    for z in range(solid.shape[0]):
        pieces += [(given[n].at[:, z], held[n].at[:, z]) for n in (0, 1)]
        pieces.append((given[2].at[z], held[2].at[z]))
    copies = [
        pltpu.make_async_copy(source, target, arrived.at[n])
        for n, (source, target) in enumerate(pieces)
    ]
    for copy in copies:
        copy.start()
    layers, across, along = solid.shape
    even = on_even()
    for copy in copies[:3]:
        copy.wait()
    spots, coeffs = slot_tables(cap, voxel, dest, coeff, ordinal)
    extra = len(UP)
    for plane in (to_near, to_next):
        plane[extra] = jnp.zeros(plane.shape[1:], f32)
        plane[extra, :, 0:WIDTH] = spots
        plane[extra, :, WIDTH : 2 * WIDTH] = coeffs
    for z in range(layers):
        for copy in copies[3 + 3 * z : 6 + 3 * z]:
            copy.wait()
        for start in range(0, along, WIDTH):
            lanes = slice(start, start + WIDTH)
            out = collide(
                [pops[i, z, :, lanes] for i in range(FLOWS)],
                [heat[j, z, :, lanes] for j in range(HEATS)],
                solid[z, :, lanes],
            )
            for i in LANES_ALL:
                post[i, z, :, lanes] = out[i]
            for face, lists, near, far in (
                (face_r, (STILL, RIGHT), across - 1, across - 2),
                (face_l, (STILL, LEFT), 0, 1),
            ):
                rows = [(i, near) for i in lists[0]] + [(i, far) for i in lists[1]]
                rows = rows + [(i, near) for i in lists[1]]
                for n, (i, column) in enumerate(rows):
                    at = n * layers + z
                    face[at : at + 1, lanes] = out[i][column : column + 1]
    for n, (above, below) in enumerate(zip(UP, DOWN)):
        above, below = post[above, layers - 1], post[below, 0]
        to_near[n] = jnp.where(even, above, below)
        to_next[n] = jnp.where(even, below, above)


def turned(tile, step):
    return tile if step == 0 else pltpu.roll(tile, step % tile.shape[1], 1)


def edge_kernel(layers, face_r, face_l, near, to_a, to_b, out_r, out_l):
    out_r[...] = face_r[...]
    out_l[...] = face_l[...]
    across = near.shape[1]
    even = on_even()
    for out, lists, edge, inside in (
        (out_r, (STILL, RIGHT), across - 1, across - 2),
        (out_l, (STILL, LEFT), 0, 1),
    ):
        rows = [(i, edge) for i in lists[0]] + [(i, inside) for i in lists[1]]
        rows = rows + [(i, edge) for i in lists[1]]
        for n, (i, column) in enumerate(rows):
            rise = VELOCITY[i][2]
            if rise == 0:
                continue
            moved = range(layers - 1, 0, -1) if rise == 1 else range(layers - 1)
            for z in moved:
                at, source = n * layers + z, n * layers + z - rise
                out[at : at + 1, :] = out[source : source + 1, :]
            z = 0 if rise == 1 else layers - 1
            at = n * layers + z
            k = (UP if rise == 1 else DOWN).index(i)
            share = near[k, column : column + 1, :]
            out[at : at + 1, :] = jnp.where(even == (rise == 1), 0.0, share)
    band_even = on_even("grp")

    def both(n):
        at = slice(n * layers, (n + 1) * layers)
        return jnp.concatenate([out_r[at, :], out_l[at, :]], axis=0)

    def send(n, tile):
        at = slice(n * layers, (n + 1) * layers)
        right, left = tile[0:layers], tile[layers : 2 * layers]
        to_a[at, :] = jnp.where(band_even, right, left)
        to_b[at, :] = jnp.where(band_even, left, right)

    sums = [[] for _ in range(SUMS)]
    for n, i in enumerate(STILL):
        _, ey, ez = VELOCITY[i]
        tile = turned(both(n), ey)
        if i >= FLOWS:
            sums[3].append((1, tile))
        else:
            sums[0].append((1, tile))
            sums[1].append((ey, tile))
            sums[2].append((ez, tile))
    for n in range(SUMS):
        send(n, signed_sum(sums[n]))
    for n, i in enumerate(RIGHT):
        send(SUMS + n, turned(both(len(STILL) + n), VELOCITY[i][1]))
    for n in range(len(STILL) + len(RIGHT), GATHERED):
        send(n - len(STILL) + SUMS, both(n))


def corner_kernel(next_, solid, to_a, to_b):
    across = next_.shape[1]
    up, right, left, ahead, behind = (
        place_of(UP, ex, ey, 1) for ex, ey in ((0, 0), (1, 0), (-1, 0), (0, 1), (0, -1))
    )
    warm = len(UP) - 1
    sides = []
    for column, inside, outward in ((across - 1, across - 2, right), (0, 1, left)):

        def row(n, at):
            return next_[n, at : at + 1, :]

        one, two = turned(row(ahead, column), 1), turned(row(behind, column), -1)
        rows = [
            row(up, column) + (one + two),
            one - two,
            row(warm, column),
            row(outward, inside),
            row(outward, column),
        ]
        rows += [solid[z, column : column + 1, :] for z in range(solid.shape[0])]
        if len(rows) < to_a.shape[0]:
            rows.append(jnp.zeros((to_a.shape[0] - len(rows), next_.shape[2]), f32))
        sides.append(jnp.concatenate(rows, axis=0))
    band_even = on_even("grp")
    to_a[...] = jnp.where(band_even, sides[0], sides[1])
    to_b[...] = jnp.where(band_even, sides[1], sides[0])


def add_corners(face, corner, layers, even, whole):
    edge = SUMS + len(RIGHT)
    for here, z, rise in ((even, 0, 1), (jnp.logical_not(even), layers - 1, -1)):
        k = place_of(RIGHT, 1, 0, rise)
        adds = [(edge + k, 1, 4)]
        if whole:
            adds += [(0, 1, 0), (1, 1, 1), (2, rise, 0), (3, 1, 2), (SUMS + k, 1, 3)]
        for n, sign, row in adds:
            at = n * layers + z
            share = jnp.where(here, corner[row : row + 1], 0.0)
            face[at : at + 1, :] = face[at : at + 1, :] + (share if sign > 0 else -share)


def second_kernel(
    post,
    near,
    next_,
    to_a,
    to_b,
    faces_a,
    faces_b,
    corner_a,
    corner_b,
    corners_a,
    corners_b,
    solid,
    own_table,
    tie,
    hot,
    motion,
    send_near,
    send_next,
    fluxes,
    moved,
    halo,
    own_r,
    own_l,
    from_l,
    from_r,
):
    layers, across, along = solid.shape
    even = on_even()
    band_even = on_even("grp")
    own_r[...] = jnp.where(band_even, to_a[...], to_b[...])
    own_l[...] = jnp.where(band_even, to_b[...], to_a[...])
    below = [jnp.where(even, next_[n], near[n]) for n in range(len(UP) + 1)]
    above = [jnp.where(even, near[n], next_[n]) for n in range(len(UP) + 1)]
    from_l[...] = jnp.where(band_even, faces_b[...], faces_a[...])
    from_r[...] = jnp.where(band_even, faces_a[...], faces_b[...])
    corners = []
    for face, one, two, whole in (
        (own_r, corner_a, corner_b, False),
        (own_l, corner_b, corner_a, False),
        (from_l, corners_b, corners_a, True),
        (from_r, corners_a, corners_b, True),
    ):
        corner = jnp.where(band_even, one[...], two[...])
        add_corners(face, corner, layers, even, whole)
        corners.append(corner)
    slot = lax.broadcasted_iota(jnp.int32, (across, along), 0)
    edge = SUMS + len(RIGHT)
    for i in LANES_ALL:
        ex, ey, ez = VELOCITY[i]
        for z in range(layers):
            if z - ez < 0:
                tile = below[UP.index(i)]
            elif z - ez >= layers:
                tile = above[DOWN.index(i)]
            else:
                tile = post[i, z - ez]
            if ex == 1:
                at = (edge + RIGHT.index(i)) * layers + z
                tile = jnp.where(slot == 0, from_l[at : at + 1, :], pltpu.roll(tile, 1, 0))
            elif ex == -1:
                at = (edge + LEFT.index(i)) * layers + z
                tile = jnp.where(
                    slot == across - 1, from_r[at : at + 1, :], pltpu.roll(tile, across - 1, 0)
                )
            moved[i, z] = turned(tile, ey)

    def halves(low, high, n):
        at = slice(n * layers, (n + 1) * layers)
        parts = [low[at, :], high[at, :]]
        if 2 * layers < 8:
            parts.append(jnp.ones((8 - 2 * layers, along), f32))
        return jnp.concatenate(parts, axis=0)

    for n in range(edge):
        halo[n] = halves(from_l, from_r, n)
    for n, i in enumerate(RIGHT):
        halo[edge + n] = turned(halves(own_l, own_r, edge + n), VELOCITY[i][1])
    edge_solid = [corner[CORNER : CORNER + layers] for corner in corners[2:]]
    if 2 * layers < 8:
        edge_solid.append(jnp.zeros((8 - 2 * layers, along), f32))
    edge_solid = jnp.concatenate(edge_solid, axis=0)
    for start in range(0, along, WIDTH):
        lanes = slice(start, start + WIDTH)
        for z in range(layers):
            out = collide(
                [moved[i, z, :, lanes] for i in range(FLOWS)],
                [moved[FLOWS + j, z, :, lanes] for j in range(HEATS)],
                solid[z, :, lanes],
            )
            for i in LANES_ALL:
                moved[i, z, :, lanes] = out[i]
        out = collide_halo(
            [halo[n, :, lanes] for n in range(SUMS)],
            [halo[SUMS + n, :, lanes] for n in range(len(RIGHT))],
            [halo[edge + n, :, lanes] for n in range(len(RIGHT))],
            edge_solid[:, lanes],
        )
        for n in range(len(RIGHT)):
            halo[SUMS + n, :, lanes] = out[n]
    sums = {}

    def add(key, sign, tile):
        if sign == 0:
            return
        if key in sums:
            sums[key] = sums[key] + tile if sign > 0 else sums[key] - tile
        else:
            sums[key] = tile if sign > 0 else -tile

    for z in range(layers):
        for i in LANES_ALL:
            ex, ey, ez = VELOCITY[i]
            if i == 0:
                continue
            tile = moved[i, z]
            if ex == 1:
                side = halo[SUMS + RIGHT.index(i), z : z + 1, :]
                tile = jnp.where(slot == 0, side, pltpu.roll(tile, 1, 0))
            elif ex == -1:
                at = layers + z
                side = halo[SUMS + LEFT.index(i), at : at + 1, :]
                tile = jnp.where(slot == across - 1, side, pltpu.roll(tile, across - 1, 0))
            tile = turned(tile, ey)
            target = z + ez
            if i >= FLOWS:
                add((3, target), 1, tile)
            else:
                add((0, target), ex, tile)
                add((1, target), ey, tile)
                add((2, target), ez, tile)
    for z in range(layers):
        hot[z] = sums[3, z]
        for axis in range(3):
            motion[axis, z] = sums[axis, z]
    for part in range(4):
        send_near[part] = jnp.where(even, sums[part, layers], sums[part, -1])
        send_next[part] = jnp.where(even, sums[part, -1], sums[part, layers])
    extra = len(UP)
    per_line = along // WIDTH
    per_layer = across * per_line

    def flux(table, planes):
        index = table[:, 0:WIDTH].astype(jnp.int32)
        place, lane = index >> 7, index & 127
        out = jnp.zeros(lane.shape, f32)
        for z, plane in planes:
            for x in range(across):
                for c in range(per_line):
                    row = plane[x : x + 1, c * WIDTH : (c + 1) * WIDTH]
                    out = jnp.where(
                        place == z * per_layer + x * per_line + c, lane_gather(row, lane), out
                    )
        return out * table[:, WIDTH : 2 * WIDTH]

    mine = own_table[extra]
    fluxes[plane_rows(0), :] = flux(mine, [(z, sums[3, z]) for z in range(layers)])
    fluxes[plane_rows(1), :] = flux(above[extra], [(0, sums[3, layers])])
    fluxes[plane_rows(2), :] = flux(below[extra], [(layers - 1, sums[3, -1])])
    fluxes[plane_rows(3), :] = mine[:, WIDTH : 2 * WIDTH]


def sublane_gather(value, index):
    return jnp.take_along_axis(value, index, axis=0, mode="promise_in_bounds")


def coupled(vector, blocks, flipped, shift):
    count = vector.shape[0]
    upright = vector.T
    ahead, back = [], []
    for b in range(count):
        column = jnp.broadcast_to(upright[:, b : b + 1], blocks.shape[1:])
        back.append(jnp.sum(blocks[b] * column, axis=0, keepdims=True))
        ahead.append(jnp.sum(flipped[b] * column, axis=0, keepdims=True))
    ahead = jnp.concatenate(ahead, axis=0)
    back = jnp.concatenate(back, axis=0)
    block = lax.broadcasted_iota(jnp.int32, vector.shape, 0)
    ahead = sublane_gather(ahead, (block + shift) & (count - 1))
    return ahead + sublane_gather(back, (block - shift) & (count - 1))


def ready_kernel(
    pattern, nodes, diagonal, source, start, coupling, tie, hits, flipped, rest, slots, turn
):
    shift = pattern[0, 0]
    turn[...] = jnp.full(turn.shape, shift, jnp.int32)
    count = start.shape[1]
    for b in range(count):
        flipped[lax.rem(b + shift, count)] = coupling[0, b].T
    vector = start[0]
    rest[...] = (
        source[0] - diagonal[0] * vector + coupled(vector, coupling.at[0], flipped, turn[...])
    )
    index = stacked(nodes[...])
    slots[...] = table_gather(vector, index)
    upright = (index & 127).astype(f32).T.astype(jnp.int32)
    lane = lax.broadcasted_iota(jnp.int32, (WIDTH, WIDTH), 1)
    for s in range(index.shape[0]):
        hit = jnp.where(upright[:, s : s + 1] == lane, 1.0, 0.0)
        hits[s * WIDTH : (s + 1) * WIDTH] = hit.astype(bf16)


def solve_kernel(
    cap,
    turn,
    nodes,
    diagonal,
    start,
    coupling,
    hits,
    flipped,
    rest,
    slots,
    come,
    res,
    img,
    go,
):
    shift = turn[...]
    count = start.shape[1]
    index = stacked(nodes[...])
    place = index >> 7
    own, low, high, coeff = (come[plane_rows(plane), :] for plane in range(4))
    if cap == WIDTH:
        low = pltpu.roll(low, 1, 0)
        high = pltpu.roll(high, low.shape[0] - 1, 0)
    parts = three_parts(own + low + high) + three_parts(coeff)
    block = lax.broadcasted_iota(jnp.int32, (count, WIDTH), 0)
    values = []
    for s in range(index.shape[0]):
        mine = block == place[s : s + 1]
        values.append(
            jnp.concatenate([jnp.where(mine, part[s : s + 1], 0.0) for part in parts], axis=0)
        )
    values = jnp.concatenate(values, axis=1).astype(bf16)
    landed = jnp.dot(values, hits[...], preferred_element_type=f32)
    landed = [landed[k * count : (k + 1) * count] for k in range(len(parts))]
    added = (landed[0] + landed[1]) + landed[2]
    extra = (landed[3] + landed[4]) + landed[5]
    whole = diagonal[0] + extra
    blocks = coupling.at[0]
    residual = rest[...] + added - extra * start[0]
    image = whole * residual - coupled(residual, blocks, flipped, shift)

    def total(value):
        return jnp.sum(jnp.sum(value, axis=0, keepdims=True), axis=1, keepdims=True)

    offset = image - SHIFT * residual
    bend = whole * offset - coupled(offset, blocks, flipped, shift)
    totals = [
        total(residual * residual),
        total(residual * offset),
        total(offset * offset),
        total(offset * bend),
    ]
    res[...] = residual
    img[...] = image
    lane = lax.broadcasted_iota(jnp.int32, (8, WIDTH), 1) & (cap - 1)
    facts = jnp.zeros((8, WIDTH), f32)
    for n, fact in enumerate(totals):
        facts = jnp.where(lane == n, fact, facts)
    residual_slots = table_gather(residual, index)
    image_slots = table_gather(image, index)
    start_slots = slots[...]
    for group in range(0, go.shape[0] // 4, 8):
        go[plane_rows(0, group), :] = start_slots
        go[plane_rows(1, group), :] = residual_slots
        go[plane_rows(2, group), :] = image_slots
        go[plane_rows(3, group), :] = facts


def last_kernel(direct, come, own, start, res, img, ordinal, temp, seen):
    places = stacked(ordinal[...])
    chunks = places.shape[0]
    if chunks < 8:
        places = jnp.concatenate([places, jnp.zeros((8 - chunks, WIDTH), jnp.int32)], axis=0)
    found = []
    for plane in range(3):
        if direct:
            table = come[plane_rows(plane, lax.axis_index("grp") * 8), :]
        else:
            table = own[plane_rows(plane), :]
        found.append(table_gather(table, places))
    facts = come[plane_rows(3, 0, come.shape[0] // 4), :]
    facts = jnp.sum(facts, axis=0, keepdims=True)
    all_norm, cross, square, energy = (
        lane_gather(facts, jnp.full((8, WIDTH), n, jnp.int32)) for n in range(4)
    )
    product = SHIFT * all_norm + cross
    inverse = 1.0 / product
    ratio = cross / all_norm
    spread_square = square - cross * ratio
    energy = energy - ratio * (2.0 * (square + SHIFT * cross) - ratio * product)
    small = spread_square * inverse
    first = all_norm * inverse
    step = spread_square / (energy - spread_square * small)
    of_residual = first + step * (1.0 + small * first)
    of_image = -step * first
    temp[0] = start[0] + of_residual * res[...] + of_image * img[...]
    found = found[0] + of_residual * found[1] + of_image * found[2]
    for c in range(chunks):
        seen[:, c * WIDTH : (c + 1) * WIDTH] = found[c : c + 1]


def join_kernel(hot, motion, near, next_, hot_out, motion_out):
    layers = hot.shape[0]
    even = on_even()
    below = [jnp.where(even, next_[n], near[n]) for n in range(4)]
    above = [jnp.where(even, near[n], next_[n]) for n in range(4)]
    for z in range(layers):
        for part in range(4):
            tile = hot[z] if part == 3 else motion[part, z]
            if z == 0:
                tile = tile + below[part]
            if z == layers - 1:
                tile = tile + above[part]
            if part == 3:
                hot_out[z] = tile
            else:
                motion_out[part, z] = tile


VMEM = pl.BlockSpec(memory_space=pltpu.VMEM)
ANYWHERE = pl.BlockSpec(memory_space=pl.ANY)
SMEM = pl.BlockSpec(memory_space=pltpu.SMEM)


def call(kernel, out, args, name, scalars=(), scratch=(), far=False):
    total = sum(int(np.prod(a.shape)) * a.dtype.itemsize for a in list(args) + list(out))
    if far:
        args = [pltpu.with_memory_space_constraint(a, pltpu.HBM) for a in args]
    return pl.pallas_call(
        kernel,
        out_shape=out,
        in_specs=[
            ANYWHERE if far else SMEM if n in scalars else VMEM for n in range(len(args))
        ],
        out_specs=[VMEM] * len(out),
        scratch_shapes=scratch,
        compiler_params=pltpu.CompilerParams(vmem_limit_bytes=24 << 20),
        cost_estimate=pl.CostEstimate(flops=1 << 20, bytes_accessed=total, transcendentals=0),
        name=name,
    )(*args)


def shape(*dims, dtype=f32):
    return jax.ShapeDtypeStruct(dims, dtype)


def swaps(axis):
    count = lax.axis_size(axis)
    assert count % 2 == 0
    near = [(k, k + 1 - 2 * (k % 2)) for k in range(count)]
    return near, [(k, (k - 1 + 2 * (k % 2)) % count) for k in range(count)]


def body(
    populations,
    heat_pops,
    solid_frac,
    coupled_grid_point,
    dest_index,
    heat_coeff,
    slot_node,
    node_diag,
    coupling,
    block_pattern,
    heat_source,
    solid_start,
):
    layers, across, along = solid_frac.shape
    slabs, bands = lax.axis_size("sub"), lax.axis_size("grp")
    slots = slot_node.shape[1]
    cap = slots // slabs
    rows = coupled_grid_point.shape[1]
    blocks, piece = node_diag.shape[1:]
    lines = slots // WIDTH
    assert lines == 8 and across == 8 and along >= 2 * WIDTH and along % WIDTH == 0
    assert piece == WIDTH and blocks == 8 and WIDTH % cap == 0 and cap >= 8
    assert rows % WIDTH == 0 and rows <= 8 * WIDTH and layers <= 4
    gathered_rows = -(-GATHERED * layers // 8) * 8
    face_rows = -(-FACE * layers // 8) * 8
    planes = len(UP) + 1
    post, to_near, to_next, face_r, face_l, ordinal = call(
        functools.partial(first_kernel, cap),
        [
            shape(FLOWS + HEATS, layers, across, along),
            shape(planes, across, along),
            shape(planes, across, along),
            shape(gathered_rows, along),
            shape(gathered_rows, along),
            shape(1, rows, dtype=jnp.int32),
        ],
        [
            populations,
            heat_pops,
            solid_frac,
            coupled_grid_point,
            dest_index.reshape(1, rows),
            heat_coeff,
        ],
        "collide_first",
        scratch=[
            pltpu.VMEM(solid_like, kind)
            for solid_like, kind in (
                (populations.shape, f32),
                (heat_pops.shape, f32),
                (solid_frac.shape, f32),
                ((1, rows), jnp.int32),
                ((1, rows), jnp.int32),
                ((1, rows), f32),
            )
        ]
        + [pltpu.SemaphoreType.DMA((3 + 3 * layers,))],
        far=True,
    )
    near_pairs, next_pairs = swaps("sub")
    near = lax.ppermute(to_near, "sub", near_pairs)
    next_ = lax.ppermute(to_next, "sub", next_pairs)
    to_a, to_b = call(
        functools.partial(edge_kernel, layers),
        [shape(face_rows, along)] * 2,
        [face_r, face_l, near],
        "x_faces",
        scratch=[pltpu.VMEM((gathered_rows, along), f32)] * 2,
    )
    side_a, side_b = swaps("grp")
    faces_a = lax.ppermute(to_a, "grp", side_a)
    faces_b = lax.ppermute(to_b, "grp", side_b)
    corner_a, corner_b = call(
        corner_kernel,
        [shape(-(-(CORNER + layers) // 8) * 8, along)] * 2,
        [next_, solid_frac],
        "x_corners",
    )
    corners_a = lax.ppermute(corner_a, "grp", side_a)
    corners_b = lax.ppermute(corner_b, "grp", side_b)
    hits, flipped, rest, start_slots, turn = call(
        ready_kernel,
        [
            shape(slots, WIDTH, dtype=bf16),
            shape(blocks, piece, piece),
            shape(blocks, piece),
            shape(lines, WIDTH),
            shape(blocks, WIDTH, dtype=jnp.int32),
        ],
        [block_pattern, slot_node, node_diag, heat_source, solid_start, coupling, corner_a],
        "solid_ready",
        scalars=(0,),
    )
    hot, motion, send_near, send_next, fluxes = call(
        second_kernel,
        [
            shape(layers, across, along),
            shape(3, layers, across, along),
            shape(4, across, along),
            shape(4, across, along),
            shape(4 * lines, WIDTH),
        ],
        [
            post,
            near,
            next_,
            to_a,
            to_b,
            faces_a,
            faces_b,
            corner_a,
            corner_b,
            corners_a,
            corners_b,
            solid_frac,
            to_near,
            rest,
        ],
        "collide_second",
        scratch=[
            pltpu.VMEM((FLOWS + HEATS, layers, across, along), f32),
            pltpu.VMEM((FACE, 8, along), f32),
        ]
        + [pltpu.VMEM((face_rows, along), f32)] * 4,
    )
    settled = cap != WIDTH
    if settled:
        fluxes = fluxes.reshape(lines, 4, WIDTH // cap, cap).transpose(0, 2, 1, 3)
    fluxes = fluxes.reshape(slabs, 4, cap)
    landed = lax.all_to_all(fluxes, "sub", split_axis=0, concat_axis=0, tiled=True)
    if settled:
        landed = jnp.stack(
            [
                landed[:, 0],
                jnp.roll(landed[:, 1], 1, axis=0),
                jnp.roll(landed[:, 2], -1, axis=0),
                landed[:, 3],
            ]
        )
        landed = landed.reshape(4, lines, WIDTH).transpose(1, 0, 2)
    landed = landed.reshape(4 * lines, WIDTH)
    from_near = lax.ppermute(send_near, "sub", near_pairs)
    from_next = lax.ppermute(send_next, "sub", next_pairs)
    residual, image, go = call(
        functools.partial(solve_kernel, cap),
        [shape(blocks, piece), shape(blocks, piece), shape(bands * lines * 4, WIDTH)],
        [
            turn,
            slot_node,
            node_diag,
            solid_start,
            coupling,
            hits,
            flipped,
            rest,
            start_slots,
            landed,
        ],
        "solve",
    )
    if settled:
        go = go.reshape(bands, lines, 4, WIDTH // cap, cap).transpose(0, 1, 3, 2, 4)
    go = go.reshape(bands * slabs, 4, cap)
    come = lax.all_to_all(go, ("grp", "sub"), split_axis=0, concat_axis=0, tiled=True)
    hot_out, motion_out = call(
        join_kernel,
        [shape(*hot.shape), shape(*motion.shape)],
        [hot, motion, from_near, from_next],
        "join",
    )
    if settled:
        own = lax.dynamic_slice_in_dim(come, lax.axis_index("grp") * slabs, slabs, 0)
        own = own.transpose(1, 0, 2).reshape(4, lines, WIDTH).transpose(1, 0, 2)
        own = own.reshape(4 * lines, WIDTH)
        come = jnp.pad(come, ((0, 0), (0, 0), (0, WIDTH - cap)))
    else:
        own = rest
    come = come.reshape(4 * bands * slabs, WIDTH)
    temp, seen = call(
        functools.partial(last_kernel, not settled),
        [shape(1, blocks, piece), shape(1, rows)],
        [
            come,
            own,
            solid_start,
            residual,
            image,
            ordinal,
        ],
        "finish",
    )
    return hot_out, motion_out, temp, seen


def solution(mesh):
    placed = (
        P(None, "sub", "grp", None),
        P(None, "sub", "grp", None),
        P("sub", "grp", None),
        P("grp", "sub"),
        P("grp", "sub", None),
        P("grp", "sub"),
        P("grp", "sub"),
        P("grp", "sub", None),
        P("grp", "sub", None, None),
        P("grp", "sub"),
        P("grp", "sub", None),
        P("grp", "sub", None),
    )
    return jax.shard_map(
        body,
        mesh=mesh,
        in_specs=placed,
        out_specs=(
            P("sub", "grp", None),
            P(None, "sub", "grp", None),
            P("grp", "sub", None),
            P("grp", "sub"),
        ),
        check_vma=False,
    )
```

```python
import functools
import jax
import jax.numpy as jnp
import numpy as np
from jax import lax
from jax.experimental import pallas as pl
from jax.experimental.pallas import tpu as pltpu
from jax.sharding import PartitionSpec as P

FLOW_VELOCITY = [
    (0, 0, 0),
    (1, 0, 0),
    (-1, 0, 0),
    (0, 1, 0),
    (0, -1, 0),
    (0, 0, 1),
    (0, 0, -1),
    (1, 1, 0),
    (-1, -1, 0),
    (1, -1, 0),
    (-1, 1, 0),
    (1, 0, 1),
    (-1, 0, -1),
    (1, 0, -1),
    (-1, 0, 1),
    (0, 1, 1),
    (0, -1, -1),
    (0, 1, -1),
    (0, -1, 1),
]
VELOCITY = FLOW_VELOCITY + FLOW_VELOCITY[:7]
FLOWS, HEATS = 19, 7
LANES_ALL = range(FLOWS + HEATS)
UP = [i for i in LANES_ALL if VELOCITY[i][2] == 1]
DOWN = [
    next(j for j in LANES_ALL if VELOCITY[j] == VELOCITY[i][:2] + (-1,) and (j < 19) == (i < 19))
    for i in UP
]
RIGHT = [i for i in LANES_ALL if VELOCITY[i][0] == 1]
LEFT = [
    next(j for j in LANES_ALL if VELOCITY[j] == (-1,) + VELOCITY[i][1:] and (j < 19) == (i < 19))
    for i in RIGHT
]
TURNED = [
    next(n for n, j in enumerate(RIGHT[:-1]) if VELOCITY[j][1:] == (-VELOCITY[i][1], -VELOCITY[i][2]))
    for i in RIGHT[:-1]
]
STILL = [i for i in LANES_ALL if VELOCITY[i][0] == 0]
GATHERED = len(STILL) + 2 * len(RIGHT)
SUMS = 4
FACE = SUMS + 2 * len(RIGHT)
CORNER = 5


def place_of(lists, ex, ey, ez):
    return next(n for n, i in enumerate(lists) if VELOCITY[i] == (ex, ey, ez))


WIDTH = 128
SHIFT = 4.0
f32 = jnp.float32
bf16 = jnp.bfloat16


def signed_sum(terms):
    total = None
    for sign, term in terms:
        if sign == 0:
            continue
        if total is None:
            total = term if sign > 0 else -term
        else:
            total = total + term if sign > 0 else total - term
    return total


def collide(flow, heat, solid):
    pairs = range(1, FLOWS, 2)
    density = flow[0]
    for i in pairs:
        density = density + (flow[i] + flow[i + 1])
    gaps = {i: flow[i] - flow[i + 1] for i in pairs}
    scale = 1.0 / density
    speed = [
        signed_sum([(FLOW_VELOCITY[i][axis], gaps[i]) for i in pairs]) * scale for axis in range(3)
    ]
    square = speed[0] * speed[0] + speed[1] * speed[1] + speed[2] * speed[2]
    base = 1.0 - 1.5 * square
    gas = 1.0 - solid
    keep = gas * (1.0 - 1.0 / 0.8)
    pull = gas * (density * (1.0 / 0.8))
    flow_post = [None] * FLOWS
    flow_post[0] = (keep + solid) * flow[0] + (pull * (1.0 / 3.0)) * base
    shares = {1: pull * (1.0 / 18.0), 2: pull * (1.0 / 36.0)}
    for i in pairs:
        share = shares[sum(abs(c) for c in FLOW_VELOCITY[i])]
        along = signed_sum([(FLOW_VELOCITY[i][axis], speed[axis]) for axis in range(3)])
        even = base + 4.5 * along * along
        odd = 3.0 * along
        flow_post[i] = keep * flow[i] + share * (even + odd) + solid * flow[i + 1]
        flow_post[i + 1] = keep * flow[i + 1] + share * (even - odd) + solid * flow[i]
    hotness = heat[0]
    for j in range(1, HEATS):
        hotness = hotness + heat[j]
    stay = 1.0 - 1.0 / 0.7
    heat_post = [stay * heat[0] + (0.25 / 0.7) * hotness]
    level = (0.125 / 0.7) * hotness
    for j in range(1, HEATS, 2):
        axis = (j - 1) // 2
        drift = 4.0 * speed[axis]
        heat_post.append(stay * heat[j] + level * (1.0 + drift))
        heat_post.append(stay * heat[j + 1] + level * (1.0 - drift))
    return flow_post + heat_post


def collide_halo(still, inward, outward, solid):
    flows = RIGHT[:-1]
    density, along_y, along_z, hotness = still
    pairs = [(a + b, a - b) for a, b in zip(inward, outward)]
    across = None
    for n, i in enumerate(flows):
        _, ey, ez = VELOCITY[i]
        whole, gap = pairs[n]
        density = density + whole
        across = gap if across is None else across + gap
        along_y = signed_sum([(1, along_y), (ey, whole)])
        along_z = signed_sum([(1, along_z), (ez, whole)])
    hotness = hotness + pairs[-1][0]
    scale = 1.0 / density
    speed = [across * scale, along_y * scale, along_z * scale]
    square = speed[0] * speed[0] + speed[1] * speed[1] + speed[2] * speed[2]
    base = 1.0 - 1.5 * square
    gas = 1.0 - solid
    keep = gas * (1.0 - 1.0 / 0.8)
    pull = gas * (density * (1.0 / 0.8))
    shares = {1: pull * (1.0 / 18.0), 2: pull * (1.0 / 36.0)}
    out = []
    for n, i in enumerate(flows):
        share = shares[sum(abs(c) for c in VELOCITY[i])]
        along = signed_sum([(VELOCITY[i][axis], speed[axis]) for axis in range(3)])
        feq = share * (base + 4.5 * along * along + 3.0 * along)
        out.append(keep * inward[n] + feq + solid * outward[TURNED[n]])
    level = (0.125 / 0.7) * hotness
    out.append((1.0 - 1.0 / 0.7) * inward[-1] + level * (1.0 + 4.0 * speed[0]))
    return out


def three_parts(value):
    high = value.astype(bf16).astype(f32)
    rest = value - high
    middle = rest.astype(bf16).astype(f32)
    return [high, middle, rest - middle]


def times_transposed(left, right):
    return lax.dot_general(
        left.astype(bf16), right.astype(bf16), (((1,), (1,)), ((), ())), preferred_element_type=f32
    )


def spread(row):
    return jnp.broadcast_to(row, (8, row.shape[-1]))


def lane_gather(row, lane):
    return jnp.take_along_axis(spread(row), lane, axis=1, mode="promise_in_bounds")


def table_gather(table, index):
    place, lane = index >> 7, index & 127
    out = jnp.zeros(index.shape, f32)
    for row in range(table.shape[0]):
        out = jnp.where(place == row, lane_gather(table[row : row + 1], lane), out)
    return out


def plane_rows(plane, first=0, count=8):
    return pl.ds(4 * first + plane, count, stride=4)


def stacked(row):
    return jnp.concatenate(
        [row[:, k * WIDTH : (k + 1) * WIDTH] for k in range(row.shape[1] // WIDTH)], axis=0
    )


def slot_tables(cap, voxel, dest, coeff, ordinal):
    rows_here = dest.shape[1]
    owner = dest[...].astype(f32)
    chunks = rows_here // WIDTH
    tall = stacked(owner)
    tall = jnp.concatenate([tall] + [jnp.zeros((8 - chunks, WIDTH), f32)] * (chunks < 8), axis=0)
    upright = tall.T
    first = lax.broadcasted_iota(jnp.int32, (WIDTH, WIDTH), 0)
    second = lax.broadcasted_iota(jnp.int32, (WIDTH, WIDTH), 1)
    slot_row = lax.broadcasted_iota(jnp.int32, (8, WIDTH), 0)
    table = jnp.zeros((40, WIDTH), f32)
    for c in range(chunks):
        lanes = slice(c * WIDTH, (c + 1) * WIDTH)
        here = owner[:, lanes]
        count = jnp.zeros((WIDTH, WIDTH), f32)
        for other in range(c + 1):
            same = upright[:, other : other + 1] == here
            if other == c:
                same = same & (first < second)
            count = count + jnp.where(same, 1.0, 0.0)
        rank = jnp.sum(count, axis=0, keepdims=True)
        place = (here * float(cap) + rank).astype(jnp.int32)
        ordinal[:, lanes] = place
        mine = slot_row == (place >> 7)
        spot = voxel[:, lanes]
        parts = [(spot >> 7).astype(f32), (spot & 127).astype(f32)] + three_parts(coeff[:, lanes])
        values = jnp.concatenate([jnp.where(mine, part, 0.0) for part in parts], axis=0)
        table = table + times_transposed(values, jnp.where(first == (place & 127), 1.0, 0.0))
    spots = table[0:8] * float(WIDTH) + table[8:16]
    coeffs = (table[16:24] + table[24:32]) + table[32:40]
    return spots, coeffs


def on_even(axis="sub"):
    return lax.rem(lax.axis_index(axis), 2) == 0


def first_kernel(cap, *refs):
    given, (post, to_near, to_next, ordinal) = refs[:6], refs[6:10]
    held, arrived = refs[10:16], refs[16]
    pops, heat, solid, voxel, dest, coeff = held
    pieces = [(given[n], held[n]) for n in (4, 3, 5)]
    for z in range(solid.shape[0]):
        pieces += [(given[n].at[:, z], held[n].at[:, z]) for n in (0, 1)]
        pieces.append((given[2].at[z], held[2].at[z]))
    copies = [
        pltpu.make_async_copy(source, target, arrived.at[n])
        for n, (source, target) in enumerate(pieces)
    ]
    for copy in copies:
        copy.start()
    layers, across, along = solid.shape
    even = on_even()
    for copy in copies[:3]:
        copy.wait()
    spots, coeffs = slot_tables(cap, voxel, dest, coeff, ordinal)
    extra = len(UP)
    for plane in (to_near, to_next):
        plane[extra] = jnp.zeros(plane.shape[1:], f32)
        plane[extra, :, 0:WIDTH] = spots
        plane[extra, :, WIDTH : 2 * WIDTH] = coeffs
    for z in range(layers):
        for copy in copies[3 + 3 * z : 6 + 3 * z]:
            copy.wait()
        for start in range(0, along, WIDTH):
            lanes = slice(start, start + WIDTH)
            out = collide(
                [pops[i, z, :, lanes] for i in range(FLOWS)],
                [heat[j, z, :, lanes] for j in range(HEATS)],
                solid[z, :, lanes],
            )
            for i in LANES_ALL:
                post[i, z, :, lanes] = out[i]
    for n, (above, below) in enumerate(zip(UP, DOWN)):
        above, below = post[above, layers - 1], post[below, 0]
        to_near[n] = jnp.where(even, above, below)
        to_next[n] = jnp.where(even, below, above)


def turned(tile, step):
    return tile if step == 0 else pltpu.roll(tile, step % tile.shape[1], 1)


def edge_kernel(post, to_a, to_b, out_r, out_l):
    layers, across, along = post.shape[1:]
    for out, lists, edge, inside in (
        (out_r, (STILL, RIGHT), across - 1, across - 2),
        (out_l, (STILL, LEFT), 0, 1),
    ):
        rows = [(i, edge) for i in lists[0]] + [(i, inside) for i in lists[1]]
        rows = rows + [(i, edge) for i in lists[1]]
        for n, (i, column) in enumerate(rows):
            for z in range(layers):
                at, source = n * layers + z, z - VELOCITY[i][2]
                if 0 <= source < layers:
                    out[at : at + 1, :] = post[i, source, column : column + 1, :]
                else:
                    out[at : at + 1, :] = jnp.zeros((1, along), f32)
    band_even = on_even("grp")

    def both(n):
        at = slice(n * layers, (n + 1) * layers)
        return jnp.concatenate([out_r[at, :], out_l[at, :]], axis=0)

    def send(n, tile):
        at = slice(n * layers, (n + 1) * layers)
        right, left = tile[0:layers], tile[layers : 2 * layers]
        to_a[at, :] = jnp.where(band_even, right, left)
        to_b[at, :] = jnp.where(band_even, left, right)

    sums = [[] for _ in range(SUMS)]
    for n, i in enumerate(STILL):
        _, ey, ez = VELOCITY[i]
        tile = turned(both(n), ey)
        if i >= FLOWS:
            sums[3].append((1, tile))
        else:
            sums[0].append((1, tile))
            sums[1].append((ey, tile))
            sums[2].append((ez, tile))
    for n in range(SUMS):
        send(n, signed_sum(sums[n]))
    for n, i in enumerate(RIGHT):
        send(SUMS + n, turned(both(len(STILL) + n), VELOCITY[i][1]))
    for n in range(len(STILL) + len(RIGHT), GATHERED):
        send(n - len(STILL) + SUMS, both(n))


def corner_kernel(near, next_, solid, to_a, to_b):
    across = next_.shape[1]
    even = on_even()
    up, right, left, ahead, behind = (
        place_of(UP, ex, ey, 1) for ex, ey in ((0, 0), (1, 0), (-1, 0), (0, 1), (0, -1))
    )
    warm = len(UP) - 1
    sides = []
    for column, inside, outward in ((across - 1, across - 2, right), (0, 1, left)):
        rows = []
        for low in (True, False):

            def row(n, at):
                one, two = next_[n, at : at + 1, :], near[n, at : at + 1, :]
                return jnp.where(even == low, one, two)

            one, two = turned(row(ahead, column), 1), turned(row(behind, column), -1)
            rows += [
                row(up, column) + (one + two),
                one - two,
                row(warm, column),
                row(outward, inside),
                row(outward, column),
            ]
        rows += [solid[z, column : column + 1, :] for z in range(solid.shape[0])]
        if len(rows) < to_a.shape[0]:
            rows.append(jnp.zeros((to_a.shape[0] - len(rows), next_.shape[2]), f32))
        sides.append(jnp.concatenate(rows, axis=0))
    band_even = on_even("grp")
    to_a[...] = jnp.where(band_even, sides[0], sides[1])
    to_b[...] = jnp.where(band_even, sides[1], sides[0])


def add_corners(face, corner, layers, whole):
    edge = SUMS + len(RIGHT)
    for first, z, rise in ((0, 0, 1), (CORNER, layers - 1, -1)):
        k = place_of(RIGHT, 1, 0, rise)
        adds = [(edge + k, 1, 4)]
        if whole:
            adds += [(0, 1, 0), (1, 1, 1), (2, rise, 0), (3, 1, 2), (SUMS + k, 1, 3)]
        for n, sign, row in adds:
            at = n * layers + z
            share = corner[first + row : first + row + 1]
            face[at : at + 1, :] = face[at : at + 1, :] + (share if sign > 0 else -share)


def second_kernel(
    post,
    near,
    next_,
    to_a,
    to_b,
    faces_a,
    faces_b,
    corner_a,
    corner_b,
    corners_a,
    corners_b,
    solid,
    own_table,
    tie,
    hot,
    motion,
    send_near,
    send_next,
    fluxes,
    moved,
    halo,
    own_r,
    own_l,
    from_l,
    from_r,
):
    layers, across, along = solid.shape
    even = on_even()
    band_even = on_even("grp")
    own_r[...] = jnp.where(band_even, to_a[...], to_b[...])
    own_l[...] = jnp.where(band_even, to_b[...], to_a[...])
    below = [jnp.where(even, next_[n], near[n]) for n in range(len(UP) + 1)]
    above = [jnp.where(even, near[n], next_[n]) for n in range(len(UP) + 1)]
    from_l[...] = jnp.where(band_even, faces_b[...], faces_a[...])
    from_r[...] = jnp.where(band_even, faces_a[...], faces_b[...])
    corners = []
    for face, one, two, whole in (
        (own_r, corner_a, corner_b, False),
        (own_l, corner_b, corner_a, False),
        (from_l, corners_b, corners_a, True),
        (from_r, corners_a, corners_b, True),
    ):
        corner = jnp.where(band_even, one[...], two[...])
        add_corners(face, corner, layers, whole)
        corners.append(corner)
    slot = lax.broadcasted_iota(jnp.int32, (across, along), 0)
    edge = SUMS + len(RIGHT)
    for i in LANES_ALL:
        ex, ey, ez = VELOCITY[i]
        for z in range(layers):
            if z - ez < 0:
                tile = below[UP.index(i)]
            elif z - ez >= layers:
                tile = above[DOWN.index(i)]
            else:
                tile = post[i, z - ez]
            if ex == 1:
                at = (edge + RIGHT.index(i)) * layers + z
                tile = jnp.where(slot == 0, from_l[at : at + 1, :], pltpu.roll(tile, 1, 0))
            elif ex == -1:
                at = (edge + LEFT.index(i)) * layers + z
                tile = jnp.where(
                    slot == across - 1, from_r[at : at + 1, :], pltpu.roll(tile, across - 1, 0)
                )
            moved[i, z] = turned(tile, ey)

    def halves(low, high, n):
        at = slice(n * layers, (n + 1) * layers)
        parts = [low[at, :], high[at, :]]
        if 2 * layers < 8:
            parts.append(jnp.ones((8 - 2 * layers, along), f32))
        return jnp.concatenate(parts, axis=0)

    for n in range(edge):
        halo[n] = halves(from_l, from_r, n)
    for n, i in enumerate(RIGHT):
        halo[edge + n] = turned(halves(own_l, own_r, edge + n), VELOCITY[i][1])
    edge_solid = [corner[2 * CORNER : 2 * CORNER + layers] for corner in corners[2:]]
    if 2 * layers < 8:
        edge_solid.append(jnp.zeros((8 - 2 * layers, along), f32))
    edge_solid = jnp.concatenate(edge_solid, axis=0)
    for start in range(0, along, WIDTH):
        lanes = slice(start, start + WIDTH)
        for z in range(layers):
            out = collide(
                [moved[i, z, :, lanes] for i in range(FLOWS)],
                [moved[FLOWS + j, z, :, lanes] for j in range(HEATS)],
                solid[z, :, lanes],
            )
            for i in LANES_ALL:
                moved[i, z, :, lanes] = out[i]
        out = collide_halo(
            [halo[n, :, lanes] for n in range(SUMS)],
            [halo[SUMS + n, :, lanes] for n in range(len(RIGHT))],
            [halo[edge + n, :, lanes] for n in range(len(RIGHT))],
            edge_solid[:, lanes],
        )
        for n in range(len(RIGHT)):
            halo[SUMS + n, :, lanes] = out[n]
    sums = {}

    def add(key, sign, tile):
        if sign == 0:
            return
        if key in sums:
            sums[key] = sums[key] + tile if sign > 0 else sums[key] - tile
        else:
            sums[key] = tile if sign > 0 else -tile

    for z in range(layers):
        for i in LANES_ALL:
            ex, ey, ez = VELOCITY[i]
            if i == 0:
                continue
            tile = moved[i, z]
            if ex == 1:
                side = halo[SUMS + RIGHT.index(i), z : z + 1, :]
                tile = jnp.where(slot == 0, side, pltpu.roll(tile, 1, 0))
            elif ex == -1:
                at = layers + z
                side = halo[SUMS + LEFT.index(i), at : at + 1, :]
                tile = jnp.where(slot == across - 1, side, pltpu.roll(tile, across - 1, 0))
            tile = turned(tile, ey)
            target = z + ez
            if i >= FLOWS:
                add((3, target), 1, tile)
            else:
                add((0, target), ex, tile)
                add((1, target), ey, tile)
                add((2, target), ez, tile)
    for z in range(layers):
        hot[z] = sums[3, z]
        for axis in range(3):
            motion[axis, z] = sums[axis, z]
    for part in range(4):
        send_near[part] = jnp.where(even, sums[part, layers], sums[part, -1])
        send_next[part] = jnp.where(even, sums[part, -1], sums[part, layers])
    extra = len(UP)
    per_line = along // WIDTH
    per_layer = across * per_line

    def flux(table, planes):
        index = table[:, 0:WIDTH].astype(jnp.int32)
        place, lane = index >> 7, index & 127
        out = jnp.zeros(lane.shape, f32)
        for z, plane in planes:
            for x in range(across):
                for c in range(per_line):
                    row = plane[x : x + 1, c * WIDTH : (c + 1) * WIDTH]
                    out = jnp.where(
                        place == z * per_layer + x * per_line + c, lane_gather(row, lane), out
                    )
        return out * table[:, WIDTH : 2 * WIDTH]

    mine = own_table[extra]
    fluxes[plane_rows(0), :] = flux(mine, [(z, sums[3, z]) for z in range(layers)])
    fluxes[plane_rows(1), :] = flux(above[extra], [(0, sums[3, layers])])
    fluxes[plane_rows(2), :] = flux(below[extra], [(layers - 1, sums[3, -1])])
    fluxes[plane_rows(3), :] = mine[:, WIDTH : 2 * WIDTH]


def sublane_gather(value, index):
    return jnp.take_along_axis(value, index, axis=0, mode="promise_in_bounds")


def coupled(vector, blocks, flipped, shift):
    count = vector.shape[0]
    upright = vector.T
    ahead, back = [], []
    for b in range(count):
        column = jnp.broadcast_to(upright[:, b : b + 1], blocks.shape[1:])
        back.append(jnp.sum(blocks[b] * column, axis=0, keepdims=True))
        ahead.append(jnp.sum(flipped[b] * column, axis=0, keepdims=True))
    ahead = jnp.concatenate(ahead, axis=0)
    back = jnp.concatenate(back, axis=0)
    block = lax.broadcasted_iota(jnp.int32, vector.shape, 0)
    ahead = sublane_gather(ahead, (block + shift) & (count - 1))
    return ahead + sublane_gather(back, (block - shift) & (count - 1))


def ready_kernel(
    pattern, nodes, diagonal, source, start, coupling, tie, hits, flipped, rest, slots, turn
):
    shift = pattern[0, 0]
    turn[...] = jnp.full(turn.shape, shift, jnp.int32)
    count = start.shape[1]
    for b in range(count):
        flipped[lax.rem(b + shift, count)] = coupling[0, b].T
    vector = start[0]
    rest[...] = (
        source[0] - diagonal[0] * vector + coupled(vector, coupling.at[0], flipped, turn[...])
    )
    index = stacked(nodes[...])
    slots[...] = table_gather(vector, index)
    upright = (index & 127).astype(f32).T.astype(jnp.int32)
    lane = lax.broadcasted_iota(jnp.int32, (WIDTH, WIDTH), 1)
    for s in range(index.shape[0]):
        hit = jnp.where(upright[:, s : s + 1] == lane, 1.0, 0.0)
        hits[s * WIDTH : (s + 1) * WIDTH] = hit.astype(bf16)


def solve_kernel(
    cap,
    turn,
    nodes,
    diagonal,
    start,
    coupling,
    hits,
    flipped,
    rest,
    slots,
    come,
    res,
    img,
    go,
):
    shift = turn[...]
    count = start.shape[1]
    index = stacked(nodes[...])
    place = index >> 7
    own, low, high, coeff = (come[plane_rows(plane), :] for plane in range(4))
    if cap == WIDTH:
        low = pltpu.roll(low, 1, 0)
        high = pltpu.roll(high, low.shape[0] - 1, 0)
    parts = three_parts(own + low + high) + three_parts(coeff)
    block = lax.broadcasted_iota(jnp.int32, (count, WIDTH), 0)
    values = []
    for s in range(index.shape[0]):
        mine = block == place[s : s + 1]
        values.append(
            jnp.concatenate([jnp.where(mine, part[s : s + 1], 0.0) for part in parts], axis=0)
        )
    values = jnp.concatenate(values, axis=1).astype(bf16)
    landed = jnp.dot(values, hits[...], preferred_element_type=f32)
    landed = [landed[k * count : (k + 1) * count] for k in range(len(parts))]
    added = (landed[0] + landed[1]) + landed[2]
    extra = (landed[3] + landed[4]) + landed[5]
    whole = diagonal[0] + extra
    blocks = coupling.at[0]
    residual = rest[...] + added - extra * start[0]
    image = whole * residual - coupled(residual, blocks, flipped, shift)

    def total(value):
        return jnp.sum(jnp.sum(value, axis=0, keepdims=True), axis=1, keepdims=True)

    offset = image - SHIFT * residual
    bend = whole * offset - coupled(offset, blocks, flipped, shift)
    totals = [
        total(residual * residual),
        total(residual * offset),
        total(offset * offset),
        total(offset * bend),
    ]
    res[...] = residual
    img[...] = image
    lane = lax.broadcasted_iota(jnp.int32, (8, WIDTH), 1) & (cap - 1)
    facts = jnp.zeros((8, WIDTH), f32)
    for n, fact in enumerate(totals):
        facts = jnp.where(lane == n, fact, facts)
    residual_slots = table_gather(residual, index)
    image_slots = table_gather(image, index)
    start_slots = slots[...]
    for group in range(0, go.shape[0] // 4, 8):
        go[plane_rows(0, group), :] = start_slots
        go[plane_rows(1, group), :] = residual_slots
        go[plane_rows(2, group), :] = image_slots
        go[plane_rows(3, group), :] = facts


def last_kernel(direct, come, own, start, res, img, ordinal, temp, seen):
    places = stacked(ordinal[...])
    chunks = places.shape[0]
    if chunks < 8:
        places = jnp.concatenate([places, jnp.zeros((8 - chunks, WIDTH), jnp.int32)], axis=0)
    found = []
    for plane in range(3):
        if direct:
            table = come[plane_rows(plane, lax.axis_index("grp") * 8), :]
        else:
            table = own[plane_rows(plane), :]
        found.append(table_gather(table, places))
    facts = come[plane_rows(3, 0, come.shape[0] // 4), :]
    facts = jnp.sum(facts, axis=0, keepdims=True)
    all_norm, cross, square, energy = (
        lane_gather(facts, jnp.full((8, WIDTH), n, jnp.int32)) for n in range(4)
    )
    product = SHIFT * all_norm + cross
    inverse = 1.0 / product
    ratio = cross / all_norm
    spread_square = square - cross * ratio
    energy = energy - ratio * (2.0 * (square + SHIFT * cross) - ratio * product)
    small = spread_square * inverse
    first = all_norm * inverse
    step = spread_square / (energy - spread_square * small)
    of_residual = first + step * (1.0 + small * first)
    of_image = -step * first
    temp[0] = start[0] + of_residual * res[...] + of_image * img[...]
    found = found[0] + of_residual * found[1] + of_image * found[2]
    for c in range(chunks):
        seen[:, c * WIDTH : (c + 1) * WIDTH] = found[c : c + 1]


def join_kernel(hot, motion, near, next_, hot_out, motion_out):
    layers = hot.shape[0]
    even = on_even()
    below = [jnp.where(even, next_[n], near[n]) for n in range(4)]
    above = [jnp.where(even, near[n], next_[n]) for n in range(4)]
    for z in range(layers):
        for part in range(4):
            tile = hot[z] if part == 3 else motion[part, z]
            if z == 0:
                tile = tile + below[part]
            if z == layers - 1:
                tile = tile + above[part]
            if part == 3:
                hot_out[z] = tile
            else:
                motion_out[part, z] = tile


VMEM = pl.BlockSpec(memory_space=pltpu.VMEM)
ANYWHERE = pl.BlockSpec(memory_space=pl.ANY)
SMEM = pl.BlockSpec(memory_space=pltpu.SMEM)


def call(kernel, out, args, name, scalars=(), scratch=(), far=False, flops=1 << 20):
    total = sum(int(np.prod(a.shape)) * a.dtype.itemsize for a in list(args) + list(out))
    if far:
        args = [pltpu.with_memory_space_constraint(a, pltpu.HBM) for a in args]
    return pl.pallas_call(
        kernel,
        out_shape=out,
        in_specs=[
            ANYWHERE if far else SMEM if n in scalars else VMEM for n in range(len(args))
        ],
        out_specs=[VMEM] * len(out),
        scratch_shapes=scratch,
        compiler_params=pltpu.CompilerParams(vmem_limit_bytes=24 << 20),
        cost_estimate=pl.CostEstimate(flops=flops, bytes_accessed=total, transcendentals=0),
        name=name,
    )(*args)


def shape(*dims, dtype=f32):
    return jax.ShapeDtypeStruct(dims, dtype)


def swaps(axis):
    count = lax.axis_size(axis)
    assert count % 2 == 0
    near = [(k, k + 1 - 2 * (k % 2)) for k in range(count)]
    return near, [(k, (k - 1 + 2 * (k % 2)) % count) for k in range(count)]


def body(
    populations,
    heat_pops,
    solid_frac,
    coupled_grid_point,
    dest_index,
    heat_coeff,
    slot_node,
    node_diag,
    coupling,
    block_pattern,
    heat_source,
    solid_start,
):
    layers, across, along = solid_frac.shape
    slabs, bands = lax.axis_size("sub"), lax.axis_size("grp")
    slots = slot_node.shape[1]
    cap = slots // slabs
    rows = coupled_grid_point.shape[1]
    blocks, piece = node_diag.shape[1:]
    lines = slots // WIDTH
    assert lines == 8 and across == 8 and along >= 2 * WIDTH and along % WIDTH == 0
    assert piece == WIDTH and blocks == 8 and WIDTH % cap == 0 and cap >= 8
    assert rows % WIDTH == 0 and rows <= 8 * WIDTH and layers <= 4
    gathered_rows = -(-GATHERED * layers // 8) * 8
    face_rows = -(-FACE * layers // 8) * 8
    planes = len(UP) + 1
    post, to_near, to_next, ordinal = call(
        functools.partial(first_kernel, cap),
        [
            shape(FLOWS + HEATS, layers, across, along),
            shape(planes, across, along),
            shape(planes, across, along),
            shape(1, rows, dtype=jnp.int32),
        ],
        [
            populations,
            heat_pops,
            solid_frac,
            coupled_grid_point,
            dest_index.reshape(1, rows),
            heat_coeff,
        ],
        "collide_first",
        scratch=[
            pltpu.VMEM(solid_like, kind)
            for solid_like, kind in (
                (populations.shape, f32),
                (heat_pops.shape, f32),
                (solid_frac.shape, f32),
                ((1, rows), jnp.int32),
                ((1, rows), jnp.int32),
                ((1, rows), f32),
            )
        ]
        + [pltpu.SemaphoreType.DMA((3 + 3 * layers,))],
        far=True,
    )
    near_pairs, next_pairs = swaps("sub")
    next_ = lax.ppermute(to_next, "sub", next_pairs)
    near = lax.ppermute(to_near, "sub", near_pairs)
    to_a, to_b = call(
        edge_kernel,
        [shape(face_rows, along)] * 2,
        [post],
        "x_faces",
        scratch=[pltpu.VMEM((gathered_rows, along), f32)] * 2,
    )
    side_a, side_b = swaps("grp")
    faces_a = lax.ppermute(to_a, "grp", side_a)
    faces_b = lax.ppermute(to_b, "grp", side_b)
    corner_a, corner_b = call(
        corner_kernel,
        [shape(-(-(2 * CORNER + layers) // 8) * 8, along)] * 2,
        [near, next_, solid_frac],
        "x_corners",
    )
    corners_a = lax.ppermute(corner_a, "grp", side_a)
    corners_b = lax.ppermute(corner_b, "grp", side_b)
    hits, flipped, rest, start_slots, turn = call(
        ready_kernel,
        [
            shape(slots, WIDTH, dtype=bf16),
            shape(blocks, piece, piece),
            shape(blocks, piece),
            shape(lines, WIDTH),
            shape(blocks, WIDTH, dtype=jnp.int32),
        ],
        [block_pattern, slot_node, node_diag, heat_source, solid_start, coupling, corner_a],
        "solid_ready",
        scalars=(0,),
    )
    hot, motion, send_near, send_next, fluxes = call(
        second_kernel,
        [
            shape(layers, across, along),
            shape(3, layers, across, along),
            shape(4, across, along),
            shape(4, across, along),
            shape(4 * lines, WIDTH),
        ],
        [
            post,
            near,
            next_,
            to_a,
            to_b,
            faces_a,
            faces_b,
            corner_a,
            corner_b,
            corners_a,
            corners_b,
            solid_frac,
            to_next,
            rest,
        ],
        "collide_second",
        scratch=[
            pltpu.VMEM((FLOWS + HEATS, layers, across, along), f32),
            pltpu.VMEM((FACE, 8, along), f32),
        ]
        + [pltpu.VMEM((face_rows, along), f32)] * 4,
    )
    settled = cap != WIDTH
    if settled:
        fluxes = fluxes.reshape(lines, 4, WIDTH // cap, cap).transpose(0, 2, 1, 3)
    fluxes = fluxes.reshape(slabs, 4, cap)
    landed = lax.all_to_all(fluxes, "sub", split_axis=0, concat_axis=0, tiled=True)
    if settled:
        landed = jnp.stack(
            [
                landed[:, 0],
                jnp.roll(landed[:, 1], 1, axis=0),
                jnp.roll(landed[:, 2], -1, axis=0),
                landed[:, 3],
            ]
        )
        landed = landed.reshape(4, lines, WIDTH).transpose(1, 0, 2)
    landed = landed.reshape(4 * lines, WIDTH)
    from_near = lax.ppermute(send_near, "sub", near_pairs)
    from_next = lax.ppermute(send_next, "sub", next_pairs)
    residual, image, go = call(
        functools.partial(solve_kernel, cap),
        [shape(blocks, piece), shape(blocks, piece), shape(bands * lines * 4, WIDTH)],
        [
            turn,
            slot_node,
            node_diag,
            solid_start,
            coupling,
            hits,
            flipped,
            rest,
            start_slots,
            landed,
        ],
        "solve",
    )
    if settled:
        go = go.reshape(bands, lines, 4, WIDTH // cap, cap).transpose(0, 1, 3, 2, 4)
    go = go.reshape(bands * slabs, 4, cap)
    come = lax.all_to_all(go, ("grp", "sub"), split_axis=0, concat_axis=0, tiled=True)
    hot_out, motion_out = call(
        join_kernel,
        [shape(*hot.shape), shape(*motion.shape)],
        [hot, motion, from_near, from_next],
        "join",
    )
    if settled:
        own = lax.dynamic_slice_in_dim(come, lax.axis_index("grp") * slabs, slabs, 0)
        own = own.transpose(1, 0, 2).reshape(4, lines, WIDTH).transpose(1, 0, 2)
        own = own.reshape(4 * lines, WIDTH)
        come = jnp.pad(come, ((0, 0), (0, 0), (0, WIDTH - cap)))
    else:
        own = rest
    come = come.reshape(4 * bands * slabs, WIDTH)
    temp, seen = call(
        functools.partial(last_kernel, not settled),
        [shape(1, blocks, piece), shape(1, rows)],
        [
            come,
            own,
            solid_start,
            residual,
            image,
            ordinal,
        ],
        "finish",
    )
    return hot_out, motion_out, temp, seen


def solution(mesh):
    placed = (
        P(None, "sub", "grp", None),
        P(None, "sub", "grp", None),
        P("sub", "grp", None),
        P("grp", "sub"),
        P("grp", "sub", None),
        P("grp", "sub"),
        P("grp", "sub"),
        P("grp", "sub", None),
        P("grp", "sub", None, None),
        P("grp", "sub"),
        P("grp", "sub", None),
        P("grp", "sub", None),
    )
    return jax.shard_map(
        body,
        mesh=mesh,
        in_specs=placed,
        out_specs=(
            P("sub", "grp", None),
            P(None, "sub", "grp", None),
            P("grp", "sub", None),
            P("grp", "sub"),
        ),
        check_vma=False,
    )
```

```python
import functools
import jax
import jax.numpy as jnp
import numpy as np
from jax import lax
from jax.experimental import pallas as pl
from jax.experimental.pallas import tpu as pltpu
from jax.sharding import PartitionSpec as P

FLOW_VELOCITY = [
    (0, 0, 0),
    (1, 0, 0),
    (-1, 0, 0),
    (0, 1, 0),
    (0, -1, 0),
    (0, 0, 1),
    (0, 0, -1),
    (1, 1, 0),
    (-1, -1, 0),
    (1, -1, 0),
    (-1, 1, 0),
    (1, 0, 1),
    (-1, 0, -1),
    (1, 0, -1),
    (-1, 0, 1),
    (0, 1, 1),
    (0, -1, -1),
    (0, 1, -1),
    (0, -1, 1),
]
VELOCITY = FLOW_VELOCITY + FLOW_VELOCITY[:7]
FLOWS, HEATS = 19, 7
LANES_ALL = range(FLOWS + HEATS)
UP = [i for i in LANES_ALL if VELOCITY[i][2] == 1]
DOWN = [
    next(j for j in LANES_ALL if VELOCITY[j] == VELOCITY[i][:2] + (-1,) and (j < 19) == (i < 19))
    for i in UP
]
RIGHT = [i for i in LANES_ALL if VELOCITY[i][0] == 1]
LEFT = [
    next(j for j in LANES_ALL if VELOCITY[j] == (-1,) + VELOCITY[i][1:] and (j < 19) == (i < 19))
    for i in RIGHT
]
TURNED = [
    next(n for n, j in enumerate(RIGHT[:-1]) if VELOCITY[j][1:] == (-VELOCITY[i][1], -VELOCITY[i][2]))
    for i in RIGHT[:-1]
]
STILL = [i for i in LANES_ALL if VELOCITY[i][0] == 0]
GATHERED = len(STILL) + 2 * len(RIGHT)
SUMS = 4
FACE = SUMS + 2 * len(RIGHT)
CORNER = 5


def place_of(lists, ex, ey, ez):
    return next(n for n, i in enumerate(lists) if VELOCITY[i] == (ex, ey, ez))


WIDTH = 128
SHIFT = 4.0
f32 = jnp.float32
bf16 = jnp.bfloat16


def signed_sum(terms):
    total = None
    for sign, term in terms:
        if sign == 0:
            continue
        if total is None:
            total = term if sign > 0 else -term
        else:
            total = total + term if sign > 0 else total - term
    return total


def collide(flow, heat, solid):
    pairs = range(1, FLOWS, 2)
    density = flow[0]
    for i in pairs:
        density = density + (flow[i] + flow[i + 1])
    gaps = {i: flow[i] - flow[i + 1] for i in pairs}
    scale = 1.0 / density
    speed = [
        signed_sum([(FLOW_VELOCITY[i][axis], gaps[i]) for i in pairs]) * scale for axis in range(3)
    ]
    square = speed[0] * speed[0] + speed[1] * speed[1] + speed[2] * speed[2]
    base = 1.0 - 1.5 * square
    gas = 1.0 - solid
    keep = gas * (1.0 - 1.0 / 0.8)
    pull = gas * (density * (1.0 / 0.8))
    flow_post = [None] * FLOWS
    flow_post[0] = (keep + solid) * flow[0] + (pull * (1.0 / 3.0)) * base
    shares = {1: pull * (1.0 / 18.0), 2: pull * (1.0 / 36.0)}
    for i in pairs:
        share = shares[sum(abs(c) for c in FLOW_VELOCITY[i])]
        along = signed_sum([(FLOW_VELOCITY[i][axis], speed[axis]) for axis in range(3)])
        even = base + 4.5 * along * along
        odd = 3.0 * along
        flow_post[i] = keep * flow[i] + share * (even + odd) + solid * flow[i + 1]
        flow_post[i + 1] = keep * flow[i + 1] + share * (even - odd) + solid * flow[i]
    hotness = heat[0]
    for j in range(1, HEATS):
        hotness = hotness + heat[j]
    stay = 1.0 - 1.0 / 0.7
    heat_post = [stay * heat[0] + (0.25 / 0.7) * hotness]
    level = (0.125 / 0.7) * hotness
    for j in range(1, HEATS, 2):
        axis = (j - 1) // 2
        drift = 4.0 * speed[axis]
        heat_post.append(stay * heat[j] + level * (1.0 + drift))
        heat_post.append(stay * heat[j + 1] + level * (1.0 - drift))
    return flow_post + heat_post


def collide_halo(still, inward, outward, solid):
    flows = RIGHT[:-1]
    density, along_y, along_z, hotness = still
    pairs = [(a + b, a - b) for a, b in zip(inward, outward)]
    across = None
    for n, i in enumerate(flows):
        _, ey, ez = VELOCITY[i]
        whole, gap = pairs[n]
        density = density + whole
        across = gap if across is None else across + gap
        along_y = signed_sum([(1, along_y), (ey, whole)])
        along_z = signed_sum([(1, along_z), (ez, whole)])
    hotness = hotness + pairs[-1][0]
    scale = 1.0 / density
    speed = [across * scale, along_y * scale, along_z * scale]
    square = speed[0] * speed[0] + speed[1] * speed[1] + speed[2] * speed[2]
    base = 1.0 - 1.5 * square
    gas = 1.0 - solid
    keep = gas * (1.0 - 1.0 / 0.8)
    pull = gas * (density * (1.0 / 0.8))
    shares = {1: pull * (1.0 / 18.0), 2: pull * (1.0 / 36.0)}
    out = []
    for n, i in enumerate(flows):
        share = shares[sum(abs(c) for c in VELOCITY[i])]
        along = signed_sum([(VELOCITY[i][axis], speed[axis]) for axis in range(3)])
        feq = share * (base + 4.5 * along * along + 3.0 * along)
        out.append(keep * inward[n] + feq + solid * outward[TURNED[n]])
    level = (0.125 / 0.7) * hotness
    out.append((1.0 - 1.0 / 0.7) * inward[-1] + level * (1.0 + 4.0 * speed[0]))
    return out


def three_parts(value):
    high = value.astype(bf16).astype(f32)
    rest = value - high
    middle = rest.astype(bf16).astype(f32)
    return [high, middle, rest - middle]


def times_transposed(left, right):
    return lax.dot_general(
        left.astype(bf16), right.astype(bf16), (((1,), (1,)), ((), ())), preferred_element_type=f32
    )


def spread(row):
    return jnp.broadcast_to(row, (8, row.shape[-1]))


def lane_gather(row, lane):
    return jnp.take_along_axis(spread(row), lane, axis=1, mode="promise_in_bounds")


def table_gather(table, index):
    place, lane = index >> 7, index & 127
    out = jnp.zeros(index.shape, f32)
    for row in range(table.shape[0]):
        out = jnp.where(place == row, lane_gather(table[row : row + 1], lane), out)
    return out


def plane_rows(plane, first=0, count=8):
    return pl.ds(4 * first + plane, count, stride=4)


def stacked(row):
    return jnp.concatenate(
        [row[:, k * WIDTH : (k + 1) * WIDTH] for k in range(row.shape[1] // WIDTH)], axis=0
    )


def slot_tables(cap, voxel, dest, coeff, ordinal):
    rows_here = dest.shape[1]
    owner = dest[...].astype(f32)
    chunks = rows_here // WIDTH
    tall = stacked(owner)
    tall = jnp.concatenate([tall] + [jnp.zeros((8 - chunks, WIDTH), f32)] * (chunks < 8), axis=0)
    upright = tall.T
    first = lax.broadcasted_iota(jnp.int32, (WIDTH, WIDTH), 0)
    second = lax.broadcasted_iota(jnp.int32, (WIDTH, WIDTH), 1)
    slot_row = lax.broadcasted_iota(jnp.int32, (8, WIDTH), 0)
    table = jnp.zeros((40, WIDTH), f32)
    for c in range(chunks):
        lanes = slice(c * WIDTH, (c + 1) * WIDTH)
        here = owner[:, lanes]
        count = jnp.zeros((WIDTH, WIDTH), f32)
        for other in range(c + 1):
            same = upright[:, other : other + 1] == here
            if other == c:
                same = same & (first < second)
            count = count + jnp.where(same, 1.0, 0.0)
        rank = jnp.sum(count, axis=0, keepdims=True)
        place = (here * float(cap) + rank).astype(jnp.int32)
        ordinal[:, lanes] = place
        mine = slot_row == (place >> 7)
        spot = voxel[:, lanes]
        parts = [(spot >> 7).astype(f32), (spot & 127).astype(f32)] + three_parts(coeff[:, lanes])
        values = jnp.concatenate([jnp.where(mine, part, 0.0) for part in parts], axis=0)
        table = table + times_transposed(values, jnp.where(first == (place & 127), 1.0, 0.0))
    spots = table[0:8] * float(WIDTH) + table[8:16]
    coeffs = (table[16:24] + table[24:32]) + table[32:40]
    return spots, coeffs


def on_even(axis="sub"):
    return lax.rem(lax.axis_index(axis), 2) == 0


def first_kernel(cap, *refs):
    given, (post, to_near, to_next, ordinal) = refs[:6], refs[6:10]
    held, arrived = refs[10:16], refs[16]
    pops, heat, solid, voxel, dest, coeff = held
    pieces = [(given[n], held[n]) for n in (4, 3, 5)]
    for z in range(solid.shape[0]):
        pieces += [(given[n].at[:, z], held[n].at[:, z]) for n in (0, 1)]
        pieces.append((given[2].at[z], held[2].at[z]))
    copies = [
        pltpu.make_async_copy(source, target, arrived.at[n])
        for n, (source, target) in enumerate(pieces)
    ]
    for copy in copies:
        copy.start()
    layers, across, along = solid.shape
    even = on_even()
    for copy in copies[:3]:
        copy.wait()
    spots, coeffs = slot_tables(cap, voxel, dest, coeff, ordinal)
    extra = len(UP)
    for plane in (to_near, to_next):
        plane[extra] = jnp.zeros(plane.shape[1:], f32)
        plane[extra, :, 0:WIDTH] = spots
        plane[extra, :, WIDTH : 2 * WIDTH] = coeffs
    for z in range(layers):
        for copy in copies[3 + 3 * z : 6 + 3 * z]:
            copy.wait()
        for start in range(0, along, WIDTH):
            lanes = slice(start, start + WIDTH)
            out = collide(
                [pops[i, z, :, lanes] for i in range(FLOWS)],
                [heat[j, z, :, lanes] for j in range(HEATS)],
                solid[z, :, lanes],
            )
            for i in LANES_ALL:
                post[i, z, :, lanes] = out[i]
    for n, (above, below) in enumerate(zip(UP, DOWN)):
        above, below = post[above, layers - 1], post[below, 0]
        to_near[n] = jnp.where(even, above, below)
        to_next[n] = jnp.where(even, below, above)


def turned(tile, step):
    return tile if step == 0 else pltpu.roll(tile, step % tile.shape[1], 1)


def edge_kernel(post, to_a, to_b, out_r, out_l):
    layers, across, along = post.shape[1:]
    for out, lists, edge, inside in (
        (out_r, (STILL, RIGHT), across - 1, across - 2),
        (out_l, (STILL, LEFT), 0, 1),
    ):
        rows = [(i, edge) for i in lists[0]] + [(i, inside) for i in lists[1]]
        rows = rows + [(i, edge) for i in lists[1]]
        for n, (i, column) in enumerate(rows):
            for z in range(layers):
                at, source = n * layers + z, z - VELOCITY[i][2]
                if 0 <= source < layers:
                    out[at : at + 1, :] = post[i, source, column : column + 1, :]
                else:
                    out[at : at + 1, :] = jnp.zeros((1, along), f32)
    band_even = on_even("grp")

    def both(n):
        at = slice(n * layers, (n + 1) * layers)
        return jnp.concatenate([out_r[at, :], out_l[at, :]], axis=0)

    def send(n, tile):
        at = slice(n * layers, (n + 1) * layers)
        right, left = tile[0:layers], tile[layers : 2 * layers]
        to_a[at, :] = jnp.where(band_even, right, left)
        to_b[at, :] = jnp.where(band_even, left, right)

    sums = [[] for _ in range(SUMS)]
    for n, i in enumerate(STILL):
        _, ey, ez = VELOCITY[i]
        tile = turned(both(n), ey)
        if i >= FLOWS:
            sums[3].append((1, tile))
        else:
            sums[0].append((1, tile))
            sums[1].append((ey, tile))
            sums[2].append((ez, tile))
    for n in range(SUMS):
        send(n, signed_sum(sums[n]))
    for n, i in enumerate(RIGHT):
        send(SUMS + n, turned(both(len(STILL) + n), VELOCITY[i][1]))
    for n in range(len(STILL) + len(RIGHT), GATHERED):
        send(n - len(STILL) + SUMS, both(n))


def corner_shares(plane):
    across = plane.shape[1]
    up, right, left, ahead, behind = (
        place_of(UP, ex, ey, 1) for ex, ey in ((0, 0), (1, 0), (-1, 0), (0, 1), (0, -1))
    )
    warm = len(UP) - 1
    sides = []
    for column, inside, outward in ((across - 1, across - 2, right), (0, 1, left)):

        def row(n, at):
            return plane[n, at : at + 1, :]

        one, two = turned(row(ahead, column), 1), turned(row(behind, column), -1)
        rows = [
            row(up, column) + (one + two),
            one - two,
            row(warm, column),
            row(outward, inside),
            row(outward, column),
        ]
        sides.append(jnp.concatenate(rows, axis=0))
    return sides


def far_corner_kernel(next_, shares):
    shares[...] = jnp.zeros(shares.shape, f32)
    for n, side in enumerate(corner_shares(next_)):
        shares[8 * n : 8 * n + CORNER] = side


def corner_kernel(near, shares, solid, to_a, to_b):
    layers, across, along = solid.shape
    even = on_even()
    sides = []
    for n, (close, column) in enumerate(zip(corner_shares(near), (across - 1, 0))):
        far = shares[8 * n : 8 * n + CORNER]
        rows = [jnp.where(even, far, close), jnp.where(even, close, far)]
        rows += [solid[z, column : column + 1, :] for z in range(layers)]
        spare = to_a.shape[0] - 2 * CORNER - layers
        if spare:
            rows.append(jnp.zeros((spare, along), f32))
        sides.append(jnp.concatenate(rows, axis=0))
    band_even = on_even("grp")
    to_a[...] = jnp.where(band_even, sides[0], sides[1])
    to_b[...] = jnp.where(band_even, sides[1], sides[0])


def add_corners(face, corner, layers, whole):
    edge = SUMS + len(RIGHT)
    for first, z, rise in ((0, 0, 1), (CORNER, layers - 1, -1)):
        k = place_of(RIGHT, 1, 0, rise)
        adds = [(edge + k, 1, 4)]
        if whole:
            adds += [(0, 1, 0), (1, 1, 1), (2, rise, 0), (3, 1, 2), (SUMS + k, 1, 3)]
        for n, sign, row in adds:
            at = n * layers + z
            share = corner[first + row : first + row + 1]
            face[at : at + 1, :] = face[at : at + 1, :] + (share if sign > 0 else -share)


def second_kernel(
    post,
    near,
    next_,
    to_a,
    to_b,
    faces_a,
    faces_b,
    corner_a,
    corner_b,
    corners_a,
    corners_b,
    solid,
    own_table,
    tie,
    hot,
    motion,
    send_near,
    send_next,
    fluxes,
    moved,
    halo,
    own_r,
    own_l,
    from_l,
    from_r,
):
    layers, across, along = solid.shape
    even = on_even()
    band_even = on_even("grp")
    own_r[...] = jnp.where(band_even, to_a[...], to_b[...])
    own_l[...] = jnp.where(band_even, to_b[...], to_a[...])
    below = [jnp.where(even, next_[n], near[n]) for n in range(len(UP) + 1)]
    above = [jnp.where(even, near[n], next_[n]) for n in range(len(UP) + 1)]
    from_l[...] = jnp.where(band_even, faces_b[...], faces_a[...])
    from_r[...] = jnp.where(band_even, faces_a[...], faces_b[...])
    corners = []
    for face, one, two, whole in (
        (own_r, corner_a, corner_b, False),
        (own_l, corner_b, corner_a, False),
        (from_l, corners_b, corners_a, True),
        (from_r, corners_a, corners_b, True),
    ):
        corner = jnp.where(band_even, one[...], two[...])
        add_corners(face, corner, layers, whole)
        corners.append(corner)
    slot = lax.broadcasted_iota(jnp.int32, (across, along), 0)
    edge = SUMS + len(RIGHT)
    for i in LANES_ALL:
        ex, ey, ez = VELOCITY[i]
        for z in range(layers):
            if z - ez < 0:
                tile = below[UP.index(i)]
            elif z - ez >= layers:
                tile = above[DOWN.index(i)]
            else:
                tile = post[i, z - ez]
            if ex == 1:
                at = (edge + RIGHT.index(i)) * layers + z
                tile = jnp.where(slot == 0, from_l[at : at + 1, :], pltpu.roll(tile, 1, 0))
            elif ex == -1:
                at = (edge + LEFT.index(i)) * layers + z
                tile = jnp.where(
                    slot == across - 1, from_r[at : at + 1, :], pltpu.roll(tile, across - 1, 0)
                )
            moved[i, z] = turned(tile, ey)

    def halves(low, high, n):
        at = slice(n * layers, (n + 1) * layers)
        parts = [low[at, :], high[at, :]]
        if 2 * layers < 8:
            parts.append(jnp.ones((8 - 2 * layers, along), f32))
        return jnp.concatenate(parts, axis=0)

    for n in range(edge):
        halo[n] = halves(from_l, from_r, n)
    for n, i in enumerate(RIGHT):
        halo[edge + n] = turned(halves(own_l, own_r, edge + n), VELOCITY[i][1])
    edge_solid = [corner[2 * CORNER : 2 * CORNER + layers] for corner in corners[2:]]
    if 2 * layers < 8:
        edge_solid.append(jnp.zeros((8 - 2 * layers, along), f32))
    edge_solid = jnp.concatenate(edge_solid, axis=0)
    for start in range(0, along, WIDTH):
        lanes = slice(start, start + WIDTH)
        for z in range(layers):
            out = collide(
                [moved[i, z, :, lanes] for i in range(FLOWS)],
                [moved[FLOWS + j, z, :, lanes] for j in range(HEATS)],
                solid[z, :, lanes],
            )
            for i in LANES_ALL:
                moved[i, z, :, lanes] = out[i]
        out = collide_halo(
            [halo[n, :, lanes] for n in range(SUMS)],
            [halo[SUMS + n, :, lanes] for n in range(len(RIGHT))],
            [halo[edge + n, :, lanes] for n in range(len(RIGHT))],
            edge_solid[:, lanes],
        )
        for n in range(len(RIGHT)):
            halo[SUMS + n, :, lanes] = out[n]
    sums = {}

    def add(key, sign, tile):
        if sign == 0:
            return
        if key in sums:
            sums[key] = sums[key] + tile if sign > 0 else sums[key] - tile
        else:
            sums[key] = tile if sign > 0 else -tile

    for z in range(layers):
        for i in LANES_ALL:
            ex, ey, ez = VELOCITY[i]
            if i == 0:
                continue
            tile = moved[i, z]
            if ex == 1:
                side = halo[SUMS + RIGHT.index(i), z : z + 1, :]
                tile = jnp.where(slot == 0, side, pltpu.roll(tile, 1, 0))
            elif ex == -1:
                at = layers + z
                side = halo[SUMS + LEFT.index(i), at : at + 1, :]
                tile = jnp.where(slot == across - 1, side, pltpu.roll(tile, across - 1, 0))
            tile = turned(tile, ey)
            target = z + ez
            if i >= FLOWS:
                add((3, target), 1, tile)
            else:
                add((0, target), ex, tile)
                add((1, target), ey, tile)
                add((2, target), ez, tile)
    for z in range(layers):
        hot[z] = sums[3, z]
        for axis in range(3):
            motion[axis, z] = sums[axis, z]
    for part in range(4):
        send_near[part] = jnp.where(even, sums[part, layers], sums[part, -1])
        send_next[part] = jnp.where(even, sums[part, -1], sums[part, layers])
    extra = len(UP)
    per_line = along // WIDTH
    per_layer = across * per_line

    def flux(table, planes):
        index = table[:, 0:WIDTH].astype(jnp.int32)
        place, lane = index >> 7, index & 127
        out = jnp.zeros(lane.shape, f32)
        for z, plane in planes:
            for x in range(across):
                for c in range(per_line):
                    row = plane[x : x + 1, c * WIDTH : (c + 1) * WIDTH]
                    out = jnp.where(
                        place == z * per_layer + x * per_line + c, lane_gather(row, lane), out
                    )
        return out * table[:, WIDTH : 2 * WIDTH]

    mine = own_table[extra]
    fluxes[plane_rows(0), :] = flux(mine, [(z, sums[3, z]) for z in range(layers)])
    fluxes[plane_rows(1), :] = flux(above[extra], [(0, sums[3, layers])])
    fluxes[plane_rows(2), :] = flux(below[extra], [(layers - 1, sums[3, -1])])
    fluxes[plane_rows(3), :] = mine[:, WIDTH : 2 * WIDTH]


def sublane_gather(value, index):
    return jnp.take_along_axis(value, index, axis=0, mode="promise_in_bounds")


def coupled(vector, blocks, flipped, shift):
    count = vector.shape[0]
    upright = vector.T
    ahead, back = [], []
    for b in range(count):
        column = jnp.broadcast_to(upright[:, b : b + 1], blocks.shape[1:])
        back.append(jnp.sum(blocks[b] * column, axis=0, keepdims=True))
        ahead.append(jnp.sum(flipped[b] * column, axis=0, keepdims=True))
    ahead = jnp.concatenate(ahead, axis=0)
    back = jnp.concatenate(back, axis=0)
    block = lax.broadcasted_iota(jnp.int32, vector.shape, 0)
    ahead = sublane_gather(ahead, (block + shift) & (count - 1))
    return ahead + sublane_gather(back, (block - shift) & (count - 1))


def ready_kernel(
    pattern, nodes, diagonal, source, start, coupling, tie, hits, flipped, rest, slots, turn
):
    shift = pattern[0, 0]
    turn[...] = jnp.full(turn.shape, shift, jnp.int32)
    count = start.shape[1]
    for b in range(count):
        flipped[lax.rem(b + shift, count)] = coupling[0, b].T
    vector = start[0]
    rest[...] = (
        source[0] - diagonal[0] * vector + coupled(vector, coupling.at[0], flipped, turn[...])
    )
    index = stacked(nodes[...])
    slots[...] = table_gather(vector, index)
    upright = (index & 127).astype(f32).T.astype(jnp.int32)
    lane = lax.broadcasted_iota(jnp.int32, (WIDTH, WIDTH), 1)
    for s in range(index.shape[0]):
        hit = jnp.where(upright[:, s : s + 1] == lane, 1.0, 0.0)
        hits[s * WIDTH : (s + 1) * WIDTH] = hit.astype(bf16)


def solve_kernel(
    cap,
    turn,
    nodes,
    diagonal,
    start,
    coupling,
    hits,
    flipped,
    rest,
    slots,
    come,
    res,
    img,
    go,
):
    shift = turn[...]
    count = start.shape[1]
    index = stacked(nodes[...])
    place = index >> 7
    own, low, high, coeff = (come[plane_rows(plane), :] for plane in range(4))
    if cap == WIDTH:
        low = pltpu.roll(low, 1, 0)
        high = pltpu.roll(high, low.shape[0] - 1, 0)
    parts = three_parts(own + low + high) + three_parts(coeff)
    block = lax.broadcasted_iota(jnp.int32, (count, WIDTH), 0)
    values = []
    for s in range(index.shape[0]):
        mine = block == place[s : s + 1]
        values.append(
            jnp.concatenate([jnp.where(mine, part[s : s + 1], 0.0) for part in parts], axis=0)
        )
    values = jnp.concatenate(values, axis=1).astype(bf16)
    landed = jnp.dot(values, hits[...], preferred_element_type=f32)
    landed = [landed[k * count : (k + 1) * count] for k in range(len(parts))]
    added = (landed[0] + landed[1]) + landed[2]
    extra = (landed[3] + landed[4]) + landed[5]
    whole = diagonal[0] + extra
    blocks = coupling.at[0]
    residual = rest[...] + added - extra * start[0]
    image = whole * residual - coupled(residual, blocks, flipped, shift)

    def total(value):
        return jnp.sum(jnp.sum(value, axis=0, keepdims=True), axis=1, keepdims=True)

    offset = image - SHIFT * residual
    bend = whole * offset - coupled(offset, blocks, flipped, shift)
    totals = [
        total(residual * residual),
        total(residual * offset),
        total(offset * offset),
        total(offset * bend),
    ]
    res[...] = residual
    img[...] = image
    lane = lax.broadcasted_iota(jnp.int32, (8, WIDTH), 1) & (cap - 1)
    facts = jnp.zeros((8, WIDTH), f32)
    for n, fact in enumerate(totals):
        facts = jnp.where(lane == n, fact, facts)
    residual_slots = table_gather(residual, index)
    image_slots = table_gather(image, index)
    start_slots = slots[...]
    for group in range(0, go.shape[0] // 4, 8):
        go[plane_rows(0, group), :] = start_slots
        go[plane_rows(1, group), :] = residual_slots
        go[plane_rows(2, group), :] = image_slots
        go[plane_rows(3, group), :] = facts


def last_kernel(direct, come, own, start, res, img, ordinal, temp, seen):
    places = stacked(ordinal[...])
    chunks = places.shape[0]
    if chunks < 8:
        places = jnp.concatenate([places, jnp.zeros((8 - chunks, WIDTH), jnp.int32)], axis=0)
    found = []
    for plane in range(3):
        if direct:
            table = come[plane_rows(plane, lax.axis_index("grp") * 8), :]
        else:
            table = own[plane_rows(plane), :]
        found.append(table_gather(table, places))
    facts = come[plane_rows(3, 0, come.shape[0] // 4), :]
    facts = jnp.sum(facts, axis=0, keepdims=True)
    all_norm, cross, square, energy = (
        lane_gather(facts, jnp.full((8, WIDTH), n, jnp.int32)) for n in range(4)
    )
    product = SHIFT * all_norm + cross
    inverse = 1.0 / product
    ratio = cross / all_norm
    spread_square = square - cross * ratio
    energy = energy - ratio * (2.0 * (square + SHIFT * cross) - ratio * product)
    small = spread_square * inverse
    first = all_norm * inverse
    step = spread_square / (energy - spread_square * small)
    of_residual = first + step * (1.0 + small * first)
    of_image = -step * first
    temp[0] = start[0] + of_residual * res[...] + of_image * img[...]
    found = found[0] + of_residual * found[1] + of_image * found[2]
    for c in range(chunks):
        seen[:, c * WIDTH : (c + 1) * WIDTH] = found[c : c + 1]


def join_kernel(hot, motion, near, next_, hot_out, motion_out):
    layers = hot.shape[0]
    even = on_even()
    below = [jnp.where(even, next_[n], near[n]) for n in range(4)]
    above = [jnp.where(even, near[n], next_[n]) for n in range(4)]
    for z in range(layers):
        for part in range(4):
            tile = hot[z] if part == 3 else motion[part, z]
            if z == 0:
                tile = tile + below[part]
            if z == layers - 1:
                tile = tile + above[part]
            if part == 3:
                hot_out[z] = tile
            else:
                motion_out[part, z] = tile


VMEM = pl.BlockSpec(memory_space=pltpu.VMEM)
ANYWHERE = pl.BlockSpec(memory_space=pl.ANY)
SMEM = pl.BlockSpec(memory_space=pltpu.SMEM)


def call(kernel, out, args, name, scalars=(), scratch=(), far=False, flops=1 << 20):
    total = sum(int(np.prod(a.shape)) * a.dtype.itemsize for a in list(args) + list(out))
    if far:
        args = [pltpu.with_memory_space_constraint(a, pltpu.HBM) for a in args]
    return pl.pallas_call(
        kernel,
        out_shape=out,
        in_specs=[
            ANYWHERE if far else SMEM if n in scalars else VMEM for n in range(len(args))
        ],
        out_specs=[VMEM] * len(out),
        scratch_shapes=scratch,
        compiler_params=pltpu.CompilerParams(vmem_limit_bytes=24 << 20),
        cost_estimate=pl.CostEstimate(flops=flops, bytes_accessed=total, transcendentals=0),
        name=name,
    )(*args)


def shape(*dims, dtype=f32):
    return jax.ShapeDtypeStruct(dims, dtype)


def swaps(axis):
    count = lax.axis_size(axis)
    assert count % 2 == 0
    near = [(k, k + 1 - 2 * (k % 2)) for k in range(count)]
    return near, [(k, (k - 1 + 2 * (k % 2)) % count) for k in range(count)]


def body(
    populations,
    heat_pops,
    solid_frac,
    coupled_grid_point,
    dest_index,
    heat_coeff,
    slot_node,
    node_diag,
    coupling,
    block_pattern,
    heat_source,
    solid_start,
):
    layers, across, along = solid_frac.shape
    slabs, bands = lax.axis_size("sub"), lax.axis_size("grp")
    slots = slot_node.shape[1]
    cap = slots // slabs
    rows = coupled_grid_point.shape[1]
    blocks, piece = node_diag.shape[1:]
    lines = slots // WIDTH
    assert lines == 8 and across == 8 and along >= 2 * WIDTH and along % WIDTH == 0
    assert piece == WIDTH and blocks == 8 and WIDTH % cap == 0 and cap >= 8
    assert rows % WIDTH == 0 and rows <= 8 * WIDTH and layers <= 4
    gathered_rows = -(-GATHERED * layers // 8) * 8
    face_rows = -(-FACE * layers // 8) * 8
    planes = len(UP) + 1
    post, to_near, to_next, ordinal = call(
        functools.partial(first_kernel, cap),
        [
            shape(FLOWS + HEATS, layers, across, along),
            shape(planes, across, along),
            shape(planes, across, along),
            shape(1, rows, dtype=jnp.int32),
        ],
        [
            populations,
            heat_pops,
            solid_frac,
            coupled_grid_point,
            dest_index.reshape(1, rows),
            heat_coeff,
        ],
        "collide_first",
        scratch=[
            pltpu.VMEM(solid_like, kind)
            for solid_like, kind in (
                (populations.shape, f32),
                (heat_pops.shape, f32),
                (solid_frac.shape, f32),
                ((1, rows), jnp.int32),
                ((1, rows), jnp.int32),
                ((1, rows), f32),
            )
        ]
        + [pltpu.SemaphoreType.DMA((3 + 3 * layers,))],
        far=True,
    )
    near_pairs, next_pairs = swaps("sub")
    next_ = lax.ppermute(to_next, "sub", next_pairs)
    near = lax.ppermute(to_near, "sub", near_pairs)
    to_a, to_b = call(
        edge_kernel,
        [shape(face_rows, along)] * 2,
        [post],
        "x_faces",
        scratch=[pltpu.VMEM((gathered_rows, along), f32)] * 2,
    )
    side_a, side_b = swaps("grp")
    faces_a = lax.ppermute(to_a, "grp", side_a)
    faces_b = lax.ppermute(to_b, "grp", side_b)
    (shares,) = call(far_corner_kernel, [shape(16, along)], [next_], "far_corners")
    corner_a, corner_b = call(
        corner_kernel,
        [shape(-(-(2 * CORNER + layers) // 8) * 8, along)] * 2,
        [near, shares, solid_frac],
        "x_corners",
    )
    corners_a = lax.ppermute(corner_a, "grp", side_a)
    corners_b = lax.ppermute(corner_b, "grp", side_b)
    hits, flipped, rest, start_slots, turn = call(
        ready_kernel,
        [
            shape(slots, WIDTH, dtype=bf16),
            shape(blocks, piece, piece),
            shape(blocks, piece),
            shape(lines, WIDTH),
            shape(blocks, WIDTH, dtype=jnp.int32),
        ],
        [block_pattern, slot_node, node_diag, heat_source, solid_start, coupling, corner_a],
        "solid_ready",
        scalars=(0,),
    )
    hot, motion, send_near, send_next, fluxes = call(
        second_kernel,
        [
            shape(layers, across, along),
            shape(3, layers, across, along),
            shape(4, across, along),
            shape(4, across, along),
            shape(4 * lines, WIDTH),
        ],
        [
            post,
            near,
            next_,
            to_a,
            to_b,
            faces_a,
            faces_b,
            corner_a,
            corner_b,
            corners_a,
            corners_b,
            solid_frac,
            to_next,
            rest,
        ],
        "collide_second",
        scratch=[
            pltpu.VMEM((FLOWS + HEATS, layers, across, along), f32),
            pltpu.VMEM((FACE, 8, along), f32),
        ]
        + [pltpu.VMEM((face_rows, along), f32)] * 4,
    )
    settled = cap != WIDTH
    if settled:
        fluxes = fluxes.reshape(lines, 4, WIDTH // cap, cap).transpose(0, 2, 1, 3)
    fluxes = fluxes.reshape(slabs, 4, cap)
    landed = lax.all_to_all(fluxes, "sub", split_axis=0, concat_axis=0, tiled=True)
    if settled:
        landed = jnp.stack(
            [
                landed[:, 0],
                jnp.roll(landed[:, 1], 1, axis=0),
                jnp.roll(landed[:, 2], -1, axis=0),
                landed[:, 3],
            ]
        )
        landed = landed.reshape(4, lines, WIDTH).transpose(1, 0, 2)
    landed = landed.reshape(4 * lines, WIDTH)
    from_near = lax.ppermute(send_near, "sub", near_pairs)
    from_next = lax.ppermute(send_next, "sub", next_pairs)
    residual, image, go = call(
        functools.partial(solve_kernel, cap),
        [shape(blocks, piece), shape(blocks, piece), shape(bands * lines * 4, WIDTH)],
        [
            turn,
            slot_node,
            node_diag,
            solid_start,
            coupling,
            hits,
            flipped,
            rest,
            start_slots,
            landed,
        ],
        "solve",
    )
    if settled:
        go = go.reshape(bands, lines, 4, WIDTH // cap, cap).transpose(0, 1, 3, 2, 4)
    go = go.reshape(bands * slabs, 4, cap)
    come = lax.all_to_all(go, ("grp", "sub"), split_axis=0, concat_axis=0, tiled=True)
    hot_out, motion_out = call(
        join_kernel,
        [shape(*hot.shape), shape(*motion.shape)],
        [hot, motion, from_near, from_next],
        "join",
    )
    if settled:
        own = lax.dynamic_slice_in_dim(come, lax.axis_index("grp") * slabs, slabs, 0)
        own = own.transpose(1, 0, 2).reshape(4, lines, WIDTH).transpose(1, 0, 2)
        own = own.reshape(4 * lines, WIDTH)
        come = jnp.pad(come, ((0, 0), (0, 0), (0, WIDTH - cap)))
    else:
        own = rest
    come = come.reshape(4 * bands * slabs, WIDTH)
    temp, seen = call(
        functools.partial(last_kernel, not settled),
        [shape(1, blocks, piece), shape(1, rows)],
        [
            come,
            own,
            solid_start,
            residual,
            image,
            ordinal,
        ],
        "finish",
    )
    return hot_out, motion_out, temp, seen


def solution(mesh):
    placed = (
        P(None, "sub", "grp", None),
        P(None, "sub", "grp", None),
        P("sub", "grp", None),
        P("grp", "sub"),
        P("grp", "sub", None),
        P("grp", "sub"),
        P("grp", "sub"),
        P("grp", "sub", None),
        P("grp", "sub", None, None),
        P("grp", "sub"),
        P("grp", "sub", None),
        P("grp", "sub", None),
    )
    return jax.shard_map(
        body,
        mesh=mesh,
        in_specs=placed,
        out_specs=(
            P("sub", "grp", None),
            P(None, "sub", "grp", None),
            P("grp", "sub", None),
            P("grp", "sub"),
        ),
        check_vma=False,
    )
```

```python
import functools
import jax
import jax.numpy as jnp
import numpy as np
from jax import lax
from jax.experimental import pallas as pl
from jax.experimental.pallas import tpu as pltpu
from jax.sharding import PartitionSpec as P

FLOW_VELOCITY = [
    (0, 0, 0),
    (1, 0, 0),
    (-1, 0, 0),
    (0, 1, 0),
    (0, -1, 0),
    (0, 0, 1),
    (0, 0, -1),
    (1, 1, 0),
    (-1, -1, 0),
    (1, -1, 0),
    (-1, 1, 0),
    (1, 0, 1),
    (-1, 0, -1),
    (1, 0, -1),
    (-1, 0, 1),
    (0, 1, 1),
    (0, -1, -1),
    (0, 1, -1),
    (0, -1, 1),
]
VELOCITY = FLOW_VELOCITY + FLOW_VELOCITY[:7]
FLOWS, HEATS = 19, 7
LANES_ALL = range(FLOWS + HEATS)
UP = [i for i in LANES_ALL if VELOCITY[i][2] == 1]
DOWN = [
    next(j for j in LANES_ALL if VELOCITY[j] == VELOCITY[i][:2] + (-1,) and (j < 19) == (i < 19))
    for i in UP
]
RIGHT = [i for i in LANES_ALL if VELOCITY[i][0] == 1]
LEFT = [
    next(j for j in LANES_ALL if VELOCITY[j] == (-1,) + VELOCITY[i][1:] and (j < 19) == (i < 19))
    for i in RIGHT
]
TURNED = [
    next(n for n, j in enumerate(RIGHT[:-1]) if VELOCITY[j][1:] == (-VELOCITY[i][1], -VELOCITY[i][2]))
    for i in RIGHT[:-1]
]
STILL = [i for i in LANES_ALL if VELOCITY[i][0] == 0]
GATHERED = len(STILL) + 2 * len(RIGHT)
SUMS = 4
FACE = SUMS + 2 * len(RIGHT) + 1
CORNER = 5


def place_of(lists, ex, ey, ez):
    return next(n for n, i in enumerate(lists) if VELOCITY[i] == (ex, ey, ez))


WIDTH = 128
SHIFT = 4.0
f32 = jnp.float32
bf16 = jnp.bfloat16


def signed_sum(terms):
    total = None
    for sign, term in terms:
        if sign == 0:
            continue
        if total is None:
            total = term if sign > 0 else -term
        else:
            total = total + term if sign > 0 else total - term
    return total


def collide(flow, heat, solid):
    pairs = range(1, FLOWS, 2)
    density = flow[0]
    for i in pairs:
        density = density + (flow[i] + flow[i + 1])
    gaps = {i: flow[i] - flow[i + 1] for i in pairs}
    scale = 1.0 / density
    speed = [
        signed_sum([(FLOW_VELOCITY[i][axis], gaps[i]) for i in pairs]) * scale for axis in range(3)
    ]
    square = speed[0] * speed[0] + speed[1] * speed[1] + speed[2] * speed[2]
    base = 1.0 - 1.5 * square
    gas = 1.0 - solid
    keep = gas * (1.0 - 1.0 / 0.8)
    pull = gas * (density * (1.0 / 0.8))
    flow_post = [None] * FLOWS
    flow_post[0] = (keep + solid) * flow[0] + (pull * (1.0 / 3.0)) * base
    shares = {1: pull * (1.0 / 18.0), 2: pull * (1.0 / 36.0)}
    for i in pairs:
        share = shares[sum(abs(c) for c in FLOW_VELOCITY[i])]
        along = signed_sum([(FLOW_VELOCITY[i][axis], speed[axis]) for axis in range(3)])
        even = base + 4.5 * along * along
        odd = 3.0 * along
        flow_post[i] = keep * flow[i] + share * (even + odd) + solid * flow[i + 1]
        flow_post[i + 1] = keep * flow[i + 1] + share * (even - odd) + solid * flow[i]
    hotness = heat[0]
    for j in range(1, HEATS):
        hotness = hotness + heat[j]
    stay = 1.0 - 1.0 / 0.7
    heat_post = [stay * heat[0] + (0.25 / 0.7) * hotness]
    level = (0.125 / 0.7) * hotness
    for j in range(1, HEATS, 2):
        axis = (j - 1) // 2
        drift = 4.0 * speed[axis]
        heat_post.append(stay * heat[j] + level * (1.0 + drift))
        heat_post.append(stay * heat[j + 1] + level * (1.0 - drift))
    return flow_post + heat_post


def collide_halo(still, inward, outward, solid):
    flows = RIGHT[:-1]
    density, along_y, along_z, hotness = still
    pairs = [(a + b, a - b) for a, b in zip(inward, outward)]
    across = None
    for n, i in enumerate(flows):
        _, ey, ez = VELOCITY[i]
        whole, gap = pairs[n]
        density = density + whole
        across = gap if across is None else across + gap
        along_y = signed_sum([(1, along_y), (ey, whole)])
        along_z = signed_sum([(1, along_z), (ez, whole)])
    hotness = hotness + pairs[-1][0]
    scale = 1.0 / density
    speed = [across * scale, along_y * scale, along_z * scale]
    square = speed[0] * speed[0] + speed[1] * speed[1] + speed[2] * speed[2]
    base = 1.0 - 1.5 * square
    gas = 1.0 - solid
    keep = gas * (1.0 - 1.0 / 0.8)
    pull = gas * (density * (1.0 / 0.8))
    shares = {1: pull * (1.0 / 18.0), 2: pull * (1.0 / 36.0)}
    out = []
    for n, i in enumerate(flows):
        share = shares[sum(abs(c) for c in VELOCITY[i])]
        along = signed_sum([(VELOCITY[i][axis], speed[axis]) for axis in range(3)])
        feq = share * (base + 4.5 * along * along + 3.0 * along)
        out.append(keep * inward[n] + feq + solid * outward[TURNED[n]])
    level = (0.125 / 0.7) * hotness
    out.append((1.0 - 1.0 / 0.7) * inward[-1] + level * (1.0 + 4.0 * speed[0]))
    return out


def three_parts(value):
    high = value.astype(bf16).astype(f32)
    rest = value - high
    middle = rest.astype(bf16).astype(f32)
    return [high, middle, rest - middle]


def times_transposed(left, right):
    return lax.dot_general(
        left.astype(bf16), right.astype(bf16), (((1,), (1,)), ((), ())), preferred_element_type=f32
    )


def spread(row):
    return jnp.broadcast_to(row, (8, row.shape[-1]))


def lane_gather(row, lane):
    return jnp.take_along_axis(spread(row), lane, axis=1, mode="promise_in_bounds")


def table_gather(table, index):
    place, lane = index >> 7, index & 127
    out = jnp.zeros(index.shape, f32)
    for row in range(table.shape[0]):
        out = jnp.where(place == row, lane_gather(table[row : row + 1], lane), out)
    return out


def plane_rows(plane, first=0, count=8):
    return pl.ds(4 * first + plane, count, stride=4)


def stacked(row):
    return jnp.concatenate(
        [row[:, k * WIDTH : (k + 1) * WIDTH] for k in range(row.shape[1] // WIDTH)], axis=0
    )


def slot_tables(cap, voxel, dest, coeff, ordinal):
    rows_here = dest.shape[1]
    owner = dest[...].astype(f32)
    chunks = rows_here // WIDTH
    tall = stacked(owner)
    tall = jnp.concatenate([tall] + [jnp.zeros((8 - chunks, WIDTH), f32)] * (chunks < 8), axis=0)
    upright = tall.T
    first = lax.broadcasted_iota(jnp.int32, (WIDTH, WIDTH), 0)
    second = lax.broadcasted_iota(jnp.int32, (WIDTH, WIDTH), 1)
    slot_row = lax.broadcasted_iota(jnp.int32, (8, WIDTH), 0)
    table = jnp.zeros((40, WIDTH), f32)
    for c in range(chunks):
        lanes = slice(c * WIDTH, (c + 1) * WIDTH)
        here = owner[:, lanes]
        count = jnp.zeros((WIDTH, WIDTH), f32)
        for other in range(c + 1):
            same = upright[:, other : other + 1] == here
            if other == c:
                same = same & (first < second)
            count = count + jnp.where(same, 1.0, 0.0)
        rank = jnp.sum(count, axis=0, keepdims=True)
        place = (here * float(cap) + rank).astype(jnp.int32)
        ordinal[:, lanes] = place
        mine = slot_row == (place >> 7)
        spot = voxel[:, lanes]
        parts = [(spot >> 7).astype(f32), (spot & 127).astype(f32)] + three_parts(coeff[:, lanes])
        values = jnp.concatenate([jnp.where(mine, part, 0.0) for part in parts], axis=0)
        table = table + times_transposed(values, jnp.where(first == (place & 127), 1.0, 0.0))
    spots = table[0:8] * float(WIDTH) + table[8:16]
    coeffs = (table[16:24] + table[24:32]) + table[32:40]
    return spots, coeffs


def on_even(axis="sub"):
    return lax.rem(lax.axis_index(axis), 2) == 0


def turned(tile, step):
    return tile if step == 0 else pltpu.roll(tile, step % tile.shape[1], 1)


def corner_shares(plane):
    across = plane.shape[1]
    up, right, left, ahead, behind = (
        place_of(UP, ex, ey, 1) for ex, ey in ((0, 0), (1, 0), (-1, 0), (0, 1), (0, -1))
    )
    warm = len(UP) - 1
    sides = []
    for column, inside, outward in ((across - 1, across - 2, right), (0, 1, left)):

        def row(n, at):
            return plane[n, at : at + 1, :]

        one, two = turned(row(ahead, column), 1), turned(row(behind, column), -1)
        rows = [
            row(up, column) + (one + two),
            one - two,
            row(warm, column),
            row(outward, inside),
            row(outward, column),
        ]
        sides.append(jnp.concatenate(rows, axis=0))
    return sides


def add_corners(face, below, above, layers):
    edge = SUMS + len(RIGHT)
    for corner, z, rise in ((below, 0, 1), (above, layers - 1, -1)):
        k = place_of(RIGHT, 1, 0, rise)
        adds = [(0, 1, 0), (1, 1, 1), (2, rise, 0), (3, 1, 2), (SUMS + k, 1, 3), (edge + k, 1, 4)]
        for n, sign, row in adds:
            at = n * layers + z
            share = corner[row : row + 1]
            face[at : at + 1, :] = face[at : at + 1, :] + (share if sign > 0 else -share)


def first_kernel(cap, *refs):
    given, (post, to_near, to_next, shares, ordinal) = refs[:6], refs[6:11]
    held, arrived = refs[11:17], refs[17]
    pops, heat, solid, voxel, dest, coeff = held
    pieces = [(given[n], held[n]) for n in (4, 3, 5)]
    for z in range(solid.shape[0]):
        pieces += [(given[n].at[:, z], held[n].at[:, z]) for n in (0, 1)]
        pieces.append((given[2].at[z], held[2].at[z]))
    copies = [
        pltpu.make_async_copy(source, target, arrived.at[n])
        for n, (source, target) in enumerate(pieces)
    ]
    for copy in copies:
        copy.start()
    layers, across, along = solid.shape
    even = on_even()
    for copy in copies[:3]:
        copy.wait()
    spots, coeffs = slot_tables(cap, voxel, dest, coeff, ordinal)
    extra = len(UP)
    for plane in (to_near, to_next):
        plane[extra] = jnp.zeros(plane.shape[1:], f32)
        plane[extra, :, 0:WIDTH] = spots
        plane[extra, :, WIDTH : 2 * WIDTH] = coeffs
    for z in range(layers):
        for copy in copies[3 + 3 * z : 6 + 3 * z]:
            copy.wait()
        for start in range(0, along, WIDTH):
            lanes = slice(start, start + WIDTH)
            out = collide(
                [pops[i, z, :, lanes] for i in range(FLOWS)],
                [heat[j, z, :, lanes] for j in range(HEATS)],
                solid[z, :, lanes],
            )
            for i in LANES_ALL:
                post[i, z, :, lanes] = out[i]
    for n, (above, below) in enumerate(zip(UP, DOWN)):
        above, below = post[above, layers - 1], post[below, 0]
        to_near[n] = jnp.where(even, above, below)
        to_next[n] = jnp.where(even, below, above)
    shares[...] = jnp.zeros(shares.shape, f32)
    for n, side in enumerate(corner_shares(to_next)):
        shares[8 * n : 8 * n + CORNER] = side


def edge_kernel(post, shares, solid, face_r, face_l, out_r, out_l):
    layers, across, along = post.shape[1:]
    for out, lists, edge, inside in (
        (out_r, (STILL, RIGHT), across - 1, across - 2),
        (out_l, (STILL, LEFT), 0, 1),
    ):
        rows = [(i, edge) for i in lists[0]] + [(i, inside) for i in lists[1]]
        rows = rows + [(i, edge) for i in lists[1]]
        for n, (i, column) in enumerate(rows):
            for z in range(layers):
                at, source = n * layers + z, z - VELOCITY[i][2]
                if 0 <= source < layers:
                    out[at : at + 1, :] = post[i, source, column : column + 1, :]
                else:
                    out[at : at + 1, :] = jnp.zeros((1, along), f32)

    def both(n):
        at = slice(n * layers, (n + 1) * layers)
        return jnp.concatenate([out_r[at, :], out_l[at, :]], axis=0)

    def send(n, tile):
        at = slice(n * layers, (n + 1) * layers)
        face_r[at, :], face_l[at, :] = tile[0:layers], tile[layers : 2 * layers]

    sums = [[] for _ in range(SUMS)]
    for n, i in enumerate(STILL):
        _, ey, ez = VELOCITY[i]
        tile = turned(both(n), ey)
        if i >= FLOWS:
            sums[3].append((1, tile))
        else:
            sums[0].append((1, tile))
            sums[1].append((ey, tile))
            sums[2].append((ez, tile))
    for n in range(SUMS):
        send(n, signed_sum(sums[n]))
    for n, i in enumerate(RIGHT):
        send(SUMS + n, turned(both(len(STILL) + n), VELOCITY[i][1]))
    for n in range(len(STILL) + len(RIGHT), GATHERED):
        send(n - len(STILL) + SUMS, both(n))
    even = on_even()
    for n, (face, column) in enumerate(((face_r, across - 1), (face_l, 0))):
        for z in range(layers):
            at = (FACE - 1) * layers + z
            face[at : at + 1, :] = solid[z, column : column + 1, :]
        far = shares[8 * n : 8 * n + CORNER]
        add_corners(face, jnp.where(even, far, 0.0), jnp.where(even, 0.0, far), layers)


def side_kernel(layers, near, face_r, face_l, to_a, to_b, sum_r, sum_l):
    even, band_even = on_even(), on_even("grp")
    sides = zip((face_r, face_l), (sum_r, sum_l), corner_shares(near))
    for face, total, close in sides:
        total[...] = face[...]
        add_corners(total, jnp.where(even, 0.0, close), jnp.where(even, close, 0.0), layers)
    right, left = sum_r[...], sum_l[...]
    to_a[...] = jnp.where(band_even, right, left)
    to_b[...] = jnp.where(band_even, left, right)


def second_kernel(
    post,
    near,
    next_,
    to_a,
    to_b,
    faces_a,
    faces_b,
    solid,
    own_table,
    tie,
    hot,
    motion,
    send_near,
    send_next,
    fluxes,
    moved,
    halo,
    own_r,
    own_l,
    from_l,
    from_r,
):
    layers, across, along = solid.shape
    even = on_even()
    band_even = on_even("grp")
    own_r[...] = jnp.where(band_even, to_a[...], to_b[...])
    own_l[...] = jnp.where(band_even, to_b[...], to_a[...])
    below = [jnp.where(even, next_[n], near[n]) for n in range(len(UP) + 1)]
    above = [jnp.where(even, near[n], next_[n]) for n in range(len(UP) + 1)]
    from_l[...] = jnp.where(band_even, faces_b[...], faces_a[...])
    from_r[...] = jnp.where(band_even, faces_a[...], faces_b[...])
    slot = lax.broadcasted_iota(jnp.int32, (across, along), 0)
    edge = SUMS + len(RIGHT)
    for i in LANES_ALL:
        ex, ey, ez = VELOCITY[i]
        for z in range(layers):
            if z - ez < 0:
                tile = below[UP.index(i)]
            elif z - ez >= layers:
                tile = above[DOWN.index(i)]
            else:
                tile = post[i, z - ez]
            if ex == 1:
                at = (edge + RIGHT.index(i)) * layers + z
                tile = jnp.where(slot == 0, from_l[at : at + 1, :], pltpu.roll(tile, 1, 0))
            elif ex == -1:
                at = (edge + LEFT.index(i)) * layers + z
                tile = jnp.where(
                    slot == across - 1, from_r[at : at + 1, :], pltpu.roll(tile, across - 1, 0)
                )
            moved[i, z] = turned(tile, ey)

    def halves(low, high, n):
        at = slice(n * layers, (n + 1) * layers)
        parts = [low[at, :], high[at, :]]
        if 2 * layers < 8:
            parts.append(jnp.ones((8 - 2 * layers, along), f32))
        return jnp.concatenate(parts, axis=0)

    for n in range(edge):
        halo[n] = halves(from_l, from_r, n)
    for n, i in enumerate(RIGHT):
        halo[edge + n] = turned(halves(own_l, own_r, edge + n), VELOCITY[i][1])
    edge_solid = halves(from_l, from_r, FACE - 1)
    for start in range(0, along, WIDTH):
        lanes = slice(start, start + WIDTH)
        for z in range(layers):
            out = collide(
                [moved[i, z, :, lanes] for i in range(FLOWS)],
                [moved[FLOWS + j, z, :, lanes] for j in range(HEATS)],
                solid[z, :, lanes],
            )
            for i in LANES_ALL:
                moved[i, z, :, lanes] = out[i]
        out = collide_halo(
            [halo[n, :, lanes] for n in range(SUMS)],
            [halo[SUMS + n, :, lanes] for n in range(len(RIGHT))],
            [halo[edge + n, :, lanes] for n in range(len(RIGHT))],
            edge_solid[:, lanes],
        )
        for n in range(len(RIGHT)):
            halo[SUMS + n, :, lanes] = out[n]
    sums = {}

    def add(key, sign, tile):
        if sign == 0:
            return
        if key in sums:
            sums[key] = sums[key] + tile if sign > 0 else sums[key] - tile
        else:
            sums[key] = tile if sign > 0 else -tile

    for z in range(layers):
        for i in LANES_ALL:
            ex, ey, ez = VELOCITY[i]
            if i == 0:
                continue
            tile = moved[i, z]
            if ex == 1:
                side = halo[SUMS + RIGHT.index(i), z : z + 1, :]
                tile = jnp.where(slot == 0, side, pltpu.roll(tile, 1, 0))
            elif ex == -1:
                at = layers + z
                side = halo[SUMS + LEFT.index(i), at : at + 1, :]
                tile = jnp.where(slot == across - 1, side, pltpu.roll(tile, across - 1, 0))
            tile = turned(tile, ey)
            target = z + ez
            if i >= FLOWS:
                add((3, target), 1, tile)
            else:
                add((0, target), ex, tile)
                add((1, target), ey, tile)
                add((2, target), ez, tile)
    for z in range(layers):
        hot[z] = sums[3, z]
        for axis in range(3):
            motion[axis, z] = sums[axis, z]
    for part in range(4):
        send_near[part] = jnp.where(even, sums[part, layers], sums[part, -1])
        send_next[part] = jnp.where(even, sums[part, -1], sums[part, layers])
    extra = len(UP)
    per_line = along // WIDTH
    per_layer = across * per_line

    def flux(table, planes):
        index = table[:, 0:WIDTH].astype(jnp.int32)
        place, lane = index >> 7, index & 127
        out = jnp.zeros(lane.shape, f32)
        for z, plane in planes:
            for x in range(across):
                for c in range(per_line):
                    row = plane[x : x + 1, c * WIDTH : (c + 1) * WIDTH]
                    out = jnp.where(
                        place == z * per_layer + x * per_line + c, lane_gather(row, lane), out
                    )
        return out * table[:, WIDTH : 2 * WIDTH]

    mine = own_table[extra]
    fluxes[plane_rows(0), :] = flux(mine, [(z, sums[3, z]) for z in range(layers)])
    fluxes[plane_rows(1), :] = flux(above[extra], [(0, sums[3, layers])])
    fluxes[plane_rows(2), :] = flux(below[extra], [(layers - 1, sums[3, -1])])
    fluxes[plane_rows(3), :] = mine[:, WIDTH : 2 * WIDTH]


def sublane_gather(value, index):
    return jnp.take_along_axis(value, index, axis=0, mode="promise_in_bounds")


def coupled(vector, blocks, flipped, shift):
    count = vector.shape[0]
    upright = vector.T
    ahead, back = [], []
    for b in range(count):
        column = jnp.broadcast_to(upright[:, b : b + 1], blocks.shape[1:])
        back.append(jnp.sum(blocks[b] * column, axis=0, keepdims=True))
        ahead.append(jnp.sum(flipped[b] * column, axis=0, keepdims=True))
    ahead = jnp.concatenate(ahead, axis=0)
    back = jnp.concatenate(back, axis=0)
    block = lax.broadcasted_iota(jnp.int32, vector.shape, 0)
    ahead = sublane_gather(ahead, (block + shift) & (count - 1))
    return ahead + sublane_gather(back, (block - shift) & (count - 1))


def ready_kernel(
    pattern, nodes, diagonal, source, start, coupling, tie, hits, flipped, rest, slots, turn
):
    shift = pattern[0, 0]
    turn[...] = jnp.full(turn.shape, shift, jnp.int32)
    count = start.shape[1]
    for b in range(count):
        flipped[lax.rem(b + shift, count)] = coupling[0, b].T
    vector = start[0]
    rest[...] = (
        source[0] - diagonal[0] * vector + coupled(vector, coupling.at[0], flipped, turn[...])
    )
    index = stacked(nodes[...])
    slots[...] = table_gather(vector, index)
    upright = (index & 127).astype(f32).T.astype(jnp.int32)
    lane = lax.broadcasted_iota(jnp.int32, (WIDTH, WIDTH), 1)
    for s in range(index.shape[0]):
        hit = jnp.where(upright[:, s : s + 1] == lane, 1.0, 0.0)
        hits[s * WIDTH : (s + 1) * WIDTH] = hit.astype(bf16)


def solve_kernel(
    cap,
    turn,
    nodes,
    diagonal,
    start,
    coupling,
    hits,
    flipped,
    rest,
    slots,
    come,
    res,
    img,
    go,
):
    shift = turn[...]
    count = start.shape[1]
    index = stacked(nodes[...])
    place = index >> 7
    own, low, high, coeff = (come[plane_rows(plane), :] for plane in range(4))
    if cap == WIDTH:
        low = pltpu.roll(low, 1, 0)
        high = pltpu.roll(high, low.shape[0] - 1, 0)
    parts = three_parts(own + low + high) + three_parts(coeff)
    block = lax.broadcasted_iota(jnp.int32, (count, WIDTH), 0)
    values = []
    for s in range(index.shape[0]):
        mine = block == place[s : s + 1]
        values.append(
            jnp.concatenate([jnp.where(mine, part[s : s + 1], 0.0) for part in parts], axis=0)
        )
    values = jnp.concatenate(values, axis=1).astype(bf16)
    landed = jnp.dot(values, hits[...], preferred_element_type=f32)
    landed = [landed[k * count : (k + 1) * count] for k in range(len(parts))]
    added = (landed[0] + landed[1]) + landed[2]
    extra = (landed[3] + landed[4]) + landed[5]
    whole = diagonal[0] + extra
    blocks = coupling.at[0]
    residual = rest[...] + added - extra * start[0]
    image = whole * residual - coupled(residual, blocks, flipped, shift)

    def total(value):
        return jnp.sum(jnp.sum(value, axis=0, keepdims=True), axis=1, keepdims=True)

    offset = image - SHIFT * residual
    bend = whole * offset - coupled(offset, blocks, flipped, shift)
    totals = [
        total(residual * residual),
        total(residual * offset),
        total(offset * offset),
        total(offset * bend),
    ]
    res[...] = residual
    img[...] = image
    lane = lax.broadcasted_iota(jnp.int32, (8, WIDTH), 1) & (cap - 1)
    facts = jnp.zeros((8, WIDTH), f32)
    for n, fact in enumerate(totals):
        facts = jnp.where(lane == n, fact, facts)
    residual_slots = table_gather(residual, index)
    image_slots = table_gather(image, index)
    start_slots = slots[...]
    for group in range(0, go.shape[0] // 4, 8):
        go[plane_rows(0, group), :] = start_slots
        go[plane_rows(1, group), :] = residual_slots
        go[plane_rows(2, group), :] = image_slots
        go[plane_rows(3, group), :] = facts


def last_kernel(direct, come, own, start, res, img, ordinal, temp, seen):
    places = stacked(ordinal[...])
    chunks = places.shape[0]
    if chunks < 8:
        places = jnp.concatenate([places, jnp.zeros((8 - chunks, WIDTH), jnp.int32)], axis=0)
    found = []
    for plane in range(3):
        if direct:
            table = come[plane_rows(plane, lax.axis_index("grp") * 8), :]
        else:
            table = own[plane_rows(plane), :]
        found.append(table_gather(table, places))
    facts = come[plane_rows(3, 0, come.shape[0] // 4), :]
    facts = jnp.sum(facts, axis=0, keepdims=True)
    all_norm, cross, square, energy = (
        lane_gather(facts, jnp.full((8, WIDTH), n, jnp.int32)) for n in range(4)
    )
    product = SHIFT * all_norm + cross
    inverse = 1.0 / product
    ratio = cross / all_norm
    spread_square = square - cross * ratio
    energy = energy - ratio * (2.0 * (square + SHIFT * cross) - ratio * product)
    small = spread_square * inverse
    first = all_norm * inverse
    step = spread_square / (energy - spread_square * small)
    of_residual = first + step * (1.0 + small * first)
    of_image = -step * first
    temp[0] = start[0] + of_residual * res[...] + of_image * img[...]
    found = found[0] + of_residual * found[1] + of_image * found[2]
    for c in range(chunks):
        seen[:, c * WIDTH : (c + 1) * WIDTH] = found[c : c + 1]


def join_kernel(hot, motion, near, next_, hot_out, motion_out):
    layers = hot.shape[0]
    even = on_even()
    below = [jnp.where(even, next_[n], near[n]) for n in range(4)]
    above = [jnp.where(even, near[n], next_[n]) for n in range(4)]
    for z in range(layers):
        for part in range(4):
            tile = hot[z] if part == 3 else motion[part, z]
            if z == 0:
                tile = tile + below[part]
            if z == layers - 1:
                tile = tile + above[part]
            if part == 3:
                hot_out[z] = tile
            else:
                motion_out[part, z] = tile


VMEM = pl.BlockSpec(memory_space=pltpu.VMEM)
ANYWHERE = pl.BlockSpec(memory_space=pl.ANY)
SMEM = pl.BlockSpec(memory_space=pltpu.SMEM)


def call(kernel, out, args, name, scalars=(), scratch=(), far=False, flops=1 << 20):
    total = sum(int(np.prod(a.shape)) * a.dtype.itemsize for a in list(args) + list(out))
    if far:
        args = [pltpu.with_memory_space_constraint(a, pltpu.HBM) for a in args]
    return pl.pallas_call(
        kernel,
        out_shape=out,
        in_specs=[
            ANYWHERE if far else SMEM if n in scalars else VMEM for n in range(len(args))
        ],
        out_specs=[VMEM] * len(out),
        scratch_shapes=scratch,
        compiler_params=pltpu.CompilerParams(vmem_limit_bytes=24 << 20),
        cost_estimate=pl.CostEstimate(flops=flops, bytes_accessed=total, transcendentals=0),
        name=name,
    )(*args)


def shape(*dims, dtype=f32):
    return jax.ShapeDtypeStruct(dims, dtype)


def swaps(axis):
    count = lax.axis_size(axis)
    assert count % 2 == 0
    near = [(k, k + 1 - 2 * (k % 2)) for k in range(count)]
    return near, [(k, (k - 1 + 2 * (k % 2)) % count) for k in range(count)]


def body(
    populations,
    heat_pops,
    solid_frac,
    coupled_grid_point,
    dest_index,
    heat_coeff,
    slot_node,
    node_diag,
    coupling,
    block_pattern,
    heat_source,
    solid_start,
):
    layers, across, along = solid_frac.shape
    slabs, bands = lax.axis_size("sub"), lax.axis_size("grp")
    slots = slot_node.shape[1]
    cap = slots // slabs
    rows = coupled_grid_point.shape[1]
    blocks, piece = node_diag.shape[1:]
    lines = slots // WIDTH
    assert lines == 8 and across == 8 and along >= 2 * WIDTH and along % WIDTH == 0
    assert piece == WIDTH and blocks == 8 and WIDTH % cap == 0 and cap >= 8
    assert rows % WIDTH == 0 and rows <= 8 * WIDTH and layers <= 4
    gathered_rows = -(-GATHERED * layers // 8) * 8
    face_rows = -(-FACE * layers // 8) * 8
    planes = len(UP) + 1
    post, to_near, to_next, to_shares, ordinal = call(
        functools.partial(first_kernel, cap),
        [
            shape(FLOWS + HEATS, layers, across, along),
            shape(planes, across, along),
            shape(planes, across, along),
            shape(16, along),
            shape(1, rows, dtype=jnp.int32),
        ],
        [
            populations,
            heat_pops,
            solid_frac,
            coupled_grid_point,
            dest_index.reshape(1, rows),
            heat_coeff,
        ],
        "collide_first",
        scratch=[
            pltpu.VMEM(solid_like, kind)
            for solid_like, kind in (
                (populations.shape, f32),
                (heat_pops.shape, f32),
                (solid_frac.shape, f32),
                ((1, rows), jnp.int32),
                ((1, rows), jnp.int32),
                ((1, rows), f32),
            )
        ]
        + [pltpu.SemaphoreType.DMA((3 + 3 * layers,))],
        far=True,
    )
    near_pairs, next_pairs = swaps("sub")
    shares = lax.ppermute(to_shares, "sub", next_pairs)
    near = lax.ppermute(to_near, "sub", near_pairs)
    next_ = lax.ppermute(to_next, "sub", next_pairs)
    faces = [shape(face_rows, along)] * 2
    face_r, face_l = call(
        edge_kernel,
        faces,
        [post, shares, solid_frac],
        "x_faces",
        scratch=[pltpu.VMEM((gathered_rows, along), f32)] * 2,
        flops=1 << 32,
    )
    to_a, to_b = call(
        functools.partial(side_kernel, layers),
        faces,
        [near, face_r, face_l],
        "x_sides",
        scratch=[pltpu.VMEM((face_rows, along), f32)] * 2,
    )
    side_a, side_b = swaps("grp")
    faces_a = lax.ppermute(to_a, "grp", side_a)
    faces_b = lax.ppermute(to_b, "grp", side_b)
    hits, flipped, rest, start_slots, turn = call(
        ready_kernel,
        [
            shape(slots, WIDTH, dtype=bf16),
            shape(blocks, piece, piece),
            shape(blocks, piece),
            shape(lines, WIDTH),
            shape(blocks, WIDTH, dtype=jnp.int32),
        ],
        [block_pattern, slot_node, node_diag, heat_source, solid_start, coupling, to_a],
        "solid_ready",
        scalars=(0,),
    )
    hot, motion, send_near, send_next, fluxes = call(
        second_kernel,
        [
            shape(layers, across, along),
            shape(3, layers, across, along),
            shape(4, across, along),
            shape(4, across, along),
            shape(4 * lines, WIDTH),
        ],
        [
            post,
            near,
            next_,
            to_a,
            to_b,
            faces_a,
            faces_b,
            solid_frac,
            to_next,
            rest,
        ],
        "collide_second",
        scratch=[
            pltpu.VMEM((FLOWS + HEATS, layers, across, along), f32),
            pltpu.VMEM((FACE, 8, along), f32),
        ]
        + [pltpu.VMEM((face_rows, along), f32)] * 4,
    )
    settled = cap != WIDTH
    if settled:
        fluxes = fluxes.reshape(lines, 4, WIDTH // cap, cap).transpose(0, 2, 1, 3)
    fluxes = fluxes.reshape(slabs, 4, cap)
    landed = lax.all_to_all(fluxes, "sub", split_axis=0, concat_axis=0, tiled=True)
    if settled:
        landed = jnp.stack(
            [
                landed[:, 0],
                jnp.roll(landed[:, 1], 1, axis=0),
                jnp.roll(landed[:, 2], -1, axis=0),
                landed[:, 3],
            ]
        )
        landed = landed.reshape(4, lines, WIDTH).transpose(1, 0, 2)
    landed = landed.reshape(4 * lines, WIDTH)
    from_near = lax.ppermute(send_near, "sub", near_pairs)
    from_next = lax.ppermute(send_next, "sub", next_pairs)
    residual, image, go = call(
        functools.partial(solve_kernel, cap),
        [shape(blocks, piece), shape(blocks, piece), shape(bands * lines * 4, WIDTH)],
        [
            turn,
            slot_node,
            node_diag,
            solid_start,
            coupling,
            hits,
            flipped,
            rest,
            start_slots,
            landed,
        ],
        "solve",
    )
    if settled:
        go = go.reshape(bands, lines, 4, WIDTH // cap, cap).transpose(0, 1, 3, 2, 4)
    go = go.reshape(bands * slabs, 4, cap)
    come = lax.all_to_all(go, ("grp", "sub"), split_axis=0, concat_axis=0, tiled=True)
    hot_out, motion_out = call(
        join_kernel,
        [shape(*hot.shape), shape(*motion.shape)],
        [hot, motion, from_near, from_next],
        "join",
    )
    if settled:
        own = lax.dynamic_slice_in_dim(come, lax.axis_index("grp") * slabs, slabs, 0)
        own = own.transpose(1, 0, 2).reshape(4, lines, WIDTH).transpose(1, 0, 2)
        own = own.reshape(4 * lines, WIDTH)
        come = jnp.pad(come, ((0, 0), (0, 0), (0, WIDTH - cap)))
    else:
        own = rest
    come = come.reshape(4 * bands * slabs, WIDTH)
    temp, seen = call(
        functools.partial(last_kernel, not settled),
        [shape(1, blocks, piece), shape(1, rows)],
        [
            come,
            own,
            solid_start,
            residual,
            image,
            ordinal,
        ],
        "finish",
    )
    return hot_out, motion_out, temp, seen


def solution(mesh):
    placed = (
        P(None, "sub", "grp", None),
        P(None, "sub", "grp", None),
        P("sub", "grp", None),
        P("grp", "sub"),
        P("grp", "sub", None),
        P("grp", "sub"),
        P("grp", "sub"),
        P("grp", "sub", None),
        P("grp", "sub", None, None),
        P("grp", "sub"),
        P("grp", "sub", None),
        P("grp", "sub", None),
    )
    return jax.shard_map(
        body,
        mesh=mesh,
        in_specs=placed,
        out_specs=(
            P("sub", "grp", None),
            P(None, "sub", "grp", None),
            P("grp", "sub", None),
            P("grp", "sub"),
        ),
        check_vma=False,
    )
```

```python
import functools
import jax
import jax.numpy as jnp
import numpy as np
from jax import lax
from jax.experimental import pallas as pl
from jax.experimental.pallas import tpu as pltpu
from jax.sharding import PartitionSpec as P

FLOW_VELOCITY = [
    (0, 0, 0),
    (1, 0, 0),
    (-1, 0, 0),
    (0, 1, 0),
    (0, -1, 0),
    (0, 0, 1),
    (0, 0, -1),
    (1, 1, 0),
    (-1, -1, 0),
    (1, -1, 0),
    (-1, 1, 0),
    (1, 0, 1),
    (-1, 0, -1),
    (1, 0, -1),
    (-1, 0, 1),
    (0, 1, 1),
    (0, -1, -1),
    (0, 1, -1),
    (0, -1, 1),
]
VELOCITY = FLOW_VELOCITY + FLOW_VELOCITY[:7]
FLOWS, HEATS = 19, 7
LANES_ALL = range(FLOWS + HEATS)
UP = [i for i in LANES_ALL if VELOCITY[i][2] == 1]
DOWN = [
    next(j for j in LANES_ALL if VELOCITY[j] == VELOCITY[i][:2] + (-1,) and (j < 19) == (i < 19))
    for i in UP
]
RIGHT = [i for i in LANES_ALL if VELOCITY[i][0] == 1]
LEFT = [
    next(j for j in LANES_ALL if VELOCITY[j] == (-1,) + VELOCITY[i][1:] and (j < 19) == (i < 19))
    for i in RIGHT
]
TURNED = [
    next(n for n, j in enumerate(RIGHT[:-1]) if VELOCITY[j][1:] == (-VELOCITY[i][1], -VELOCITY[i][2]))
    for i in RIGHT[:-1]
]
STILL = [i for i in LANES_ALL if VELOCITY[i][0] == 0]
GATHERED = len(STILL) + 2 * len(RIGHT)
SUMS = 4
FACE = SUMS + 2 * len(RIGHT) + 1
CORNER = 5


def place_of(lists, ex, ey, ez):
    return next(n for n, i in enumerate(lists) if VELOCITY[i] == (ex, ey, ez))


WIDTH = 128
SHIFT = 4.0
f32 = jnp.float32
bf16 = jnp.bfloat16


def signed_sum(terms):
    total = None
    for sign, term in terms:
        if sign == 0:
            continue
        if total is None:
            total = term if sign > 0 else -term
        else:
            total = total + term if sign > 0 else total - term
    return total


def collide(flow, heat, solid):
    pairs = range(1, FLOWS, 2)
    density = flow[0]
    for i in pairs:
        density = density + (flow[i] + flow[i + 1])
    gaps = {i: flow[i] - flow[i + 1] for i in pairs}
    scale = 1.0 / density
    speed = [
        signed_sum([(FLOW_VELOCITY[i][axis], gaps[i]) for i in pairs]) * scale for axis in range(3)
    ]
    square = speed[0] * speed[0] + speed[1] * speed[1] + speed[2] * speed[2]
    base = 1.0 - 1.5 * square
    gas = 1.0 - solid
    keep = gas * (1.0 - 1.0 / 0.8)
    pull = gas * (density * (1.0 / 0.8))
    flow_post = [None] * FLOWS
    flow_post[0] = (keep + solid) * flow[0] + (pull * (1.0 / 3.0)) * base
    shares = {1: pull * (1.0 / 18.0), 2: pull * (1.0 / 36.0)}
    for i in pairs:
        share = shares[sum(abs(c) for c in FLOW_VELOCITY[i])]
        along = signed_sum([(FLOW_VELOCITY[i][axis], speed[axis]) for axis in range(3)])
        even = base + 4.5 * along * along
        odd = 3.0 * along
        flow_post[i] = keep * flow[i] + share * (even + odd) + solid * flow[i + 1]
        flow_post[i + 1] = keep * flow[i + 1] + share * (even - odd) + solid * flow[i]
    hotness = heat[0]
    for j in range(1, HEATS):
        hotness = hotness + heat[j]
    stay = 1.0 - 1.0 / 0.7
    heat_post = [stay * heat[0] + (0.25 / 0.7) * hotness]
    level = (0.125 / 0.7) * hotness
    for j in range(1, HEATS, 2):
        axis = (j - 1) // 2
        drift = 4.0 * speed[axis]
        heat_post.append(stay * heat[j] + level * (1.0 + drift))
        heat_post.append(stay * heat[j + 1] + level * (1.0 - drift))
    return flow_post + heat_post


def collide_halo(still, inward, outward, solid):
    flows = RIGHT[:-1]
    density, along_y, along_z, hotness = still
    pairs = [(a + b, a - b) for a, b in zip(inward, outward)]
    across = None
    for n, i in enumerate(flows):
        _, ey, ez = VELOCITY[i]
        whole, gap = pairs[n]
        density = density + whole
        across = gap if across is None else across + gap
        along_y = signed_sum([(1, along_y), (ey, whole)])
        along_z = signed_sum([(1, along_z), (ez, whole)])
    hotness = hotness + pairs[-1][0]
    scale = 1.0 / density
    speed = [across * scale, along_y * scale, along_z * scale]
    square = speed[0] * speed[0] + speed[1] * speed[1] + speed[2] * speed[2]
    base = 1.0 - 1.5 * square
    gas = 1.0 - solid
    keep = gas * (1.0 - 1.0 / 0.8)
    pull = gas * (density * (1.0 / 0.8))
    shares = {1: pull * (1.0 / 18.0), 2: pull * (1.0 / 36.0)}
    out = []
    for n, i in enumerate(flows):
        share = shares[sum(abs(c) for c in VELOCITY[i])]
        along = signed_sum([(VELOCITY[i][axis], speed[axis]) for axis in range(3)])
        feq = share * (base + 4.5 * along * along + 3.0 * along)
        out.append(keep * inward[n] + feq + solid * outward[TURNED[n]])
    level = (0.125 / 0.7) * hotness
    out.append((1.0 - 1.0 / 0.7) * inward[-1] + level * (1.0 + 4.0 * speed[0]))
    return out


def three_parts(value):
    high = value.astype(bf16).astype(f32)
    rest = value - high
    middle = rest.astype(bf16).astype(f32)
    return [high, middle, rest - middle]


def times_transposed(left, right):
    return lax.dot_general(
        left.astype(bf16), right.astype(bf16), (((1,), (1,)), ((), ())), preferred_element_type=f32
    )


def spread(row):
    return jnp.broadcast_to(row, (8, row.shape[-1]))


def lane_gather(row, lane):
    return jnp.take_along_axis(spread(row), lane, axis=1, mode="promise_in_bounds")


def table_gather(table, index):
    place, lane = index >> 7, index & 127
    out = jnp.zeros(index.shape, f32)
    for row in range(table.shape[0]):
        out = jnp.where(place == row, lane_gather(table[row : row + 1], lane), out)
    return out


def plane_rows(plane, first=0, count=8):
    return pl.ds(4 * first + plane, count, stride=4)


def stacked(row):
    return jnp.concatenate(
        [row[:, k * WIDTH : (k + 1) * WIDTH] for k in range(row.shape[1] // WIDTH)], axis=0
    )


def slot_tables(cap, voxel, dest, coeff, ordinal):
    rows_here = dest.shape[1]
    owner = dest[...].astype(f32)
    chunks = rows_here // WIDTH
    tall = stacked(owner)
    tall = jnp.concatenate([tall] + [jnp.zeros((8 - chunks, WIDTH), f32)] * (chunks < 8), axis=0)
    upright = tall.T
    first = lax.broadcasted_iota(jnp.int32, (WIDTH, WIDTH), 0)
    second = lax.broadcasted_iota(jnp.int32, (WIDTH, WIDTH), 1)
    slot_row = lax.broadcasted_iota(jnp.int32, (8, WIDTH), 0)
    table = jnp.zeros((40, WIDTH), f32)
    for c in range(chunks):
        lanes = slice(c * WIDTH, (c + 1) * WIDTH)
        here = owner[:, lanes]
        count = jnp.zeros((WIDTH, WIDTH), f32)
        for other in range(c + 1):
            same = upright[:, other : other + 1] == here
            if other == c:
                same = same & (first < second)
            count = count + jnp.where(same, 1.0, 0.0)
        rank = jnp.sum(count, axis=0, keepdims=True)
        place = (here * float(cap) + rank).astype(jnp.int32)
        ordinal[:, lanes] = place
        mine = slot_row == (place >> 7)
        spot = voxel[:, lanes]
        parts = [(spot >> 7).astype(f32), (spot & 127).astype(f32)] + three_parts(coeff[:, lanes])
        values = jnp.concatenate([jnp.where(mine, part, 0.0) for part in parts], axis=0)
        table = table + times_transposed(values, jnp.where(first == (place & 127), 1.0, 0.0))
    spots = table[0:8] * float(WIDTH) + table[8:16]
    coeffs = (table[16:24] + table[24:32]) + table[32:40]
    return spots, coeffs


def on_even(axis="sub"):
    return lax.rem(lax.axis_index(axis), 2) == 0


def turned(tile, step):
    return tile if step == 0 else pltpu.roll(tile, step % tile.shape[1], 1)


def corner_shares(plane):
    across = plane.shape[1]
    up, right, left, ahead, behind = (
        place_of(UP, ex, ey, 1) for ex, ey in ((0, 0), (1, 0), (-1, 0), (0, 1), (0, -1))
    )
    warm = len(UP) - 1
    sides = []
    for column, inside, outward in ((across - 1, across - 2, right), (0, 1, left)):

        def row(n, at):
            return plane[n, at : at + 1, :]

        one, two = turned(row(ahead, column), 1), turned(row(behind, column), -1)
        rows = [
            row(up, column) + (one + two),
            one - two,
            row(warm, column),
            row(outward, inside),
            row(outward, column),
        ]
        sides.append(jnp.concatenate(rows, axis=0))
    return sides


def add_corners(face, below, above, layers):
    edge = SUMS + len(RIGHT)
    for corner, z, rise in ((below, 0, 1), (above, layers - 1, -1)):
        k = place_of(RIGHT, 1, 0, rise)
        adds = [(0, 1, 0), (1, 1, 1), (2, rise, 0), (3, 1, 2), (SUMS + k, 1, 3), (edge + k, 1, 4)]
        for n, sign, row in adds:
            at = n * layers + z
            share = corner[row : row + 1]
            face[at : at + 1, :] = face[at : at + 1, :] + (share if sign > 0 else -share)


def early_kernel(pops, heat, solid, pops_here, heat_here, solid_here, shares, planes, arrived):
    layers, _, along = solid.shape
    even = on_even()
    facing = jnp.where(even, 0, layers - 1)
    pairs = ((pops, pops_here), (heat, heat_here))
    pieces = []
    for step in range(layers):
        z = lax.rem(facing + step, layers)
        pieces += [(source.at[:, z], target.at[:, z]) for source, target in pairs]
        pieces.append((solid.at[z], solid_here.at[z]))
    copies = [
        pltpu.make_async_copy(source, target, arrived.at[n])
        for n, (source, target) in enumerate(pieces)
    ]
    for copy in copies:
        copy.start()
    for copy in copies[:3]:
        copy.wait()
    for start in range(0, along, WIDTH):
        lanes = slice(start, start + WIDTH)
        out = collide(
            [pops_here[i, facing, :, lanes] for i in range(FLOWS)],
            [heat_here[j, facing, :, lanes] for j in range(HEATS)],
            solid_here[facing, :, lanes],
        )
        for n, (above, below) in enumerate(zip(UP, DOWN)):
            planes[n, :, lanes] = jnp.where(even, out[below], out[above])
    shares[...] = jnp.zeros(shares.shape, f32)
    for n, side in enumerate(corner_shares(planes)):
        shares[8 * n : 8 * n + CORNER] = side
    for copy in copies[3:]:
        copy.wait()


def first_kernel(
    cap, pops, heat, solid, voxel, dest, coeff, post, to_near, to_next, ordinal
):
    layers, across, along = solid.shape
    even = on_even()
    spots, coeffs = slot_tables(cap, voxel, dest, coeff, ordinal)
    extra = len(UP)
    for plane in (to_near, to_next):
        plane[extra] = jnp.zeros(plane.shape[1:], f32)
        plane[extra, :, 0:WIDTH] = spots
        plane[extra, :, WIDTH : 2 * WIDTH] = coeffs
    for z in range(layers):
        for start in range(0, along, WIDTH):
            lanes = slice(start, start + WIDTH)
            out = collide(
                [pops[i, z, :, lanes] for i in range(FLOWS)],
                [heat[j, z, :, lanes] for j in range(HEATS)],
                solid[z, :, lanes],
            )
            for i in LANES_ALL:
                post[i, z, :, lanes] = out[i]
    for n, (above, below) in enumerate(zip(UP, DOWN)):
        above, below = post[above, layers - 1], post[below, 0]
        to_near[n] = jnp.where(even, above, below)
        to_next[n] = jnp.where(even, below, above)


def edge_kernel(post, shares, solid, face_r, face_l, out_r, out_l):
    layers, across, along = post.shape[1:]
    for out, lists, edge, inside in (
        (out_r, (STILL, RIGHT), across - 1, across - 2),
        (out_l, (STILL, LEFT), 0, 1),
    ):
        rows = [(i, edge) for i in lists[0]] + [(i, inside) for i in lists[1]]
        rows = rows + [(i, edge) for i in lists[1]]
        for n, (i, column) in enumerate(rows):
            for z in range(layers):
                at, source = n * layers + z, z - VELOCITY[i][2]
                if 0 <= source < layers:
                    out[at : at + 1, :] = post[i, source, column : column + 1, :]
                else:
                    out[at : at + 1, :] = jnp.zeros((1, along), f32)

    def both(n):
        at = slice(n * layers, (n + 1) * layers)
        return jnp.concatenate([out_r[at, :], out_l[at, :]], axis=0)

    def send(n, tile):
        at = slice(n * layers, (n + 1) * layers)
        face_r[at, :], face_l[at, :] = tile[0:layers], tile[layers : 2 * layers]

    sums = [[] for _ in range(SUMS)]
    for n, i in enumerate(STILL):
        _, ey, ez = VELOCITY[i]
        tile = turned(both(n), ey)
        if i >= FLOWS:
            sums[3].append((1, tile))
        else:
            sums[0].append((1, tile))
            sums[1].append((ey, tile))
            sums[2].append((ez, tile))
    for n in range(SUMS):
        send(n, signed_sum(sums[n]))
    for n, i in enumerate(RIGHT):
        send(SUMS + n, turned(both(len(STILL) + n), VELOCITY[i][1]))
    for n in range(len(STILL) + len(RIGHT), GATHERED):
        send(n - len(STILL) + SUMS, both(n))
    even = on_even()
    for n, (face, column) in enumerate(((face_r, across - 1), (face_l, 0))):
        for z in range(layers):
            at = (FACE - 1) * layers + z
            face[at : at + 1, :] = solid[z, column : column + 1, :]
        far = shares[8 * n : 8 * n + CORNER]
        add_corners(face, jnp.where(even, far, 0.0), jnp.where(even, 0.0, far), layers)


def side_kernel(layers, near, face_r, face_l, to_a, to_b, sum_r, sum_l):
    even, band_even = on_even(), on_even("grp")
    sides = zip((face_r, face_l), (sum_r, sum_l), corner_shares(near))
    for face, total, close in sides:
        total[...] = face[...]
        add_corners(total, jnp.where(even, 0.0, close), jnp.where(even, close, 0.0), layers)
    right, left = sum_r[...], sum_l[...]
    to_a[...] = jnp.where(band_even, right, left)
    to_b[...] = jnp.where(band_even, left, right)


def second_kernel(
    post,
    near,
    next_,
    to_a,
    to_b,
    faces_a,
    faces_b,
    solid,
    own_table,
    tie,
    hot,
    motion,
    send_near,
    send_next,
    fluxes,
    moved,
    halo,
    own_r,
    own_l,
    from_l,
    from_r,
):
    layers, across, along = solid.shape
    even = on_even()
    band_even = on_even("grp")
    own_r[...] = jnp.where(band_even, to_a[...], to_b[...])
    own_l[...] = jnp.where(band_even, to_b[...], to_a[...])
    below = [jnp.where(even, next_[n], near[n]) for n in range(len(UP) + 1)]
    above = [jnp.where(even, near[n], next_[n]) for n in range(len(UP) + 1)]
    from_l[...] = jnp.where(band_even, faces_b[...], faces_a[...])
    from_r[...] = jnp.where(band_even, faces_a[...], faces_b[...])
    slot = lax.broadcasted_iota(jnp.int32, (across, along), 0)
    edge = SUMS + len(RIGHT)
    for i in LANES_ALL:
        ex, ey, ez = VELOCITY[i]
        for z in range(layers):
            if z - ez < 0:
                tile = below[UP.index(i)]
            elif z - ez >= layers:
                tile = above[DOWN.index(i)]
            else:
                tile = post[i, z - ez]
            if ex == 1:
                at = (edge + RIGHT.index(i)) * layers + z
                tile = jnp.where(slot == 0, from_l[at : at + 1, :], pltpu.roll(tile, 1, 0))
            elif ex == -1:
                at = (edge + LEFT.index(i)) * layers + z
                tile = jnp.where(
                    slot == across - 1, from_r[at : at + 1, :], pltpu.roll(tile, across - 1, 0)
                )
            moved[i, z] = turned(tile, ey)

    def halves(low, high, n):
        at = slice(n * layers, (n + 1) * layers)
        parts = [low[at, :], high[at, :]]
        if 2 * layers < 8:
            parts.append(jnp.ones((8 - 2 * layers, along), f32))
        return jnp.concatenate(parts, axis=0)

    for n in range(edge):
        halo[n] = halves(from_l, from_r, n)
    for n, i in enumerate(RIGHT):
        halo[edge + n] = turned(halves(own_l, own_r, edge + n), VELOCITY[i][1])
    edge_solid = halves(from_l, from_r, FACE - 1)
    for start in range(0, along, WIDTH):
        lanes = slice(start, start + WIDTH)
        for z in range(layers):
            out = collide(
                [moved[i, z, :, lanes] for i in range(FLOWS)],
                [moved[FLOWS + j, z, :, lanes] for j in range(HEATS)],
                solid[z, :, lanes],
            )
            for i in LANES_ALL:
                moved[i, z, :, lanes] = out[i]
        out = collide_halo(
            [halo[n, :, lanes] for n in range(SUMS)],
            [halo[SUMS + n, :, lanes] for n in range(len(RIGHT))],
            [halo[edge + n, :, lanes] for n in range(len(RIGHT))],
            edge_solid[:, lanes],
        )
        for n in range(len(RIGHT)):
            halo[SUMS + n, :, lanes] = out[n]
    sums = {}

    def add(key, sign, tile):
        if sign == 0:
            return
        if key in sums:
            sums[key] = sums[key] + tile if sign > 0 else sums[key] - tile
        else:
            sums[key] = tile if sign > 0 else -tile

    for z in range(layers):
        for i in LANES_ALL:
            ex, ey, ez = VELOCITY[i]
            if i == 0:
                continue
            tile = moved[i, z]
            if ex == 1:
                side = halo[SUMS + RIGHT.index(i), z : z + 1, :]
                tile = jnp.where(slot == 0, side, pltpu.roll(tile, 1, 0))
            elif ex == -1:
                at = layers + z
                side = halo[SUMS + LEFT.index(i), at : at + 1, :]
                tile = jnp.where(slot == across - 1, side, pltpu.roll(tile, across - 1, 0))
            tile = turned(tile, ey)
            target = z + ez
            if i >= FLOWS:
                add((3, target), 1, tile)
            else:
                add((0, target), ex, tile)
                add((1, target), ey, tile)
                add((2, target), ez, tile)
    for z in range(layers):
        hot[z] = sums[3, z]
        for axis in range(3):
            motion[axis, z] = sums[axis, z]
    for part in range(4):
        send_near[part] = jnp.where(even, sums[part, layers], sums[part, -1])
        send_next[part] = jnp.where(even, sums[part, -1], sums[part, layers])
    extra = len(UP)
    per_line = along // WIDTH
    per_layer = across * per_line

    def flux(table, planes):
        index = table[:, 0:WIDTH].astype(jnp.int32)
        place, lane = index >> 7, index & 127
        out = jnp.zeros(lane.shape, f32)
        for z, plane in planes:
            for x in range(across):
                for c in range(per_line):
                    row = plane[x : x + 1, c * WIDTH : (c + 1) * WIDTH]
                    out = jnp.where(
                        place == z * per_layer + x * per_line + c, lane_gather(row, lane), out
                    )
        return out * table[:, WIDTH : 2 * WIDTH]

    mine = own_table[extra]
    fluxes[plane_rows(0), :] = flux(mine, [(z, sums[3, z]) for z in range(layers)])
    fluxes[plane_rows(1), :] = flux(above[extra], [(0, sums[3, layers])])
    fluxes[plane_rows(2), :] = flux(below[extra], [(layers - 1, sums[3, -1])])
    fluxes[plane_rows(3), :] = mine[:, WIDTH : 2 * WIDTH]


def sublane_gather(value, index):
    return jnp.take_along_axis(value, index, axis=0, mode="promise_in_bounds")


def coupled(vector, blocks, flipped, shift):
    count = vector.shape[0]
    upright = vector.T
    ahead, back = [], []
    for b in range(count):
        column = jnp.broadcast_to(upright[:, b : b + 1], blocks.shape[1:])
        back.append(jnp.sum(blocks[b] * column, axis=0, keepdims=True))
        ahead.append(jnp.sum(flipped[b] * column, axis=0, keepdims=True))
    ahead = jnp.concatenate(ahead, axis=0)
    back = jnp.concatenate(back, axis=0)
    block = lax.broadcasted_iota(jnp.int32, vector.shape, 0)
    ahead = sublane_gather(ahead, (block + shift) & (count - 1))
    return ahead + sublane_gather(back, (block - shift) & (count - 1))


def ready_kernel(
    pattern, nodes, diagonal, source, start, coupling, tie, hits, flipped, rest, slots, turn
):
    shift = pattern[0, 0]
    turn[...] = jnp.full(turn.shape, shift, jnp.int32)
    count = start.shape[1]
    for b in range(count):
        flipped[lax.rem(b + shift, count)] = coupling[0, b].T
    vector = start[0]
    rest[...] = (
        source[0] - diagonal[0] * vector + coupled(vector, coupling.at[0], flipped, turn[...])
    )
    index = stacked(nodes[...])
    slots[...] = table_gather(vector, index)
    upright = (index & 127).astype(f32).T.astype(jnp.int32)
    lane = lax.broadcasted_iota(jnp.int32, (WIDTH, WIDTH), 1)
    for s in range(index.shape[0]):
        hit = jnp.where(upright[:, s : s + 1] == lane, 1.0, 0.0)
        hits[s * WIDTH : (s + 1) * WIDTH] = hit.astype(bf16)


def solve_kernel(
    cap,
    turn,
    nodes,
    diagonal,
    start,
    coupling,
    hits,
    flipped,
    rest,
    slots,
    come,
    res,
    img,
    go,
):
    shift = turn[...]
    count = start.shape[1]
    index = stacked(nodes[...])
    place = index >> 7
    own, low, high, coeff = (come[plane_rows(plane), :] for plane in range(4))
    if cap == WIDTH:
        low = pltpu.roll(low, 1, 0)
        high = pltpu.roll(high, low.shape[0] - 1, 0)
    parts = three_parts(own + low + high) + three_parts(coeff)
    block = lax.broadcasted_iota(jnp.int32, (count, WIDTH), 0)
    values = []
    for s in range(index.shape[0]):
        mine = block == place[s : s + 1]
        values.append(
            jnp.concatenate([jnp.where(mine, part[s : s + 1], 0.0) for part in parts], axis=0)
        )
    values = jnp.concatenate(values, axis=1).astype(bf16)
    landed = jnp.dot(values, hits[...], preferred_element_type=f32)
    landed = [landed[k * count : (k + 1) * count] for k in range(len(parts))]
    added = (landed[0] + landed[1]) + landed[2]
    extra = (landed[3] + landed[4]) + landed[5]
    whole = diagonal[0] + extra
    blocks = coupling.at[0]
    residual = rest[...] + added - extra * start[0]
    image = whole * residual - coupled(residual, blocks, flipped, shift)

    def total(value):
        return jnp.sum(jnp.sum(value, axis=0, keepdims=True), axis=1, keepdims=True)

    offset = image - SHIFT * residual
    bend = whole * offset - coupled(offset, blocks, flipped, shift)
    totals = [
        total(residual * residual),
        total(residual * offset),
        total(offset * offset),
        total(offset * bend),
    ]
    res[...] = residual
    img[...] = image
    lane = lax.broadcasted_iota(jnp.int32, (8, WIDTH), 1) & (cap - 1)
    facts = jnp.zeros((8, WIDTH), f32)
    for n, fact in enumerate(totals):
        facts = jnp.where(lane == n, fact, facts)
    residual_slots = table_gather(residual, index)
    image_slots = table_gather(image, index)
    start_slots = slots[...]
    for group in range(0, go.shape[0] // 4, 8):
        go[plane_rows(0, group), :] = start_slots
        go[plane_rows(1, group), :] = residual_slots
        go[plane_rows(2, group), :] = image_slots
        go[plane_rows(3, group), :] = facts


def last_kernel(direct, come, own, start, res, img, ordinal, temp, seen):
    places = stacked(ordinal[...])
    chunks = places.shape[0]
    if chunks < 8:
        places = jnp.concatenate([places, jnp.zeros((8 - chunks, WIDTH), jnp.int32)], axis=0)
    found = []
    for plane in range(3):
        if direct:
            table = come[plane_rows(plane, lax.axis_index("grp") * 8), :]
        else:
            table = own[plane_rows(plane), :]
        found.append(table_gather(table, places))
    facts = come[plane_rows(3, 0, come.shape[0] // 4), :]
    facts = jnp.sum(facts, axis=0, keepdims=True)
    all_norm, cross, square, energy = (
        lane_gather(facts, jnp.full((8, WIDTH), n, jnp.int32)) for n in range(4)
    )
    product = SHIFT * all_norm + cross
    inverse = 1.0 / product
    ratio = cross / all_norm
    spread_square = square - cross * ratio
    energy = energy - ratio * (2.0 * (square + SHIFT * cross) - ratio * product)
    small = spread_square * inverse
    first = all_norm * inverse
    step = spread_square / (energy - spread_square * small)
    of_residual = first + step * (1.0 + small * first)
    of_image = -step * first
    temp[0] = start[0] + of_residual * res[...] + of_image * img[...]
    found = found[0] + of_residual * found[1] + of_image * found[2]
    for c in range(chunks):
        seen[:, c * WIDTH : (c + 1) * WIDTH] = found[c : c + 1]


def join_kernel(hot, motion, near, next_, hot_out, motion_out):
    layers = hot.shape[0]
    even = on_even()
    below = [jnp.where(even, next_[n], near[n]) for n in range(4)]
    above = [jnp.where(even, near[n], next_[n]) for n in range(4)]
    for z in range(layers):
        for part in range(4):
            tile = hot[z] if part == 3 else motion[part, z]
            if z == 0:
                tile = tile + below[part]
            if z == layers - 1:
                tile = tile + above[part]
            if part == 3:
                hot_out[z] = tile
            else:
                motion_out[part, z] = tile


VMEM = pl.BlockSpec(memory_space=pltpu.VMEM)
ANYWHERE = pl.BlockSpec(memory_space=pl.ANY)
SMEM = pl.BlockSpec(memory_space=pltpu.SMEM)


def call(kernel, out, args, name, scalars=(), scratch=(), far=False, flops=1 << 20):
    total = sum(int(np.prod(a.shape)) * a.dtype.itemsize for a in list(args) + list(out))
    if far:
        args = [pltpu.with_memory_space_constraint(a, pltpu.HBM) for a in args]
    return pl.pallas_call(
        kernel,
        out_shape=out,
        in_specs=[
            ANYWHERE if far else SMEM if n in scalars else VMEM for n in range(len(args))
        ],
        out_specs=[VMEM] * len(out),
        scratch_shapes=scratch,
        compiler_params=pltpu.CompilerParams(vmem_limit_bytes=24 << 20),
        cost_estimate=pl.CostEstimate(flops=flops, bytes_accessed=total, transcendentals=0),
        name=name,
    )(*args)


def shape(*dims, dtype=f32):
    return jax.ShapeDtypeStruct(dims, dtype)


def swaps(axis):
    count = lax.axis_size(axis)
    assert count % 2 == 0
    near = [(k, k + 1 - 2 * (k % 2)) for k in range(count)]
    return near, [(k, (k - 1 + 2 * (k % 2)) % count) for k in range(count)]


def body(
    populations,
    heat_pops,
    solid_frac,
    coupled_grid_point,
    dest_index,
    heat_coeff,
    slot_node,
    node_diag,
    coupling,
    block_pattern,
    heat_source,
    solid_start,
):
    layers, across, along = solid_frac.shape
    slabs, bands = lax.axis_size("sub"), lax.axis_size("grp")
    slots = slot_node.shape[1]
    cap = slots // slabs
    rows = coupled_grid_point.shape[1]
    blocks, piece = node_diag.shape[1:]
    lines = slots // WIDTH
    assert lines == 8 and across == 8 and along >= 2 * WIDTH and along % WIDTH == 0
    assert piece == WIDTH and blocks == 8 and WIDTH % cap == 0 and cap >= 8
    assert rows % WIDTH == 0 and rows <= 8 * WIDTH and layers <= 4
    gathered_rows = -(-GATHERED * layers // 8) * 8
    face_rows = -(-FACE * layers // 8) * 8
    planes = len(UP) + 1
    near_pairs, next_pairs = swaps("sub")
    pops_here, heat_here, solid_here, to_shares = call(
        early_kernel,
        [
            shape(*populations.shape),
            shape(*heat_pops.shape),
            shape(*solid_frac.shape),
            shape(16, along),
        ],
        [populations, heat_pops, solid_frac],
        "collide_early",
        scratch=[
            pltpu.VMEM((len(UP), across, along), f32),
            pltpu.SemaphoreType.DMA((3 * layers,)),
        ],
        far=True,
    )
    shares = lax.ppermute(to_shares, "sub", next_pairs)
    post, to_near, to_next, ordinal = call(
        functools.partial(first_kernel, cap),
        [
            shape(FLOWS + HEATS, layers, across, along),
            shape(planes, across, along),
            shape(planes, across, along),
            shape(1, rows, dtype=jnp.int32),
        ],
        [
            pops_here,
            heat_here,
            solid_here,
            coupled_grid_point,
            dest_index.reshape(1, rows),
            heat_coeff,
        ],
        "collide_first",
    )
    near = lax.ppermute(to_near, "sub", near_pairs)
    next_ = lax.ppermute(to_next, "sub", next_pairs)
    faces = [shape(face_rows, along)] * 2
    face_r, face_l = call(
        edge_kernel,
        faces,
        [post, shares, solid_here],
        "x_faces",
        scratch=[pltpu.VMEM((gathered_rows, along), f32)] * 2,
        flops=1 << 32,
    )
    to_a, to_b = call(
        functools.partial(side_kernel, layers),
        faces,
        [near, face_r, face_l],
        "x_sides",
        scratch=[pltpu.VMEM((face_rows, along), f32)] * 2,
    )
    side_a, side_b = swaps("grp")
    faces_a = lax.ppermute(to_a, "grp", side_a)
    faces_b = lax.ppermute(to_b, "grp", side_b)
    hits, flipped, rest, start_slots, turn = call(
        ready_kernel,
        [
            shape(slots, WIDTH, dtype=bf16),
            shape(blocks, piece, piece),
            shape(blocks, piece),
            shape(lines, WIDTH),
            shape(blocks, WIDTH, dtype=jnp.int32),
        ],
        [block_pattern, slot_node, node_diag, heat_source, solid_start, coupling, to_a],
        "solid_ready",
        scalars=(0,),
    )
    hot, motion, send_near, send_next, fluxes = call(
        second_kernel,
        [
            shape(layers, across, along),
            shape(3, layers, across, along),
            shape(4, across, along),
            shape(4, across, along),
            shape(4 * lines, WIDTH),
        ],
        [
            post,
            near,
            next_,
            to_a,
            to_b,
            faces_a,
            faces_b,
            solid_here,
            to_next,
            rest,
        ],
        "collide_second",
        scratch=[
            pltpu.VMEM((FLOWS + HEATS, layers, across, along), f32),
            pltpu.VMEM((FACE, 8, along), f32),
        ]
        + [pltpu.VMEM((face_rows, along), f32)] * 4,
    )
    settled = cap != WIDTH
    if settled:
        fluxes = fluxes.reshape(lines, 4, WIDTH // cap, cap).transpose(0, 2, 1, 3)
    fluxes = fluxes.reshape(slabs, 4, cap)
    landed = lax.all_to_all(fluxes, "sub", split_axis=0, concat_axis=0, tiled=True)
    if settled:
        landed = jnp.stack(
            [
                landed[:, 0],
                jnp.roll(landed[:, 1], 1, axis=0),
                jnp.roll(landed[:, 2], -1, axis=0),
                landed[:, 3],
            ]
        )
        landed = landed.reshape(4, lines, WIDTH).transpose(1, 0, 2)
    landed = landed.reshape(4 * lines, WIDTH)
    from_near = lax.ppermute(send_near, "sub", near_pairs)
    from_next = lax.ppermute(send_next, "sub", next_pairs)
    residual, image, go = call(
        functools.partial(solve_kernel, cap),
        [shape(blocks, piece), shape(blocks, piece), shape(bands * lines * 4, WIDTH)],
        [
            turn,
            slot_node,
            node_diag,
            solid_start,
            coupling,
            hits,
            flipped,
            rest,
            start_slots,
            landed,
        ],
        "solve",
    )
    if settled:
        go = go.reshape(bands, lines, 4, WIDTH // cap, cap).transpose(0, 1, 3, 2, 4)
    go = go.reshape(bands * slabs, 4, cap)
    come = lax.all_to_all(go, ("grp", "sub"), split_axis=0, concat_axis=0, tiled=True)
    hot_out, motion_out = call(
        join_kernel,
        [shape(*hot.shape), shape(*motion.shape)],
        [hot, motion, from_near, from_next],
        "join",
    )
    if settled:
        own = lax.dynamic_slice_in_dim(come, lax.axis_index("grp") * slabs, slabs, 0)
        own = own.transpose(1, 0, 2).reshape(4, lines, WIDTH).transpose(1, 0, 2)
        own = own.reshape(4 * lines, WIDTH)
        come = jnp.pad(come, ((0, 0), (0, 0), (0, WIDTH - cap)))
    else:
        own = rest
    come = come.reshape(4 * bands * slabs, WIDTH)
    temp, seen = call(
        functools.partial(last_kernel, not settled),
        [shape(1, blocks, piece), shape(1, rows)],
        [
            come,
            own,
            solid_start,
            residual,
            image,
            ordinal,
        ],
        "finish",
    )
    return hot_out, motion_out, temp, seen


def solution(mesh):
    placed = (
        P(None, "sub", "grp", None),
        P(None, "sub", "grp", None),
        P("sub", "grp", None),
        P("grp", "sub"),
        P("grp", "sub", None),
        P("grp", "sub"),
        P("grp", "sub"),
        P("grp", "sub", None),
        P("grp", "sub", None, None),
        P("grp", "sub"),
        P("grp", "sub", None),
        P("grp", "sub", None),
    )
    return jax.shard_map(
        body,
        mesh=mesh,
        in_specs=placed,
        out_specs=(
            P("sub", "grp", None),
            P(None, "sub", "grp", None),
            P("grp", "sub", None),
            P("grp", "sub"),
        ),
        check_vma=False,
    )
```

```python
import functools
import jax
import jax.numpy as jnp
import numpy as np
from jax import lax
from jax.experimental import pallas as pl
from jax.experimental.pallas import tpu as pltpu
from jax.sharding import PartitionSpec as P

FLOW_VELOCITY = [
    (0, 0, 0),
    (1, 0, 0),
    (-1, 0, 0),
    (0, 1, 0),
    (0, -1, 0),
    (0, 0, 1),
    (0, 0, -1),
    (1, 1, 0),
    (-1, -1, 0),
    (1, -1, 0),
    (-1, 1, 0),
    (1, 0, 1),
    (-1, 0, -1),
    (1, 0, -1),
    (-1, 0, 1),
    (0, 1, 1),
    (0, -1, -1),
    (0, 1, -1),
    (0, -1, 1),
]
VELOCITY = FLOW_VELOCITY + FLOW_VELOCITY[:7]
FLOWS, HEATS = 19, 7
LANES_ALL = range(FLOWS + HEATS)
UP = [i for i in LANES_ALL if VELOCITY[i][2] == 1]
DOWN = [
    next(j for j in LANES_ALL if VELOCITY[j] == VELOCITY[i][:2] + (-1,) and (j < 19) == (i < 19))
    for i in UP
]
RIGHT = [i for i in LANES_ALL if VELOCITY[i][0] == 1]
LEFT = [
    next(j for j in LANES_ALL if VELOCITY[j] == (-1,) + VELOCITY[i][1:] and (j < 19) == (i < 19))
    for i in RIGHT
]
TURNED = [
    next(n for n, j in enumerate(RIGHT[:-1]) if VELOCITY[j][1:] == (-VELOCITY[i][1], -VELOCITY[i][2]))
    for i in RIGHT[:-1]
]
STILL = [i for i in LANES_ALL if VELOCITY[i][0] == 0]
GATHERED = len(STILL) + 2 * len(RIGHT)
SUMS = 4
FACE = SUMS + 2 * len(RIGHT) + 1
CORNER = 5


def place_of(lists, ex, ey, ez):
    return next(n for n, i in enumerate(lists) if VELOCITY[i] == (ex, ey, ez))


WIDTH = 128
SHIFT = 4.0
f32 = jnp.float32
bf16 = jnp.bfloat16


def signed_sum(terms):
    total = None
    for sign, term in terms:
        if sign == 0:
            continue
        if total is None:
            total = term if sign > 0 else -term
        else:
            total = total + term if sign > 0 else total - term
    return total


def collide(flow, heat, solid):
    pairs = range(1, FLOWS, 2)
    density = flow[0]
    for i in pairs:
        density = density + (flow[i] + flow[i + 1])
    gaps = {i: flow[i] - flow[i + 1] for i in pairs}
    scale = 1.0 / density
    speed = [
        signed_sum([(FLOW_VELOCITY[i][axis], gaps[i]) for i in pairs]) * scale for axis in range(3)
    ]
    square = speed[0] * speed[0] + speed[1] * speed[1] + speed[2] * speed[2]
    base = 1.0 - 1.5 * square
    gas = 1.0 - solid
    keep = gas * (1.0 - 1.0 / 0.8)
    pull = gas * (density * (1.0 / 0.8))
    flow_post = [None] * FLOWS
    flow_post[0] = (keep + solid) * flow[0] + (pull * (1.0 / 3.0)) * base
    shares = {1: pull * (1.0 / 18.0), 2: pull * (1.0 / 36.0)}
    for i in pairs:
        share = shares[sum(abs(c) for c in FLOW_VELOCITY[i])]
        along = signed_sum([(FLOW_VELOCITY[i][axis], speed[axis]) for axis in range(3)])
        even = base + 4.5 * along * along
        odd = 3.0 * along
        flow_post[i] = keep * flow[i] + share * (even + odd) + solid * flow[i + 1]
        flow_post[i + 1] = keep * flow[i + 1] + share * (even - odd) + solid * flow[i]
    hotness = heat[0]
    for j in range(1, HEATS):
        hotness = hotness + heat[j]
    stay = 1.0 - 1.0 / 0.7
    heat_post = [stay * heat[0] + (0.25 / 0.7) * hotness]
    level = (0.125 / 0.7) * hotness
    for j in range(1, HEATS, 2):
        axis = (j - 1) // 2
        drift = 4.0 * speed[axis]
        heat_post.append(stay * heat[j] + level * (1.0 + drift))
        heat_post.append(stay * heat[j + 1] + level * (1.0 - drift))
    return flow_post + heat_post


def collide_halo(still, inward, outward, solid):
    flows = RIGHT[:-1]
    density, along_y, along_z, hotness = still
    pairs = [(a + b, a - b) for a, b in zip(inward, outward)]
    across = None
    for n, i in enumerate(flows):
        _, ey, ez = VELOCITY[i]
        whole, gap = pairs[n]
        density = density + whole
        across = gap if across is None else across + gap
        along_y = signed_sum([(1, along_y), (ey, whole)])
        along_z = signed_sum([(1, along_z), (ez, whole)])
    hotness = hotness + pairs[-1][0]
    scale = 1.0 / density
    speed = [across * scale, along_y * scale, along_z * scale]
    square = speed[0] * speed[0] + speed[1] * speed[1] + speed[2] * speed[2]
    base = 1.0 - 1.5 * square
    gas = 1.0 - solid
    keep = gas * (1.0 - 1.0 / 0.8)
    pull = gas * (density * (1.0 / 0.8))
    shares = {1: pull * (1.0 / 18.0), 2: pull * (1.0 / 36.0)}
    out = []
    for n, i in enumerate(flows):
        share = shares[sum(abs(c) for c in VELOCITY[i])]
        along = signed_sum([(VELOCITY[i][axis], speed[axis]) for axis in range(3)])
        feq = share * (base + 4.5 * along * along + 3.0 * along)
        out.append(keep * inward[n] + feq + solid * outward[TURNED[n]])
    level = (0.125 / 0.7) * hotness
    out.append((1.0 - 1.0 / 0.7) * inward[-1] + level * (1.0 + 4.0 * speed[0]))
    return out


def three_parts(value):
    high = value.astype(bf16).astype(f32)
    rest = value - high
    middle = rest.astype(bf16).astype(f32)
    return [high, middle, rest - middle]


def times_transposed(left, right):
    return lax.dot_general(
        left.astype(bf16), right.astype(bf16), (((1,), (1,)), ((), ())), preferred_element_type=f32
    )


def spread(row):
    return jnp.broadcast_to(row, (8, row.shape[-1]))


def lane_gather(row, lane):
    return jnp.take_along_axis(spread(row), lane, axis=1, mode="promise_in_bounds")


def table_gather(table, index):
    place, lane = index >> 7, index & 127
    out = jnp.zeros(index.shape, f32)
    for row in range(table.shape[0]):
        out = jnp.where(place == row, lane_gather(table[row : row + 1], lane), out)
    return out


def plane_rows(plane, first=0, count=8):
    return pl.ds(4 * first + plane, count, stride=4)


def stacked(row):
    return jnp.concatenate(
        [row[:, k * WIDTH : (k + 1) * WIDTH] for k in range(row.shape[1] // WIDTH)], axis=0
    )


def slot_tables(cap, voxel, dest, coeff, ordinal):
    rows_here = dest.shape[1]
    owner = dest[...].astype(f32)
    chunks = rows_here // WIDTH
    tall = stacked(owner)
    tall = jnp.concatenate([tall] + [jnp.zeros((8 - chunks, WIDTH), f32)] * (chunks < 8), axis=0)
    upright = tall.T
    first = lax.broadcasted_iota(jnp.int32, (WIDTH, WIDTH), 0)
    second = lax.broadcasted_iota(jnp.int32, (WIDTH, WIDTH), 1)
    slot_row = lax.broadcasted_iota(jnp.int32, (8, WIDTH), 0)
    table = jnp.zeros((40, WIDTH), f32)
    for c in range(chunks):
        lanes = slice(c * WIDTH, (c + 1) * WIDTH)
        here = owner[:, lanes]
        count = jnp.zeros((WIDTH, WIDTH), f32)
        for other in range(c + 1):
            same = upright[:, other : other + 1] == here
            if other == c:
                same = same & (first < second)
            count = count + jnp.where(same, 1.0, 0.0)
        rank = jnp.sum(count, axis=0, keepdims=True)
        place = (here * float(cap) + rank).astype(jnp.int32)
        ordinal[:, lanes] = place
        mine = slot_row == (place >> 7)
        spot = voxel[:, lanes]
        parts = [(spot >> 7).astype(f32), (spot & 127).astype(f32)] + three_parts(coeff[:, lanes])
        values = jnp.concatenate([jnp.where(mine, part, 0.0) for part in parts], axis=0)
        table = table + times_transposed(values, jnp.where(first == (place & 127), 1.0, 0.0))
    spots = table[0:8] * float(WIDTH) + table[8:16]
    coeffs = (table[16:24] + table[24:32]) + table[32:40]
    return spots, coeffs


def on_even(axis="sub"):
    return lax.rem(lax.axis_index(axis), 2) == 0


def turned(tile, step):
    return tile if step == 0 else pltpu.roll(tile, step % tile.shape[1], 1)


def corner_shares(plane):
    across = plane.shape[1]
    up, right, left, ahead, behind = (
        place_of(UP, ex, ey, 1) for ex, ey in ((0, 0), (1, 0), (-1, 0), (0, 1), (0, -1))
    )
    warm = len(UP) - 1
    sides = []
    for column, inside, outward in ((across - 1, across - 2, right), (0, 1, left)):

        def row(n, at):
            return plane[n, at : at + 1, :]

        one, two = turned(row(ahead, column), 1), turned(row(behind, column), -1)
        rows = [
            row(up, column) + (one + two),
            one - two,
            row(warm, column),
            row(outward, inside),
            row(outward, column),
        ]
        sides.append(jnp.concatenate(rows, axis=0))
    return sides


def add_corners(face, below, above, layers):
    edge = SUMS + len(RIGHT)
    for corner, z, rise in ((below, 0, 1), (above, layers - 1, -1)):
        k = place_of(RIGHT, 1, 0, rise)
        adds = [(0, 1, 0), (1, 1, 1), (2, rise, 0), (3, 1, 2), (SUMS + k, 1, 3), (edge + k, 1, 4)]
        for n, sign, row in adds:
            at = n * layers + z
            share = corner[row : row + 1]
            face[at : at + 1, :] = face[at : at + 1, :] + (share if sign > 0 else -share)


def early_kernel(*refs):
    given, held, (shares, planes, arrived) = refs[:6], refs[6:12], refs[12:]
    pops, heat, solid = given[:3]
    pops_here, heat_here, solid_here = held[:3]
    layers, _, along = solid.shape
    even = on_even()
    facing = jnp.where(even, 0, layers - 1)
    pairs = ((pops, pops_here), (heat, heat_here))
    pieces = []
    for step in range(layers):
        z = lax.rem(facing + step, layers)
        pieces += [(source.at[:, z], target.at[:, z]) for source, target in pairs]
        pieces.append((solid.at[z], solid_here.at[z]))
    pieces += zip(given[3:], held[3:])
    copies = [
        pltpu.make_async_copy(source, target, arrived.at[n])
        for n, (source, target) in enumerate(pieces)
    ]
    for copy in copies:
        copy.start()
    for copy in copies[:3]:
        copy.wait()
    for start in range(0, along, WIDTH):
        lanes = slice(start, start + WIDTH)
        out = collide(
            [pops_here[i, facing, :, lanes] for i in range(FLOWS)],
            [heat_here[j, facing, :, lanes] for j in range(HEATS)],
            solid_here[facing, :, lanes],
        )
        for n, (above, below) in enumerate(zip(UP, DOWN)):
            planes[n, :, lanes] = jnp.where(even, out[below], out[above])
    shares[...] = jnp.zeros(shares.shape, f32)
    for n, side in enumerate(corner_shares(planes)):
        shares[8 * n : 8 * n + CORNER] = side
    for copy in copies[3:]:
        copy.wait()


def first_kernel(
    cap, pops, heat, solid, voxel, dest, coeff, post, to_near, to_next, ordinal
):
    layers, across, along = solid.shape
    even = on_even()
    spots, coeffs = slot_tables(cap, voxel, dest, coeff, ordinal)
    extra = len(UP)
    for plane in (to_near, to_next):
        plane[extra] = jnp.zeros(plane.shape[1:], f32)
        plane[extra, :, 0:WIDTH] = spots
        plane[extra, :, WIDTH : 2 * WIDTH] = coeffs
    for z in range(layers):
        for start in range(0, along, WIDTH):
            lanes = slice(start, start + WIDTH)
            out = collide(
                [pops[i, z, :, lanes] for i in range(FLOWS)],
                [heat[j, z, :, lanes] for j in range(HEATS)],
                solid[z, :, lanes],
            )
            for i in LANES_ALL:
                post[i, z, :, lanes] = out[i]
    for n, (above, below) in enumerate(zip(UP, DOWN)):
        above, below = post[above, layers - 1], post[below, 0]
        to_near[n] = jnp.where(even, above, below)
        to_next[n] = jnp.where(even, below, above)


def edge_kernel(post, shares, solid, face_r, face_l, out_r, out_l):
    layers, across, along = post.shape[1:]
    for out, lists, edge, inside in (
        (out_r, (STILL, RIGHT), across - 1, across - 2),
        (out_l, (STILL, LEFT), 0, 1),
    ):
        rows = [(i, edge) for i in lists[0]] + [(i, inside) for i in lists[1]]
        rows = rows + [(i, edge) for i in lists[1]]
        for n, (i, column) in enumerate(rows):
            for z in range(layers):
                at, source = n * layers + z, z - VELOCITY[i][2]
                if 0 <= source < layers:
                    out[at : at + 1, :] = post[i, source, column : column + 1, :]
                else:
                    out[at : at + 1, :] = jnp.zeros((1, along), f32)

    def both(n):
        at = slice(n * layers, (n + 1) * layers)
        return jnp.concatenate([out_r[at, :], out_l[at, :]], axis=0)

    def send(n, tile):
        at = slice(n * layers, (n + 1) * layers)
        face_r[at, :], face_l[at, :] = tile[0:layers], tile[layers : 2 * layers]

    sums = [[] for _ in range(SUMS)]
    for n, i in enumerate(STILL):
        _, ey, ez = VELOCITY[i]
        tile = turned(both(n), ey)
        if i >= FLOWS:
            sums[3].append((1, tile))
        else:
            sums[0].append((1, tile))
            sums[1].append((ey, tile))
            sums[2].append((ez, tile))
    for n in range(SUMS):
        send(n, signed_sum(sums[n]))
    for n, i in enumerate(RIGHT):
        send(SUMS + n, turned(both(len(STILL) + n), VELOCITY[i][1]))
    for n in range(len(STILL) + len(RIGHT), GATHERED):
        send(n - len(STILL) + SUMS, both(n))
    even = on_even()
    for n, (face, column) in enumerate(((face_r, across - 1), (face_l, 0))):
        for z in range(layers):
            at = (FACE - 1) * layers + z
            face[at : at + 1, :] = solid[z, column : column + 1, :]
        far = shares[8 * n : 8 * n + CORNER]
        add_corners(face, jnp.where(even, far, 0.0), jnp.where(even, 0.0, far), layers)


def side_kernel(layers, near, face_r, face_l, to_a, to_b, sum_r, sum_l):
    even, band_even = on_even(), on_even("grp")
    sides = zip((face_r, face_l), (sum_r, sum_l), corner_shares(near))
    for face, total, close in sides:
        total[...] = face[...]
        add_corners(total, jnp.where(even, 0.0, close), jnp.where(even, close, 0.0), layers)
    right, left = sum_r[...], sum_l[...]
    to_a[...] = jnp.where(band_even, right, left)
    to_b[...] = jnp.where(band_even, left, right)


def second_kernel(
    post,
    near,
    next_,
    to_a,
    to_b,
    faces_a,
    faces_b,
    solid,
    own_table,
    tie,
    hot,
    motion,
    send_near,
    send_next,
    fluxes,
    moved,
    halo,
    own_r,
    own_l,
    from_l,
    from_r,
):
    layers, across, along = solid.shape
    even = on_even()
    band_even = on_even("grp")
    own_r[...] = jnp.where(band_even, to_a[...], to_b[...])
    own_l[...] = jnp.where(band_even, to_b[...], to_a[...])
    below = [jnp.where(even, next_[n], near[n]) for n in range(len(UP) + 1)]
    above = [jnp.where(even, near[n], next_[n]) for n in range(len(UP) + 1)]
    from_l[...] = jnp.where(band_even, faces_b[...], faces_a[...])
    from_r[...] = jnp.where(band_even, faces_a[...], faces_b[...])
    slot = lax.broadcasted_iota(jnp.int32, (across, along), 0)
    edge = SUMS + len(RIGHT)
    for i in LANES_ALL:
        ex, ey, ez = VELOCITY[i]
        for z in range(layers):
            if z - ez < 0:
                tile = below[UP.index(i)]
            elif z - ez >= layers:
                tile = above[DOWN.index(i)]
            else:
                tile = post[i, z - ez]
            if ex == 1:
                at = (edge + RIGHT.index(i)) * layers + z
                tile = jnp.where(slot == 0, from_l[at : at + 1, :], pltpu.roll(tile, 1, 0))
            elif ex == -1:
                at = (edge + LEFT.index(i)) * layers + z
                tile = jnp.where(
                    slot == across - 1, from_r[at : at + 1, :], pltpu.roll(tile, across - 1, 0)
                )
            moved[i, z] = turned(tile, ey)

    def halves(low, high, n):
        at = slice(n * layers, (n + 1) * layers)
        parts = [low[at, :], high[at, :]]
        if 2 * layers < 8:
            parts.append(jnp.ones((8 - 2 * layers, along), f32))
        return jnp.concatenate(parts, axis=0)

    for n in range(edge):
        halo[n] = halves(from_l, from_r, n)
    for n, i in enumerate(RIGHT):
        halo[edge + n] = turned(halves(own_l, own_r, edge + n), VELOCITY[i][1])
    edge_solid = halves(from_l, from_r, FACE - 1)
    for start in range(0, along, WIDTH):
        lanes = slice(start, start + WIDTH)
        for z in range(layers):
            out = collide(
                [moved[i, z, :, lanes] for i in range(FLOWS)],
                [moved[FLOWS + j, z, :, lanes] for j in range(HEATS)],
                solid[z, :, lanes],
            )
            for i in LANES_ALL:
                moved[i, z, :, lanes] = out[i]
        out = collide_halo(
            [halo[n, :, lanes] for n in range(SUMS)],
            [halo[SUMS + n, :, lanes] for n in range(len(RIGHT))],
            [halo[edge + n, :, lanes] for n in range(len(RIGHT))],
            edge_solid[:, lanes],
        )
        for n in range(len(RIGHT)):
            halo[SUMS + n, :, lanes] = out[n]
    sums = {}

    def add(key, sign, tile):
        if sign == 0:
            return
        if key in sums:
            sums[key] = sums[key] + tile if sign > 0 else sums[key] - tile
        else:
            sums[key] = tile if sign > 0 else -tile

    for z in range(layers):
        for i in LANES_ALL:
            ex, ey, ez = VELOCITY[i]
            if i == 0:
                continue
            tile = moved[i, z]
            if ex == 1:
                side = halo[SUMS + RIGHT.index(i), z : z + 1, :]
                tile = jnp.where(slot == 0, side, pltpu.roll(tile, 1, 0))
            elif ex == -1:
                at = layers + z
                side = halo[SUMS + LEFT.index(i), at : at + 1, :]
                tile = jnp.where(slot == across - 1, side, pltpu.roll(tile, across - 1, 0))
            tile = turned(tile, ey)
            target = z + ez
            if i >= FLOWS:
                add((3, target), 1, tile)
            else:
                add((0, target), ex, tile)
                add((1, target), ey, tile)
                add((2, target), ez, tile)
    for z in range(layers):
        hot[z] = sums[3, z]
        for axis in range(3):
            motion[axis, z] = sums[axis, z]
    for part in range(4):
        send_near[part] = jnp.where(even, sums[part, layers], sums[part, -1])
        send_next[part] = jnp.where(even, sums[part, -1], sums[part, layers])
    extra = len(UP)
    per_line = along // WIDTH
    per_layer = across * per_line

    def flux(table, planes):
        index = table[:, 0:WIDTH].astype(jnp.int32)
        place, lane = index >> 7, index & 127
        out = jnp.zeros(lane.shape, f32)
        for z, plane in planes:
            for x in range(across):
                for c in range(per_line):
                    row = plane[x : x + 1, c * WIDTH : (c + 1) * WIDTH]
                    out = jnp.where(
                        place == z * per_layer + x * per_line + c, lane_gather(row, lane), out
                    )
        return out * table[:, WIDTH : 2 * WIDTH]

    mine = own_table[extra]
    fluxes[plane_rows(0), :] = flux(mine, [(z, sums[3, z]) for z in range(layers)])
    fluxes[plane_rows(1), :] = flux(above[extra], [(0, sums[3, layers])])
    fluxes[plane_rows(2), :] = flux(below[extra], [(layers - 1, sums[3, -1])])
    fluxes[plane_rows(3), :] = mine[:, WIDTH : 2 * WIDTH]


def sublane_gather(value, index):
    return jnp.take_along_axis(value, index, axis=0, mode="promise_in_bounds")


def coupled(vector, blocks, flipped, shift):
    count = vector.shape[0]
    upright = vector.T
    ahead, back = [], []
    for b in range(count):
        column = jnp.broadcast_to(upright[:, b : b + 1], blocks.shape[1:])
        back.append(jnp.sum(blocks[b] * column, axis=0, keepdims=True))
        ahead.append(jnp.sum(flipped[b] * column, axis=0, keepdims=True))
    ahead = jnp.concatenate(ahead, axis=0)
    back = jnp.concatenate(back, axis=0)
    block = lax.broadcasted_iota(jnp.int32, vector.shape, 0)
    ahead = sublane_gather(ahead, (block + shift) & (count - 1))
    return ahead + sublane_gather(back, (block - shift) & (count - 1))


def ready_kernel(
    pattern, nodes, diagonal, source, start, coupling, tie, hits, flipped, rest, slots, turn
):
    shift = pattern[0, 0]
    turn[...] = jnp.full(turn.shape, shift, jnp.int32)
    count = start.shape[1]
    for b in range(count):
        flipped[lax.rem(b + shift, count)] = coupling[0, b].T
    vector = start[0]
    rest[...] = (
        source[0] - diagonal[0] * vector + coupled(vector, coupling.at[0], flipped, turn[...])
    )
    index = stacked(nodes[...])
    slots[...] = table_gather(vector, index)
    upright = (index & 127).astype(f32).T.astype(jnp.int32)
    lane = lax.broadcasted_iota(jnp.int32, (WIDTH, WIDTH), 1)
    for s in range(index.shape[0]):
        hit = jnp.where(upright[:, s : s + 1] == lane, 1.0, 0.0)
        hits[s * WIDTH : (s + 1) * WIDTH] = hit.astype(bf16)


def solve_kernel(
    cap,
    turn,
    nodes,
    diagonal,
    start,
    coupling,
    hits,
    flipped,
    rest,
    slots,
    come,
    res,
    img,
    go,
):
    shift = turn[...]
    count = start.shape[1]
    index = stacked(nodes[...])
    place = index >> 7
    own, low, high, coeff = (come[plane_rows(plane), :] for plane in range(4))
    if cap == WIDTH:
        low = pltpu.roll(low, 1, 0)
        high = pltpu.roll(high, low.shape[0] - 1, 0)
    parts = three_parts(own + low + high) + three_parts(coeff)
    block = lax.broadcasted_iota(jnp.int32, (count, WIDTH), 0)
    values = []
    for s in range(index.shape[0]):
        mine = block == place[s : s + 1]
        values.append(
            jnp.concatenate([jnp.where(mine, part[s : s + 1], 0.0) for part in parts], axis=0)
        )
    values = jnp.concatenate(values, axis=1).astype(bf16)
    landed = jnp.dot(values, hits[...], preferred_element_type=f32)
    landed = [landed[k * count : (k + 1) * count] for k in range(len(parts))]
    added = (landed[0] + landed[1]) + landed[2]
    extra = (landed[3] + landed[4]) + landed[5]
    whole = diagonal[0] + extra
    blocks = coupling.at[0]
    residual = rest[...] + added - extra * start[0]
    image = whole * residual - coupled(residual, blocks, flipped, shift)

    def total(value):
        return jnp.sum(jnp.sum(value, axis=0, keepdims=True), axis=1, keepdims=True)

    offset = image - SHIFT * residual
    bend = whole * offset - coupled(offset, blocks, flipped, shift)
    totals = [
        total(residual * residual),
        total(residual * offset),
        total(offset * offset),
        total(offset * bend),
    ]
    res[...] = residual
    img[...] = image
    lane = lax.broadcasted_iota(jnp.int32, (8, WIDTH), 1) & (cap - 1)
    facts = jnp.zeros((8, WIDTH), f32)
    for n, fact in enumerate(totals):
        facts = jnp.where(lane == n, fact, facts)
    residual_slots = table_gather(residual, index)
    image_slots = table_gather(image, index)
    start_slots = slots[...]
    for group in range(0, go.shape[0] // 4, 8):
        go[plane_rows(0, group), :] = start_slots
        go[plane_rows(1, group), :] = residual_slots
        go[plane_rows(2, group), :] = image_slots
        go[plane_rows(3, group), :] = facts


def last_kernel(direct, come, own, start, res, img, ordinal, temp, seen):
    places = stacked(ordinal[...])
    chunks = places.shape[0]
    if chunks < 8:
        places = jnp.concatenate([places, jnp.zeros((8 - chunks, WIDTH), jnp.int32)], axis=0)
    found = []
    for plane in range(3):
        if direct:
            table = come[plane_rows(plane, lax.axis_index("grp") * 8), :]
        else:
            table = own[plane_rows(plane), :]
        found.append(table_gather(table, places))
    facts = come[plane_rows(3, 0, come.shape[0] // 4), :]
    facts = jnp.sum(facts, axis=0, keepdims=True)
    all_norm, cross, square, energy = (
        lane_gather(facts, jnp.full((8, WIDTH), n, jnp.int32)) for n in range(4)
    )
    product = SHIFT * all_norm + cross
    inverse = 1.0 / product
    ratio = cross / all_norm
    spread_square = square - cross * ratio
    energy = energy - ratio * (2.0 * (square + SHIFT * cross) - ratio * product)
    small = spread_square * inverse
    first = all_norm * inverse
    step = spread_square / (energy - spread_square * small)
    of_residual = first + step * (1.0 + small * first)
    of_image = -step * first
    temp[0] = start[0] + of_residual * res[...] + of_image * img[...]
    found = found[0] + of_residual * found[1] + of_image * found[2]
    for c in range(chunks):
        seen[:, c * WIDTH : (c + 1) * WIDTH] = found[c : c + 1]


def join_kernel(hot, motion, near, next_, hot_out, motion_out):
    layers = hot.shape[0]
    even = on_even()
    below = [jnp.where(even, next_[n], near[n]) for n in range(4)]
    above = [jnp.where(even, near[n], next_[n]) for n in range(4)]
    for z in range(layers):
        for part in range(4):
            tile = hot[z] if part == 3 else motion[part, z]
            if z == 0:
                tile = tile + below[part]
            if z == layers - 1:
                tile = tile + above[part]
            if part == 3:
                hot_out[z] = tile
            else:
                motion_out[part, z] = tile


VMEM = pl.BlockSpec(memory_space=pltpu.VMEM)
ANYWHERE = pl.BlockSpec(memory_space=pl.ANY)
SMEM = pl.BlockSpec(memory_space=pltpu.SMEM)


def call(kernel, out, args, name, scalars=(), scratch=(), far=False, flops=1 << 20):
    total = sum(int(np.prod(a.shape)) * a.dtype.itemsize for a in list(args) + list(out))
    if far:
        args = [pltpu.with_memory_space_constraint(a, pltpu.HBM) for a in args]
    return pl.pallas_call(
        kernel,
        out_shape=out,
        in_specs=[
            ANYWHERE if far else SMEM if n in scalars else VMEM for n in range(len(args))
        ],
        out_specs=[VMEM] * len(out),
        scratch_shapes=scratch,
        compiler_params=pltpu.CompilerParams(vmem_limit_bytes=24 << 20),
        cost_estimate=pl.CostEstimate(flops=flops, bytes_accessed=total, transcendentals=0),
        name=name,
    )(*args)


def shape(*dims, dtype=f32):
    return jax.ShapeDtypeStruct(dims, dtype)


def swaps(axis):
    count = lax.axis_size(axis)
    assert count % 2 == 0
    near = [(k, k + 1 - 2 * (k % 2)) for k in range(count)]
    return near, [(k, (k - 1 + 2 * (k % 2)) % count) for k in range(count)]


def body(
    populations,
    heat_pops,
    solid_frac,
    coupled_grid_point,
    dest_index,
    heat_coeff,
    slot_node,
    node_diag,
    coupling,
    block_pattern,
    heat_source,
    solid_start,
):
    layers, across, along = solid_frac.shape
    slabs, bands = lax.axis_size("sub"), lax.axis_size("grp")
    slots = slot_node.shape[1]
    cap = slots // slabs
    rows = coupled_grid_point.shape[1]
    blocks, piece = node_diag.shape[1:]
    lines = slots // WIDTH
    assert lines == 8 and across == 8 and along >= 2 * WIDTH and along % WIDTH == 0
    assert piece == WIDTH and blocks == 8 and WIDTH % cap == 0 and cap >= 8
    assert rows % WIDTH == 0 and rows <= 8 * WIDTH and layers <= 4
    gathered_rows = -(-GATHERED * layers // 8) * 8
    face_rows = -(-FACE * layers // 8) * 8
    planes = len(UP) + 1
    near_pairs, next_pairs = swaps("sub")
    pops_here, heat_here, solid_here, voxel, dest, coeff, to_shares = call(
        early_kernel,
        [
            shape(*populations.shape),
            shape(*heat_pops.shape),
            shape(*solid_frac.shape),
            shape(1, rows, dtype=jnp.int32),
            shape(1, rows, dtype=jnp.int32),
            shape(1, rows),
            shape(16, along),
        ],
        [
            populations,
            heat_pops,
            solid_frac,
            coupled_grid_point,
            dest_index.reshape(1, rows),
            heat_coeff,
        ],
        "collide_early",
        scratch=[
            pltpu.VMEM((len(UP), across, along), f32),
            pltpu.SemaphoreType.DMA((3 * layers + 3,)),
        ],
        far=True,
    )
    shares = lax.ppermute(to_shares, "sub", next_pairs)
    post, to_near, to_next, ordinal = call(
        functools.partial(first_kernel, cap),
        [
            shape(FLOWS + HEATS, layers, across, along),
            shape(planes, across, along),
            shape(planes, across, along),
            shape(1, rows, dtype=jnp.int32),
        ],
        [
            pops_here,
            heat_here,
            solid_here,
            voxel,
            dest,
            coeff,
        ],
        "collide_first",
    )
    near = lax.ppermute(to_near, "sub", near_pairs)
    next_ = lax.ppermute(to_next, "sub", next_pairs)
    faces = [shape(face_rows, along)] * 2
    face_r, face_l = call(
        edge_kernel,
        faces,
        [post, shares, solid_here],
        "x_faces",
        scratch=[pltpu.VMEM((gathered_rows, along), f32)] * 2,
        flops=1 << 32,
    )
    to_a, to_b = call(
        functools.partial(side_kernel, layers),
        faces,
        [near, face_r, face_l],
        "x_sides",
        scratch=[pltpu.VMEM((face_rows, along), f32)] * 2,
    )
    side_a, side_b = swaps("grp")
    faces_a = lax.ppermute(to_a, "grp", side_a)
    faces_b = lax.ppermute(to_b, "grp", side_b)
    hits, flipped, rest, start_slots, turn = call(
        ready_kernel,
        [
            shape(slots, WIDTH, dtype=bf16),
            shape(blocks, piece, piece),
            shape(blocks, piece),
            shape(lines, WIDTH),
            shape(blocks, WIDTH, dtype=jnp.int32),
        ],
        [block_pattern, slot_node, node_diag, heat_source, solid_start, coupling, to_a],
        "solid_ready",
        scalars=(0,),
    )
    hot, motion, send_near, send_next, fluxes = call(
        second_kernel,
        [
            shape(layers, across, along),
            shape(3, layers, across, along),
            shape(4, across, along),
            shape(4, across, along),
            shape(4 * lines, WIDTH),
        ],
        [
            post,
            near,
            next_,
            to_a,
            to_b,
            faces_a,
            faces_b,
            solid_here,
            to_next,
            rest,
        ],
        "collide_second",
        scratch=[
            pltpu.VMEM((FLOWS + HEATS, layers, across, along), f32),
            pltpu.VMEM((FACE, 8, along), f32),
        ]
        + [pltpu.VMEM((face_rows, along), f32)] * 4,
    )
    settled = cap != WIDTH
    if settled:
        fluxes = fluxes.reshape(lines, 4, WIDTH // cap, cap).transpose(0, 2, 1, 3)
    fluxes = fluxes.reshape(slabs, 4, cap)
    landed = lax.all_to_all(fluxes, "sub", split_axis=0, concat_axis=0, tiled=True)
    if settled:
        landed = jnp.stack(
            [
                landed[:, 0],
                jnp.roll(landed[:, 1], 1, axis=0),
                jnp.roll(landed[:, 2], -1, axis=0),
                landed[:, 3],
            ]
        )
        landed = landed.reshape(4, lines, WIDTH).transpose(1, 0, 2)
    landed = landed.reshape(4 * lines, WIDTH)
    from_near = lax.ppermute(send_near, "sub", near_pairs)
    from_next = lax.ppermute(send_next, "sub", next_pairs)
    residual, image, go = call(
        functools.partial(solve_kernel, cap),
        [shape(blocks, piece), shape(blocks, piece), shape(bands * lines * 4, WIDTH)],
        [
            turn,
            slot_node,
            node_diag,
            solid_start,
            coupling,
            hits,
            flipped,
            rest,
            start_slots,
            landed,
        ],
        "solve",
    )
    if settled:
        go = go.reshape(bands, lines, 4, WIDTH // cap, cap).transpose(0, 1, 3, 2, 4)
    go = go.reshape(bands * slabs, 4, cap)
    come = lax.all_to_all(go, ("grp", "sub"), split_axis=0, concat_axis=0, tiled=True)
    hot_out, motion_out = call(
        join_kernel,
        [shape(*hot.shape), shape(*motion.shape)],
        [hot, motion, from_near, from_next],
        "join",
    )
    if settled:
        own = lax.dynamic_slice_in_dim(come, lax.axis_index("grp") * slabs, slabs, 0)
        own = own.transpose(1, 0, 2).reshape(4, lines, WIDTH).transpose(1, 0, 2)
        own = own.reshape(4 * lines, WIDTH)
        come = jnp.pad(come, ((0, 0), (0, 0), (0, WIDTH - cap)))
    else:
        own = rest
    come = come.reshape(4 * bands * slabs, WIDTH)
    temp, seen = call(
        functools.partial(last_kernel, not settled),
        [shape(1, blocks, piece), shape(1, rows)],
        [
            come,
            own,
            solid_start,
            residual,
            image,
            ordinal,
        ],
        "finish",
    )
    return hot_out, motion_out, temp, seen


def solution(mesh):
    placed = (
        P(None, "sub", "grp", None),
        P(None, "sub", "grp", None),
        P("sub", "grp", None),
        P("grp", "sub"),
        P("grp", "sub", None),
        P("grp", "sub"),
        P("grp", "sub"),
        P("grp", "sub", None),
        P("grp", "sub", None, None),
        P("grp", "sub"),
        P("grp", "sub", None),
        P("grp", "sub", None),
    )
    return jax.shard_map(
        body,
        mesh=mesh,
        in_specs=placed,
        out_specs=(
            P("sub", "grp", None),
            P(None, "sub", "grp", None),
            P("grp", "sub", None),
            P("grp", "sub"),
        ),
        check_vma=False,
    )
```

```python
import functools
import jax
import jax.numpy as jnp
import numpy as np
from jax import lax
from jax.experimental import pallas as pl
from jax.experimental.pallas import tpu as pltpu
from jax.sharding import PartitionSpec as P

FLOW_VELOCITY = [
    (0, 0, 0),
    (1, 0, 0),
    (-1, 0, 0),
    (0, 1, 0),
    (0, -1, 0),
    (0, 0, 1),
    (0, 0, -1),
    (1, 1, 0),
    (-1, -1, 0),
    (1, -1, 0),
    (-1, 1, 0),
    (1, 0, 1),
    (-1, 0, -1),
    (1, 0, -1),
    (-1, 0, 1),
    (0, 1, 1),
    (0, -1, -1),
    (0, 1, -1),
    (0, -1, 1),
]
VELOCITY = FLOW_VELOCITY + FLOW_VELOCITY[:7]
FLOWS, HEATS = 19, 7
LANES_ALL = range(FLOWS + HEATS)
UP = [i for i in LANES_ALL if VELOCITY[i][2] == 1]
DOWN = [
    next(j for j in LANES_ALL if VELOCITY[j] == VELOCITY[i][:2] + (-1,) and (j < 19) == (i < 19))
    for i in UP
]
RIGHT = [i for i in LANES_ALL if VELOCITY[i][0] == 1]
LEFT = [
    next(j for j in LANES_ALL if VELOCITY[j] == (-1,) + VELOCITY[i][1:] and (j < 19) == (i < 19))
    for i in RIGHT
]
TURNED = [
    next(n for n, j in enumerate(RIGHT[:-1]) if VELOCITY[j][1:] == (-VELOCITY[i][1], -VELOCITY[i][2]))
    for i in RIGHT[:-1]
]
STILL = [i for i in LANES_ALL if VELOCITY[i][0] == 0]
GATHERED = len(STILL) + 2 * len(RIGHT)
SUMS = 4
FACE = SUMS + 2 * len(RIGHT) + 1
CORNER = 5


def place_of(lists, ex, ey, ez):
    return next(n for n, i in enumerate(lists) if VELOCITY[i] == (ex, ey, ez))


WIDTH = 128
SHIFT = 4.0
f32 = jnp.float32
bf16 = jnp.bfloat16


def signed_sum(terms):
    total = None
    for sign, term in terms:
        if sign == 0:
            continue
        if total is None:
            total = term if sign > 0 else -term
        else:
            total = total + term if sign > 0 else total - term
    return total


def collide(flow, heat, solid):
    pairs = range(1, FLOWS, 2)
    density = flow[0]
    for i in pairs:
        density = density + (flow[i] + flow[i + 1])
    gaps = {i: flow[i] - flow[i + 1] for i in pairs}
    scale = 1.0 / density
    speed = [
        signed_sum([(FLOW_VELOCITY[i][axis], gaps[i]) for i in pairs]) * scale for axis in range(3)
    ]
    square = speed[0] * speed[0] + speed[1] * speed[1] + speed[2] * speed[2]
    base = 1.0 - 1.5 * square
    gas = 1.0 - solid
    keep = gas * (1.0 - 1.0 / 0.8)
    pull = gas * (density * (1.0 / 0.8))
    flow_post = [None] * FLOWS
    flow_post[0] = (keep + solid) * flow[0] + (pull * (1.0 / 3.0)) * base
    shares = {1: pull * (1.0 / 18.0), 2: pull * (1.0 / 36.0)}
    for i in pairs:
        share = shares[sum(abs(c) for c in FLOW_VELOCITY[i])]
        along = signed_sum([(FLOW_VELOCITY[i][axis], speed[axis]) for axis in range(3)])
        even = base + 4.5 * along * along
        odd = 3.0 * along
        flow_post[i] = keep * flow[i] + share * (even + odd) + solid * flow[i + 1]
        flow_post[i + 1] = keep * flow[i + 1] + share * (even - odd) + solid * flow[i]
    hotness = heat[0]
    for j in range(1, HEATS):
        hotness = hotness + heat[j]
    stay = 1.0 - 1.0 / 0.7
    heat_post = [stay * heat[0] + (0.25 / 0.7) * hotness]
    level = (0.125 / 0.7) * hotness
    for j in range(1, HEATS, 2):
        axis = (j - 1) // 2
        drift = 4.0 * speed[axis]
        heat_post.append(stay * heat[j] + level * (1.0 + drift))
        heat_post.append(stay * heat[j + 1] + level * (1.0 - drift))
    return flow_post + heat_post


def collide_halo(still, inward, outward, solid):
    flows = RIGHT[:-1]
    density, along_y, along_z, hotness = still
    pairs = [(a + b, a - b) for a, b in zip(inward, outward)]
    across = None
    for n, i in enumerate(flows):
        _, ey, ez = VELOCITY[i]
        whole, gap = pairs[n]
        density = density + whole
        across = gap if across is None else across + gap
        along_y = signed_sum([(1, along_y), (ey, whole)])
        along_z = signed_sum([(1, along_z), (ez, whole)])
    hotness = hotness + pairs[-1][0]
    scale = 1.0 / density
    speed = [across * scale, along_y * scale, along_z * scale]
    square = speed[0] * speed[0] + speed[1] * speed[1] + speed[2] * speed[2]
    base = 1.0 - 1.5 * square
    gas = 1.0 - solid
    keep = gas * (1.0 - 1.0 / 0.8)
    pull = gas * (density * (1.0 / 0.8))
    shares = {1: pull * (1.0 / 18.0), 2: pull * (1.0 / 36.0)}
    out = []
    for n, i in enumerate(flows):
        share = shares[sum(abs(c) for c in VELOCITY[i])]
        along = signed_sum([(VELOCITY[i][axis], speed[axis]) for axis in range(3)])
        feq = share * (base + 4.5 * along * along + 3.0 * along)
        out.append(keep * inward[n] + feq + solid * outward[TURNED[n]])
    level = (0.125 / 0.7) * hotness
    out.append((1.0 - 1.0 / 0.7) * inward[-1] + level * (1.0 + 4.0 * speed[0]))
    return out


def three_parts(value):
    high = value.astype(bf16).astype(f32)
    rest = value - high
    middle = rest.astype(bf16).astype(f32)
    return [high, middle, rest - middle]


def times_transposed(left, right):
    return lax.dot_general(
        left.astype(bf16), right.astype(bf16), (((1,), (1,)), ((), ())), preferred_element_type=f32
    )


def spread(row):
    return jnp.broadcast_to(row, (8, row.shape[-1]))


def lane_gather(row, lane):
    return jnp.take_along_axis(spread(row), lane, axis=1, mode="promise_in_bounds")


def table_gather(table, index):
    place, lane = index >> 7, index & 127
    out = jnp.zeros(index.shape, f32)
    for row in range(table.shape[0]):
        out = jnp.where(place == row, lane_gather(table[row : row + 1], lane), out)
    return out


def plane_rows(plane, first=0, count=8):
    return pl.ds(4 * first + plane, count, stride=4)


def stacked(row):
    return jnp.concatenate(
        [row[:, k * WIDTH : (k + 1) * WIDTH] for k in range(row.shape[1] // WIDTH)], axis=0
    )


def slot_tables(cap, voxel, dest, coeff, ordinal):
    rows_here = dest.shape[1]
    owner = dest[...].astype(f32)
    chunks = rows_here // WIDTH
    tall = stacked(owner)
    tall = jnp.concatenate([tall] + [jnp.zeros((8 - chunks, WIDTH), f32)] * (chunks < 8), axis=0)
    upright = tall.T
    first = lax.broadcasted_iota(jnp.int32, (WIDTH, WIDTH), 0)
    second = lax.broadcasted_iota(jnp.int32, (WIDTH, WIDTH), 1)
    slot_row = lax.broadcasted_iota(jnp.int32, (8, WIDTH), 0)
    table = jnp.zeros((40, WIDTH), f32)
    for c in range(chunks):
        lanes = slice(c * WIDTH, (c + 1) * WIDTH)
        here = owner[:, lanes]
        count = jnp.zeros((WIDTH, WIDTH), f32)
        for other in range(c + 1):
            same = upright[:, other : other + 1] == here
            if other == c:
                same = same & (first < second)
            count = count + jnp.where(same, 1.0, 0.0)
        rank = jnp.sum(count, axis=0, keepdims=True)
        place = (here * float(cap) + rank).astype(jnp.int32)
        ordinal[:, lanes] = place
        mine = slot_row == (place >> 7)
        spot = voxel[:, lanes]
        parts = [(spot >> 7).astype(f32), (spot & 127).astype(f32)] + three_parts(coeff[:, lanes])
        values = jnp.concatenate([jnp.where(mine, part, 0.0) for part in parts], axis=0)
        table = table + times_transposed(values, jnp.where(first == (place & 127), 1.0, 0.0))
    spots = table[0:8] * float(WIDTH) + table[8:16]
    coeffs = (table[16:24] + table[24:32]) + table[32:40]
    return spots, coeffs


def on_even(axis="sub"):
    return lax.rem(lax.axis_index(axis), 2) == 0


def turned(tile, step):
    return tile if step == 0 else pltpu.roll(tile, step % tile.shape[1], 1)


def corner_shares(plane):
    across = plane.shape[1]
    up, right, left, ahead, behind = (
        place_of(UP, ex, ey, 1) for ex, ey in ((0, 0), (1, 0), (-1, 0), (0, 1), (0, -1))
    )
    warm = len(UP) - 1
    sides = []
    for column, inside, outward in ((across - 1, across - 2, right), (0, 1, left)):

        def row(n, at):
            return plane[n, at : at + 1, :]

        one, two = turned(row(ahead, column), 1), turned(row(behind, column), -1)
        rows = [
            row(up, column) + (one + two),
            one - two,
            row(warm, column),
            row(outward, inside),
            row(outward, column),
        ]
        sides.append(jnp.concatenate(rows, axis=0))
    return sides


def add_corners(face, below, above, layers):
    edge = SUMS + len(RIGHT)
    for corner, z, rise in ((below, 0, 1), (above, layers - 1, -1)):
        k = place_of(RIGHT, 1, 0, rise)
        adds = [(0, 1, 0), (1, 1, 1), (2, rise, 0), (3, 1, 2), (SUMS + k, 1, 3), (edge + k, 1, 4)]
        for n, sign, row in adds:
            at = n * layers + z
            share = corner[row : row + 1]
            face[at : at + 1, :] = face[at : at + 1, :] + (share if sign > 0 else -share)


def early_kernel(*refs):
    given, held, (shares, planes, arrived) = refs[:6], refs[6:12], refs[12:]
    pops, heat, solid = given[:3]
    pops_here, heat_here, solid_here = held[:3]
    layers, _, along = solid.shape
    even = on_even()
    facing = jnp.where(even, 0, layers - 1)
    pairs = ((pops, pops_here), (heat, heat_here))
    pieces = []
    for step in range(layers):
        z = lax.rem(facing + step, layers)
        pieces += [(source.at[:, z], target.at[:, z]) for source, target in pairs]
        pieces.append((solid.at[z], solid_here.at[z]))
    pieces += zip(given[3:], held[3:])
    copies = [
        pltpu.make_async_copy(source, target, arrived.at[n])
        for n, (source, target) in enumerate(pieces)
    ]
    for copy in copies:
        copy.start()
    for copy in copies[:3]:
        copy.wait()
    for start in range(0, along, WIDTH):
        lanes = slice(start, start + WIDTH)
        out = collide(
            [pops_here[i, facing, :, lanes] for i in range(FLOWS)],
            [heat_here[j, facing, :, lanes] for j in range(HEATS)],
            solid_here[facing, :, lanes],
        )
        for n, (above, below) in enumerate(zip(UP, DOWN)):
            planes[n, :, lanes] = jnp.where(even, out[below], out[above])
    shares[...] = jnp.zeros(shares.shape, f32)
    for n, side in enumerate(corner_shares(planes)):
        shares[8 * n : 8 * n + CORNER] = side
    for copy in copies[3:]:
        copy.wait()


def first_kernel(
    cap, pops, heat, solid, voxel, dest, coeff, post, to_near, to_next, ordinal
):
    layers, across, along = solid.shape
    even = on_even()
    spots, coeffs = slot_tables(cap, voxel, dest, coeff, ordinal)
    extra = len(UP)
    for plane in (to_near, to_next):
        plane[extra] = jnp.zeros(plane.shape[1:], f32)
        plane[extra, :, 0:WIDTH] = spots
        plane[extra, :, WIDTH : 2 * WIDTH] = coeffs
    for z in range(layers):
        for start in range(0, along, WIDTH):
            lanes = slice(start, start + WIDTH)
            out = collide(
                [pops[i, z, :, lanes] for i in range(FLOWS)],
                [heat[j, z, :, lanes] for j in range(HEATS)],
                solid[z, :, lanes],
            )
            for i in LANES_ALL:
                post[i, z, :, lanes] = out[i]
    for n, (above, below) in enumerate(zip(UP, DOWN)):
        above, below = post[above, layers - 1], post[below, 0]
        to_near[n] = jnp.where(even, above, below)
        to_next[n] = jnp.where(even, below, above)


def edge_kernel(post, shares, solid, face_r, face_l, out_r, out_l):
    layers, across, along = post.shape[1:]
    for out, lists, edge, inside in (
        (out_r, (STILL, RIGHT), across - 1, across - 2),
        (out_l, (STILL, LEFT), 0, 1),
    ):
        rows = [(i, edge) for i in lists[0]] + [(i, inside) for i in lists[1]]
        rows = rows + [(i, edge) for i in lists[1]]
        for n, (i, column) in enumerate(rows):
            for z in range(layers):
                at, source = n * layers + z, z - VELOCITY[i][2]
                if 0 <= source < layers:
                    out[at : at + 1, :] = post[i, source, column : column + 1, :]
                else:
                    out[at : at + 1, :] = jnp.zeros((1, along), f32)

    def both(n):
        at = slice(n * layers, (n + 1) * layers)
        return jnp.concatenate([out_r[at, :], out_l[at, :]], axis=0)

    def send(n, tile):
        at = slice(n * layers, (n + 1) * layers)
        face_r[at, :], face_l[at, :] = tile[0:layers], tile[layers : 2 * layers]

    sums = [[] for _ in range(SUMS)]
    for n, i in enumerate(STILL):
        _, ey, ez = VELOCITY[i]
        tile = turned(both(n), ey)
        if i >= FLOWS:
            sums[3].append((1, tile))
        else:
            sums[0].append((1, tile))
            sums[1].append((ey, tile))
            sums[2].append((ez, tile))
    for n in range(SUMS):
        send(n, signed_sum(sums[n]))
    for n, i in enumerate(RIGHT):
        send(SUMS + n, turned(both(len(STILL) + n), VELOCITY[i][1]))
    for n in range(len(STILL) + len(RIGHT), GATHERED):
        send(n - len(STILL) + SUMS, both(n))
    even = on_even()
    for n, (face, column) in enumerate(((face_r, across - 1), (face_l, 0))):
        for z in range(layers):
            at = (FACE - 1) * layers + z
            face[at : at + 1, :] = solid[z, column : column + 1, :]
        far = shares[8 * n : 8 * n + CORNER]
        add_corners(face, jnp.where(even, far, 0.0), jnp.where(even, 0.0, far), layers)


def side_kernel(layers, near, face_r, face_l, to_a, to_b, sum_r, sum_l):
    even, band_even = on_even(), on_even("grp")
    sides = zip((face_r, face_l), (sum_r, sum_l), corner_shares(near))
    for face, total, close in sides:
        total[...] = face[...]
        add_corners(total, jnp.where(even, 0.0, close), jnp.where(even, close, 0.0), layers)
    right, left = sum_r[...], sum_l[...]
    to_a[...] = jnp.where(band_even, right, left)
    to_b[...] = jnp.where(band_even, left, right)


def second_kernel(
    post,
    near,
    next_,
    to_a,
    to_b,
    faces_a,
    faces_b,
    solid,
    own_table,
    tie,
    hot,
    motion,
    send_near,
    send_next,
    fluxes,
    moved,
    halo,
    own_r,
    own_l,
    from_l,
    from_r,
):
    layers, across, along = solid.shape
    even = on_even()
    band_even = on_even("grp")
    own_r[...] = jnp.where(band_even, to_a[...], to_b[...])
    own_l[...] = jnp.where(band_even, to_b[...], to_a[...])
    below = [jnp.where(even, next_[n], near[n]) for n in range(len(UP) + 1)]
    above = [jnp.where(even, near[n], next_[n]) for n in range(len(UP) + 1)]
    from_l[...] = jnp.where(band_even, faces_b[...], faces_a[...])
    from_r[...] = jnp.where(band_even, faces_a[...], faces_b[...])
    slot = lax.broadcasted_iota(jnp.int32, (across, along), 0)
    edge = SUMS + len(RIGHT)
    for i in LANES_ALL:
        ex, ey, ez = VELOCITY[i]
        for z in range(layers):
            if z - ez < 0:
                tile = below[UP.index(i)]
            elif z - ez >= layers:
                tile = above[DOWN.index(i)]
            else:
                tile = post[i, z - ez]
            if ex == 1:
                at = (edge + RIGHT.index(i)) * layers + z
                tile = jnp.where(slot == 0, from_l[at : at + 1, :], pltpu.roll(tile, 1, 0))
            elif ex == -1:
                at = (edge + LEFT.index(i)) * layers + z
                tile = jnp.where(
                    slot == across - 1, from_r[at : at + 1, :], pltpu.roll(tile, across - 1, 0)
                )
            moved[i, z] = turned(tile, ey)

    def halves(low, high, n):
        at = slice(n * layers, (n + 1) * layers)
        parts = [low[at, :], high[at, :]]
        if 2 * layers < 8:
            parts.append(jnp.ones((8 - 2 * layers, along), f32))
        return jnp.concatenate(parts, axis=0)

    for n in range(edge):
        halo[n] = halves(from_l, from_r, n)
    for n, i in enumerate(RIGHT):
        halo[edge + n] = turned(halves(own_l, own_r, edge + n), VELOCITY[i][1])
    edge_solid = halves(from_l, from_r, FACE - 1)
    for start in range(0, along, WIDTH):
        lanes = slice(start, start + WIDTH)
        for z in range(layers):
            out = collide(
                [moved[i, z, :, lanes] for i in range(FLOWS)],
                [moved[FLOWS + j, z, :, lanes] for j in range(HEATS)],
                solid[z, :, lanes],
            )
            for i in LANES_ALL:
                moved[i, z, :, lanes] = out[i]
        out = collide_halo(
            [halo[n, :, lanes] for n in range(SUMS)],
            [halo[SUMS + n, :, lanes] for n in range(len(RIGHT))],
            [halo[edge + n, :, lanes] for n in range(len(RIGHT))],
            edge_solid[:, lanes],
        )
        for n in range(len(RIGHT)):
            halo[SUMS + n, :, lanes] = out[n]
    sums = {}

    def add(key, sign, tile):
        if sign == 0:
            return
        if key in sums:
            sums[key] = sums[key] + tile if sign > 0 else sums[key] - tile
        else:
            sums[key] = tile if sign > 0 else -tile

    for z in range(layers):
        for i in LANES_ALL:
            ex, ey, ez = VELOCITY[i]
            if i == 0:
                continue
            tile = moved[i, z]
            if ex == 1:
                side = halo[SUMS + RIGHT.index(i), z : z + 1, :]
                tile = jnp.where(slot == 0, side, pltpu.roll(tile, 1, 0))
            elif ex == -1:
                at = layers + z
                side = halo[SUMS + LEFT.index(i), at : at + 1, :]
                tile = jnp.where(slot == across - 1, side, pltpu.roll(tile, across - 1, 0))
            tile = turned(tile, ey)
            target = z + ez
            if i >= FLOWS:
                add((3, target), 1, tile)
            else:
                add((0, target), ex, tile)
                add((1, target), ey, tile)
                add((2, target), ez, tile)
    for z in range(layers):
        hot[z] = sums[3, z]
        for axis in range(3):
            motion[axis, z] = sums[axis, z]
    for part in range(4):
        send_near[part] = jnp.where(even, sums[part, layers], sums[part, -1])
        send_next[part] = jnp.where(even, sums[part, -1], sums[part, layers])
    extra = len(UP)
    per_line = along // WIDTH
    per_layer = across * per_line

    def flux(table, planes):
        index = table[:, 0:WIDTH].astype(jnp.int32)
        place, lane = index >> 7, index & 127
        out = jnp.zeros(lane.shape, f32)
        for z, plane in planes:
            for x in range(across):
                for c in range(per_line):
                    row = plane[x : x + 1, c * WIDTH : (c + 1) * WIDTH]
                    out = jnp.where(
                        place == z * per_layer + x * per_line + c, lane_gather(row, lane), out
                    )
        return out * table[:, WIDTH : 2 * WIDTH]

    mine = own_table[extra]
    fluxes[plane_rows(0), :] = flux(mine, [(z, sums[3, z]) for z in range(layers)])
    fluxes[plane_rows(1), :] = flux(above[extra], [(0, sums[3, layers])])
    fluxes[plane_rows(2), :] = flux(below[extra], [(layers - 1, sums[3, -1])])
    fluxes[plane_rows(3), :] = mine[:, WIDTH : 2 * WIDTH]


def sublane_gather(value, index):
    return jnp.take_along_axis(value, index, axis=0, mode="promise_in_bounds")


def coupled(vector, blocks, flipped, shift):
    count = vector.shape[0]
    upright = vector.T
    ahead, back = [], []
    for b in range(count):
        column = jnp.broadcast_to(upright[:, b : b + 1], blocks.shape[1:])
        back.append(jnp.sum(blocks[b] * column, axis=0, keepdims=True))
        ahead.append(jnp.sum(flipped[b] * column, axis=0, keepdims=True))
    ahead = jnp.concatenate(ahead, axis=0)
    back = jnp.concatenate(back, axis=0)
    block = lax.broadcasted_iota(jnp.int32, vector.shape, 0)
    ahead = sublane_gather(ahead, (block + shift) & (count - 1))
    return ahead + sublane_gather(back, (block - shift) & (count - 1))


def ready_kernel(
    pattern, nodes, diagonal, source, start, coupling, tie, hits, flipped, rest, slots, turn
):
    shift = pattern[0, 0]
    turn[...] = jnp.full(turn.shape, shift, jnp.int32)
    count = start.shape[1]
    for b in range(count):
        flipped[lax.rem(b + shift, count)] = coupling[0, b].T
    vector = start[0]
    rest[...] = (
        source[0] - diagonal[0] * vector + coupled(vector, coupling.at[0], flipped, turn[...])
    )
    index = stacked(nodes[...])
    slots[...] = table_gather(vector, index)
    upright = (index & 127).astype(f32).T.astype(jnp.int32)
    lane = lax.broadcasted_iota(jnp.int32, (WIDTH, WIDTH), 1)
    for s in range(index.shape[0]):
        hit = jnp.where(upright[:, s : s + 1] == lane, 1.0, 0.0)
        hits[s * WIDTH : (s + 1) * WIDTH] = hit.astype(bf16)


def solve_kernel(
    cap,
    turn,
    nodes,
    diagonal,
    start,
    coupling,
    hits,
    flipped,
    rest,
    slots,
    come,
    res,
    img,
    go,
):
    shift = turn[...]
    count = start.shape[1]
    index = stacked(nodes[...])
    place = index >> 7
    own, low, high, coeff = (come[plane_rows(plane), :] for plane in range(4))
    if cap == WIDTH:
        low = pltpu.roll(low, 1, 0)
        high = pltpu.roll(high, low.shape[0] - 1, 0)
    parts = three_parts(own + low + high) + three_parts(coeff)
    block = lax.broadcasted_iota(jnp.int32, (count, WIDTH), 0)
    values = []
    for s in range(index.shape[0]):
        mine = block == place[s : s + 1]
        values.append(
            jnp.concatenate([jnp.where(mine, part[s : s + 1], 0.0) for part in parts], axis=0)
        )
    values = jnp.concatenate(values, axis=1).astype(bf16)
    landed = jnp.dot(values, hits[...], preferred_element_type=f32)
    landed = [landed[k * count : (k + 1) * count] for k in range(len(parts))]
    added = (landed[0] + landed[1]) + landed[2]
    extra = (landed[3] + landed[4]) + landed[5]
    whole = diagonal[0] + extra
    blocks = coupling.at[0]
    residual = rest[...] + added - extra * start[0]
    image = whole * residual - coupled(residual, blocks, flipped, shift)

    def total(value):
        return jnp.sum(jnp.sum(value, axis=0, keepdims=True), axis=1, keepdims=True)

    offset = image - SHIFT * residual
    bend = whole * offset - coupled(offset, blocks, flipped, shift)
    totals = [
        total(residual * residual),
        total(residual * offset),
        total(offset * offset),
        total(offset * bend),
    ]
    res[...] = residual
    img[...] = image
    lane = lax.broadcasted_iota(jnp.int32, (8, WIDTH), 1) & (cap - 1)
    facts = jnp.zeros((8, WIDTH), f32)
    for n, fact in enumerate(totals):
        facts = jnp.where(lane == n, fact, facts)
    residual_slots = table_gather(residual, index)
    image_slots = table_gather(image, index)
    start_slots = slots[...]
    for group in range(0, go.shape[0] // 4, 8):
        go[plane_rows(0, group), :] = start_slots
        go[plane_rows(1, group), :] = residual_slots
        go[plane_rows(2, group), :] = image_slots
        go[plane_rows(3, group), :] = facts


def last_kernel(direct, come, own, start, res, img, ordinal, temp, seen, mine):
    places = stacked(ordinal[...])
    chunks = places.shape[0]
    if chunks < 8:
        places = jnp.concatenate([places, jnp.zeros((8 - chunks, WIDTH), jnp.int32)], axis=0)
    strip = own
    if direct:
        strip = mine
        first = lax.axis_index("grp") * strip.shape[0]
        strip[...] = come[pl.ds(pl.multiple_of(first, 8), strip.shape[0]), :]
    found = [table_gather(strip[plane_rows(plane), :], places) for plane in range(3)]
    facts = come[plane_rows(3, 0, come.shape[0] // 4), :]
    facts = jnp.sum(facts, axis=0, keepdims=True)
    all_norm, cross, square, energy = (
        lane_gather(facts, jnp.full((8, WIDTH), n, jnp.int32)) for n in range(4)
    )
    product = SHIFT * all_norm + cross
    inverse = 1.0 / product
    ratio = cross / all_norm
    spread_square = square - cross * ratio
    energy = energy - ratio * (2.0 * (square + SHIFT * cross) - ratio * product)
    small = spread_square * inverse
    first = all_norm * inverse
    step = spread_square / (energy - spread_square * small)
    of_residual = first + step * (1.0 + small * first)
    of_image = -step * first
    temp[0] = start[0] + of_residual * res[...] + of_image * img[...]
    found = found[0] + of_residual * found[1] + of_image * found[2]
    for c in range(chunks):
        seen[:, c * WIDTH : (c + 1) * WIDTH] = found[c : c + 1]


def join_kernel(hot, motion, near, next_, hot_out, motion_out):
    layers = hot.shape[0]
    even = on_even()
    below = [jnp.where(even, next_[n], near[n]) for n in range(4)]
    above = [jnp.where(even, near[n], next_[n]) for n in range(4)]
    for z in range(layers):
        for part in range(4):
            tile = hot[z] if part == 3 else motion[part, z]
            if z == 0:
                tile = tile + below[part]
            if z == layers - 1:
                tile = tile + above[part]
            if part == 3:
                hot_out[z] = tile
            else:
                motion_out[part, z] = tile


VMEM = pl.BlockSpec(memory_space=pltpu.VMEM)
ANYWHERE = pl.BlockSpec(memory_space=pl.ANY)
SMEM = pl.BlockSpec(memory_space=pltpu.SMEM)


def call(kernel, out, args, name, scalars=(), scratch=(), far=False, flops=1 << 20):
    total = sum(int(np.prod(a.shape)) * a.dtype.itemsize for a in list(args) + list(out))
    if far:
        args = [pltpu.with_memory_space_constraint(a, pltpu.HBM) for a in args]
    return pl.pallas_call(
        kernel,
        out_shape=out,
        in_specs=[
            ANYWHERE if far else SMEM if n in scalars else VMEM for n in range(len(args))
        ],
        out_specs=[VMEM] * len(out),
        scratch_shapes=scratch,
        compiler_params=pltpu.CompilerParams(vmem_limit_bytes=24 << 20),
        cost_estimate=pl.CostEstimate(flops=flops, bytes_accessed=total, transcendentals=0),
        name=name,
    )(*args)


def shape(*dims, dtype=f32):
    return jax.ShapeDtypeStruct(dims, dtype)


def swaps(axis):
    count = lax.axis_size(axis)
    assert count % 2 == 0
    near = [(k, k + 1 - 2 * (k % 2)) for k in range(count)]
    return near, [(k, (k - 1 + 2 * (k % 2)) % count) for k in range(count)]


def body(
    populations,
    heat_pops,
    solid_frac,
    coupled_grid_point,
    dest_index,
    heat_coeff,
    slot_node,
    node_diag,
    coupling,
    block_pattern,
    heat_source,
    solid_start,
):
    layers, across, along = solid_frac.shape
    slabs, bands = lax.axis_size("sub"), lax.axis_size("grp")
    slots = slot_node.shape[1]
    cap = slots // slabs
    rows = coupled_grid_point.shape[1]
    blocks, piece = node_diag.shape[1:]
    lines = slots // WIDTH
    assert lines == 8 and across == 8 and along >= 2 * WIDTH and along % WIDTH == 0
    assert piece == WIDTH and blocks == 8 and WIDTH % cap == 0 and cap >= 8
    assert rows % WIDTH == 0 and rows <= 8 * WIDTH and layers <= 4
    gathered_rows = -(-GATHERED * layers // 8) * 8
    face_rows = -(-FACE * layers // 8) * 8
    planes = len(UP) + 1
    near_pairs, next_pairs = swaps("sub")
    pops_here, heat_here, solid_here, voxel, dest, coeff, to_shares = call(
        early_kernel,
        [
            shape(*populations.shape),
            shape(*heat_pops.shape),
            shape(*solid_frac.shape),
            shape(1, rows, dtype=jnp.int32),
            shape(1, rows, dtype=jnp.int32),
            shape(1, rows),
            shape(16, along),
        ],
        [
            populations,
            heat_pops,
            solid_frac,
            coupled_grid_point,
            dest_index.reshape(1, rows),
            heat_coeff,
        ],
        "collide_early",
        scratch=[
            pltpu.VMEM((len(UP), across, along), f32),
            pltpu.SemaphoreType.DMA((3 * layers + 3,)),
        ],
        far=True,
    )
    shares = lax.ppermute(to_shares, "sub", next_pairs)
    post, to_near, to_next, ordinal = call(
        functools.partial(first_kernel, cap),
        [
            shape(FLOWS + HEATS, layers, across, along),
            shape(planes, across, along),
            shape(planes, across, along),
            shape(1, rows, dtype=jnp.int32),
        ],
        [
            pops_here,
            heat_here,
            solid_here,
            voxel,
            dest,
            coeff,
        ],
        "collide_first",
    )
    near = lax.ppermute(to_near, "sub", near_pairs)
    next_ = lax.ppermute(to_next, "sub", next_pairs)
    faces = [shape(face_rows, along)] * 2
    face_r, face_l = call(
        edge_kernel,
        faces,
        [post, shares, solid_here],
        "x_faces",
        scratch=[pltpu.VMEM((gathered_rows, along), f32)] * 2,
        flops=1 << 32,
    )
    to_a, to_b = call(
        functools.partial(side_kernel, layers),
        faces,
        [near, face_r, face_l],
        "x_sides",
        scratch=[pltpu.VMEM((face_rows, along), f32)] * 2,
    )
    side_a, side_b = swaps("grp")
    faces_a = lax.ppermute(to_a, "grp", side_a)
    faces_b = lax.ppermute(to_b, "grp", side_b)
    hits, flipped, rest, start_slots, turn = call(
        ready_kernel,
        [
            shape(slots, WIDTH, dtype=bf16),
            shape(blocks, piece, piece),
            shape(blocks, piece),
            shape(lines, WIDTH),
            shape(blocks, WIDTH, dtype=jnp.int32),
        ],
        [block_pattern, slot_node, node_diag, heat_source, solid_start, coupling, to_a],
        "solid_ready",
        scalars=(0,),
    )
    hot, motion, send_near, send_next, fluxes = call(
        second_kernel,
        [
            shape(layers, across, along),
            shape(3, layers, across, along),
            shape(4, across, along),
            shape(4, across, along),
            shape(4 * lines, WIDTH),
        ],
        [
            post,
            near,
            next_,
            to_a,
            to_b,
            faces_a,
            faces_b,
            solid_here,
            to_next,
            rest,
        ],
        "collide_second",
        scratch=[
            pltpu.VMEM((FLOWS + HEATS, layers, across, along), f32),
            pltpu.VMEM((FACE, 8, along), f32),
        ]
        + [pltpu.VMEM((face_rows, along), f32)] * 4,
    )
    settled = cap != WIDTH
    if settled:
        fluxes = fluxes.reshape(lines, 4, WIDTH // cap, cap).transpose(0, 2, 1, 3)
    fluxes = fluxes.reshape(slabs, 4, cap)
    landed = lax.all_to_all(fluxes, "sub", split_axis=0, concat_axis=0, tiled=True)
    if settled:
        landed = jnp.stack(
            [
                landed[:, 0],
                jnp.roll(landed[:, 1], 1, axis=0),
                jnp.roll(landed[:, 2], -1, axis=0),
                landed[:, 3],
            ]
        )
        landed = landed.reshape(4, lines, WIDTH).transpose(1, 0, 2)
    landed = landed.reshape(4 * lines, WIDTH)
    from_near = lax.ppermute(send_near, "sub", near_pairs)
    from_next = lax.ppermute(send_next, "sub", next_pairs)
    residual, image, go = call(
        functools.partial(solve_kernel, cap),
        [shape(blocks, piece), shape(blocks, piece), shape(bands * lines * 4, WIDTH)],
        [
            turn,
            slot_node,
            node_diag,
            solid_start,
            coupling,
            hits,
            flipped,
            rest,
            start_slots,
            landed,
        ],
        "solve",
    )
    if settled:
        go = go.reshape(bands, lines, 4, WIDTH // cap, cap).transpose(0, 1, 3, 2, 4)
    go = go.reshape(bands * slabs, 4, cap)
    come = lax.all_to_all(go, ("grp", "sub"), split_axis=0, concat_axis=0, tiled=True)
    hot_out, motion_out = call(
        join_kernel,
        [shape(*hot.shape), shape(*motion.shape)],
        [hot, motion, from_near, from_next],
        "join",
    )
    if settled:
        own = lax.dynamic_slice_in_dim(come, lax.axis_index("grp") * slabs, slabs, 0)
        own = own.transpose(1, 0, 2).reshape(4, lines, WIDTH).transpose(1, 0, 2)
        own = own.reshape(4 * lines, WIDTH)
        come = jnp.pad(come, ((0, 0), (0, 0), (0, WIDTH - cap)))
    else:
        own = rest
    come = come.reshape(4 * bands * slabs, WIDTH)
    temp, seen = call(
        functools.partial(last_kernel, not settled),
        [shape(1, blocks, piece), shape(1, rows)],
        [
            come,
            own,
            solid_start,
            residual,
            image,
            ordinal,
        ],
        "finish",
        scratch=[pltpu.VMEM((4 * lines, WIDTH), f32)],
    )
    return hot_out, motion_out, temp, seen


def solution(mesh):
    placed = (
        P(None, "sub", "grp", None),
        P(None, "sub", "grp", None),
        P("sub", "grp", None),
        P("grp", "sub"),
        P("grp", "sub", None),
        P("grp", "sub"),
        P("grp", "sub"),
        P("grp", "sub", None),
        P("grp", "sub", None, None),
        P("grp", "sub"),
        P("grp", "sub", None),
        P("grp", "sub", None),
    )
    return jax.shard_map(
        body,
        mesh=mesh,
        in_specs=placed,
        out_specs=(
            P("sub", "grp", None),
            P(None, "sub", "grp", None),
            P("grp", "sub", None),
            P("grp", "sub"),
        ),
        check_vma=False,
    )
```

```python
import functools
import jax
import jax.numpy as jnp
import numpy as np
from jax import lax
from jax.experimental import pallas as pl
from jax.experimental.pallas import tpu as pltpu
from jax.sharding import PartitionSpec as P

FLOW_VELOCITY = [
    (0, 0, 0),
    (1, 0, 0),
    (-1, 0, 0),
    (0, 1, 0),
    (0, -1, 0),
    (0, 0, 1),
    (0, 0, -1),
    (1, 1, 0),
    (-1, -1, 0),
    (1, -1, 0),
    (-1, 1, 0),
    (1, 0, 1),
    (-1, 0, -1),
    (1, 0, -1),
    (-1, 0, 1),
    (0, 1, 1),
    (0, -1, -1),
    (0, 1, -1),
    (0, -1, 1),
]
VELOCITY = FLOW_VELOCITY + FLOW_VELOCITY[:7]
FLOWS, HEATS = 19, 7
LANES_ALL = range(FLOWS + HEATS)
UP = [i for i in LANES_ALL if VELOCITY[i][2] == 1]
DOWN = [
    next(j for j in LANES_ALL if VELOCITY[j] == VELOCITY[i][:2] + (-1,) and (j < 19) == (i < 19))
    for i in UP
]
RIGHT = [i for i in LANES_ALL if VELOCITY[i][0] == 1]
LEFT = [
    next(j for j in LANES_ALL if VELOCITY[j] == (-1,) + VELOCITY[i][1:] and (j < 19) == (i < 19))
    for i in RIGHT
]
TURNED = [
    next(n for n, j in enumerate(RIGHT[:-1]) if VELOCITY[j][1:] == (-VELOCITY[i][1], -VELOCITY[i][2]))
    for i in RIGHT[:-1]
]
STILL = [i for i in LANES_ALL if VELOCITY[i][0] == 0]
GATHERED = len(STILL) + 2 * len(RIGHT)
SUMS = 4
FACE = SUMS + 2 * len(RIGHT) + 1
CORNER = 5


def place_of(lists, ex, ey, ez):
    return next(n for n, i in enumerate(lists) if VELOCITY[i] == (ex, ey, ez))


WIDTH = 128
SHIFT = 4.0
f32 = jnp.float32
bf16 = jnp.bfloat16


def signed_sum(terms):
    total = None
    for sign, term in terms:
        if sign == 0:
            continue
        if total is None:
            total = term if sign > 0 else -term
        else:
            total = total + term if sign > 0 else total - term
    return total


def collide(flow, heat, solid):
    pairs = range(1, FLOWS, 2)
    density = flow[0]
    for i in pairs:
        density = density + (flow[i] + flow[i + 1])
    gaps = {i: flow[i] - flow[i + 1] for i in pairs}
    scale = 1.0 / density
    speed = [
        signed_sum([(FLOW_VELOCITY[i][axis], gaps[i]) for i in pairs]) * scale for axis in range(3)
    ]
    square = speed[0] * speed[0] + speed[1] * speed[1] + speed[2] * speed[2]
    base = 1.0 - 1.5 * square
    gas = 1.0 - solid
    keep = gas * (1.0 - 1.0 / 0.8)
    pull = gas * (density * (1.0 / 0.8))
    flow_post = [None] * FLOWS
    flow_post[0] = (keep + solid) * flow[0] + (pull * (1.0 / 3.0)) * base
    shares = {1: pull * (1.0 / 18.0), 2: pull * (1.0 / 36.0)}
    for i in pairs:
        share = shares[sum(abs(c) for c in FLOW_VELOCITY[i])]
        along = signed_sum([(FLOW_VELOCITY[i][axis], speed[axis]) for axis in range(3)])
        even = base + 4.5 * along * along
        odd = 3.0 * along
        flow_post[i] = keep * flow[i] + share * (even + odd) + solid * flow[i + 1]
        flow_post[i + 1] = keep * flow[i + 1] + share * (even - odd) + solid * flow[i]
    hotness = heat[0]
    for j in range(1, HEATS):
        hotness = hotness + heat[j]
    stay = 1.0 - 1.0 / 0.7
    heat_post = [stay * heat[0] + (0.25 / 0.7) * hotness]
    level = (0.125 / 0.7) * hotness
    for j in range(1, HEATS, 2):
        axis = (j - 1) // 2
        drift = 4.0 * speed[axis]
        heat_post.append(stay * heat[j] + level * (1.0 + drift))
        heat_post.append(stay * heat[j + 1] + level * (1.0 - drift))
    return flow_post + heat_post


def collide_halo(still, inward, outward, solid):
    flows = RIGHT[:-1]
    density, along_y, along_z, hotness = still
    pairs = [(a + b, a - b) for a, b in zip(inward, outward)]
    across = None
    for n, i in enumerate(flows):
        _, ey, ez = VELOCITY[i]
        whole, gap = pairs[n]
        density = density + whole
        across = gap if across is None else across + gap
        along_y = signed_sum([(1, along_y), (ey, whole)])
        along_z = signed_sum([(1, along_z), (ez, whole)])
    hotness = hotness + pairs[-1][0]
    scale = 1.0 / density
    speed = [across * scale, along_y * scale, along_z * scale]
    square = speed[0] * speed[0] + speed[1] * speed[1] + speed[2] * speed[2]
    base = 1.0 - 1.5 * square
    gas = 1.0 - solid
    keep = gas * (1.0 - 1.0 / 0.8)
    pull = gas * (density * (1.0 / 0.8))
    shares = {1: pull * (1.0 / 18.0), 2: pull * (1.0 / 36.0)}
    out = []
    for n, i in enumerate(flows):
        share = shares[sum(abs(c) for c in VELOCITY[i])]
        along = signed_sum([(VELOCITY[i][axis], speed[axis]) for axis in range(3)])
        feq = share * (base + 4.5 * along * along + 3.0 * along)
        out.append(keep * inward[n] + feq + solid * outward[TURNED[n]])
    level = (0.125 / 0.7) * hotness
    out.append((1.0 - 1.0 / 0.7) * inward[-1] + level * (1.0 + 4.0 * speed[0]))
    return out


def three_parts(value):
    high = value.astype(bf16).astype(f32)
    rest = value - high
    middle = rest.astype(bf16).astype(f32)
    return [high, middle, rest - middle]


def times_transposed(left, right):
    return lax.dot_general(
        left.astype(bf16), right.astype(bf16), (((1,), (1,)), ((), ())), preferred_element_type=f32
    )


def spread(row):
    return jnp.broadcast_to(row, (8, row.shape[-1]))


def lane_gather(row, lane):
    return jnp.take_along_axis(spread(row), lane, axis=1, mode="promise_in_bounds")


def table_gather(table, index):
    place, lane = index >> 7, index & 127
    out = jnp.zeros(index.shape, f32)
    for row in range(table.shape[0]):
        out = jnp.where(place == row, lane_gather(table[row : row + 1], lane), out)
    return out


def plane_rows(plane, first=0, count=8):
    return pl.ds(4 * first + plane, count, stride=4)


def stacked(row):
    return jnp.concatenate(
        [row[:, k * WIDTH : (k + 1) * WIDTH] for k in range(row.shape[1] // WIDTH)], axis=0
    )


def slot_tables(cap, voxel, dest, coeff, ordinal):
    rows_here = dest.shape[1]
    owner = dest[...].astype(f32)
    chunks = rows_here // WIDTH
    tall = stacked(owner)
    tall = jnp.concatenate([tall] + [jnp.zeros((8 - chunks, WIDTH), f32)] * (chunks < 8), axis=0)
    upright = tall.T
    first = lax.broadcasted_iota(jnp.int32, (WIDTH, WIDTH), 0)
    second = lax.broadcasted_iota(jnp.int32, (WIDTH, WIDTH), 1)
    slot_row = lax.broadcasted_iota(jnp.int32, (8, WIDTH), 0)
    table = jnp.zeros((40, WIDTH), f32)
    for c in range(chunks):
        lanes = slice(c * WIDTH, (c + 1) * WIDTH)
        here = owner[:, lanes]
        count = jnp.zeros((WIDTH, WIDTH), f32)
        for other in range(c + 1):
            same = upright[:, other : other + 1] == here
            if other == c:
                same = same & (first < second)
            count = count + jnp.where(same, 1.0, 0.0)
        rank = jnp.sum(count, axis=0, keepdims=True)
        place = (here * float(cap) + rank).astype(jnp.int32)
        ordinal[:, lanes] = place
        mine = slot_row == (place >> 7)
        spot = voxel[:, lanes]
        parts = [(spot >> 7).astype(f32), (spot & 127).astype(f32)] + three_parts(coeff[:, lanes])
        values = jnp.concatenate([jnp.where(mine, part, 0.0) for part in parts], axis=0)
        table = table + times_transposed(values, jnp.where(first == (place & 127), 1.0, 0.0))
    spots = table[0:8] * float(WIDTH) + table[8:16]
    coeffs = (table[16:24] + table[24:32]) + table[32:40]
    return spots, coeffs


def on_even(axis="sub"):
    return lax.rem(lax.axis_index(axis), 2) == 0


def turned(tile, step):
    return tile if step == 0 else pltpu.roll(tile, step % tile.shape[1], 1)


def corner_shares(plane):
    across = plane.shape[1]
    up, right, left, ahead, behind = (
        place_of(UP, ex, ey, 1) for ex, ey in ((0, 0), (1, 0), (-1, 0), (0, 1), (0, -1))
    )
    warm = len(UP) - 1
    sides = []
    for column, inside, outward in ((across - 1, across - 2, right), (0, 1, left)):

        def row(n, at):
            return plane[n, at : at + 1, :]

        one, two = turned(row(ahead, column), 1), turned(row(behind, column), -1)
        rows = [
            row(up, column) + (one + two),
            one - two,
            row(warm, column),
            row(outward, inside),
            row(outward, column),
        ]
        sides.append(jnp.concatenate(rows, axis=0))
    return sides


def add_corners(face, below, above, layers):
    edge = SUMS + len(RIGHT)
    for corner, z, rise in ((below, 0, 1), (above, layers - 1, -1)):
        k = place_of(RIGHT, 1, 0, rise)
        adds = [(0, 1, 0), (1, 1, 1), (2, rise, 0), (3, 1, 2), (SUMS + k, 1, 3), (edge + k, 1, 4)]
        for n, sign, row in adds:
            at = n * layers + z
            share = corner[row : row + 1]
            face[at : at + 1, :] = face[at : at + 1, :] + (share if sign > 0 else -share)


def early_kernel(*refs):
    given, held, (shares, planes, arrived) = refs[:6], refs[6:12], refs[12:]
    pops, heat, solid = given[:3]
    pops_here, heat_here, solid_here = held[:3]
    layers, _, along = solid.shape
    even = on_even()
    facing = jnp.where(even, 0, layers - 1)
    pairs = ((pops, pops_here), (heat, heat_here))
    pieces = []
    for step in range(layers):
        z = lax.rem(facing + step, layers)
        pieces += [(source.at[:, z], target.at[:, z]) for source, target in pairs]
        pieces.append((solid.at[z], solid_here.at[z]))
    pieces += zip(given[3:], held[3:])
    copies = [
        pltpu.make_async_copy(source, target, arrived.at[n])
        for n, (source, target) in enumerate(pieces)
    ]
    for copy in copies:
        copy.start()
    for copy in copies[:3]:
        copy.wait()
    for start in range(0, along, WIDTH):
        lanes = slice(start, start + WIDTH)
        out = collide(
            [pops_here[i, facing, :, lanes] for i in range(FLOWS)],
            [heat_here[j, facing, :, lanes] for j in range(HEATS)],
            solid_here[facing, :, lanes],
        )
        for n, (above, below) in enumerate(zip(UP, DOWN)):
            planes[n, :, lanes] = jnp.where(even, out[below], out[above])
    shares[...] = jnp.zeros(shares.shape, f32)
    for n, side in enumerate(corner_shares(planes)):
        shares[8 * n : 8 * n + CORNER] = side
    for copy in copies[3:]:
        copy.wait()


def first_kernel(
    cap, pops, heat, solid, voxel, dest, coeff, post, to_near, to_next, ordinal
):
    layers, across, along = solid.shape
    even = on_even()
    spots, coeffs = slot_tables(cap, voxel, dest, coeff, ordinal)
    extra = len(UP)
    for plane in (to_near, to_next):
        plane[extra] = jnp.zeros(plane.shape[1:], f32)
        plane[extra, :, 0:WIDTH] = spots
        plane[extra, :, WIDTH : 2 * WIDTH] = coeffs
    for z in range(layers):
        for start in range(0, along, WIDTH):
            lanes = slice(start, start + WIDTH)
            out = collide(
                [pops[i, z, :, lanes] for i in range(FLOWS)],
                [heat[j, z, :, lanes] for j in range(HEATS)],
                solid[z, :, lanes],
            )
            for i in LANES_ALL:
                post[i, z, :, lanes] = out[i]
    for n, (above, below) in enumerate(zip(UP, DOWN)):
        above, below = post[above, layers - 1], post[below, 0]
        to_near[n] = jnp.where(even, above, below)
        to_next[n] = jnp.where(even, below, above)


def edge_kernel(post, shares, solid, face_r, face_l, out_r, out_l):
    layers, across, along = post.shape[1:]
    for out, lists, edge, inside in (
        (out_r, (STILL, RIGHT), across - 1, across - 2),
        (out_l, (STILL, LEFT), 0, 1),
    ):
        rows = [(i, edge) for i in lists[0]] + [(i, inside) for i in lists[1]]
        rows = rows + [(i, edge) for i in lists[1]]
        for n, (i, column) in enumerate(rows):
            for z in range(layers):
                at, source = n * layers + z, z - VELOCITY[i][2]
                if 0 <= source < layers:
                    out[at : at + 1, :] = post[i, source, column : column + 1, :]
                else:
                    out[at : at + 1, :] = jnp.zeros((1, along), f32)

    def both(n):
        at = slice(n * layers, (n + 1) * layers)
        return jnp.concatenate([out_r[at, :], out_l[at, :]], axis=0)

    def send(n, tile):
        at = slice(n * layers, (n + 1) * layers)
        face_r[at, :], face_l[at, :] = tile[0:layers], tile[layers : 2 * layers]

    sums = [[] for _ in range(SUMS)]
    for n, i in enumerate(STILL):
        _, ey, ez = VELOCITY[i]
        tile = turned(both(n), ey)
        if i >= FLOWS:
            sums[3].append((1, tile))
        else:
            sums[0].append((1, tile))
            sums[1].append((ey, tile))
            sums[2].append((ez, tile))
    for n in range(SUMS):
        send(n, signed_sum(sums[n]))
    for n, i in enumerate(RIGHT):
        send(SUMS + n, turned(both(len(STILL) + n), VELOCITY[i][1]))
    for n in range(len(STILL) + len(RIGHT), GATHERED):
        send(n - len(STILL) + SUMS, both(n))
    even = on_even()
    for n, (face, column) in enumerate(((face_r, across - 1), (face_l, 0))):
        for z in range(layers):
            at = (FACE - 1) * layers + z
            face[at : at + 1, :] = solid[z, column : column + 1, :]
        far = shares[8 * n : 8 * n + CORNER]
        add_corners(face, jnp.where(even, far, 0.0), jnp.where(even, 0.0, far), layers)


def side_kernel(layers, near, face_r, face_l, to_a, to_b, sum_r, sum_l):
    even, band_even = on_even(), on_even("grp")
    sides = zip((face_r, face_l), (sum_r, sum_l), corner_shares(near))
    for face, total, close in sides:
        total[...] = face[...]
        add_corners(total, jnp.where(even, 0.0, close), jnp.where(even, close, 0.0), layers)
    right, left = sum_r[...], sum_l[...]
    to_a[...] = jnp.where(band_even, right, left)
    to_b[...] = jnp.where(band_even, left, right)


def streamed_sums(moved, halo, chosen, layers):
    across, along = moved.shape[2:]
    slot = lax.broadcasted_iota(jnp.int32, (across, along), 0)
    sums = {}

    def add(key, sign, tile):
        if sign == 0:
            return
        if key in sums:
            sums[key] = sums[key] + tile if sign > 0 else sums[key] - tile
        else:
            sums[key] = tile if sign > 0 else -tile

    for z in range(layers):
        for i in chosen:
            ex, ey, ez = VELOCITY[i]
            if i == 0:
                continue
            tile = moved[i, z]
            if ex == 1:
                side = halo[SUMS + RIGHT.index(i), z : z + 1, :]
                tile = jnp.where(slot == 0, side, pltpu.roll(tile, 1, 0))
            elif ex == -1:
                at = layers + z
                side = halo[SUMS + LEFT.index(i), at : at + 1, :]
                tile = jnp.where(slot == across - 1, side, pltpu.roll(tile, across - 1, 0))
            tile = turned(tile, ey)
            target = z + ez
            if i >= FLOWS:
                add((3, target), 1, tile)
            else:
                add((0, target), ex, tile)
                add((1, target), ey, tile)
                add((2, target), ez, tile)
    return sums


def motion_kernel(moved, halo, rims, tie, motion, send_near, send_next):
    layers = moved.shape[1]
    even = on_even()
    sums = streamed_sums(moved, halo, range(1, FLOWS), layers)
    sums[3, layers], sums[3, -1] = rims[0], rims[1]
    for z in range(layers):
        for axis in range(3):
            motion[axis, z] = sums[axis, z]
    for part in range(4):
        send_near[part] = jnp.where(even, sums[part, layers], sums[part, -1])
        send_next[part] = jnp.where(even, sums[part, -1], sums[part, layers])


def second_kernel(
    post,
    near,
    next_,
    to_a,
    to_b,
    faces_a,
    faces_b,
    solid,
    own_table,
    tie,
    hot,
    rims,
    fluxes,
    moved,
    halo,
    own_r,
    own_l,
    from_l,
    from_r,
):
    layers, across, along = solid.shape
    even = on_even()
    band_even = on_even("grp")
    own_r[...] = jnp.where(band_even, to_a[...], to_b[...])
    own_l[...] = jnp.where(band_even, to_b[...], to_a[...])
    below = [jnp.where(even, next_[n], near[n]) for n in range(len(UP) + 1)]
    above = [jnp.where(even, near[n], next_[n]) for n in range(len(UP) + 1)]
    from_l[...] = jnp.where(band_even, faces_b[...], faces_a[...])
    from_r[...] = jnp.where(band_even, faces_a[...], faces_b[...])
    slot = lax.broadcasted_iota(jnp.int32, (across, along), 0)
    edge = SUMS + len(RIGHT)
    for i in LANES_ALL:
        ex, ey, ez = VELOCITY[i]
        for z in range(layers):
            if z - ez < 0:
                tile = below[UP.index(i)]
            elif z - ez >= layers:
                tile = above[DOWN.index(i)]
            else:
                tile = post[i, z - ez]
            if ex == 1:
                at = (edge + RIGHT.index(i)) * layers + z
                tile = jnp.where(slot == 0, from_l[at : at + 1, :], pltpu.roll(tile, 1, 0))
            elif ex == -1:
                at = (edge + LEFT.index(i)) * layers + z
                tile = jnp.where(
                    slot == across - 1, from_r[at : at + 1, :], pltpu.roll(tile, across - 1, 0)
                )
            moved[i, z] = turned(tile, ey)

    def halves(low, high, n):
        at = slice(n * layers, (n + 1) * layers)
        parts = [low[at, :], high[at, :]]
        if 2 * layers < 8:
            parts.append(jnp.ones((8 - 2 * layers, along), f32))
        return jnp.concatenate(parts, axis=0)

    for n in range(edge):
        halo[n] = halves(from_l, from_r, n)
    for n, i in enumerate(RIGHT):
        halo[edge + n] = turned(halves(own_l, own_r, edge + n), VELOCITY[i][1])
    edge_solid = halves(from_l, from_r, FACE - 1)
    for start in range(0, along, WIDTH):
        lanes = slice(start, start + WIDTH)
        for z in range(layers):
            out = collide(
                [moved[i, z, :, lanes] for i in range(FLOWS)],
                [moved[FLOWS + j, z, :, lanes] for j in range(HEATS)],
                solid[z, :, lanes],
            )
            for i in LANES_ALL:
                moved[i, z, :, lanes] = out[i]
        out = collide_halo(
            [halo[n, :, lanes] for n in range(SUMS)],
            [halo[SUMS + n, :, lanes] for n in range(len(RIGHT))],
            [halo[edge + n, :, lanes] for n in range(len(RIGHT))],
            edge_solid[:, lanes],
        )
        for n in range(len(RIGHT)):
            halo[SUMS + n, :, lanes] = out[n]
    sums = streamed_sums(moved, halo, range(FLOWS, FLOWS + HEATS), layers)
    for z in range(layers):
        hot[z] = sums[3, z]
    rims[0], rims[1] = sums[3, layers], sums[3, -1]
    extra = len(UP)
    per_line = along // WIDTH
    per_layer = across * per_line

    def flux(table, planes):
        index = table[:, 0:WIDTH].astype(jnp.int32)
        place, lane = index >> 7, index & 127
        out = jnp.zeros(lane.shape, f32)
        for z, plane in planes:
            for x in range(across):
                for c in range(per_line):
                    row = plane[x : x + 1, c * WIDTH : (c + 1) * WIDTH]
                    out = jnp.where(
                        place == z * per_layer + x * per_line + c, lane_gather(row, lane), out
                    )
        return out * table[:, WIDTH : 2 * WIDTH]

    mine = own_table[extra]
    fluxes[plane_rows(0), :] = flux(mine, [(z, sums[3, z]) for z in range(layers)])
    fluxes[plane_rows(1), :] = flux(above[extra], [(0, sums[3, layers])])
    fluxes[plane_rows(2), :] = flux(below[extra], [(layers - 1, sums[3, -1])])
    fluxes[plane_rows(3), :] = mine[:, WIDTH : 2 * WIDTH]


def sublane_gather(value, index):
    return jnp.take_along_axis(value, index, axis=0, mode="promise_in_bounds")


def coupled(vector, blocks, flipped, shift):
    count = vector.shape[0]
    upright = vector.T
    ahead, back = [], []
    for b in range(count):
        column = jnp.broadcast_to(upright[:, b : b + 1], blocks.shape[1:])
        back.append(jnp.sum(blocks[b] * column, axis=0, keepdims=True))
        ahead.append(jnp.sum(flipped[b] * column, axis=0, keepdims=True))
    ahead = jnp.concatenate(ahead, axis=0)
    back = jnp.concatenate(back, axis=0)
    block = lax.broadcasted_iota(jnp.int32, vector.shape, 0)
    ahead = sublane_gather(ahead, (block + shift) & (count - 1))
    return ahead + sublane_gather(back, (block - shift) & (count - 1))


def ready_kernel(
    pattern, nodes, diagonal, source, start, coupling, tie, hits, flipped, rest, slots, turn
):
    shift = pattern[0, 0]
    turn[...] = jnp.full(turn.shape, shift, jnp.int32)
    count = start.shape[1]
    for b in range(count):
        flipped[lax.rem(b + shift, count)] = coupling[0, b].T
    vector = start[0]
    rest[...] = (
        source[0] - diagonal[0] * vector + coupled(vector, coupling.at[0], flipped, turn[...])
    )
    index = stacked(nodes[...])
    slots[...] = table_gather(vector, index)
    upright = (index & 127).astype(f32).T.astype(jnp.int32)
    lane = lax.broadcasted_iota(jnp.int32, (WIDTH, WIDTH), 1)
    for s in range(index.shape[0]):
        hit = jnp.where(upright[:, s : s + 1] == lane, 1.0, 0.0)
        hits[s * WIDTH : (s + 1) * WIDTH] = hit.astype(bf16)


def solve_kernel(
    cap,
    turn,
    nodes,
    diagonal,
    start,
    coupling,
    hits,
    flipped,
    rest,
    slots,
    come,
    res,
    img,
    go,
):
    shift = turn[...]
    count = start.shape[1]
    index = stacked(nodes[...])
    place = index >> 7
    own, low, high, coeff = (come[plane_rows(plane), :] for plane in range(4))
    if cap == WIDTH:
        low = pltpu.roll(low, 1, 0)
        high = pltpu.roll(high, low.shape[0] - 1, 0)
    parts = three_parts(own + low + high) + three_parts(coeff)
    block = lax.broadcasted_iota(jnp.int32, (count, WIDTH), 0)
    values = []
    for s in range(index.shape[0]):
        mine = block == place[s : s + 1]
        values.append(
            jnp.concatenate([jnp.where(mine, part[s : s + 1], 0.0) for part in parts], axis=0)
        )
    values = jnp.concatenate(values, axis=1).astype(bf16)
    landed = jnp.dot(values, hits[...], preferred_element_type=f32)
    landed = [landed[k * count : (k + 1) * count] for k in range(len(parts))]
    added = (landed[0] + landed[1]) + landed[2]
    extra = (landed[3] + landed[4]) + landed[5]
    whole = diagonal[0] + extra
    blocks = coupling.at[0]
    residual = rest[...] + added - extra * start[0]
    image = whole * residual - coupled(residual, blocks, flipped, shift)

    def total(value):
        return jnp.sum(jnp.sum(value, axis=0, keepdims=True), axis=1, keepdims=True)

    offset = image - SHIFT * residual
    bend = whole * offset - coupled(offset, blocks, flipped, shift)
    totals = [
        total(residual * residual),
        total(residual * offset),
        total(offset * offset),
        total(offset * bend),
    ]
    res[...] = residual
    img[...] = image
    lane = lax.broadcasted_iota(jnp.int32, (8, WIDTH), 1) & (cap - 1)
    facts = jnp.zeros((8, WIDTH), f32)
    for n, fact in enumerate(totals):
        facts = jnp.where(lane == n, fact, facts)
    residual_slots = table_gather(residual, index)
    image_slots = table_gather(image, index)
    start_slots = slots[...]
    for group in range(0, go.shape[0] // 4, 8):
        go[plane_rows(0, group), :] = start_slots
        go[plane_rows(1, group), :] = residual_slots
        go[plane_rows(2, group), :] = image_slots
        go[plane_rows(3, group), :] = facts


def last_kernel(direct, come, own, start, res, img, ordinal, temp, seen, mine):
    places = stacked(ordinal[...])
    chunks = places.shape[0]
    if chunks < 8:
        places = jnp.concatenate([places, jnp.zeros((8 - chunks, WIDTH), jnp.int32)], axis=0)
    strip = own
    if direct:
        strip = mine
        first = lax.axis_index("grp") * strip.shape[0]
        strip[...] = come[pl.ds(pl.multiple_of(first, 8), strip.shape[0]), :]
    found = [table_gather(strip[plane_rows(plane), :], places) for plane in range(3)]
    facts = come[plane_rows(3, 0, come.shape[0] // 4), :]
    facts = jnp.sum(facts, axis=0, keepdims=True)
    all_norm, cross, square, energy = (
        lane_gather(facts, jnp.full((8, WIDTH), n, jnp.int32)) for n in range(4)
    )
    product = SHIFT * all_norm + cross
    inverse = 1.0 / product
    ratio = cross / all_norm
    spread_square = square - cross * ratio
    energy = energy - ratio * (2.0 * (square + SHIFT * cross) - ratio * product)
    small = spread_square * inverse
    first = all_norm * inverse
    step = spread_square / (energy - spread_square * small)
    of_residual = first + step * (1.0 + small * first)
    of_image = -step * first
    temp[0] = start[0] + of_residual * res[...] + of_image * img[...]
    found = found[0] + of_residual * found[1] + of_image * found[2]
    for c in range(chunks):
        seen[:, c * WIDTH : (c + 1) * WIDTH] = found[c : c + 1]


def join_kernel(hot, motion, near, next_, hot_out, motion_out):
    layers = hot.shape[0]
    even = on_even()
    below = [jnp.where(even, next_[n], near[n]) for n in range(4)]
    above = [jnp.where(even, near[n], next_[n]) for n in range(4)]
    for z in range(layers):
        for part in range(4):
            tile = hot[z] if part == 3 else motion[part, z]
            if z == 0:
                tile = tile + below[part]
            if z == layers - 1:
                tile = tile + above[part]
            if part == 3:
                hot_out[z] = tile
            else:
                motion_out[part, z] = tile


VMEM = pl.BlockSpec(memory_space=pltpu.VMEM)
ANYWHERE = pl.BlockSpec(memory_space=pl.ANY)
SMEM = pl.BlockSpec(memory_space=pltpu.SMEM)


def call(kernel, out, args, name, scalars=(), scratch=(), far=False, flops=1 << 20):
    total = sum(int(np.prod(a.shape)) * a.dtype.itemsize for a in list(args) + list(out))
    if far:
        args = [pltpu.with_memory_space_constraint(a, pltpu.HBM) for a in args]
    return pl.pallas_call(
        kernel,
        out_shape=out,
        in_specs=[
            ANYWHERE if far else SMEM if n in scalars else VMEM for n in range(len(args))
        ],
        out_specs=[VMEM] * len(out),
        scratch_shapes=scratch,
        compiler_params=pltpu.CompilerParams(vmem_limit_bytes=24 << 20),
        cost_estimate=pl.CostEstimate(flops=flops, bytes_accessed=total, transcendentals=0),
        name=name,
    )(*args)


def shape(*dims, dtype=f32):
    return jax.ShapeDtypeStruct(dims, dtype)


def swaps(axis):
    count = lax.axis_size(axis)
    assert count % 2 == 0
    near = [(k, k + 1 - 2 * (k % 2)) for k in range(count)]
    return near, [(k, (k - 1 + 2 * (k % 2)) % count) for k in range(count)]


def body(
    populations,
    heat_pops,
    solid_frac,
    coupled_grid_point,
    dest_index,
    heat_coeff,
    slot_node,
    node_diag,
    coupling,
    block_pattern,
    heat_source,
    solid_start,
):
    layers, across, along = solid_frac.shape
    slabs, bands = lax.axis_size("sub"), lax.axis_size("grp")
    slots = slot_node.shape[1]
    cap = slots // slabs
    rows = coupled_grid_point.shape[1]
    blocks, piece = node_diag.shape[1:]
    lines = slots // WIDTH
    assert lines == 8 and across == 8 and along >= 2 * WIDTH and along % WIDTH == 0
    assert piece == WIDTH and blocks == 8 and WIDTH % cap == 0 and cap >= 8
    assert rows % WIDTH == 0 and rows <= 8 * WIDTH and layers <= 4
    gathered_rows = -(-GATHERED * layers // 8) * 8
    face_rows = -(-FACE * layers // 8) * 8
    planes = len(UP) + 1
    near_pairs, next_pairs = swaps("sub")
    pops_here, heat_here, solid_here, voxel, dest, coeff, to_shares = call(
        early_kernel,
        [
            shape(*populations.shape),
            shape(*heat_pops.shape),
            shape(*solid_frac.shape),
            shape(1, rows, dtype=jnp.int32),
            shape(1, rows, dtype=jnp.int32),
            shape(1, rows),
            shape(16, along),
        ],
        [
            populations,
            heat_pops,
            solid_frac,
            coupled_grid_point,
            dest_index.reshape(1, rows),
            heat_coeff,
        ],
        "collide_early",
        scratch=[
            pltpu.VMEM((len(UP), across, along), f32),
            pltpu.SemaphoreType.DMA((3 * layers + 3,)),
        ],
        far=True,
    )
    shares = lax.ppermute(to_shares, "sub", next_pairs)
    post, to_near, to_next, ordinal = call(
        functools.partial(first_kernel, cap),
        [
            shape(FLOWS + HEATS, layers, across, along),
            shape(planes, across, along),
            shape(planes, across, along),
            shape(1, rows, dtype=jnp.int32),
        ],
        [
            pops_here,
            heat_here,
            solid_here,
            voxel,
            dest,
            coeff,
        ],
        "collide_first",
    )
    near = lax.ppermute(to_near, "sub", near_pairs)
    next_ = lax.ppermute(to_next, "sub", next_pairs)
    faces = [shape(face_rows, along)] * 2
    face_r, face_l = call(
        edge_kernel,
        faces,
        [post, shares, solid_here],
        "x_faces",
        scratch=[pltpu.VMEM((gathered_rows, along), f32)] * 2,
        flops=1 << 32,
    )
    to_a, to_b = call(
        functools.partial(side_kernel, layers),
        faces,
        [near, face_r, face_l],
        "x_sides",
        scratch=[pltpu.VMEM((face_rows, along), f32)] * 2,
    )
    side_a, side_b = swaps("grp")
    faces_a = lax.ppermute(to_a, "grp", side_a)
    faces_b = lax.ppermute(to_b, "grp", side_b)
    hits, flipped, rest, start_slots, turn = call(
        ready_kernel,
        [
            shape(slots, WIDTH, dtype=bf16),
            shape(blocks, piece, piece),
            shape(blocks, piece),
            shape(lines, WIDTH),
            shape(blocks, WIDTH, dtype=jnp.int32),
        ],
        [block_pattern, slot_node, node_diag, heat_source, solid_start, coupling, to_a],
        "solid_ready",
        scalars=(0,),
    )
    hot, rims, fluxes, moved, halo = call(
        second_kernel,
        [
            shape(layers, across, along),
            shape(2, across, along),
            shape(4 * lines, WIDTH),
            shape(FLOWS + HEATS, layers, across, along),
            shape(FACE, 8, along),
        ],
        [
            post,
            near,
            next_,
            to_a,
            to_b,
            faces_a,
            faces_b,
            solid_here,
            to_next,
            rest,
        ],
        "collide_second",
        scratch=[pltpu.VMEM((face_rows, along), f32)] * 4,
    )
    settled = cap != WIDTH
    if settled:
        fluxes = fluxes.reshape(lines, 4, WIDTH // cap, cap).transpose(0, 2, 1, 3)
    fluxes = fluxes.reshape(slabs, 4, cap)
    landed = lax.all_to_all(fluxes, "sub", split_axis=0, concat_axis=0, tiled=True)
    if settled:
        landed = jnp.stack(
            [
                landed[:, 0],
                jnp.roll(landed[:, 1], 1, axis=0),
                jnp.roll(landed[:, 2], -1, axis=0),
                landed[:, 3],
            ]
        )
        landed = landed.reshape(4, lines, WIDTH).transpose(1, 0, 2)
    landed = landed.reshape(4 * lines, WIDTH)
    residual, image, go = call(
        functools.partial(solve_kernel, cap),
        [shape(blocks, piece), shape(blocks, piece), shape(bands * lines * 4, WIDTH)],
        [
            turn,
            slot_node,
            node_diag,
            solid_start,
            coupling,
            hits,
            flipped,
            rest,
            start_slots,
            landed,
        ],
        "solve",
    )
    motion, send_near, send_next = call(
        motion_kernel,
        [
            shape(3, layers, across, along),
            shape(4, across, along),
            shape(4, across, along),
        ],
        [moved, halo, rims, residual],
        "motion",
    )
    from_near = lax.ppermute(send_near, "sub", near_pairs)
    from_next = lax.ppermute(send_next, "sub", next_pairs)
    if settled:
        go = go.reshape(bands, lines, 4, WIDTH // cap, cap).transpose(0, 1, 3, 2, 4)
    go = go.reshape(bands * slabs, 4, cap)
    come = lax.all_to_all(go, ("grp", "sub"), split_axis=0, concat_axis=0, tiled=True)
    hot_out, motion_out = call(
        join_kernel,
        [shape(*hot.shape), shape(*motion.shape)],
        [hot, motion, from_near, from_next],
        "join",
    )
    if settled:
        own = lax.dynamic_slice_in_dim(come, lax.axis_index("grp") * slabs, slabs, 0)
        own = own.transpose(1, 0, 2).reshape(4, lines, WIDTH).transpose(1, 0, 2)
        own = own.reshape(4 * lines, WIDTH)
        come = jnp.pad(come, ((0, 0), (0, 0), (0, WIDTH - cap)))
    else:
        own = rest
    come = come.reshape(4 * bands * slabs, WIDTH)
    temp, seen = call(
        functools.partial(last_kernel, not settled),
        [shape(1, blocks, piece), shape(1, rows)],
        [
            come,
            own,
            solid_start,
            residual,
            image,
            ordinal,
        ],
        "finish",
        scratch=[pltpu.VMEM((4 * lines, WIDTH), f32)],
    )
    return hot_out, motion_out, temp, seen


def solution(mesh):
    placed = (
        P(None, "sub", "grp", None),
        P(None, "sub", "grp", None),
        P("sub", "grp", None),
        P("grp", "sub"),
        P("grp", "sub", None),
        P("grp", "sub"),
        P("grp", "sub"),
        P("grp", "sub", None),
        P("grp", "sub", None, None),
        P("grp", "sub"),
        P("grp", "sub", None),
        P("grp", "sub", None),
    )
    return jax.shard_map(
        body,
        mesh=mesh,
        in_specs=placed,
        out_specs=(
            P("sub", "grp", None),
            P(None, "sub", "grp", None),
            P("grp", "sub", None),
            P("grp", "sub"),
        ),
        check_vma=False,
    )
```

```python
import functools
import jax
import jax.numpy as jnp
import numpy as np
from jax import lax
from jax.experimental import pallas as pl
from jax.experimental.pallas import tpu as pltpu
from jax.sharding import PartitionSpec as P

FLOW_VELOCITY = [
    (0, 0, 0),
    (1, 0, 0),
    (-1, 0, 0),
    (0, 1, 0),
    (0, -1, 0),
    (0, 0, 1),
    (0, 0, -1),
    (1, 1, 0),
    (-1, -1, 0),
    (1, -1, 0),
    (-1, 1, 0),
    (1, 0, 1),
    (-1, 0, -1),
    (1, 0, -1),
    (-1, 0, 1),
    (0, 1, 1),
    (0, -1, -1),
    (0, 1, -1),
    (0, -1, 1),
]
VELOCITY = FLOW_VELOCITY + FLOW_VELOCITY[:7]
FLOWS, HEATS = 19, 7
LANES_ALL = range(FLOWS + HEATS)
UP = [i for i in LANES_ALL if VELOCITY[i][2] == 1]
DOWN = [
    next(j for j in LANES_ALL if VELOCITY[j] == VELOCITY[i][:2] + (-1,) and (j < 19) == (i < 19))
    for i in UP
]
RIGHT = [i for i in LANES_ALL if VELOCITY[i][0] == 1]
LEFT = [
    next(j for j in LANES_ALL if VELOCITY[j] == (-1,) + VELOCITY[i][1:] and (j < 19) == (i < 19))
    for i in RIGHT
]
TURNED = [
    next(n for n, j in enumerate(RIGHT[:-1]) if VELOCITY[j][1:] == (-VELOCITY[i][1], -VELOCITY[i][2]))
    for i in RIGHT[:-1]
]
STILL = [i for i in LANES_ALL if VELOCITY[i][0] == 0]
GATHERED = len(STILL) + 2 * len(RIGHT)
SUMS = 4
FACE = SUMS + 2 * len(RIGHT) + 1
CORNER = 5


def place_of(lists, ex, ey, ez):
    return next(n for n, i in enumerate(lists) if VELOCITY[i] == (ex, ey, ez))


WIDTH = 128
SHIFT = 4.0
f32 = jnp.float32
bf16 = jnp.bfloat16


def signed_sum(terms):
    total = None
    for sign, term in terms:
        if sign == 0:
            continue
        if total is None:
            total = term if sign > 0 else -term
        else:
            total = total + term if sign > 0 else total - term
    return total


def collide(flow, heat, solid):
    pairs = range(1, FLOWS, 2)
    density = flow[0]
    for i in pairs:
        density = density + (flow[i] + flow[i + 1])
    gaps = {i: flow[i] - flow[i + 1] for i in pairs}
    scale = 1.0 / density
    speed = [
        signed_sum([(FLOW_VELOCITY[i][axis], gaps[i]) for i in pairs]) * scale for axis in range(3)
    ]
    square = speed[0] * speed[0] + speed[1] * speed[1] + speed[2] * speed[2]
    base = 1.0 - 1.5 * square
    gas = 1.0 - solid
    keep = gas * (1.0 - 1.0 / 0.8)
    pull = gas * (density * (1.0 / 0.8))
    flow_post = [None] * FLOWS
    flow_post[0] = (keep + solid) * flow[0] + (pull * (1.0 / 3.0)) * base
    shares = {1: pull * (1.0 / 18.0), 2: pull * (1.0 / 36.0)}
    for i in pairs:
        share = shares[sum(abs(c) for c in FLOW_VELOCITY[i])]
        along = signed_sum([(FLOW_VELOCITY[i][axis], speed[axis]) for axis in range(3)])
        even = base + 4.5 * along * along
        odd = 3.0 * along
        flow_post[i] = keep * flow[i] + share * (even + odd) + solid * flow[i + 1]
        flow_post[i + 1] = keep * flow[i + 1] + share * (even - odd) + solid * flow[i]
    hotness = heat[0]
    for j in range(1, HEATS):
        hotness = hotness + heat[j]
    stay = 1.0 - 1.0 / 0.7
    heat_post = [stay * heat[0] + (0.25 / 0.7) * hotness]
    level = (0.125 / 0.7) * hotness
    for j in range(1, HEATS, 2):
        axis = (j - 1) // 2
        drift = 4.0 * speed[axis]
        heat_post.append(stay * heat[j] + level * (1.0 + drift))
        heat_post.append(stay * heat[j + 1] + level * (1.0 - drift))
    return flow_post + heat_post


def collide_halo(still, inward, outward, solid):
    flows = RIGHT[:-1]
    density, along_y, along_z, hotness = still
    pairs = [(a + b, a - b) for a, b in zip(inward, outward)]
    across = None
    for n, i in enumerate(flows):
        _, ey, ez = VELOCITY[i]
        whole, gap = pairs[n]
        density = density + whole
        across = gap if across is None else across + gap
        along_y = signed_sum([(1, along_y), (ey, whole)])
        along_z = signed_sum([(1, along_z), (ez, whole)])
    hotness = hotness + pairs[-1][0]
    scale = 1.0 / density
    speed = [across * scale, along_y * scale, along_z * scale]
    square = speed[0] * speed[0] + speed[1] * speed[1] + speed[2] * speed[2]
    base = 1.0 - 1.5 * square
    gas = 1.0 - solid
    keep = gas * (1.0 - 1.0 / 0.8)
    pull = gas * (density * (1.0 / 0.8))
    shares = {1: pull * (1.0 / 18.0), 2: pull * (1.0 / 36.0)}
    out = []
    for n, i in enumerate(flows):
        share = shares[sum(abs(c) for c in VELOCITY[i])]
        along = signed_sum([(VELOCITY[i][axis], speed[axis]) for axis in range(3)])
        feq = share * (base + 4.5 * along * along + 3.0 * along)
        out.append(keep * inward[n] + feq + solid * outward[TURNED[n]])
    level = (0.125 / 0.7) * hotness
    out.append((1.0 - 1.0 / 0.7) * inward[-1] + level * (1.0 + 4.0 * speed[0]))
    return out


def three_parts(value):
    high = value.astype(bf16).astype(f32)
    rest = value - high
    middle = rest.astype(bf16).astype(f32)
    return [high, middle, rest - middle]


def two_parts(value):
    high = value.astype(bf16).astype(f32)
    return [high, value - high]


def times_transposed(left, right):
    return lax.dot_general(
        left.astype(bf16), right.astype(bf16), (((1,), (1,)), ((), ())), preferred_element_type=f32
    )


def spread(row):
    return jnp.broadcast_to(row, (8, row.shape[-1]))


def lane_gather(row, lane):
    return jnp.take_along_axis(spread(row), lane, axis=1, mode="promise_in_bounds")


def table_gather(table, index):
    place, lane = index >> 7, index & 127
    out = jnp.zeros(index.shape, f32)
    for row in range(table.shape[0]):
        out = jnp.where(place == row, lane_gather(table[row : row + 1], lane), out)
    return out


def plane_rows(plane, first=0, count=8):
    return pl.ds(4 * first + plane, count, stride=4)


def stacked(row):
    return jnp.concatenate(
        [row[:, k * WIDTH : (k + 1) * WIDTH] for k in range(row.shape[1] // WIDTH)], axis=0
    )


def slot_tables(cap, voxel, dest, coeff, ordinal):
    rows_here = dest.shape[1]
    owner = dest[...].astype(f32)
    chunks = rows_here // WIDTH
    tall = stacked(owner)
    tall = jnp.concatenate([tall] + [jnp.zeros((8 - chunks, WIDTH), f32)] * (chunks < 8), axis=0)
    upright = tall.T
    first = lax.broadcasted_iota(jnp.int32, (WIDTH, WIDTH), 0)
    second = lax.broadcasted_iota(jnp.int32, (WIDTH, WIDTH), 1)
    slot_row = lax.broadcasted_iota(jnp.int32, (8, WIDTH), 0)
    table = jnp.zeros((40, WIDTH), f32)
    for c in range(chunks):
        lanes = slice(c * WIDTH, (c + 1) * WIDTH)
        here = owner[:, lanes]
        count = jnp.zeros((WIDTH, WIDTH), f32)
        for other in range(c + 1):
            same = upright[:, other : other + 1] == here
            if other == c:
                same = same & (first < second)
            count = count + jnp.where(same, 1.0, 0.0)
        rank = jnp.sum(count, axis=0, keepdims=True)
        place = (here * float(cap) + rank).astype(jnp.int32)
        ordinal[:, lanes] = place
        mine = slot_row == (place >> 7)
        spot = voxel[:, lanes]
        parts = [(spot >> 7).astype(f32), (spot & 127).astype(f32)] + three_parts(coeff[:, lanes])
        values = jnp.concatenate([jnp.where(mine, part, 0.0) for part in parts], axis=0)
        table = table + times_transposed(values, jnp.where(first == (place & 127), 1.0, 0.0))
    spots = table[0:8] * float(WIDTH) + table[8:16]
    coeffs = (table[16:24] + table[24:32]) + table[32:40]
    return spots, coeffs


def on_even(axis="sub"):
    return lax.rem(lax.axis_index(axis), 2) == 0


def turned(tile, step):
    return tile if step == 0 else pltpu.roll(tile, step % tile.shape[1], 1)


def corner_shares(plane):
    across = plane.shape[1]
    up, right, left, ahead, behind = (
        place_of(UP, ex, ey, 1) for ex, ey in ((0, 0), (1, 0), (-1, 0), (0, 1), (0, -1))
    )
    warm = len(UP) - 1
    sides = []
    for column, inside, outward in ((across - 1, across - 2, right), (0, 1, left)):

        def row(n, at):
            return plane[n, at : at + 1, :]

        one, two = turned(row(ahead, column), 1), turned(row(behind, column), -1)
        rows = [
            row(up, column) + (one + two),
            one - two,
            row(warm, column),
            row(outward, inside),
            row(outward, column),
        ]
        sides.append(jnp.concatenate(rows, axis=0))
    return sides


def add_corners(face, below, above, layers):
    edge = SUMS + len(RIGHT)
    for corner, z, rise in ((below, 0, 1), (above, layers - 1, -1)):
        k = place_of(RIGHT, 1, 0, rise)
        adds = [(0, 1, 0), (1, 1, 1), (2, rise, 0), (3, 1, 2), (SUMS + k, 1, 3), (edge + k, 1, 4)]
        for n, sign, row in adds:
            at = n * layers + z
            share = corner[row : row + 1]
            face[at : at + 1, :] = face[at : at + 1, :] + (share if sign > 0 else -share)


def early_kernel(*refs):
    given, held, (shares, planes, arrived) = refs[:6], refs[6:12], refs[12:]
    pops, heat, solid = given[:3]
    pops_here, heat_here, solid_here = held[:3]
    layers, _, along = solid.shape
    even = on_even()
    facing = jnp.where(even, 0, layers - 1)
    pairs = ((pops, pops_here), (heat, heat_here))
    pieces = []
    for step in range(layers):
        z = lax.rem(facing + step, layers)
        pieces += [(source.at[:, z], target.at[:, z]) for source, target in pairs]
        pieces.append((solid.at[z], solid_here.at[z]))
    pieces += zip(given[3:], held[3:])
    copies = [
        pltpu.make_async_copy(source, target, arrived.at[n])
        for n, (source, target) in enumerate(pieces)
    ]
    for copy in copies:
        copy.start()
    for copy in copies[:3]:
        copy.wait()
    for start in range(0, along, WIDTH):
        lanes = slice(start, start + WIDTH)
        out = collide(
            [pops_here[i, facing, :, lanes] for i in range(FLOWS)],
            [heat_here[j, facing, :, lanes] for j in range(HEATS)],
            solid_here[facing, :, lanes],
        )
        for n, (above, below) in enumerate(zip(UP, DOWN)):
            planes[n, :, lanes] = jnp.where(even, out[below], out[above])
    shares[...] = jnp.zeros(shares.shape, f32)
    for n, side in enumerate(corner_shares(planes)):
        shares[8 * n : 8 * n + CORNER] = side
    for copy in copies[3:]:
        copy.wait()


def first_kernel(
    cap, pops, heat, solid, voxel, dest, coeff, post, to_near, to_next, ordinal
):
    layers, across, along = solid.shape
    even = on_even()
    spots, coeffs = slot_tables(cap, voxel, dest, coeff, ordinal)
    extra = len(UP)
    for plane in (to_near, to_next):
        plane[extra] = jnp.zeros(plane.shape[1:], f32)
        plane[extra, :, 0:WIDTH] = spots
        plane[extra, :, WIDTH : 2 * WIDTH] = coeffs
    for z in range(layers):
        for start in range(0, along, WIDTH):
            lanes = slice(start, start + WIDTH)
            out = collide(
                [pops[i, z, :, lanes] for i in range(FLOWS)],
                [heat[j, z, :, lanes] for j in range(HEATS)],
                solid[z, :, lanes],
            )
            for i in LANES_ALL:
                post[i, z, :, lanes] = out[i]
    for n, (above, below) in enumerate(zip(UP, DOWN)):
        above, below = post[above, layers - 1], post[below, 0]
        to_near[n] = jnp.where(even, above, below)
        to_next[n] = jnp.where(even, below, above)


def edge_kernel(post, shares, solid, face_r, face_l, out_r, out_l):
    layers, across, along = post.shape[1:]
    for out, lists, edge, inside in (
        (out_r, (STILL, RIGHT), across - 1, across - 2),
        (out_l, (STILL, LEFT), 0, 1),
    ):
        rows = [(i, edge) for i in lists[0]] + [(i, inside) for i in lists[1]]
        rows = rows + [(i, edge) for i in lists[1]]
        for n, (i, column) in enumerate(rows):
            for z in range(layers):
                at, source = n * layers + z, z - VELOCITY[i][2]
                if 0 <= source < layers:
                    out[at : at + 1, :] = post[i, source, column : column + 1, :]
                else:
                    out[at : at + 1, :] = jnp.zeros((1, along), f32)

    def both(n):
        at = slice(n * layers, (n + 1) * layers)
        return jnp.concatenate([out_r[at, :], out_l[at, :]], axis=0)

    def send(n, tile):
        at = slice(n * layers, (n + 1) * layers)
        face_r[at, :], face_l[at, :] = tile[0:layers], tile[layers : 2 * layers]

    sums = [[] for _ in range(SUMS)]
    for n, i in enumerate(STILL):
        _, ey, ez = VELOCITY[i]
        tile = turned(both(n), ey)
        if i >= FLOWS:
            sums[3].append((1, tile))
        else:
            sums[0].append((1, tile))
            sums[1].append((ey, tile))
            sums[2].append((ez, tile))
    for n in range(SUMS):
        send(n, signed_sum(sums[n]))
    for n, i in enumerate(RIGHT):
        send(SUMS + n, turned(both(len(STILL) + n), VELOCITY[i][1]))
    for n in range(len(STILL) + len(RIGHT), GATHERED):
        send(n - len(STILL) + SUMS, both(n))
    even = on_even()
    for n, (face, column) in enumerate(((face_r, across - 1), (face_l, 0))):
        for z in range(layers):
            at = (FACE - 1) * layers + z
            face[at : at + 1, :] = solid[z, column : column + 1, :]
        far = shares[8 * n : 8 * n + CORNER]
        add_corners(face, jnp.where(even, far, 0.0), jnp.where(even, 0.0, far), layers)


def side_kernel(layers, near, face_r, face_l, to_a, to_b, sum_r, sum_l):
    even, band_even = on_even(), on_even("grp")
    sides = zip((face_r, face_l), (sum_r, sum_l), corner_shares(near))
    for face, total, close in sides:
        total[...] = face[...]
        add_corners(total, jnp.where(even, 0.0, close), jnp.where(even, close, 0.0), layers)
    right, left = sum_r[...], sum_l[...]
    to_a[...] = jnp.where(band_even, right, left)
    to_b[...] = jnp.where(band_even, left, right)


def second_kernel(
    post,
    near,
    next_,
    to_a,
    to_b,
    faces_a,
    faces_b,
    solid,
    own_table,
    tie,
    hot,
    motion,
    send_near,
    send_next,
    fluxes,
    moved,
    halo,
    own_r,
    own_l,
    from_l,
    from_r,
):
    layers, across, along = solid.shape
    even = on_even()
    band_even = on_even("grp")
    own_r[...] = jnp.where(band_even, to_a[...], to_b[...])
    own_l[...] = jnp.where(band_even, to_b[...], to_a[...])
    below = [jnp.where(even, next_[n], near[n]) for n in range(len(UP) + 1)]
    above = [jnp.where(even, near[n], next_[n]) for n in range(len(UP) + 1)]
    from_l[...] = jnp.where(band_even, faces_b[...], faces_a[...])
    from_r[...] = jnp.where(band_even, faces_a[...], faces_b[...])
    slot = lax.broadcasted_iota(jnp.int32, (across, along), 0)
    edge = SUMS + len(RIGHT)
    for i in LANES_ALL:
        ex, ey, ez = VELOCITY[i]
        for z in range(layers):
            if z - ez < 0:
                tile = below[UP.index(i)]
            elif z - ez >= layers:
                tile = above[DOWN.index(i)]
            else:
                tile = post[i, z - ez]
            if ex == 1:
                at = (edge + RIGHT.index(i)) * layers + z
                tile = jnp.where(slot == 0, from_l[at : at + 1, :], pltpu.roll(tile, 1, 0))
            elif ex == -1:
                at = (edge + LEFT.index(i)) * layers + z
                tile = jnp.where(
                    slot == across - 1, from_r[at : at + 1, :], pltpu.roll(tile, across - 1, 0)
                )
            moved[i, z] = turned(tile, ey)

    def halves(low, high, n):
        at = slice(n * layers, (n + 1) * layers)
        parts = [low[at, :], high[at, :]]
        if 2 * layers < 8:
            parts.append(jnp.ones((8 - 2 * layers, along), f32))
        return jnp.concatenate(parts, axis=0)

    for n in range(edge):
        halo[n] = halves(from_l, from_r, n)
    for n, i in enumerate(RIGHT):
        halo[edge + n] = turned(halves(own_l, own_r, edge + n), VELOCITY[i][1])
    edge_solid = halves(from_l, from_r, FACE - 1)
    for start in range(0, along, WIDTH):
        lanes = slice(start, start + WIDTH)
        for z in range(layers):
            out = collide(
                [moved[i, z, :, lanes] for i in range(FLOWS)],
                [moved[FLOWS + j, z, :, lanes] for j in range(HEATS)],
                solid[z, :, lanes],
            )
            for i in LANES_ALL:
                moved[i, z, :, lanes] = out[i]
        out = collide_halo(
            [halo[n, :, lanes] for n in range(SUMS)],
            [halo[SUMS + n, :, lanes] for n in range(len(RIGHT))],
            [halo[edge + n, :, lanes] for n in range(len(RIGHT))],
            edge_solid[:, lanes],
        )
        for n in range(len(RIGHT)):
            halo[SUMS + n, :, lanes] = out[n]
    sums = {}

    def add(key, sign, tile):
        if sign == 0:
            return
        if key in sums:
            sums[key] = sums[key] + tile if sign > 0 else sums[key] - tile
        else:
            sums[key] = tile if sign > 0 else -tile

    for z in range(layers):
        for i in LANES_ALL:
            ex, ey, ez = VELOCITY[i]
            if i == 0:
                continue
            tile = moved[i, z]
            if ex == 1:
                side = halo[SUMS + RIGHT.index(i), z : z + 1, :]
                tile = jnp.where(slot == 0, side, pltpu.roll(tile, 1, 0))
            elif ex == -1:
                at = layers + z
                side = halo[SUMS + LEFT.index(i), at : at + 1, :]
                tile = jnp.where(slot == across - 1, side, pltpu.roll(tile, across - 1, 0))
            tile = turned(tile, ey)
            target = z + ez
            if i >= FLOWS:
                add((3, target), 1, tile)
            else:
                add((0, target), ex, tile)
                add((1, target), ey, tile)
                add((2, target), ez, tile)
    for z in range(layers):
        hot[z] = sums[3, z]
        for axis in range(3):
            motion[axis, z] = sums[axis, z]
    for part in range(4):
        send_near[part] = jnp.where(even, sums[part, layers], sums[part, -1])
        send_next[part] = jnp.where(even, sums[part, -1], sums[part, layers])
    extra = len(UP)
    per_line = along // WIDTH
    per_layer = across * per_line

    def flux(table, planes):
        index = table[:, 0:WIDTH].astype(jnp.int32)
        place, lane = index >> 7, index & 127
        out = jnp.zeros(lane.shape, f32)
        for z, plane in planes:
            for x in range(across):
                for c in range(per_line):
                    row = plane[x : x + 1, c * WIDTH : (c + 1) * WIDTH]
                    out = jnp.where(
                        place == z * per_layer + x * per_line + c, lane_gather(row, lane), out
                    )
        return out * table[:, WIDTH : 2 * WIDTH]

    mine = own_table[extra]
    fluxes[plane_rows(0), :] = flux(mine, [(z, sums[3, z]) for z in range(layers)])
    fluxes[plane_rows(1), :] = flux(above[extra], [(0, sums[3, layers])])
    fluxes[plane_rows(2), :] = flux(below[extra], [(layers - 1, sums[3, -1])])
    fluxes[plane_rows(3), :] = mine[:, WIDTH : 2 * WIDTH]


def sublane_gather(value, index):
    return jnp.take_along_axis(value, index, axis=0, mode="promise_in_bounds")


def coupled(vector, blocks, flipped, shift):
    count = vector.shape[0]
    upright = vector.T
    ahead, back = [], []
    for b in range(count):
        column = jnp.broadcast_to(upright[:, b : b + 1], blocks.shape[1:])
        back.append(jnp.sum(blocks[b] * column, axis=0, keepdims=True))
        ahead.append(jnp.sum(flipped[b] * column, axis=0, keepdims=True))
    ahead = jnp.concatenate(ahead, axis=0)
    back = jnp.concatenate(back, axis=0)
    block = lax.broadcasted_iota(jnp.int32, vector.shape, 0)
    ahead = sublane_gather(ahead, (block + shift) & (count - 1))
    return ahead + sublane_gather(back, (block - shift) & (count - 1))


def ready_kernel(
    pattern, nodes, diagonal, source, start, coupling, tie, hits, flipped, rest, slots, turn
):
    shift = pattern[0, 0]
    turn[...] = jnp.full(turn.shape, shift, jnp.int32)
    count = start.shape[1]
    for b in range(count):
        flipped[lax.rem(b + shift, count)] = coupling[0, b].T
    vector = start[0]
    rest[...] = (
        source[0] - diagonal[0] * vector + coupled(vector, coupling.at[0], flipped, turn[...])
    )
    index = stacked(nodes[...])
    slots[...] = table_gather(vector, index)
    upright = (index & 127).astype(f32).T.astype(jnp.int32)
    lane = lax.broadcasted_iota(jnp.int32, (WIDTH, WIDTH), 1)
    for s in range(index.shape[0]):
        hit = jnp.where(upright[:, s : s + 1] == lane, 1.0, 0.0)
        hits[s * WIDTH : (s + 1) * WIDTH] = hit.astype(bf16)


def solve_kernel(
    cap,
    turn,
    nodes,
    diagonal,
    start,
    coupling,
    hits,
    flipped,
    rest,
    slots,
    come,
    res,
    img,
    go,
):
    shift = turn[...]
    count = start.shape[1]
    index = stacked(nodes[...])
    place = index >> 7
    own, low, high, coeff = (come[plane_rows(plane), :] for plane in range(4))
    if cap == WIDTH:
        low = pltpu.roll(low, 1, 0)
        high = pltpu.roll(high, low.shape[0] - 1, 0)
    parts = two_parts(own + low + high) + two_parts(coeff)
    block = lax.broadcasted_iota(jnp.int32, (count, WIDTH), 0)
    values = []
    for s in range(index.shape[0]):
        mine = block == place[s : s + 1]
        values.append(
            jnp.concatenate([jnp.where(mine, part[s : s + 1], 0.0) for part in parts], axis=0)
        )
    values = jnp.concatenate(values, axis=1).astype(bf16)
    landed = jnp.dot(values, hits[...], preferred_element_type=f32)
    landed = [landed[k * count : (k + 1) * count] for k in range(len(parts))]
    added = landed[0] + landed[1]
    extra = landed[2] + landed[3]
    whole = diagonal[0] + extra
    blocks = coupling.at[0]
    residual = rest[...] + added - extra * start[0]
    image = whole * residual - coupled(residual, blocks, flipped, shift)

    def total(value):
        return jnp.sum(jnp.sum(value, axis=0, keepdims=True), axis=1, keepdims=True)

    offset = image - SHIFT * residual
    bend = whole * offset - coupled(offset, blocks, flipped, shift)
    totals = [
        total(residual * residual),
        total(residual * offset),
        total(offset * offset),
        total(offset * bend),
    ]
    res[...] = residual
    img[...] = image
    lane = lax.broadcasted_iota(jnp.int32, (8, WIDTH), 1) & (cap - 1)
    facts = jnp.zeros((8, WIDTH), f32)
    for n, fact in enumerate(totals):
        facts = jnp.where(lane == n, fact, facts)
    residual_slots = table_gather(residual, index)
    image_slots = table_gather(image, index)
    start_slots = slots[...]
    for group in range(0, go.shape[0] // 4, 8):
        go[plane_rows(0, group), :] = start_slots
        go[plane_rows(1, group), :] = residual_slots
        go[plane_rows(2, group), :] = image_slots
        go[plane_rows(3, group), :] = facts


def last_kernel(direct, come, own, start, res, img, ordinal, temp, seen, mine):
    places = stacked(ordinal[...])
    chunks = places.shape[0]
    if chunks < 8:
        places = jnp.concatenate([places, jnp.zeros((8 - chunks, WIDTH), jnp.int32)], axis=0)
    strip = own
    if direct:
        strip = mine
        first = lax.axis_index("grp") * strip.shape[0]
        strip[...] = come[pl.ds(pl.multiple_of(first, 8), strip.shape[0]), :]
    found = [table_gather(strip[plane_rows(plane), :], places) for plane in range(3)]
    facts = come[plane_rows(3, 0, come.shape[0] // 4), :]
    facts = jnp.sum(facts, axis=0, keepdims=True)
    all_norm, cross, square, energy = (
        lane_gather(facts, jnp.full((8, WIDTH), n, jnp.int32)) for n in range(4)
    )
    product = SHIFT * all_norm + cross
    inverse = 1.0 / product
    ratio = cross / all_norm
    spread_square = square - cross * ratio
    energy = energy - ratio * (2.0 * (square + SHIFT * cross) - ratio * product)
    small = spread_square * inverse
    first = all_norm * inverse
    step = spread_square / (energy - spread_square * small)
    of_residual = first + step * (1.0 + small * first)
    of_image = -step * first
    temp[0] = start[0] + of_residual * res[...] + of_image * img[...]
    found = found[0] + of_residual * found[1] + of_image * found[2]
    for c in range(chunks):
        seen[:, c * WIDTH : (c + 1) * WIDTH] = found[c : c + 1]


def join_kernel(hot, motion, near, next_, hot_out, motion_out):
    layers = hot.shape[0]
    even = on_even()
    below = [jnp.where(even, next_[n], near[n]) for n in range(4)]
    above = [jnp.where(even, near[n], next_[n]) for n in range(4)]
    for z in range(layers):
        for part in range(4):
            tile = hot[z] if part == 3 else motion[part, z]
            if z == 0:
                tile = tile + below[part]
            if z == layers - 1:
                tile = tile + above[part]
            if part == 3:
                hot_out[z] = tile
            else:
                motion_out[part, z] = tile


VMEM = pl.BlockSpec(memory_space=pltpu.VMEM)
ANYWHERE = pl.BlockSpec(memory_space=pl.ANY)
SMEM = pl.BlockSpec(memory_space=pltpu.SMEM)


def call(kernel, out, args, name, scalars=(), scratch=(), far=False, flops=1 << 20):
    total = sum(int(np.prod(a.shape)) * a.dtype.itemsize for a in list(args) + list(out))
    if far:
        args = [pltpu.with_memory_space_constraint(a, pltpu.HBM) for a in args]
    return pl.pallas_call(
        kernel,
        out_shape=out,
        in_specs=[
            ANYWHERE if far else SMEM if n in scalars else VMEM for n in range(len(args))
        ],
        out_specs=[VMEM] * len(out),
        scratch_shapes=scratch,
        compiler_params=pltpu.CompilerParams(vmem_limit_bytes=24 << 20),
        cost_estimate=pl.CostEstimate(flops=flops, bytes_accessed=total, transcendentals=0),
        name=name,
    )(*args)


def shape(*dims, dtype=f32):
    return jax.ShapeDtypeStruct(dims, dtype)


def swaps(axis):
    count = lax.axis_size(axis)
    assert count % 2 == 0
    near = [(k, k + 1 - 2 * (k % 2)) for k in range(count)]
    return near, [(k, (k - 1 + 2 * (k % 2)) % count) for k in range(count)]


def body(
    populations,
    heat_pops,
    solid_frac,
    coupled_grid_point,
    dest_index,
    heat_coeff,
    slot_node,
    node_diag,
    coupling,
    block_pattern,
    heat_source,
    solid_start,
):
    layers, across, along = solid_frac.shape
    slabs, bands = lax.axis_size("sub"), lax.axis_size("grp")
    slots = slot_node.shape[1]
    cap = slots // slabs
    rows = coupled_grid_point.shape[1]
    blocks, piece = node_diag.shape[1:]
    lines = slots // WIDTH
    assert lines == 8 and across == 8 and along >= 2 * WIDTH and along % WIDTH == 0
    assert piece == WIDTH and blocks == 8 and WIDTH % cap == 0 and cap >= 8
    assert rows % WIDTH == 0 and rows <= 8 * WIDTH and layers <= 4
    gathered_rows = -(-GATHERED * layers // 8) * 8
    face_rows = -(-FACE * layers // 8) * 8
    planes = len(UP) + 1
    near_pairs, next_pairs = swaps("sub")
    pops_here, heat_here, solid_here, voxel, dest, coeff, to_shares = call(
        early_kernel,
        [
            shape(*populations.shape),
            shape(*heat_pops.shape),
            shape(*solid_frac.shape),
            shape(1, rows, dtype=jnp.int32),
            shape(1, rows, dtype=jnp.int32),
            shape(1, rows),
            shape(16, along),
        ],
        [
            populations,
            heat_pops,
            solid_frac,
            coupled_grid_point,
            dest_index.reshape(1, rows),
            heat_coeff,
        ],
        "collide_early",
        scratch=[
            pltpu.VMEM((len(UP), across, along), f32),
            pltpu.SemaphoreType.DMA((3 * layers + 3,)),
        ],
        far=True,
    )
    shares = lax.ppermute(to_shares, "sub", next_pairs)
    post, to_near, to_next, ordinal = call(
        functools.partial(first_kernel, cap),
        [
            shape(FLOWS + HEATS, layers, across, along),
            shape(planes, across, along),
            shape(planes, across, along),
            shape(1, rows, dtype=jnp.int32),
        ],
        [
            pops_here,
            heat_here,
            solid_here,
            voxel,
            dest,
            coeff,
        ],
        "collide_first",
    )
    near = lax.ppermute(to_near, "sub", near_pairs)
    next_ = lax.ppermute(to_next, "sub", next_pairs)
    faces = [shape(face_rows, along)] * 2
    face_r, face_l = call(
        edge_kernel,
        faces,
        [post, shares, solid_here],
        "x_faces",
        scratch=[pltpu.VMEM((gathered_rows, along), f32)] * 2,
        flops=1 << 32,
    )
    to_a, to_b = call(
        functools.partial(side_kernel, layers),
        faces,
        [near, face_r, face_l],
        "x_sides",
        scratch=[pltpu.VMEM((face_rows, along), f32)] * 2,
    )
    side_a, side_b = swaps("grp")
    faces_a = lax.ppermute(to_a, "grp", side_a)
    faces_b = lax.ppermute(to_b, "grp", side_b)
    hits, flipped, rest, start_slots, turn = call(
        ready_kernel,
        [
            shape(slots, WIDTH, dtype=bf16),
            shape(blocks, piece, piece),
            shape(blocks, piece),
            shape(lines, WIDTH),
            shape(blocks, WIDTH, dtype=jnp.int32),
        ],
        [block_pattern, slot_node, node_diag, heat_source, solid_start, coupling, to_a],
        "solid_ready",
        scalars=(0,),
    )
    hot, motion, send_near, send_next, fluxes = call(
        second_kernel,
        [
            shape(layers, across, along),
            shape(3, layers, across, along),
            shape(4, across, along),
            shape(4, across, along),
            shape(4 * lines, WIDTH),
        ],
        [
            post,
            near,
            next_,
            to_a,
            to_b,
            faces_a,
            faces_b,
            solid_here,
            to_next,
            rest,
        ],
        "collide_second",
        scratch=[
            pltpu.VMEM((FLOWS + HEATS, layers, across, along), f32),
            pltpu.VMEM((FACE, 8, along), f32),
        ]
        + [pltpu.VMEM((face_rows, along), f32)] * 4,
    )
    settled = cap != WIDTH
    if settled:
        fluxes = fluxes.reshape(lines, 4, WIDTH // cap, cap).transpose(0, 2, 1, 3)
    fluxes = fluxes.reshape(slabs, 4, cap)
    landed = lax.all_to_all(fluxes, "sub", split_axis=0, concat_axis=0, tiled=True)
    if settled:
        landed = jnp.stack(
            [
                landed[:, 0],
                jnp.roll(landed[:, 1], 1, axis=0),
                jnp.roll(landed[:, 2], -1, axis=0),
                landed[:, 3],
            ]
        )
        landed = landed.reshape(4, lines, WIDTH).transpose(1, 0, 2)
    landed = landed.reshape(4 * lines, WIDTH)
    from_near = lax.ppermute(send_near, "sub", near_pairs)
    from_next = lax.ppermute(send_next, "sub", next_pairs)
    residual, image, go = call(
        functools.partial(solve_kernel, cap),
        [shape(blocks, piece), shape(blocks, piece), shape(bands * lines * 4, WIDTH)],
        [
            turn,
            slot_node,
            node_diag,
            solid_start,
            coupling,
            hits,
            flipped,
            rest,
            start_slots,
            landed,
        ],
        "solve",
    )
    if settled:
        go = go.reshape(bands, lines, 4, WIDTH // cap, cap).transpose(0, 1, 3, 2, 4)
    go = go.reshape(bands * slabs, 4, cap)
    come = lax.all_to_all(go, ("grp", "sub"), split_axis=0, concat_axis=0, tiled=True)
    hot_out, motion_out = call(
        join_kernel,
        [shape(*hot.shape), shape(*motion.shape)],
        [hot, motion, from_near, from_next],
        "join",
    )
    if settled:
        own = lax.dynamic_slice_in_dim(come, lax.axis_index("grp") * slabs, slabs, 0)
        own = own.transpose(1, 0, 2).reshape(4, lines, WIDTH).transpose(1, 0, 2)
        own = own.reshape(4 * lines, WIDTH)
        come = jnp.pad(come, ((0, 0), (0, 0), (0, WIDTH - cap)))
    else:
        own = rest
    come = come.reshape(4 * bands * slabs, WIDTH)
    temp, seen = call(
        functools.partial(last_kernel, not settled),
        [shape(1, blocks, piece), shape(1, rows)],
        [
            come,
            own,
            solid_start,
            residual,
            image,
            ordinal,
        ],
        "finish",
        scratch=[pltpu.VMEM((4 * lines, WIDTH), f32)],
    )
    return hot_out, motion_out, temp, seen


def solution(mesh):
    placed = (
        P(None, "sub", "grp", None),
        P(None, "sub", "grp", None),
        P("sub", "grp", None),
        P("grp", "sub"),
        P("grp", "sub", None),
        P("grp", "sub"),
        P("grp", "sub"),
        P("grp", "sub", None),
        P("grp", "sub", None, None),
        P("grp", "sub"),
        P("grp", "sub", None),
        P("grp", "sub", None),
    )
    return jax.shard_map(
        body,
        mesh=mesh,
        in_specs=placed,
        out_specs=(
            P("sub", "grp", None),
            P(None, "sub", "grp", None),
            P("grp", "sub", None),
            P("grp", "sub"),
        ),
        check_vma=False,
    )
```
